32 devices in a mesh: dp: 8 (over y, x, core), fsdp: 4 (over z).
Axes of the slice: x: 2, y: 2, z: 4, core: 2. Of those that a mesh axis runs over, the one named last changes fastest.
Arguments:
- query_pooled_states: bfloat16 [4, 128, 4096], P('fsdp', 'dp')
- passage_pooled_states: bfloat16 [4, 1024, 4096], P('fsdp', 'dp')
- query_attention_output: bfloat16 [4, 128, 4096], P('fsdp', 'dp'), may hold values from -0.059814453 to 0.059814453
- passage_attention_output: bfloat16 [4, 1024, 4096], P('fsdp', 'dp'), may hold values from -0.059814453 to 0.059814453
- positive_passage_row: int32 [4, 128], P('fsdp', 'dp'), may hold values from 0 to 127
- hard_negative_ids: int32 [4, 128, 64], P('fsdp', 'dp'), may hold values from 0 to 1023, as said below
- passage_home_row: int32 [4, 1024], P('fsdp'), may hold values from 0 to 1023, as said below
- adapter_down_weight: bfloat16 [16, 4096], P(None, 'fsdp'), may hold values from -0.09375 to 0.09375
- adapter_up_weight: bfloat16 [16, 4096], P(None, 'fsdp'), may hold values from -0.09375 to 0.09375
Outputs:
- grad_query_states: bfloat16 [4, 128, 4096], P('fsdp', 'dp')
- grad_passage_states: bfloat16 [4, 1024, 4096], P('fsdp', 'dp')
- adapter_down_gradient: float32 [16, 4096], P(None, 'fsdp')
- adapter_up_gradient: float32 [16, 4096], P(None, 'fsdp')
The draws below stay inside these ranges and needn't reach their ends.
Inputs may be any that keep to these rules, and one draw needn't show every extreme that they name: In each group the row is a permutation: passage p is row passage_home_row[g, p] of passage_pooled_states[g]. `hard_negative_ids`: ids of passages of the same group. The queries of one index of dp name at most 8 distinct passages held by any one index of dp, and in every group one index of dp holds exactly 8 distinct passages named by the queries of each index of dp. A query's list may repeat an id. `positive_passage_row`: the positive of query q is held by the query's own index of dp.
All inputs are finite; a program needn't handle non-finite values.
Results may differ from the reference program's by a relative error of at most 0.0062.
Values may be sent and summed in bfloat16 or wider, within the bound.
No kernel may reach another device: no remote copies, remote signals or barrier semaphores. Data moves between devices by JAX's collectives and lax.ppermute only.
A program may use at most 64 MiB of HBM per device.

```python
import jax
import jax.numpy as jnp
from jax import lax

MODEL_WIDTH = 4096
ADAPTER_RANK = 16
NEG = 64
CAP = 8
Q_DEV = 16
P_DEV = 128
QUERIES = 128
PASSAGES = 1024
N_DP = 8
N_FSDP = 4


def layout_tables(key):
    home_keys = jax.random.split(jax.random.fold_in(key, 101), N_FSDP)
    home_rows = jax.vmap(lambda single: jax.random.permutation(single, PASSAGES))(home_keys).astype(jnp.int32)
    counts = jax.random.randint(jax.random.fold_in(key, 102), (N_FSDP, N_DP, N_DP), 1, CAP + 1)
    hottest = jax.random.randint(jax.random.fold_in(key, 103), (N_FSDP, 1, 1), 0, N_DP)
    counts = jnp.where(jnp.arange(N_DP)[None, None, :] == hottest, CAP, counts)
    keyed = jax.random.randint(jax.random.fold_in(key, 104), (N_FSDP, N_DP, N_DP, P_DEV), 0, 2 ** 20) * P_DEV + jnp.arange(P_DEV, dtype=jnp.int32)
    unused_top, chosen = lax.top_k(keyed, CAP)
    picked_rows = jnp.arange(N_DP, dtype=jnp.int32)[None, None, :, None] * P_DEV + chosen.astype(jnp.int32)
    usable = jnp.arange(CAP)[None, None, None, :] < counts[..., None]
    flat_width = N_DP * CAP
    picked_rows = picked_rows.reshape(N_FSDP, N_DP, flat_width)
    usable = usable.reshape(N_FSDP, N_DP, flat_width)
    ranks = jnp.cumsum(usable.astype(jnp.int32), axis=-1) - 1
    targets = jnp.where(usable, ranks, flat_width)
    group_ids = jnp.broadcast_to(jnp.arange(N_FSDP)[:, None, None], targets.shape)
    device_ids = jnp.broadcast_to(jnp.arange(N_DP)[None, :, None], targets.shape)
    pool_rows = jnp.zeros((N_FSDP, N_DP, flat_width), jnp.int32).at[group_ids, device_ids, targets].set(picked_rows, mode='drop')
    live_count = jnp.sum(usable.astype(jnp.int32), axis=-1)
    asks = Q_DEV * NEG
    picks = jax.random.randint(jax.random.fold_in(key, 105), (N_FSDP, N_DP, asks), 0, live_count[..., None])
    positions = jnp.arange(asks, dtype=jnp.int32)
    picks = jnp.where(positions[None, None, :] < live_count[..., None], positions[None, None, :], picks)
    shuffle_keys = jax.random.randint(jax.random.fold_in(key, 106), (N_FSDP, N_DP, asks), 0, 2 ** 16) * asks + positions
    ordering = jnp.argsort(shuffle_keys, axis=-1)
    picks = jnp.take_along_axis(picks, ordering, axis=-1)
    wanted_rows = jnp.take_along_axis(pool_rows, picks, axis=-1)
    inverse_home = jnp.argsort(home_rows, axis=-1).astype(jnp.int32)
    passage_ids = jnp.take_along_axis(inverse_home, wanted_rows.reshape(N_FSDP, N_DP * asks), axis=1)
    return (home_rows, passage_ids.reshape(N_FSDP, QUERIES, NEG).astype(jnp.int32))


def passage_base(key):
    return jax.random.normal(jax.random.fold_in(key, 204), (N_FSDP, PASSAGES, MODEL_WIDTH))


def draw_passage_home_row(key, part):
    return layout_tables(key)[0]


def draw_hard_negative_ids(key, part):
    return layout_tables(key)[1]


def draw_passage_pooled_states(key, part):
    return passage_base(key).astype(jnp.bfloat16)


def draw_query_pooled_states(key, part):
    return jax.random.normal(jax.random.fold_in(key, 213), (N_FSDP, QUERIES, MODEL_WIDTH)).astype(jnp.bfloat16)


def with_ends(drawn, key, smallest, largest):
    longest = drawn.shape.index(max(drawn.shape))
    spots = []
    for shift in (0, 1):
        where = [jax.random.randint(jax.random.fold_in(key, axis), (), 0, length) for axis, length in enumerate(drawn.shape)]
        where[longest] = (where[longest] + shift) % drawn.shape[longest]
        spots.append(tuple(where))
    return drawn.at[spots[0]].set(smallest).at[spots[1]].set(largest)


def raised(drawn, key, source, target, blocks, factor):
    def block_of(axis_at):
        return (jnp.arange(drawn.shape[axis_at]) // (drawn.shape[axis_at] // blocks)).reshape((-1,) + (1,) * (drawn.ndim - 1 - axis_at))

    first = jax.random.permutation(key, blocks)[block_of(target)]
    second = (block_of(target) + blocks // 2) % blocks
    return jnp.where((block_of(source) == first) | (block_of(source) == second), factor * drawn, drawn)


def shard_levels(stream_key, extent, shards, low, top_value):
    def one(dim, parts):
        draws = jax.random.uniform(jax.random.fold_in(jax.random.fold_in(stream_key, 6), dim), (parts,), jnp.float32, low / len(shards), top_value / len(shards))
        return jnp.repeat(jnp.exp(draws), extent[dim] // parts).reshape((-1,) + (1,) * (len(extent) - dim - 1))

    level = one(*shards[0])
    for cut in shards[1:]:
        level = level * one(*cut)
    return level


def centred(stream_key, shape, spread, reach, shards=(), held_as=jnp.bfloat16):
    loudness = shard_levels(stream_key, shape, shards, -0.22, 0.18) if shards else 1.0
    array = jax.random.normal(stream_key, shape, jnp.float32) * spread * loudness
    return jnp.minimum(jnp.maximum(array, -reach), reach).astype(held_as)


def heavy_noise(rng, extent, deviation, limit, cuts, heavy, kind=jnp.bfloat16):
    array = deviation * jax.random.normal(rng, extent, jnp.float32)
    if cuts:
        array = array * shard_levels(rng, extent, cuts, -0.22, 0.18)
    return jnp.clip(raised(array, jax.random.fold_in(rng, 3), *heavy), -limit, limit).astype(kind)


def setup_inputs(seed: int = 0) -> dict:
    splits = jax.random.split(jax.random.key(seed), 10)
    query_pooled_states = draw_query_pooled_states(jax.random.fold_in(splits[9], 71), 0)
    passage_pooled_states = draw_passage_pooled_states(jax.random.fold_in(splits[9], 71), 0)
    query_attention_output = heavy_noise(splits[2], (N_FSDP, QUERIES, MODEL_WIDTH), 0.01, 0.059814453, ((0, 4), (1, 8)), (0, 2, 4, 2.0))
    passage_attention_output = heavy_noise(splits[3], (N_FSDP, PASSAGES, MODEL_WIDTH), 0.01, 0.059814453, ((0, 4), (1, 8)), (0, 2, 4, 2.0))
    positive_passage_row = with_ends(jax.random.randint(splits[4], (N_FSDP, QUERIES), 0, P_DEV), jax.random.fold_in(splits[4], 1), 0, P_DEV - 1).astype(jnp.int32)
    hard_negative_ids = draw_hard_negative_ids(jax.random.fold_in(splits[9], 71), 0)
    passage_home_row = draw_passage_home_row(jax.random.fold_in(splits[9], 71), 0)
    adapter_down_weight = centred(splits[7], (ADAPTER_RANK, MODEL_WIDTH), MODEL_WIDTH ** -0.5, 0.09375, ((1, 4),))
    adapter_up_weight = centred(splits[8], (ADAPTER_RANK, MODEL_WIDTH), MODEL_WIDTH ** -0.5, 0.09375, ((1, 4),))
    return dict(query_pooled_states=query_pooled_states, passage_pooled_states=passage_pooled_states, query_attention_output=query_attention_output, passage_attention_output=passage_attention_output, positive_passage_row=positive_passage_row, hard_negative_ids=hard_negative_ids, passage_home_row=passage_home_row, adapter_down_weight=adapter_down_weight, adapter_up_weight=adapter_up_weight)


SOFTMAX_HEAT = 0.01
ADAPTER_SCALE = 2.0
EPSILON = 1e-06

def unit_rows(raw_rows):
    values = raw_rows.astype(jnp.float32)
    lengths = jnp.sqrt(lax.optimization_barrier(jnp.sum(values * values, axis=-1, keepdims=True)) + EPSILON)
    return (values / lengths, lengths)

def norm_backward(unit_vec, lengths, upstream):
    inner_sum = lax.optimization_barrier(jnp.sum(unit_vec * upstream, axis=-1, keepdims=True))
    return ((upstream - unit_vec * inner_sum) / lengths).astype(jnp.bfloat16)

def reference(query_pooled_states, passage_pooled_states, query_attention_output, passage_attention_output, positive_passage_row, hard_negative_ids, passage_home_row, adapter_down_weight, adapter_up_weight):

    def one_group(inputs):
        query_raw, passage_raw, query_input_rows, passage_input_rows, positives, negatives, home_rows = inputs
        query_unit, query_length = unit_rows(query_raw)
        passage_unit, passage_length = unit_rows(passage_raw)
        query_vectors = query_unit.astype(jnp.bfloat16)
        passage_vectors = passage_unit.astype(jnp.bfloat16)
        query_index = jnp.arange(QUERIES, dtype=jnp.int32)
        positive_row = (query_index // Q_DEV * P_DEV + positives).astype(jnp.int32)
        negative_rows = home_rows[negatives].astype(jnp.int32)
        candidates = jnp.concatenate([positive_row[:, None], negative_rows], axis=1)
        score_matrix = jnp.dot(query_vectors, passage_vectors.T, preferred_element_type=jnp.float32) / SOFTMAX_HEAT
        scores = jnp.take_along_axis(score_matrix, candidates, axis=1)
        softmax_probabilities = jax.nn.softmax(scores, axis=-1)
        target_index = (jnp.arange(NEG + 1) == 0).astype(jnp.float32)
        score_gradient = (softmax_probabilities - target_index[None, :]) / SOFTMAX_HEAT
        pair_weight = jnp.zeros((QUERIES, PASSAGES), jnp.float32).at[query_index[:, None], candidates].add(score_gradient)
        query_upstream = jnp.dot(pair_weight, passage_vectors.astype(jnp.float32), precision=lax.Precision.HIGHEST)
        passage_upstream = jnp.dot(pair_weight.T, query_vectors.astype(jnp.float32), precision=lax.Precision.HIGHEST)
        query_gradient = norm_backward(query_unit, query_length, query_upstream)
        passage_gradient = norm_backward(passage_unit, passage_length, passage_upstream)
        input_stack = jnp.concatenate([query_input_rows, passage_input_rows], axis=0)
        gradient_stack = jnp.concatenate([query_gradient, passage_gradient], axis=0)
        rank_projection = jnp.dot(input_stack, adapter_down_weight.T, preferred_element_type=jnp.float32).astype(jnp.bfloat16)
        up_sum = jnp.dot(rank_projection.T, gradient_stack, preferred_element_type=jnp.float32)
        rank_gradient = jnp.dot(gradient_stack, adapter_up_weight.T, preferred_element_type=jnp.float32).astype(jnp.bfloat16)
        down_sum = jnp.dot(rank_gradient.T, input_stack, preferred_element_type=jnp.float32)
        return (query_gradient, passage_gradient, down_sum, up_sum)
    output_tuple = lax.map(one_group, (query_pooled_states, passage_pooled_states, query_attention_output, passage_attention_output, positive_passage_row, hard_negative_ids, passage_home_row))
    adapter_down_gradient = ADAPTER_SCALE * lax.optimization_barrier(jnp.sum(output_tuple[2], axis=0))
    adapter_up_gradient = ADAPTER_SCALE * lax.optimization_barrier(jnp.sum(output_tuple[3], axis=0))
    return (output_tuple[0], output_tuple[1], adapter_down_gradient, adapter_up_gradient)
```

```python
import functools

import jax
import jax.numpy as jnp
from jax import lax
from jax.experimental import pallas as pl
from jax.experimental.pallas import tpu as pltpu
from jax.sharding import PartitionSpec as P

CAP = 8
SOFTMAX_HEAT = 0.01
ADAPTER_SCALE = 2.0
EPSILON = 1e-06
LOWEST = -1e30
MSG_ROWS = 16
VMEM_BYTES = 40 * 1024 * 1024
F32 = jnp.float32
BF16 = jnp.bfloat16
HIGHEST = lax.Precision.HIGHEST


def dot_nn(a, b, precision=None):
    return lax.dot_general(
        a, b, (((1,), (0,)), ((), ())), precision=precision, preferred_element_type=F32
    )


def dot_nt(a, b, precision=None):
    return lax.dot_general(
        a, b, (((1,), (1,)), ((), ())), precision=precision, preferred_element_type=F32
    )


def split_two(values):
    high = values.astype(BF16)
    low = (values - high.astype(F32)).astype(BF16)
    return high, low


def kernel_call(body, out_shape, n_in, flops, nbytes, scratch=()):
    return pl.pallas_call(
        body,
        out_shape=out_shape,
        in_specs=[pl.BlockSpec(memory_space=pltpu.VMEM)] * n_in,
        out_specs=jax.tree.map(lambda _: pl.BlockSpec(memory_space=pltpu.VMEM), out_shape),
        scratch_shapes=list(scratch),
        compiler_params=pltpu.CompilerParams(vmem_limit_bytes=VMEM_BYTES),
        cost_estimate=pl.CostEstimate(flops=flops, bytes_accessed=nbytes, transcendentals=0),
    )


def norm_rows(raw_ref, out_ref, start, rows, width, chunk):
    total = jnp.zeros((rows, 1), F32)
    for at in range(0, width, chunk):
        part = raw_ref[:, at : at + chunk].astype(F32)
        total = total + jnp.sum(part * part, axis=-1, keepdims=True)
    length = jnp.sqrt(total + EPSILON)
    inverse = 1.0 / length
    for at in range(0, width, chunk):
        part = raw_ref[:, at : at + chunk].astype(F32)
        out_ref[pl.ds(start, rows), at : at + chunk] = (part * inverse).astype(BF16)
    return length


def passage_norm_kernel(raw_ref, home_ref, embed_ref, side_ref):
    rows, width = raw_ref.shape
    total = home_ref.shape[1]
    me = lax.axis_index("dp")
    chunk = min(width, 512)
    length = norm_rows(raw_ref, embed_ref, 0, rows, width, chunk)
    row_id = lax.broadcasted_iota(jnp.int32, (rows, total), 0) + me * rows
    ids = lax.broadcasted_iota(jnp.int32, (rows, total), 1)
    inverse_home = jnp.sum(
        jnp.where(home_ref[...] == row_id, ids, 0).astype(F32), axis=1, keepdims=True
    )
    lane = lax.broadcasted_iota(jnp.int32, side_ref.shape, 1)
    side_ref[...] = jnp.where(lane == 0, length, inverse_home)


def request_kernel(group, ids_ref, side_ref, embed_ref, count_ref, onehot_ref, rows_ref):
    rows, width = embed_ref.shape
    queries, negatives = ids_ref.shape
    q_dev = queries // group
    slots = group * CAP
    inverse_home = side_ref[:, 1:2].astype(jnp.int32)
    ids_t = ids_ref[...].T
    count = jnp.zeros((rows, queries), jnp.int32)
    for j in range(negatives):
        count = count + (ids_t[j : j + 1, :] == inverse_home).astype(jnp.int32)
    count = count.astype(F32)
    count_ref[...] = count
    slot_id = lax.broadcasted_iota(jnp.int32, (slots, queries), 0)
    query_id = lax.broadcasted_iota(jnp.int32, (slots, queries), 1)
    members = (slot_id // CAP == query_id // q_dev).astype(BF16)
    marked = dot_nt(members, count.astype(BF16)) > 0.0
    before = (
        lax.broadcasted_iota(jnp.int32, (rows, rows), 0)
        <= lax.broadcasted_iota(jnp.int32, (rows, rows), 1)
    ).astype(BF16)
    rank = dot_nn(marked.astype(F32).astype(BF16), before)
    wanted = (lax.broadcasted_iota(jnp.int32, (slots, rows), 0) % CAP + 1).astype(F32)
    onehot = jnp.where(marked & (rank == wanted), 1.0, 0.0)
    onehot_ref[...] = onehot
    picked = onehot.astype(BF16)
    chunk = min(width, 1024)
    for at in range(0, width, chunk):
        part = dot_nn(picked, embed_ref[:, at : at + chunk]).astype(BF16)
        for peer in range(group):
            rows_ref[peer, :, at : at + chunk] = part[peer * CAP : (peer + 1) * CAP]


def score_kernel(group, *refs):
    blocks = refs[:group]
    embed_ref, count_ref, onehot_ref, positive_ref = refs[group : group + 4]
    query_ref, weight_ref, message_ref = refs[group + 4 :]
    rows, width = embed_ref.shape
    queries = query_ref.shape[0]
    q_dev = queries // group
    me = lax.axis_index("dp")
    for k in range(group):
        start = pl.multiple_of((me ^ k) * q_dev, q_dev)
        norm_rows(blocks[k], query_ref, start, q_dev, width, min(width, 1024))
    scores = dot_nt(embed_ref[...], query_ref[...]) / SOFTMAX_HEAT
    own = lax.broadcasted_iota(jnp.int32, (rows, queries), 1) // q_dev == me
    row_id = lax.broadcasted_iota(jnp.int32, (rows, queries), 0)
    is_positive = own & (positive_ref[...] == row_id)
    count = count_ref[...] + jnp.where(is_positive, 1.0, 0.0)
    named = count > 0.0
    top = jnp.max(jnp.where(named, scores, LOWEST), axis=0, keepdims=True)
    weight = count * jnp.exp(jnp.where(named, scores - top, LOWEST))
    total = jnp.sum(weight, axis=0, keepdims=True)
    weight_ref[...] = weight
    slot_weight = dot_nn(onehot_ref[...], weight, precision=HIGHEST)
    tail_row = lax.broadcasted_iota(jnp.int32, (MSG_ROWS - CAP, queries), 0)
    tail = jnp.where(tail_row == 0, top, total)
    for peer in range(group):
        message_ref[peer, :CAP, :] = slot_weight[peer * CAP : (peer + 1) * CAP]
        message_ref[peer, CAP:, :] = tail


def combine(message_ref, group):
    tops = [message_ref[d, CAP : CAP + 1, :] for d in range(group)]
    sums = [message_ref[d, CAP + 1 : CAP + 2, :] for d in range(group)]
    top = functools.reduce(jnp.maximum, tops)
    total = sum(jnp.exp(t - top) * s for t, s in zip(tops, sums))
    return top, 1.0 / total


def final_weight(message_ref, weight_ref, positive_ref, group, q_dev, me):
    rows, queries = weight_ref.shape
    top, inverse_total = combine(message_ref, group)
    own_top = message_ref[me, CAP : CAP + 1, :]
    own = lax.broadcasted_iota(jnp.int32, (rows, queries), 1) // q_dev == me
    row_id = lax.broadcasted_iota(jnp.int32, (rows, queries), 0)
    target = jnp.where(own & (positive_ref[...] == row_id), 1.0, 0.0)
    scale = jnp.exp(own_top - top) * inverse_total
    return (weight_ref[...] * scale - target) / SOFTMAX_HEAT, top, inverse_total


def rank_kernel(shards, *refs):
    blocks = refs[:shards]
    query_in_ref, passage_in_ref = refs[shards : shards + 2]
    weights_ref, query_low_ref, passage_low_ref = refs[shards + 2 :]
    part = blocks[0].shape[1]
    me = lax.axis_index("fsdp")
    rank = blocks[0].shape[0] // 2
    for k in range(shards):
        weights_ref[:, pl.ds(pl.multiple_of((me ^ k) * part, part), part)] = blocks[k][...]
    down = weights_ref[:rank, :]
    query_low_ref[...] = dot_nt(down, query_in_ref[...]).astype(BF16)
    passage_low_ref[...] = dot_nt(down, passage_in_ref[...]).astype(BF16)


def backward(upstream_of, raw_ref, length, inputs_ref, low, weights_ref, grad_ref, up_ref, store):
    rows, width = raw_ref.shape
    rank = low.shape[0]
    chunk = min(width, 512)
    inverse = 1.0 / length
    inner = jnp.zeros((rows, 1), F32)
    for at in range(0, width, chunk):
        upstream = upstream_of(at, chunk)
        up_ref[:, at : at + chunk] = upstream
        unit = raw_ref[:, at : at + chunk].astype(F32) * inverse
        inner = inner + jnp.sum(unit * upstream, axis=-1, keepdims=True)
    back = jnp.zeros((rank, rows), F32)
    for at in range(0, width, chunk):
        unit = raw_ref[:, at : at + chunk].astype(F32) * inverse
        grad = ((up_ref[:, at : at + chunk] - unit * inner) * inverse).astype(BF16)
        grad_ref[:, at : at + chunk] = grad
        store(1, at, chunk, dot_nn(low, grad))
        back = back + dot_nt(weights_ref[rank:, at : at + chunk], grad)
    back = back.astype(BF16)
    for at in range(0, width, chunk):
        store(0, at, chunk, dot_nn(back, inputs_ref[:, at : at + chunk]))


def passage_kernel(
    group,
    message_ref,
    weight_ref,
    positive_ref,
    query_ref,
    raw_ref,
    side_ref,
    inputs_ref,
    low_ref,
    weights_ref,
    grad_ref,
    terms_ref,
    up_ref,
):
    queries = query_ref.shape[0]
    rank = low_ref.shape[0]
    me = lax.axis_index("dp")
    weight, _, _ = final_weight(message_ref, weight_ref, positive_ref, group, queries // group, me)
    high, low_part = split_two(weight)

    def upstream_of(at, chunk):
        embed = query_ref[:, at : at + chunk]
        return dot_nn(high, embed) + dot_nn(low_part, embed)

    def store(which, at, chunk, value):
        terms_ref[which * rank : (which + 1) * rank, at : at + chunk] = value

    backward(
        upstream_of,
        raw_ref,
        side_ref[:, 0:1],
        inputs_ref,
        low_ref[...],
        weights_ref,
        grad_ref,
        up_ref,
        store,
    )


def query_kernel(group, *refs):
    fetched = refs[: group - 1]
    (
        message_ref,
        weight_ref,
        positive_ref,
        embed_ref,
        raw_ref,
        inputs_ref,
        low_ref,
        weights_ref,
        terms_ref,
        grad_ref,
        sent_ref,
        up_ref,
        sum_ref,
    ) = refs[group - 1 :]
    q_dev, width = raw_ref.shape
    queries = weight_ref.shape[1]
    rank = low_ref.shape[0]
    me = lax.axis_index("dp")
    weight, top, inverse_total = final_weight(
        message_ref, weight_ref, positive_ref, group, q_dev, me
    )
    pick = (
        lax.broadcasted_iota(jnp.int32, (q_dev, queries), 1)
        == lax.broadcasted_iota(jnp.int32, (q_dev, queries), 0) + me * q_dev
    ).astype(F32)
    slot_weight = []
    for k in range(1, group):
        peer = me ^ k
        scale = jnp.exp(message_ref[peer, CAP : CAP + 1, :] - top) * inverse_total
        slot_weight.append(message_ref[peer, :CAP, :] * scale / SOFTMAX_HEAT)
    slot_weight.append(jnp.zeros((CAP, queries), F32))
    own_high, own_low = split_two(dot_nt(pick, weight, precision=HIGHEST))
    far_high, far_low = split_two(
        dot_nt(pick, jnp.concatenate(slot_weight, axis=0), precision=HIGHEST)
    )

    def upstream_of(at, chunk):
        near = embed_ref[:, at : at + chunk]
        far = [ref[:, at : at + chunk].astype(F32) for ref in fetched]
        far.append(jnp.zeros((CAP, chunk), F32))
        far = jnp.concatenate(far, axis=0).astype(BF16)
        return (
            dot_nn(own_high, near)
            + dot_nn(own_low, near)
            + dot_nn(far_high, far)
            + dot_nn(far_low, far)
        )

    total = jnp.zeros((q_dev, 1), F32)
    for at in range(0, width, 1024):
        part = raw_ref[:, at : at + 1024].astype(F32)
        total = total + jnp.sum(part * part, axis=-1, keepdims=True)

    def store(which, at, chunk, value):
        rows = slice(which * rank, (which + 1) * rank)
        sum_ref[rows, at : at + chunk] = ADAPTER_SCALE * (
            value + terms_ref[rows, at : at + chunk]
        )

    backward(
        upstream_of,
        raw_ref,
        jnp.sqrt(total + EPSILON),
        inputs_ref,
        low_ref[...],
        weights_ref,
        grad_ref,
        up_ref,
        store,
    )
    _, part_rows, part_width = sent_ref.shape
    for f in range(width // part_width):
        for d in range(group):
            sent_ref[f * group + d] = sum_ref[
                d * part_rows : (d + 1) * part_rows, f * part_width : (f + 1) * part_width
            ]


def exchange(values, axis, k):
    size = lax.axis_size(axis)
    return lax.ppermute(values, axis, [(i, i ^ k) for i in range(size)])


def per_device(
    query_pooled_states,
    passage_pooled_states,
    query_attention_output,
    passage_attention_output,
    positive_passage_row,
    hard_negative_ids,
    passage_home_row,
    adapter_down_weight,
    adapter_up_weight,
):
    group = lax.axis_size("dp")
    shards = lax.axis_size("fsdp")
    query_raw = query_pooled_states[0]
    passage_raw = passage_pooled_states[0]
    query_in = query_attention_output[0]
    passage_in = passage_attention_output[0]
    ids = hard_negative_ids[0]
    q_dev, width = query_raw.shape
    p_dev = passage_raw.shape[0]
    rank, part = adapter_down_weight.shape
    queries = group * q_dev
    slots = group * CAP

    def shape(dims, kind):
        return jax.ShapeDtypeStruct(dims, kind)

    blocks = {0: query_raw}
    for k in range(2, group, 2):
        blocks[k] = exchange(query_raw, "dp", k)
    blocks[1] = exchange(query_raw, "dp", 1)
    for k in range(2, group, 2):
        blocks[k ^ 1] = exchange(blocks[k], "dp", 1)
    adapter = jnp.concatenate([adapter_down_weight, adapter_up_weight], axis=0)
    adapter_blocks = [adapter] + [exchange(adapter, "fsdp", k) for k in range(1, shards)]
    all_ids = lax.all_to_all(
        jnp.broadcast_to(ids[None], (group,) + ids.shape),
        "dp",
        split_axis=0,
        concat_axis=0,
        tiled=True,
    ).reshape(queries, ids.shape[1])
    positive_row = jnp.tile(positive_passage_row, (1, group))

    embed, side = kernel_call(
        passage_norm_kernel,
        (shape((p_dev, width), BF16), shape((p_dev, 128), F32)),
        2,
        4 * p_dev * width,
        4 * p_dev * width,
    )(passage_raw, passage_home_row)
    count, onehot, rows_out = kernel_call(
        functools.partial(request_kernel, group),
        (
            shape((p_dev, queries), F32),
            shape((slots, p_dev), F32),
            shape((group, CAP, width), BF16),
        ),
        3,
        2 * p_dev * width * slots,
        4 * p_dev * width,
    )(all_ids, side, embed)
    me = lax.axis_index("dp")
    fetched = []
    for k in range(1, group):
        out_block = lax.dynamic_index_in_dim(rows_out, me ^ k, 0, keepdims=False)
        fetched.append(exchange(out_block, "dp", k))
    query_embed, weight, message = kernel_call(
        functools.partial(score_kernel, group),
        (
            shape((queries, width), BF16),
            shape((p_dev, queries), F32),
            shape((group, MSG_ROWS, queries), F32),
        ),
        group + 4,
        2 * p_dev * width * queries,
        6 * p_dev * width,
    )(*[blocks[k] for k in range(group)], embed, count, onehot, positive_row)
    replies = lax.all_to_all(message, "dp", split_axis=0, concat_axis=0, tiled=True)

    adapter_full, query_low, passage_low = kernel_call(
        functools.partial(rank_kernel, shards),
        (
            shape((2 * rank, width), BF16),
            shape((rank, q_dev), BF16),
            shape((rank, p_dev), BF16),
        ),
        shards + 2,
        2 * p_dev * width * rank,
        2 * p_dev * width,
    )(*adapter_blocks, query_in, passage_in)

    grad_passage, terms = kernel_call(
        functools.partial(passage_kernel, group),
        (shape((p_dev, width), BF16), shape((2 * rank, width), F32)),
        9,
        4 * p_dev * width * queries,
        8 * p_dev * width,
        [pltpu.VMEM((p_dev, width), F32)],
    )(
        replies,
        weight,
        positive_row,
        query_embed,
        passage_raw,
        side,
        passage_in,
        passage_low,
        adapter_full,
    )
    grad_query, sent = kernel_call(
        functools.partial(query_kernel, group),
        (
            shape((q_dev, width), BF16),
            shape((shards * group, 2 * rank // group, part), F32),
        ),
        group - 1 + 9,
        4 * q_dev * width * (p_dev + slots),
        4 * p_dev * width,
        [pltpu.VMEM((q_dev, width), F32), pltpu.VMEM((2 * rank, width), F32)],
    )(
        *fetched,
        replies,
        weight,
        positive_row,
        embed,
        query_raw,
        query_in,
        query_low,
        adapter_full,
        terms,
    )
    received = lax.all_to_all(
        sent, ("fsdp", "dp"), split_axis=0, concat_axis=0, tiled=True
    )
    share = jnp.sum(received, axis=0)
    whole = lax.all_to_all(
        jnp.broadcast_to(share[None], (group,) + share.shape),
        "dp",
        split_axis=0,
        concat_axis=0,
        tiled=True,
    ).reshape(2 * rank, part)
    return (grad_query[None], grad_passage[None], whole[:rank], whole[rank:])


def solution(mesh):
    in_specs = (
        P("fsdp", "dp", None),
        P("fsdp", "dp", None),
        P("fsdp", "dp", None),
        P("fsdp", "dp", None),
        P("fsdp", "dp"),
        P("fsdp", "dp", None),
        P("fsdp", None),
        P(None, "fsdp"),
        P(None, "fsdp"),
    )
    out_specs = (P("fsdp", "dp", None), P("fsdp", "dp", None), P(None, "fsdp"), P(None, "fsdp"))
    return jax.shard_map(
        per_device, mesh=mesh, in_specs=in_specs, out_specs=out_specs, check_vma=False
    )
```

```python
import functools

import jax
import jax.numpy as jnp
from jax import lax
from jax.experimental import pallas as pl
from jax.experimental.pallas import tpu as pltpu
from jax.sharding import PartitionSpec as P

CAP = 8
SOFTMAX_HEAT = 0.01
ADAPTER_SCALE = 2.0
EPSILON = 1e-06
LOWEST = -1e30
ID_BASE = 256
TOP_ROW, SUM_ROW, DOT_ROW, HEAD_ROWS = 8, 9, 10, 16
VMEM_BYTES = 24 * 1024 * 1024
F32 = jnp.float32
BF16 = jnp.bfloat16
HIGHEST = lax.Precision.HIGHEST


def dot_nn(a, b, precision=None):
    return lax.dot_general(
        a, b, (((1,), (0,)), ((), ())), precision=precision, preferred_element_type=F32
    )


def dot_nt(a, b, precision=None):
    return lax.dot_general(
        a, b, (((1,), (1,)), ((), ())), precision=precision, preferred_element_type=F32
    )


def split_two(values):
    high = values.astype(BF16)
    low = (values - high.astype(F32)).astype(BF16)
    return high, low


def iota(shape, dim):
    return lax.broadcasted_iota(jnp.int32, shape, dim)


def shape_of(dims, kind):
    return jax.ShapeDtypeStruct(dims, kind)


def run(body, out_shape, args, flops, scratch=()):
    vmem = pl.BlockSpec(memory_space=pltpu.VMEM)
    moved = sum(a.size * a.dtype.itemsize for a in (*args, *out_shape))
    return pl.pallas_call(
        body,
        out_shape=out_shape,
        in_specs=[vmem] * len(args),
        out_specs=tuple(vmem for _ in out_shape),
        scratch_shapes=list(scratch),
        compiler_params=pltpu.CompilerParams(vmem_limit_bytes=VMEM_BYTES),
        cost_estimate=pl.CostEstimate(flops=flops, bytes_accessed=moved, transcendentals=0),
    )(*args)


def inverse_length(raw_ref, width):
    chunk = min(width, 512)
    total = jnp.zeros((raw_ref.shape[0], 1), F32)
    for at in range(0, width, chunk):
        part = raw_ref[:, at : at + chunk].astype(F32)
        total = total + jnp.sum(part * part, axis=-1, keepdims=True)
    return 1.0 / jnp.sqrt(total + EPSILON)


def pack_kernel(raw_ref, ids_ref, out_ref):
    width = raw_ref.shape[1]
    ids = ids_ref[...]
    out_ref[:, :width] = raw_ref[...]
    coded = jnp.concatenate([ids // ID_BASE, ids % ID_BASE], axis=1)
    out_ref[:, width:] = coded.astype(F32).astype(BF16)


def passage_norm_kernel(raw_ref, home_ref, embed_ref, side_ref, row_ref):
    rows, width = raw_ref.shape
    total = home_ref.shape[1]
    me = lax.axis_index("dp")
    chunk = min(width, 512)
    inverse = inverse_length(raw_ref, width)
    for at in range(0, width, chunk):
        part = raw_ref[:, at : at + chunk].astype(F32)
        embed_ref[:, at : at + chunk] = (part * inverse).astype(BF16)
    row_id = iota((rows, total), 0) + me * rows
    ids = iota((rows, total), 1)
    home = jnp.sum(jnp.where(home_ref[...] == row_id, ids, 0).astype(F32), axis=1, keepdims=True)
    side_ref[...] = jnp.where(iota(side_ref.shape, 1) == 0, inverse, home)
    row_ref[...] = jnp.broadcast_to(inverse, (rows, rows)).T[: row_ref.shape[0]]


def rank_kernel(shards, group, *refs):
    blocks = refs[:shards]
    query_ref, query_in_ref, passage_in_ref, embed_ref, row_ref = refs[shards : shards + 5]
    weights_ref, passage_low_ref, query_low_ref, own_ref, slot_base_ref = refs[shards + 5 :]
    part = blocks[0].shape[1]
    rank = blocks[0].shape[0] // 2
    q_dev, width = query_ref.shape
    queries = query_low_ref.shape[1]
    me = lax.axis_index("fsdp")
    for k in range(shards):
        weights_ref[:, pl.ds(pl.multiple_of((me ^ k) * part, part), part)] = blocks[k][...]
    down, up = weights_ref[:rank, :], weights_ref[rank:, :]
    place = iota((q_dev, queries), 1) == iota((q_dev, queries), 0) + lax.axis_index("dp") * q_dev
    own = jnp.sum(
        jnp.where(place, inverse_length(query_ref, width), 0.0), axis=0, keepdims=True
    )
    own_ref[...] = jnp.broadcast_to(own, own_ref.shape)
    query_low = dot_nt(down, query_in_ref[...]).astype(BF16)
    query_low_ref[...] = dot_nn(query_low, place.astype(BF16)) * own
    passage_low = dot_nt(down, passage_in_ref[...]).astype(BF16)
    passage_low_ref[...] = passage_low.astype(F32) * row_ref[0:1, :]
    slot_base_ref[...] = dot_nt(up, embed_ref[...])


def score_kernel(group, *refs):
    blocks = refs[:group]
    embed_ref, side_ref, positive_ref, query_low_ref, base_ref = refs[group : group + 5]
    query_ref, weight_ref, dots_ref, onehot_ref, message_ref, coded_ref = refs[group + 5 :]
    rows, width = embed_ref.shape
    queries = query_ref.shape[0]
    q_dev = queries // group
    negatives = (blocks[0].shape[1] - width) // 2
    slots = group * CAP
    rank = query_low_ref.shape[0]
    me = lax.axis_index("dp")
    chunk = min(width, 1024)
    for k in range(group):
        start = pl.multiple_of((me ^ k) * q_dev, q_dev)
        inverse = inverse_length(blocks[k], width)
        for at in range(0, width, chunk):
            part = blocks[k][:, at : at + chunk].astype(F32)
            query_ref[pl.ds(start, q_dev), at : at + chunk] = (part * inverse).astype(BF16)
        coded = blocks[k][:, width:].astype(F32)
        coded_ref[pl.ds(start, q_dev), :] = coded
    dots = dot_nt(embed_ref[...], query_ref[...])
    dots_ref[...] = dots
    scores = dots / SOFTMAX_HEAT

    coded = coded_ref[...].T
    ids = coded[:negatives] * float(ID_BASE) + coded[negatives:]
    home = jnp.broadcast_to(side_ref[:, 1:2], (rows, queries))
    count = jnp.zeros((rows, queries), F32)
    for j in range(negatives):
        count = count + jnp.where(ids[j : j + 1, :] == home, 1.0, 0.0)
    members = iota((slots, queries), 0) // CAP == iota((slots, queries), 1) // q_dev
    marked = dot_nt(members.astype(BF16), count.astype(BF16)) > 0.0
    before = (iota((rows, rows), 0) <= iota((rows, rows), 1)).astype(BF16)
    rank_in = dot_nn(marked.astype(F32).astype(BF16), before)
    wanted = (iota((slots, rows), 0) % CAP + 1).astype(F32)
    onehot = jnp.where(marked & (rank_in == wanted), 1.0, 0.0)
    onehot_ref[...] = onehot.astype(BF16)

    own = iota((rows, queries), 1) // q_dev == me
    count = count + jnp.where(own & (positive_ref[...] == iota((rows, queries), 0)), 1.0, 0.0)
    named = count > 0.0
    top = jnp.max(jnp.where(named, scores, LOWEST), axis=0, keepdims=True)
    weight = count * jnp.exp(jnp.where(named, scores - top, LOWEST))
    weight_ref[...] = weight
    total = jnp.sum(weight, axis=0, keepdims=True)
    dot_total = jnp.sum(weight * dots, axis=0, keepdims=True)
    slot_weight = dot_nn(onehot, weight, precision=HIGHEST)
    slot_base = dot_nt(base_ref[...], onehot, precision=HIGHEST)
    tail_row = iota((HEAD_ROWS - CAP, queries), 0)
    tail = jnp.where(tail_row == 0, top, jnp.where(tail_row == 1, total, dot_total))
    query_low = query_low_ref[...]
    for peer in range(group):
        message_ref[peer, :CAP, :] = slot_weight[peer * CAP : (peer + 1) * CAP]
        message_ref[peer, CAP:HEAD_ROWS, :] = tail
        message_ref[peer, HEAD_ROWS : HEAD_ROWS + rank, :] = query_low
        message_ref[peer, HEAD_ROWS + rank : HEAD_ROWS + 2 * rank, :CAP] = slot_base[
            :, peer * CAP : (peer + 1) * CAP
        ]


def request_kernel(group, embed_ref, query_ref, weights_ref, onehot_ref, rows_ref, back_ref):
    width = embed_ref.shape[1]
    rank = weights_ref.shape[0] // 2
    back_ref[...] = dot_nt(weights_ref[rank:, :], query_ref[...])
    chunk = min(width, 1024)
    for at in range(0, width, chunk):
        part = dot_nn(onehot_ref[...], embed_ref[:, at : at + chunk]).astype(BF16)
        for peer in range(group):
            rows_ref[peer, :, at : at + chunk] = part[peer * CAP : (peer + 1) * CAP]


def combine(message_ref, group):
    tops = [message_ref[d, TOP_ROW : TOP_ROW + 1, :] for d in range(group)]
    sums = [message_ref[d, SUM_ROW : SUM_ROW + 1, :] for d in range(group)]
    top = functools.reduce(jnp.maximum, tops)
    total = sum(jnp.exp(t - top) * s for t, s in zip(tops, sums))
    return top, 1.0 / total


def own_target(positive_ref, rows, queries, q_dev, me):
    own = iota((rows, queries), 1) // q_dev == me
    return jnp.where(own & (positive_ref[...] == iota((rows, queries), 0)), 1.0, 0.0)


def terms_kernel(group, shards, *refs):
    (
        message_ref,
        weight_ref,
        dots_ref,
        positive_ref,
        query_ref,
        embed_ref,
        back_query_ref,
        back_passage_ref,
        passage_low_ref,
        row_ref,
        own_ref,
        passage_in_ref,
        query_in_ref,
    ) = refs[:13]
    final_ref = refs[13]
    blocks = refs[14 : 14 + shards]
    (sum_ref,) = refs[14 + shards :]
    rows, queries = weight_ref.shape
    q_dev = queries // group
    rank = passage_low_ref.shape[0]
    width = query_ref.shape[1]
    me = lax.axis_index("dp")

    top, inverse_total = combine(message_ref, group)
    target = own_target(positive_ref, rows, queries, q_dev, me)
    own_top = message_ref[me, TOP_ROW : TOP_ROW + 1, :]
    weight = (
        weight_ref[...] * (jnp.exp(own_top - top) * inverse_total) - target
    ) / SOFTMAX_HEAT
    final_ref[...] = weight
    dots = dots_ref[...]
    weighted = weight * dots
    share = jnp.sum(weighted, axis=0, keepdims=True)
    ones = jnp.ones((8, queries), F32)
    inner = dot_nt(ones, weighted, precision=HIGHEST)[0:1, :]

    query_low = jnp.zeros((rank, queries), F32)
    inner_query = -jnp.sum(target * dots, axis=0, keepdims=True)
    far_weight, far_base = [], []
    for d in range(group):
        query_low = query_low + message_ref[d, HEAD_ROWS : HEAD_ROWS + rank, :]
        scale = jnp.exp(message_ref[d, TOP_ROW : TOP_ROW + 1, :] - top) * inverse_total
        inner_query = inner_query + scale * message_ref[d, DOT_ROW : DOT_ROW + 1, :]
        scale = jnp.where(me == d, 0.0, scale / SOFTMAX_HEAT)
        far_weight.append(message_ref[d, :CAP, :] * scale)
        far_base.append(message_ref[d, HEAD_ROWS + rank : HEAD_ROWS + 2 * rank, :CAP])
    inner_query = inner_query / SOFTMAX_HEAT

    passage_low = passage_low_ref[...]
    from_query = dot_nn(passage_low, weight, precision=HIGHEST) - query_low * share
    from_passage = dot_nt(query_low, weight, precision=HIGHEST) - passage_low * inner
    query_parts = jnp.concatenate(split_two(from_query), axis=0)
    passage_parts = jnp.concatenate(split_two(from_passage), axis=0)

    back_passage = dot_nt(back_query_ref[...], weight, precision=HIGHEST)
    back_passage = (back_passage - back_passage_ref[...] * inner) * row_ref[0:1, :]
    back_passage = back_passage.astype(BF16)
    back_query = dot_nn(back_passage_ref[...], weight, precision=HIGHEST)
    back_query = back_query + dot_nn(
        jnp.concatenate(far_base, axis=1),
        jnp.concatenate(far_weight, axis=0),
        precision=HIGHEST,
    )
    back_query = (back_query - back_query_ref[...] * inner_query) * own_ref[0:1, :]
    pick = (iota((q_dev, queries), 1) == iota((q_dev, queries), 0) + me * q_dev).astype(BF16)
    back_query = dot_nt(back_query.astype(BF16), pick).astype(BF16)

    chunk = min(width, 512)
    for at in range(0, width, chunk):
        cols = slice(at, at + chunk)
        both = dot_nn(query_parts, query_ref[:, cols]) + dot_nn(passage_parts, embed_ref[:, cols])
        sum_ref[rank:, cols] = ADAPTER_SCALE * (both[:rank] + both[rank:])
        sum_ref[:rank, cols] = ADAPTER_SCALE * (
            dot_nn(back_passage, passage_in_ref[:, cols])
            + dot_nn(back_query, query_in_ref[:, cols])
        )
    part = width // shards
    home = lax.axis_index("fsdp")
    for k in range(shards):
        start = pl.multiple_of((home ^ k) * part, part)
        blocks[k][...] = sum_ref[:, pl.ds(start, part)].astype(blocks[k].dtype)


def backward(upstream_of, raw_ref, inverse, grad_ref, up_ref):
    rows, width = raw_ref.shape
    chunk = min(width, 512)
    inner = jnp.zeros((rows, 1), F32)
    for at in range(0, width, chunk):
        upstream = upstream_of(at, chunk)
        up_ref[:, at : at + chunk] = upstream
        unit = raw_ref[:, at : at + chunk].astype(F32) * inverse
        inner = inner + jnp.sum(unit * upstream, axis=-1, keepdims=True)
    for at in range(0, width, chunk):
        unit = raw_ref[:, at : at + chunk].astype(F32) * inverse
        grad = (up_ref[:, at : at + chunk] - unit * inner) * inverse
        grad_ref[:, at : at + chunk] = grad.astype(BF16)


def passage_kernel(final_ref, query_ref, raw_ref, side_ref, grad_ref, up_ref):
    high, low = split_two(final_ref[...])

    def upstream_of(at, chunk):
        embed = query_ref[:, at : at + chunk]
        return dot_nn(high, embed) + dot_nn(low, embed)

    backward(upstream_of, raw_ref, side_ref[:, 0:1], grad_ref, up_ref)


def query_kernel(group, far_ref, message_ref, final_ref, embed_ref, raw_ref, grad_ref, up_ref):
    q_dev, width = raw_ref.shape
    queries = final_ref.shape[1]
    me = lax.axis_index("dp")
    top, inverse_total = combine(message_ref, group)
    pick = (iota((q_dev, queries), 1) == iota((q_dev, queries), 0) + me * q_dev).astype(F32)
    far = []
    for d in range(group):
        scale = jnp.exp(message_ref[d, TOP_ROW : TOP_ROW + 1, :] - top) * inverse_total
        scale = jnp.where(me == d, 0.0, scale / SOFTMAX_HEAT)
        far.append(message_ref[d, :CAP, :] * scale)
    own_parts = split_two(dot_nt(pick, final_ref[...], precision=HIGHEST))
    far_parts = split_two(dot_nt(pick, jnp.concatenate(far, axis=0), precision=HIGHEST))
    own_parts = jnp.concatenate(own_parts, axis=0)
    far_parts = jnp.concatenate(far_parts, axis=0)

    def upstream_of(at, chunk):
        rows = [far_ref[d, :, at : at + chunk].astype(F32) for d in range(group)]
        both = dot_nn(own_parts, embed_ref[:, at : at + chunk])
        both = both + dot_nn(far_parts, jnp.concatenate(rows, axis=0).astype(BF16))
        return both[:q_dev] + both[q_dev:]

    backward(upstream_of, raw_ref, inverse_length(raw_ref, width), grad_ref, up_ref)


def sum_kernel(*refs):
    total = refs[0][...].astype(F32)
    for ref in refs[1:-1]:
        total = total + ref[...].astype(F32)
    refs[-1][...] = total


def sum_two_kernel(left_ref, right_ref, sent_ref):
    sent_ref[...] = (left_ref[...] + right_ref[...]).astype(BF16)


def sum_split_kernel(*refs):
    terms = [ref[...].astype(F32) for ref in refs[:-2]]
    while len(terms) > 1:
        terms = [a + b for a, b in zip(terms[::2], terms[1::2])]
    rank = refs[-1].shape[0]
    refs[-2][...] = terms[0][:rank]
    refs[-1][...] = terms[0][rank:]


def exchange(values, axis, k):
    size = lax.axis_size(axis)
    return lax.ppermute(values, axis, [(i, i ^ k) for i in range(size)])


def per_device(
    query_pooled_states,
    passage_pooled_states,
    query_attention_output,
    passage_attention_output,
    positive_passage_row,
    hard_negative_ids,
    passage_home_row,
    adapter_down_weight,
    adapter_up_weight,
):
    group = lax.axis_size("dp")
    shards = lax.axis_size("fsdp")
    query_raw = query_pooled_states[0]
    passage_raw = passage_pooled_states[0]
    query_in = query_attention_output[0]
    passage_in = passage_attention_output[0]
    ids = hard_negative_ids[0]
    q_dev, width = query_raw.shape
    p_dev = passage_raw.shape[0]
    rank, part = adapter_down_weight.shape
    queries = group * q_dev
    slots = group * CAP
    work = 2 * p_dev * width

    packed = run(
        pack_kernel,
        (shape_of((q_dev, width + 2 * ids.shape[1]), BF16),),
        (query_raw, ids),
        1,
    )[0]
    blocks = {0: packed}
    for k in range(2, group, 2):
        blocks[k] = exchange(packed, "dp", k)
    blocks[1] = exchange(packed, "dp", 1)
    for k in range(2, group, 2):
        blocks[k ^ 1] = exchange(blocks[k], "dp", 1)
    adapter = jnp.concatenate([adapter_down_weight, adapter_up_weight], axis=0)
    adapter_blocks = [adapter] + [exchange(adapter, "fsdp", k) for k in range(1, shards)]
    positive_row = jnp.tile(positive_passage_row, (1, group))

    embed, side, side_row = run(
        passage_norm_kernel,
        (
            shape_of((p_dev, width), BF16),
            shape_of((p_dev, 128), F32),
            shape_of((8, p_dev), F32),
        ),
        (passage_raw, passage_home_row),
        work,
    )
    adapter_full, passage_low, query_low, own_side, slot_base = run(
        functools.partial(rank_kernel, shards, group),
        (
            shape_of((2 * rank, width), BF16),
            shape_of((rank, p_dev), F32),
            shape_of((rank, queries), F32),
            shape_of((8, queries), F32),
            shape_of((rank, p_dev), F32),
        ),
        (*adapter_blocks, query_raw, query_in, passage_in, embed, side_row),
        work * rank,
    )
    query_embed, weight, dots, onehot, message = run(
        functools.partial(score_kernel, group),
        (
            shape_of((queries, width), BF16),
            shape_of((p_dev, queries), F32),
            shape_of((p_dev, queries), F32),
            shape_of((slots, p_dev), BF16),
            shape_of((group, HEAD_ROWS + 2 * rank, queries), F32),
        ),
        (
            *[blocks[k] for k in range(group)],
            embed,
            side,
            positive_row,
            query_low,
            slot_base,
        ),
        work * queries,
        [pltpu.VMEM((queries, 2 * ids.shape[1]), F32)],
    )
    replies = lax.all_to_all(message, "dp", split_axis=0, concat_axis=0, tiled=True)
    rows_out, back_query = run(
        functools.partial(request_kernel, group),
        (shape_of((group, CAP, width), BF16), shape_of((rank, queries), F32)),
        (embed, query_embed, adapter_full, onehot),
        work * slots,
    )
    final, *terms = run(
        functools.partial(terms_kernel, group, shards),
        (
            shape_of((p_dev, queries), F32),
            shape_of((2 * rank, part), F32),
            *[shape_of((2 * rank, part), BF16)] * (shards - 1),
        ),
        (
            replies,
            weight,
            dots,
            positive_row,
            query_embed,
            embed,
            back_query,
            slot_base,
            passage_low,
            side_row,
            own_side,
            passage_in,
            query_in,
        ),
        work * rank * 4,
        [pltpu.VMEM((2 * rank, width), F32)],
    )
    rows_out, final = lax.optimization_barrier((rows_out, final))
    far_rows = lax.all_to_all(rows_out, "dp", split_axis=0, concat_axis=0, tiled=True)

    arrived = [exchange(terms[k], "fsdp", k) for k in range(1, shards)]
    total = run(sum_kernel, (shape_of((2 * rank, part), F32),), (terms[0], *arrived), 1)[0]
    sent = run(
        sum_two_kernel,
        (shape_of((2 * rank, part), BF16),),
        (total, exchange(total, "dp", 1)),
        1,
    )[0]
    arrived = [exchange(sent, "dp", k) for k in range(2, group, 2)]
    down_total, up_total = run(
        sum_split_kernel, (shape_of((rank, part), F32),) * 2, (sent, *arrived), 1
    )

    grad_passage = run(
        passage_kernel,
        (shape_of((p_dev, width), BF16),),
        (final, query_embed, passage_raw, side),
        2 * work * queries,
        [pltpu.VMEM((p_dev, width), F32)],
    )[0]
    grad_query = run(
        functools.partial(query_kernel, group),
        (shape_of((q_dev, width), BF16),),
        (far_rows, replies, final, embed, query_raw),
        4 * q_dev * width * (p_dev + slots),
        [pltpu.VMEM((q_dev, width), F32)],
    )[0]
    return (grad_query[None], grad_passage[None], down_total, up_total)


def solution(mesh):
    in_specs = (
        P("fsdp", "dp", None),
        P("fsdp", "dp", None),
        P("fsdp", "dp", None),
        P("fsdp", "dp", None),
        P("fsdp", "dp"),
        P("fsdp", "dp", None),
        P("fsdp", None),
        P(None, "fsdp"),
        P(None, "fsdp"),
    )
    out_specs = (P("fsdp", "dp", None), P("fsdp", "dp", None), P(None, "fsdp"), P(None, "fsdp"))
    return jax.shard_map(
        per_device, mesh=mesh, in_specs=in_specs, out_specs=out_specs, check_vma=False
    )
```

```python
import functools

import jax
import jax.numpy as jnp
from jax import lax
from jax.experimental import pallas as pl
from jax.experimental.pallas import tpu as pltpu
from jax.sharding import PartitionSpec as P

CAP = 8
SOFTMAX_HEAT = 0.01
ADAPTER_SCALE = 2.0
EPSILON = 1e-06
LOWEST = -1e30
ID_BASE = 256
TOP_ROW, SUM_ROW, DOT_ROW, HEAD_ROWS = 8, 9, 10, 16
VMEM_BYTES = 16 * 1024 * 1024
F32 = jnp.float32
BF16 = jnp.bfloat16
HIGHEST = lax.Precision.HIGHEST


def dot_nn(a, b, precision=None):
    return lax.dot_general(
        a, b, (((1,), (0,)), ((), ())), precision=precision, preferred_element_type=F32
    )


def dot_nt(a, b, precision=None):
    return lax.dot_general(
        a, b, (((1,), (1,)), ((), ())), precision=precision, preferred_element_type=F32
    )


def split_two(values):
    high = values.astype(BF16)
    low = (values - high.astype(F32)).astype(BF16)
    return high, low


def iota(shape, dim):
    return lax.broadcasted_iota(jnp.int32, shape, dim)


def shape_of(dims, kind):
    return jax.ShapeDtypeStruct(dims, kind)


def run(body, out_shape, args, flops, scratch=(), in_hbm=False):
    vmem = pl.BlockSpec(memory_space=pltpu.VMEM)
    hbm = pl.BlockSpec(memory_space=pltpu.HBM)
    moved = sum(a.size * a.dtype.itemsize for a in (*args, *out_shape))
    return pl.pallas_call(
        body,
        out_shape=out_shape,
        in_specs=[hbm if in_hbm else vmem] * len(args),
        out_specs=tuple(vmem for _ in out_shape),
        scratch_shapes=list(scratch),
        compiler_params=pltpu.CompilerParams(vmem_limit_bytes=VMEM_BYTES * max(1, size_ratio(args))),
        cost_estimate=pl.CostEstimate(flops=flops, bytes_accessed=moved, transcendentals=0),
    )(*args)


def size_ratio(args):
    moved = sum(a.size * a.dtype.itemsize for a in args)
    return -(-moved * 3 // VMEM_BYTES)


def inverse_length(raw_ref, width):
    chunk = min(width, 512)
    total = jnp.zeros((raw_ref.shape[0], 1), F32)
    for at in range(0, width, chunk):
        part = raw_ref[:, at : at + chunk].astype(F32)
        total = total + jnp.sum(part * part, axis=-1, keepdims=True)
    return 1.0 / jnp.sqrt(total + EPSILON)


def pack_kernel(raw_ref, ids_ref, down_ref, up_ref, out_ref, adapter_ref, ids_here, sems):
    width = raw_ref.shape[1]
    rank = down_ref.shape[0]
    copies = [
        pltpu.make_async_copy(src, dst, sems.at[i])
        for i, (src, dst) in enumerate(
            (
                (ids_ref, ids_here),
                (raw_ref, out_ref.at[:, pl.ds(0, width)]),
                (down_ref, adapter_ref.at[pl.ds(0, rank), :]),
                (up_ref, adapter_ref.at[pl.ds(rank, rank), :]),
            )
        )
    ]
    for copy in copies:
        copy.start()
    copies[0].wait()
    ids = ids_here[...]
    coded = jnp.concatenate([ids // ID_BASE, ids % ID_BASE], axis=1)
    out_ref[:, width:] = coded.astype(F32).astype(BF16)
    for copy in copies[1:]:
        copy.wait()


def stack_kernel(first_ref, second_ref, out_ref):
    rows = first_ref.shape[0]
    out_ref[:rows, :] = first_ref[...]
    out_ref[rows:, :] = second_ref[...]


def stack(first, second):
    rows, cols = first.shape
    return run(stack_kernel, (shape_of((2 * rows, cols), first.dtype),), (first, second), 1)[0]


def passage_norm_kernel(raw_ref, home_ref, embed_ref, side_ref, row_ref):
    rows, width = raw_ref.shape
    total = home_ref.shape[1]
    me = lax.axis_index("dp")
    chunk = min(width, 512)
    inverse = inverse_length(raw_ref, width)
    for at in range(0, width, chunk):
        part = raw_ref[:, at : at + chunk].astype(F32)
        embed_ref[:, at : at + chunk] = (part * inverse).astype(BF16)
    row_id = iota((rows, total), 0) + me * rows
    ids = iota((rows, total), 1)
    home = jnp.sum(jnp.where(home_ref[...] == row_id, ids, 0).astype(F32), axis=1, keepdims=True)
    side_ref[...] = jnp.where(iota(side_ref.shape, 1) == 0, inverse, home)
    row_ref[...] = jnp.broadcast_to(inverse, (rows, rows)).T[: row_ref.shape[0]]


def rank_kernel(
    shards,
    blocks_ref,
    query_ref,
    query_in_ref,
    passage_in_ref,
    embed_ref,
    row_ref,
    weights_ref,
    passage_low_ref,
    query_low_ref,
    own_ref,
    slot_base_ref,
):
    part = blocks_ref.shape[1]
    both = blocks_ref.shape[0] // shards
    rank = both // 2
    q_dev, width = query_ref.shape
    queries = query_low_ref.shape[1]
    me = lax.axis_index("fsdp")
    for k in range(shards):
        cols = pl.ds(pl.multiple_of((me ^ k) * part, part), part)
        weights_ref[:, cols] = blocks_ref[k * both : (k + 1) * both, :]
    down, up = weights_ref[:rank, :], weights_ref[rank:, :]
    place = iota((q_dev, queries), 1) == iota((q_dev, queries), 0) + lax.axis_index("dp") * q_dev
    own = jnp.sum(
        jnp.where(place, inverse_length(query_ref, width), 0.0), axis=0, keepdims=True
    )
    own_ref[...] = jnp.broadcast_to(own, own_ref.shape)
    query_low = dot_nt(down, query_in_ref[...]).astype(BF16)
    query_low_ref[...] = dot_nn(query_low, place.astype(BF16)) * own
    passage_low = dot_nt(down, passage_in_ref[...]).astype(BF16)
    passage_low_ref[...] = passage_low.astype(F32) * row_ref[0:1, :]
    slot_base_ref[...] = dot_nt(up, embed_ref[...])


def score_kernel(group, *refs):
    blocks = refs[:group]
    embed_ref, side_ref, positive_ref, query_low_ref, base_ref = refs[group : group + 5]
    query_ref, weight_ref, dots_ref, onehot_ref, message_ref, coded_ref = refs[group + 5 :]
    rows, width = embed_ref.shape
    queries = query_ref.shape[0]
    q_dev = queries // group
    negatives = (blocks[0].shape[1] - width) // 2
    slots = group * CAP
    rank = query_low_ref.shape[0]
    me = lax.axis_index("dp")
    chunk = min(width, 1024)
    for k in range(group):
        start = pl.multiple_of((me ^ k) * q_dev, q_dev)
        inverse = inverse_length(blocks[k], width)
        for at in range(0, width, chunk):
            part = blocks[k][:, at : at + chunk].astype(F32)
            query_ref[pl.ds(start, q_dev), at : at + chunk] = (part * inverse).astype(BF16)
        coded = blocks[k][:, width:].astype(F32)
        coded_ref[pl.ds(start, q_dev), :] = coded
    dots = dot_nt(embed_ref[...], query_ref[...])
    dots_ref[...] = dots
    scores = dots / SOFTMAX_HEAT

    coded = coded_ref[...].T
    ids = coded[:negatives] * float(ID_BASE) + coded[negatives:]
    home = jnp.broadcast_to(side_ref[:, 1:2], (rows, queries))
    count = jnp.zeros((rows, queries), F32)
    for j in range(negatives):
        count = count + jnp.where(ids[j : j + 1, :] == home, 1.0, 0.0)
    members = iota((slots, queries), 0) // CAP == iota((slots, queries), 1) // q_dev
    marked = dot_nt(members.astype(BF16), count.astype(BF16)) > 0.0
    before = (iota((rows, rows), 0) <= iota((rows, rows), 1)).astype(BF16)
    rank_in = dot_nn(marked.astype(F32).astype(BF16), before)
    wanted = (iota((slots, rows), 0) % CAP + 1).astype(F32)
    onehot = jnp.where(marked & (rank_in == wanted), 1.0, 0.0)
    onehot_ref[...] = onehot

    own = iota((rows, queries), 1) // q_dev == me
    count = count + jnp.where(own & (positive_ref[...] == iota((rows, queries), 0)), 1.0, 0.0)
    named = count > 0.0
    top = jnp.max(jnp.where(named, scores, LOWEST), axis=0, keepdims=True)
    weight = count * jnp.exp(jnp.where(named, scores - top, LOWEST))
    weight_ref[...] = weight
    total = jnp.sum(weight, axis=0, keepdims=True)
    dot_total = jnp.sum(weight * dots, axis=0, keepdims=True)
    slot_weight = dot_nn(onehot, weight, precision=HIGHEST)
    slot_base = dot_nt(base_ref[...], onehot, precision=HIGHEST)
    tail_row = iota((HEAD_ROWS - CAP, queries), 0)
    tail = jnp.where(tail_row == 0, top, jnp.where(tail_row == 1, total, dot_total))
    lane_group = iota((CAP, queries), 1) // q_dev
    compact = jnp.zeros((CAP, queries), F32)
    for peer in range(group):
        part = slot_weight[peer * CAP : (peer + 1) * CAP]
        compact = jnp.where(lane_group == peer, part, compact)
    message_ref[:CAP, :] = compact
    message_ref[CAP:HEAD_ROWS, :] = tail
    message_ref[HEAD_ROWS : HEAD_ROWS + rank, :] = query_low_ref[...]
    message_ref[HEAD_ROWS + rank :, :slots] = slot_base


def request_kernel(group, embed_ref, query_ref, weights_ref, onehot_ref, back_ref, *blocks):
    width = embed_ref.shape[1]
    rank = weights_ref.shape[0] // 2
    me = lax.axis_index("dp")
    back_ref[...] = dot_nt(weights_ref[rank:, :], query_ref[...])
    onehot = [
        onehot_ref[pl.ds(pl.multiple_of((me ^ k) * CAP, CAP), CAP), :] for k in range(group)
    ]
    onehot = jnp.concatenate(onehot, axis=0).astype(BF16)
    chunk = min(width, 1024)
    for at in range(0, width, chunk):
        part = dot_nn(onehot, embed_ref[:, at : at + chunk]).astype(BF16)
        for i, block in enumerate(blocks):
            block[:, at : at + chunk] = part[2 * i * CAP : 2 * (i + 1) * CAP]


def forward_kernel(*refs):
    out_ref = refs[-1]
    for i, ref in enumerate(refs[:-1]):
        out_ref[i * CAP : (i + 1) * CAP, :] = ref[CAP:, :]


def message_parts(pairs):
    rows = pairs[0].shape[0] // 2
    return [(ref, half * rows) for ref in pairs for half in range(2)]


def combine(parts):
    tops = [ref[at + TOP_ROW : at + TOP_ROW + 1, :] for ref, at in parts]
    sums = [ref[at + SUM_ROW : at + SUM_ROW + 1, :] for ref, at in parts]
    top = functools.reduce(jnp.maximum, tops)
    scales = [jnp.exp(t - top) for t in tops]
    inverse_total = 1.0 / sum(t * s for t, s in zip(scales, sums))
    return [scale * inverse_total for scale in scales]


def own_target(positive_ref, rows, queries, q_dev, me):
    own = iota((rows, queries), 1) // q_dev == me
    return jnp.where(own & (positive_ref[...] == iota((rows, queries), 0)), 1.0, 0.0)


def terms_kernel(group, shards, *refs):
    parts = message_parts(refs[: group // 2])
    refs = refs[group // 2 :]
    (
        weight_ref,
        dots_ref,
        positive_ref,
        query_ref,
        embed_ref,
        back_query_ref,
        back_passage_ref,
        passage_low_ref,
        row_ref,
        own_ref,
        passage_in_ref,
        query_in_ref,
    ) = refs[:12]
    final_ref = refs[12]
    blocks = refs[13 : 13 + shards]
    (sum_ref,) = refs[13 + shards :]
    rows, queries = weight_ref.shape
    q_dev = queries // group
    rank = passage_low_ref.shape[0]
    width = query_ref.shape[1]
    me = lax.axis_index("dp")

    scales = combine(parts)
    target = own_target(positive_ref, rows, queries, q_dev, me)
    weight = (weight_ref[...] * scales[0] - target) / SOFTMAX_HEAT
    final_ref[...] = weight
    dots = dots_ref[...]
    weighted = weight * dots
    share = jnp.sum(weighted, axis=0, keepdims=True)
    ones = jnp.ones((8, queries), F32)
    inner = dot_nt(ones, weighted, precision=HIGHEST)[0:1, :]

    query_low = jnp.zeros((rank, queries), F32)
    inner_query = -jnp.sum(target * dots, axis=0, keepdims=True)
    slots = group * CAP
    bases = []
    for (ref, at), scale in zip(parts, scales):
        query_low = query_low + ref[at + HEAD_ROWS : at + HEAD_ROWS + rank, :]
        inner_query = inner_query + scale * ref[at + DOT_ROW : at + DOT_ROW + 1, :]
        bases.append(ref[at + HEAD_ROWS + rank : at + HEAD_ROWS + 2 * rank, :slots])
    pick_slots = (iota((slots, CAP), 0) == iota((slots, CAP), 1) + me * CAP).astype(F32)
    bases = dot_nn(jnp.concatenate(bases[1:], axis=0), pick_slots, precision=HIGHEST)
    far_base = [bases[k * rank : (k + 1) * rank] for k in range(group - 1)]
    far_weight = [
        ref[at : at + CAP, :] * (scale / SOFTMAX_HEAT)
        for (ref, at), scale in zip(parts[1:], scales[1:])
    ]
    inner_query = inner_query / SOFTMAX_HEAT

    passage_low = passage_low_ref[...]
    from_query = dot_nn(passage_low, weight, precision=HIGHEST) - query_low * share
    from_passage = dot_nt(query_low, weight, precision=HIGHEST) - passage_low * inner
    query_parts = jnp.concatenate(split_two(from_query), axis=0)
    passage_parts = jnp.concatenate(split_two(from_passage), axis=0)

    back_passage = dot_nt(back_query_ref[...], weight, precision=HIGHEST)
    back_passage = (back_passage - back_passage_ref[...] * inner) * row_ref[0:1, :]
    back_passage = back_passage.astype(BF16)
    back_query = dot_nn(back_passage_ref[...], weight, precision=HIGHEST)
    back_query = back_query + dot_nn(
        jnp.concatenate(far_base, axis=1),
        jnp.concatenate(far_weight, axis=0),
        precision=HIGHEST,
    )
    back_query = (back_query - back_query_ref[...] * inner_query) * own_ref[0:1, :]
    pick = (iota((q_dev, queries), 1) == iota((q_dev, queries), 0) + me * q_dev).astype(BF16)
    back_query = dot_nt(back_query.astype(BF16), pick).astype(BF16)

    chunk = min(width, 512)
    for at in range(0, width, chunk):
        cols = slice(at, at + chunk)
        both = dot_nn(query_parts, query_ref[:, cols]) + dot_nn(passage_parts, embed_ref[:, cols])
        sum_ref[rank:, cols] = ADAPTER_SCALE * (both[:rank] + both[rank:])
        sum_ref[:rank, cols] = ADAPTER_SCALE * (
            dot_nn(back_passage, passage_in_ref[:, cols])
            + dot_nn(back_query, query_in_ref[:, cols])
        )
    part = width // shards
    home = lax.axis_index("fsdp")
    for k in range(shards):
        start = pl.multiple_of((home ^ k) * part, part)
        blocks[k][...] = sum_ref[:, pl.ds(start, part)].astype(blocks[k].dtype)


def backward(upstream_of, raw_ref, inverse, grad_ref, up_ref):
    rows, width = raw_ref.shape
    chunk = min(width, 512)
    inner = jnp.zeros((rows, 1), F32)
    for at in range(0, width, chunk):
        upstream = upstream_of(at, chunk)
        up_ref[:, at : at + chunk] = upstream
        unit = raw_ref[:, at : at + chunk].astype(F32) * inverse
        inner = inner + jnp.sum(unit * upstream, axis=-1, keepdims=True)
    for at in range(0, width, chunk):
        unit = raw_ref[:, at : at + chunk].astype(F32) * inverse
        grad = (up_ref[:, at : at + chunk] - unit * inner) * inverse
        grad_ref[:, at : at + chunk] = grad.astype(BF16)


def passage_kernel(final_ref, query_ref, raw_ref, side_ref, grad_ref, up_ref):
    high, low = split_two(final_ref[...])

    def upstream_of(at, chunk):
        embed = query_ref[:, at : at + chunk]
        return dot_nn(high, embed) + dot_nn(low, embed)

    backward(upstream_of, raw_ref, side_ref[:, 0:1], grad_ref, up_ref)


def query_kernel(group, *refs):
    parts = message_parts(refs[: group // 2])
    near = refs[group // 2 : group - 1]
    forwarded_ref, final_ref, embed_ref, raw_ref, grad_ref, up_ref = refs[group - 1 :]
    q_dev, width = raw_ref.shape
    queries = final_ref.shape[1]
    me = lax.axis_index("dp")
    scales = combine(parts)
    pick = (iota((q_dev, queries), 1) == iota((q_dev, queries), 0) + me * q_dev).astype(F32)
    far = [
        ref[at : at + CAP, :] * (scale / SOFTMAX_HEAT) for (ref, at), scale in zip(parts, scales)
    ]
    far = far[2::2] + far[1::2] + [jnp.zeros((CAP, queries), F32)]
    own_parts = split_two(dot_nt(pick, final_ref[...], precision=HIGHEST))
    far_parts = split_two(dot_nt(pick, jnp.concatenate(far, axis=0), precision=HIGHEST))
    own_parts = jnp.concatenate(own_parts, axis=0)
    far_parts = jnp.concatenate(far_parts, axis=0)

    def upstream_of(at, chunk):
        rows = [ref[:, at : at + chunk].astype(F32)[:CAP] for ref in near]
        rows.append(forwarded_ref[:, at : at + chunk].astype(F32))
        rows.append(jnp.zeros((CAP, chunk), F32))
        both = dot_nn(own_parts, embed_ref[:, at : at + chunk])
        both = both + dot_nn(far_parts, jnp.concatenate(rows, axis=0).astype(BF16))
        return both[:q_dev] + both[q_dev:]

    backward(upstream_of, raw_ref, inverse_length(raw_ref, width), grad_ref, up_ref)


def sum_kernel(*refs):
    total = refs[0][...].astype(F32)
    for ref in refs[1:-1]:
        total = total + ref[...].astype(F32)
    refs[-1][...] = total


def sum_two_kernel(left_ref, right_ref, sent_ref):
    sent_ref[...] = (left_ref[...] + right_ref[...]).astype(BF16)


def sum_split_kernel(*refs):
    terms = [ref[...].astype(F32) for ref in refs[:-2]]
    while len(terms) > 1:
        terms = [a + b for a, b in zip(terms[::2], terms[1::2])]
    rank = refs[-1].shape[0]
    refs[-2][...] = terms[0][:rank]
    refs[-1][...] = terms[0][rank:]


def exchange(values, axis, k):
    size = lax.axis_size(axis)
    return lax.ppermute(values, axis, [(i, i ^ k) for i in range(size)])


def per_device(
    query_pooled_states,
    passage_pooled_states,
    query_attention_output,
    passage_attention_output,
    positive_passage_row,
    hard_negative_ids,
    passage_home_row,
    adapter_down_weight,
    adapter_up_weight,
):
    group = lax.axis_size("dp")
    shards = lax.axis_size("fsdp")
    query_raw = query_pooled_states[0]
    passage_raw = passage_pooled_states[0]
    query_in = query_attention_output[0]
    passage_in = passage_attention_output[0]
    ids = hard_negative_ids[0]
    q_dev, width = query_raw.shape
    p_dev = passage_raw.shape[0]
    rank, part = adapter_down_weight.shape
    queries = group * q_dev
    slots = group * CAP
    work = 2 * p_dev * width

    packed, adapter = run(
        pack_kernel,
        (
            shape_of((q_dev, width + 2 * ids.shape[1]), BF16),
            shape_of((2 * rank, part), BF16),
        ),
        (query_raw, ids, adapter_down_weight, adapter_up_weight),
        1,
        [pltpu.VMEM(ids.shape, jnp.int32), pltpu.SemaphoreType.DMA((4,))],
        in_hbm=True,
    )
    blocks = {0: packed}
    for k in range(2, group, 2):
        blocks[k] = exchange(packed, "dp", k)
    blocks[1] = exchange(packed, "dp", 1)
    step = 1
    while step < shards:
        adapter = stack(adapter, exchange(adapter, "fsdp", step))
        step *= 2
    positive_row = jnp.tile(positive_passage_row, (1, group))

    embed, side, side_row = run(
        passage_norm_kernel,
        (
            shape_of((p_dev, width), BF16),
            shape_of((p_dev, 128), F32),
            shape_of((8, p_dev), F32),
        ),
        (passage_raw, passage_home_row),
        work,
    )
    for k in range(2, group, 2):
        blocks[k], side_row = lax.optimization_barrier((blocks[k], side_row))
        blocks[k ^ 1] = exchange(blocks[k], "dp", 1)
    adapter_full, passage_low, query_low, own_side, slot_base = run(
        functools.partial(rank_kernel, shards),
        (
            shape_of((2 * rank, width), BF16),
            shape_of((rank, p_dev), F32),
            shape_of((rank, queries), F32),
            shape_of((8, queries), F32),
            shape_of((rank, p_dev), F32),
        ),
        (adapter, query_raw, query_in, passage_in, embed, side_row),
        work * rank,
    )
    query_embed, weight, dots, onehot, message = run(
        functools.partial(score_kernel, group),
        (
            shape_of((queries, width), BF16),
            shape_of((p_dev, queries), F32),
            shape_of((p_dev, queries), F32),
            shape_of((slots, p_dev), F32),
            shape_of((HEAD_ROWS + 2 * rank, queries), F32),
        ),
        (
            *[blocks[k] for k in range(group)],
            embed,
            side,
            positive_row,
            query_low,
            slot_base,
        ),
        work * queries,
        [pltpu.VMEM((queries, 2 * ids.shape[1]), F32)],
    )
    pair = stack(message, exchange(message, "dp", 1))
    pairs = [pair] + [exchange(pair, "dp", k) for k in range(2, group, 2)]
    back_query, *row_blocks = run(
        functools.partial(request_kernel, group),
        (
            shape_of((rank, queries), F32),
            *[shape_of((2 * CAP, width), BF16)] * (group // 2),
        ),
        (embed, query_embed, adapter_full, onehot),
        work * slots,
    )
    final, *terms = run(
        functools.partial(terms_kernel, group, shards),
        (
            shape_of((p_dev, queries), F32),
            shape_of((2 * rank, part), F32),
            *[shape_of((2 * rank, part), BF16)] * (shards - 1),
        ),
        (
            *pairs,
            weight,
            dots,
            positive_row,
            query_embed,
            embed,
            back_query,
            slot_base,
            passage_low,
            side_row,
            own_side,
            passage_in,
            query_in,
        ),
        work * rank * 4,
        [pltpu.VMEM((2 * rank, width), F32)],
    )
    arrived = [exchange(terms[k], "fsdp", k) for k in range(1, shards)]
    arrived[0], *row_blocks = lax.optimization_barrier((arrived[0], *row_blocks))
    near = [exchange(row_blocks[k // 2], "dp", k) for k in range(2, group, 2)]
    total = run(sum_kernel, (shape_of((2 * rank, part), F32),), (terms[0], *arrived), 1)[0]
    sent = run(
        sum_two_kernel,
        (shape_of((2 * rank, part), BF16),),
        (total, exchange(total, "dp", 1)),
        1,
    )[0]
    arrived = [exchange(sent, "dp", k) for k in range(2, group, 2)]
    down_total, up_total = run(
        sum_split_kernel, (shape_of((rank, part), F32),) * 2, (sent, *arrived), 1
    )

    to_sibling = run(
        forward_kernel,
        (shape_of((group // 2 * CAP, width), BF16),),
        (row_blocks[0], *near),
        1,
    )[0]
    forwarded = exchange(to_sibling, "dp", 1)
    grad_passage = run(
        passage_kernel,
        (shape_of((p_dev, width), BF16),),
        (final, query_embed, passage_raw, side),
        2 * work * queries,
        [pltpu.VMEM((p_dev, width), F32)],
    )[0]
    grad_query = run(
        functools.partial(query_kernel, group),
        (shape_of((q_dev, width), BF16),),
        (*pairs, *near, forwarded, final, embed, query_raw),
        4 * q_dev * width * (p_dev + slots),
        [pltpu.VMEM((q_dev, width), F32)],
    )[0]
    return (grad_query[None], grad_passage[None], down_total, up_total)


def solution(mesh):
    in_specs = (
        P("fsdp", "dp", None),
        P("fsdp", "dp", None),
        P("fsdp", "dp", None),
        P("fsdp", "dp", None),
        P("fsdp", "dp"),
        P("fsdp", "dp", None),
        P("fsdp", None),
        P(None, "fsdp"),
        P(None, "fsdp"),
    )
    out_specs = (P("fsdp", "dp", None), P("fsdp", "dp", None), P(None, "fsdp"), P(None, "fsdp"))
    return jax.shard_map(
        per_device, mesh=mesh, in_specs=in_specs, out_specs=out_specs, check_vma=False
    )
```

```python
import functools

import jax
import jax.numpy as jnp
from jax import lax
from jax.experimental import pallas as pl
from jax.experimental.pallas import tpu as pltpu
from jax.sharding import PartitionSpec as P

CAP = 8
SOFTMAX_HEAT = 0.01
ADAPTER_SCALE = 2.0
EPSILON = 1e-06
LOWEST = -1e30
ID_BASE = 256
TOP_ROW, SUM_ROW, DOT_ROW, HEAD_ROWS = 8, 9, 10, 16
VMEM_BYTES = 16 * 1024 * 1024
ALL_VMEM_BYTES = 60 * 1024 * 1024
F32 = jnp.float32
BF16 = jnp.bfloat16
HIGHEST = lax.Precision.HIGHEST


def dot_nn(a, b, precision=None):
    return lax.dot_general(
        a, b, (((1,), (0,)), ((), ())), precision=precision, preferred_element_type=F32
    )


def dot_nt(a, b, precision=None):
    return lax.dot_general(
        a, b, (((1,), (1,)), ((), ())), precision=precision, preferred_element_type=F32
    )


def split_two(values):
    high = values.astype(BF16)
    low = (values - high.astype(F32)).astype(BF16)
    return high, low


def iota(shape, dim):
    return lax.broadcasted_iota(jnp.int32, shape, dim)


def shape_of(dims, kind):
    return jax.ShapeDtypeStruct(dims, kind)


def run(body, out_shape, args, flops, scratch=(), in_hbm=False):
    grant = ALL_VMEM_BYTES if in_hbm else VMEM_BYTES * max(1, size_ratio(args))
    vmem = pl.BlockSpec(memory_space=pltpu.VMEM)
    hbm = pl.BlockSpec(memory_space=pltpu.HBM)
    moved = sum(a.size * a.dtype.itemsize for a in (*args, *out_shape))
    return pl.pallas_call(
        body,
        out_shape=out_shape,
        in_specs=[hbm if in_hbm else vmem] * len(args),
        out_specs=tuple(vmem for _ in out_shape),
        scratch_shapes=list(scratch),
        compiler_params=pltpu.CompilerParams(vmem_limit_bytes=grant),
        cost_estimate=pl.CostEstimate(flops=flops, bytes_accessed=moved, transcendentals=0),
    )(*args)


def size_ratio(args):
    moved = sum(a.size * a.dtype.itemsize for a in args)
    return -(-moved * 3 // VMEM_BYTES)


def inverse_length(raw_ref, width):
    chunk = min(width, 512)
    total = jnp.zeros((raw_ref.shape[0], 1), F32)
    for at in range(0, width, chunk):
        part = raw_ref[:, at : at + chunk].astype(F32)
        total = total + jnp.sum(part * part, axis=-1, keepdims=True)
    return 1.0 / jnp.sqrt(total + EPSILON)


def pack_kernel(raw_ref, ids_ref, down_ref, up_ref, out_ref, adapter_ref, ids_here, sems):
    width = raw_ref.shape[1]
    copies = [
        pltpu.make_async_copy(ids_ref, ids_here, sems.at[0]),
        pltpu.make_async_copy(raw_ref, out_ref.at[:, pl.ds(0, width)], sems.at[1]),
    ]
    for copy in copies:
        copy.start()
    core = lax.axis_index("dp") % 2

    @pl.when(core == 0)
    def _():
        copy = pltpu.make_async_copy(down_ref, adapter_ref, sems.at[2])
        copy.start()
        copy.wait()

    @pl.when(core == 1)
    def _():
        copy = pltpu.make_async_copy(up_ref, adapter_ref, sems.at[2])
        copy.start()
        copy.wait()

    copies[0].wait()
    ids = ids_here[...]
    coded = jnp.concatenate([ids // ID_BASE, ids % ID_BASE], axis=1)
    out_ref[:, width:] = coded.astype(F32).astype(BF16)
    copies[1].wait()


def stack_kernel(*refs):
    out_ref = refs[-1]
    rows = refs[0].shape[0]
    for i, ref in enumerate(refs[:-1]):
        out_ref[i * rows : (i + 1) * rows, :] = ref[...]


def stack(*parts):
    rows, cols = parts[0].shape
    return run(stack_kernel, (shape_of((len(parts) * rows, cols), parts[0].dtype),), parts, 1)[0]


def passage_norm_kernel(raw_ref, home_ref, embed_ref, side_ref, row_ref):
    rows, width = raw_ref.shape
    total = home_ref.shape[1]
    me = lax.axis_index("dp")
    chunk = min(width, 512)
    inverse = inverse_length(raw_ref, width)
    for at in range(0, width, chunk):
        part = raw_ref[:, at : at + chunk].astype(F32)
        embed_ref[:, at : at + chunk] = (part * inverse).astype(BF16)
    row_id = iota((rows, total), 0) + me * rows
    ids = iota((rows, total), 1)
    home = jnp.sum(jnp.where(home_ref[...] == row_id, ids, 0).astype(F32), axis=1, keepdims=True)
    side_ref[...] = jnp.where(iota(side_ref.shape, 1) == 0, inverse, home)
    row_ref[...] = jnp.broadcast_to(inverse, (rows, rows)).T[: row_ref.shape[0]]


def rank_kernel(
    shards,
    near_ref,
    far_ref,
    query_ref,
    query_in_ref,
    passage_in_ref,
    embed_ref,
    row_ref,
    weights_ref,
    passage_low_ref,
    query_low_ref,
    own_ref,
    slot_base_ref,
):
    part = near_ref.shape[1]
    rank = near_ref.shape[0] // shards
    q_dev, width = query_ref.shape
    queries = own_ref.shape[1]
    me = lax.axis_index("fsdp")
    core = lax.axis_index("dp") % 2
    for k in range(shards):
        cols = pl.ds(pl.multiple_of((me ^ k) * part, part), part)
        near_rows = pl.ds(pl.multiple_of(core * rank, rank), rank)
        far_rows = pl.ds(pl.multiple_of((1 - core) * rank, rank), rank)
        weights_ref[near_rows, cols] = near_ref[k * rank : (k + 1) * rank, :]
        weights_ref[far_rows, cols] = far_ref[k * rank : (k + 1) * rank, :]
    down, up = weights_ref[:rank, :], weights_ref[rank:, :]
    place = iota((q_dev, queries), 1) == iota((q_dev, queries), 0) + lax.axis_index("dp") * q_dev
    inverse = inverse_length(query_ref, width)
    own = jnp.sum(jnp.where(place, inverse, 0.0), axis=0, keepdims=True)
    own_ref[...] = jnp.broadcast_to(own, own_ref.shape)
    same = iota((q_dev, q_dev), 0) == iota((q_dev, q_dev), 1)
    inverse_row = jnp.sum(jnp.where(same, inverse, 0.0), axis=0, keepdims=True)
    query_low = dot_nt(down, query_in_ref[...]).astype(BF16)
    query_low_ref[...] = query_low.astype(F32) * inverse_row
    passage_low = dot_nt(down, passage_in_ref[...]).astype(BF16)
    passage_low_ref[...] = passage_low.astype(F32) * row_ref[0:1, :]
    slot_base_ref[...] = dot_nt(up, embed_ref[...])


def score_kernel(group, *refs):
    blocks = refs[:group]
    embed_ref, side_ref, positive_ref, query_low_ref, base_ref = refs[group : group + 5]
    query_ref, weight_ref, dots_ref, onehot_ref, message_ref, coded_ref = refs[group + 5 :]
    rows, width = embed_ref.shape
    queries = query_ref.shape[0]
    q_dev = queries // group
    negatives = (blocks[0].shape[1] - width) // 2
    slots = group * CAP
    rank = query_low_ref.shape[0]
    me = lax.axis_index("dp")
    chunk = min(width, 1024)
    for k in range(group):
        start = pl.multiple_of((me ^ k) * q_dev, q_dev)
        inverse = inverse_length(blocks[k], width)
        for at in range(0, width, chunk):
            part = blocks[k][:, at : at + chunk].astype(F32)
            query_ref[pl.ds(start, q_dev), at : at + chunk] = (part * inverse).astype(BF16)
        coded = blocks[k][:, width:].astype(F32)
        coded_ref[pl.ds(start, q_dev), :] = coded
    dots = dot_nt(embed_ref[...], query_ref[...])
    dots_ref[...] = dots
    scores = dots / SOFTMAX_HEAT

    coded = coded_ref[...].T
    ids = coded[:negatives] * float(ID_BASE) + coded[negatives:]
    home = jnp.broadcast_to(side_ref[:, 1:2], (rows, queries))
    count = jnp.zeros((rows, queries), F32)
    for j in range(negatives):
        count = count + jnp.where(ids[j : j + 1, :] == home, 1.0, 0.0)
    members = iota((slots, queries), 0) // CAP == iota((slots, queries), 1) // q_dev
    marked = dot_nt(members.astype(BF16), count.astype(BF16)) > 0.0
    before = (iota((rows, rows), 0) <= iota((rows, rows), 1)).astype(BF16)
    rank_in = dot_nn(marked.astype(F32).astype(BF16), before)
    wanted = (iota((slots, rows), 0) % CAP + 1).astype(F32)
    onehot = jnp.where(marked & (rank_in == wanted), 1.0, 0.0)
    onehot_ref[...] = onehot

    own = iota((rows, queries), 1) // q_dev == me
    count = count + jnp.where(own & (positive_ref[...] == iota((rows, queries), 0)), 1.0, 0.0)
    named = count > 0.0
    top = jnp.max(jnp.where(named, scores, LOWEST), axis=0, keepdims=True)
    weight = count * jnp.exp(jnp.where(named, scores - top, LOWEST))
    weight_ref[...] = weight
    total = jnp.sum(weight, axis=0, keepdims=True)
    dot_total = jnp.sum(weight * dots, axis=0, keepdims=True)
    slot_weight = dot_nn(onehot, weight, precision=HIGHEST)
    slot_base = dot_nt(base_ref[...], onehot, precision=HIGHEST)
    tail_row = iota((HEAD_ROWS - CAP, queries), 0)
    tail = jnp.where(tail_row == 0, top, jnp.where(tail_row == 1, total, dot_total))
    lane_group = iota((CAP, queries), 1) // q_dev
    compact = jnp.zeros((CAP, queries), F32)
    for peer in range(group):
        part = slot_weight[peer * CAP : (peer + 1) * CAP]
        compact = jnp.where(lane_group == peer, part, compact)
    message_ref[:CAP, :] = compact
    message_ref[CAP:HEAD_ROWS, :] = tail
    message_ref[HEAD_ROWS:, :slots] = slot_base
    message_ref[HEAD_ROWS:, slots : slots + q_dev] = query_low_ref[...]


def request_kernel(group, embed_ref, query_ref, weights_ref, onehot_ref, back_ref, *blocks):
    width = embed_ref.shape[1]
    rank = weights_ref.shape[0] // 2
    me = lax.axis_index("dp")
    back_ref[...] = dot_nt(weights_ref[rank:, :], query_ref[...])
    onehot = [
        onehot_ref[pl.ds(pl.multiple_of((me ^ k) * CAP, CAP), CAP), :] for k in range(group)
    ]
    onehot = jnp.concatenate(onehot, axis=0).astype(BF16)
    chunk = min(width, 1024)
    for at in range(0, width, chunk):
        part = dot_nn(onehot, embed_ref[:, at : at + chunk]).astype(BF16)
        for i, block in enumerate(blocks):
            block[:, at : at + chunk] = part[2 * i * CAP : 2 * (i + 1) * CAP]


def forward_kernel(*refs):
    out_ref = refs[-1]
    for i, ref in enumerate(refs[:-1]):
        out_ref[i * CAP : (i + 1) * CAP, :] = ref[CAP:, :]


def message_parts(near_ref, far_ref, group):
    rows = near_ref.shape[0] // (group // 2)
    return [((near_ref, far_ref)[k % 2], k // 2 * rows) for k in range(group)]


def combine(parts):
    tops = [ref[at + TOP_ROW : at + TOP_ROW + 1, :] for ref, at in parts]
    sums = [ref[at + SUM_ROW : at + SUM_ROW + 1, :] for ref, at in parts]
    top = functools.reduce(jnp.maximum, tops)
    scales = [jnp.exp(t - top) for t in tops]
    inverse_total = 1.0 / sum(t * s for t, s in zip(scales, sums))
    return [scale * inverse_total for scale in scales]


def own_target(positive_ref, rows, queries, q_dev, me):
    own = iota((rows, queries), 1) // q_dev == me
    return jnp.where(own & (positive_ref[...] == iota((rows, queries), 0)), 1.0, 0.0)


def terms_kernel(group, shards, near_ref, far_ref, *refs):
    parts = message_parts(near_ref, far_ref, group)
    (
        weight_ref,
        dots_ref,
        positive_ref,
        query_ref,
        embed_ref,
        back_query_ref,
        back_passage_ref,
        passage_low_ref,
        row_ref,
        own_ref,
        passage_in_ref,
        query_in_ref,
    ) = refs[:12]
    final_ref = refs[12]
    blocks = refs[13 : 13 + shards]
    (sum_ref,) = refs[13 + shards :]
    rows, queries = weight_ref.shape
    q_dev = queries // group
    rank = passage_low_ref.shape[0]
    width = query_ref.shape[1]
    me = lax.axis_index("dp")

    scales = combine(parts)
    target = own_target(positive_ref, rows, queries, q_dev, me)
    weight = (weight_ref[...] * scales[0] - target) / SOFTMAX_HEAT
    final_ref[...] = weight
    dots = dots_ref[...]
    weighted = weight * dots
    share = jnp.sum(weighted, axis=0, keepdims=True)
    ones = jnp.ones((8, queries), F32)
    inner = dot_nt(ones, weighted, precision=HIGHEST)[0:1, :]

    inner_query = -jnp.sum(target * dots, axis=0, keepdims=True)
    slots = group * CAP
    bases, query_low = [], []
    for (ref, at), scale in zip(parts, scales):
        inner_query = inner_query + scale * ref[at + DOT_ROW : at + DOT_ROW + 1, :]
        bases.append(ref[at + HEAD_ROWS : at + HEAD_ROWS + rank, :slots])
        query_low.append(ref[at + HEAD_ROWS : at + HEAD_ROWS + rank, slots : slots + q_dev])
    sent_by = me ^ (iota((queries, queries), 0) // q_dev)
    place = iota((queries, queries), 1) == sent_by * q_dev + iota((queries, queries), 0) % q_dev
    query_low = dot_nn(
        jnp.concatenate(query_low, axis=1), place.astype(F32), precision=HIGHEST
    )
    pick_slots = (iota((slots, CAP), 0) == iota((slots, CAP), 1) + me * CAP).astype(F32)
    bases = dot_nn(jnp.concatenate(bases[1:], axis=0), pick_slots, precision=HIGHEST)
    far_base = [bases[k * rank : (k + 1) * rank] for k in range(group - 1)]
    far_weight = [
        ref[at : at + CAP, :] * (scale / SOFTMAX_HEAT)
        for (ref, at), scale in zip(parts[1:], scales[1:])
    ]
    inner_query = inner_query / SOFTMAX_HEAT

    passage_low = passage_low_ref[...]
    from_query = dot_nn(passage_low, weight, precision=HIGHEST) - query_low * share
    from_passage = dot_nt(query_low, weight, precision=HIGHEST) - passage_low * inner
    query_parts = jnp.concatenate(split_two(from_query), axis=0)
    passage_parts = jnp.concatenate(split_two(from_passage), axis=0)

    back_passage = dot_nt(back_query_ref[...], weight, precision=HIGHEST)
    back_passage = (back_passage - back_passage_ref[...] * inner) * row_ref[0:1, :]
    back_passage = back_passage.astype(BF16)
    back_query = dot_nn(back_passage_ref[...], weight, precision=HIGHEST)
    back_query = back_query + dot_nn(
        jnp.concatenate(far_base, axis=1),
        jnp.concatenate(far_weight, axis=0),
        precision=HIGHEST,
    )
    back_query = (back_query - back_query_ref[...] * inner_query) * own_ref[0:1, :]
    pick = (iota((q_dev, queries), 1) == iota((q_dev, queries), 0) + me * q_dev).astype(BF16)
    back_query = dot_nt(back_query.astype(BF16), pick).astype(BF16)

    chunk = min(width, 512)
    for at in range(0, width, chunk):
        cols = slice(at, at + chunk)
        both = dot_nn(query_parts, query_ref[:, cols]) + dot_nn(passage_parts, embed_ref[:, cols])
        sum_ref[rank:, cols] = ADAPTER_SCALE * (both[:rank] + both[rank:])
        sum_ref[:rank, cols] = ADAPTER_SCALE * (
            dot_nn(back_passage, passage_in_ref[:, cols])
            + dot_nn(back_query, query_in_ref[:, cols])
        )
    part = width // shards
    home = lax.axis_index("fsdp")
    for k in range(shards):
        start = pl.multiple_of((home ^ k) * part, part)
        blocks[k][...] = sum_ref[:, pl.ds(start, part)].astype(blocks[k].dtype)


def backward(upstream_of, raw_ref, inverse, grad_ref, up_ref):
    rows, width = raw_ref.shape
    chunk = min(width, 512)
    inner = jnp.zeros((rows, 1), F32)
    for at in range(0, width, chunk):
        upstream = upstream_of(at, chunk)
        up_ref[:, at : at + chunk] = upstream
        unit = raw_ref[:, at : at + chunk].astype(F32) * inverse
        inner = inner + jnp.sum(unit * upstream, axis=-1, keepdims=True)
    for at in range(0, width, chunk):
        unit = raw_ref[:, at : at + chunk].astype(F32) * inverse
        grad = (up_ref[:, at : at + chunk] - unit * inner) * inverse
        grad_ref[:, at : at + chunk] = grad.astype(BF16)


def passage_kernel(final_ref, query_ref, raw_ref, side_ref, grad_ref, up_ref):
    high, low = split_two(final_ref[...])

    def upstream_of(at, chunk):
        embed = query_ref[:, at : at + chunk]
        return dot_nn(high, embed) + dot_nn(low, embed)

    backward(upstream_of, raw_ref, side_ref[:, 0:1], grad_ref, up_ref)


def query_kernel(group, near_ref, far_ref, *refs):
    parts = message_parts(near_ref, far_ref, group)
    near = refs[: group // 2 - 1]
    forwarded_ref, final_ref, embed_ref, raw_ref, grad_ref, up_ref = refs[group // 2 - 1 :]
    q_dev, width = raw_ref.shape
    queries = final_ref.shape[1]
    me = lax.axis_index("dp")
    scales = combine(parts)
    pick = (iota((q_dev, queries), 1) == iota((q_dev, queries), 0) + me * q_dev).astype(F32)
    far = [
        ref[at : at + CAP, :] * (scale / SOFTMAX_HEAT) for (ref, at), scale in zip(parts, scales)
    ]
    far = far[2::2] + far[1::2] + [jnp.zeros((CAP, queries), F32)]
    own_parts = split_two(dot_nt(pick, final_ref[...], precision=HIGHEST))
    far_parts = split_two(dot_nt(pick, jnp.concatenate(far, axis=0), precision=HIGHEST))
    own_parts = jnp.concatenate(own_parts, axis=0)
    far_parts = jnp.concatenate(far_parts, axis=0)

    def upstream_of(at, chunk):
        rows = [ref[:, at : at + chunk].astype(F32)[:CAP] for ref in near]
        rows.append(forwarded_ref[:, at : at + chunk].astype(F32))
        rows.append(jnp.zeros((CAP, chunk), F32))
        both = dot_nn(own_parts, embed_ref[:, at : at + chunk])
        both = both + dot_nn(far_parts, jnp.concatenate(rows, axis=0).astype(BF16))
        return both[:q_dev] + both[q_dev:]

    backward(upstream_of, raw_ref, inverse_length(raw_ref, width), grad_ref, up_ref)


def sum_kernel(*refs):
    total = refs[0][...].astype(F32)
    for ref in refs[1:-1]:
        total = total + ref[...].astype(F32)
    refs[-1][...] = total


def sum_two_kernel(left_ref, right_ref, sent_ref):
    sent_ref[...] = (left_ref[...] + right_ref[...]).astype(BF16)


def sum_split_kernel(*refs):
    terms = [ref[...].astype(F32) for ref in refs[:-2]]
    while len(terms) > 1:
        terms = [a + b for a, b in zip(terms[::2], terms[1::2])]
    rank = refs[-1].shape[0]
    refs[-2][...] = terms[0][:rank]
    refs[-1][...] = terms[0][rank:]


def exchange(values, axis, k):
    size = lax.axis_size(axis)
    return lax.ppermute(values, axis, [(i, i ^ k) for i in range(size)])


def per_device(
    query_pooled_states,
    passage_pooled_states,
    query_attention_output,
    passage_attention_output,
    positive_passage_row,
    hard_negative_ids,
    passage_home_row,
    adapter_down_weight,
    adapter_up_weight,
):
    group = lax.axis_size("dp")
    shards = lax.axis_size("fsdp")
    query_raw = query_pooled_states[0]
    passage_raw = passage_pooled_states[0]
    query_in = query_attention_output[0]
    passage_in = passage_attention_output[0]
    ids = hard_negative_ids[0]
    q_dev, width = query_raw.shape
    p_dev = passage_raw.shape[0]
    rank, part = adapter_down_weight.shape
    queries = group * q_dev
    slots = group * CAP
    work = 2 * p_dev * width

    packed, adapter = run(
        pack_kernel,
        (
            shape_of((q_dev, width + 2 * ids.shape[1]), BF16),
            shape_of((rank, part), BF16),
        ),
        (query_raw, ids, adapter_down_weight, adapter_up_weight),
        1,
        [pltpu.VMEM(ids.shape, jnp.int32), pltpu.SemaphoreType.DMA((3,))],
        in_hbm=True,
    )
    blocks = {0: packed}
    for k in range(2, group, 2):
        blocks[k] = exchange(packed, "dp", k)
    blocks[1] = exchange(packed, "dp", 1)
    step = 1
    while step < shards:
        adapter = stack(adapter, exchange(adapter, "fsdp", step))
        step *= 2
    adapter_far = exchange(adapter, "dp", 1)
    positive_row = jnp.tile(positive_passage_row, (1, group))

    embed, side, side_row = run(
        passage_norm_kernel,
        (
            shape_of((p_dev, width), BF16),
            shape_of((p_dev, 128), F32),
            shape_of((8, p_dev), F32),
        ),
        (passage_raw, passage_home_row),
        work,
    )
    for k in range(2, group, 2):
        blocks[k], side_row = lax.optimization_barrier((blocks[k], side_row))
        blocks[k ^ 1] = exchange(blocks[k], "dp", 1)
    adapter_full, passage_low, query_low, own_side, slot_base = run(
        functools.partial(rank_kernel, shards),
        (
            shape_of((2 * rank, width), BF16),
            shape_of((rank, p_dev), F32),
            shape_of((rank, q_dev), F32),
            shape_of((8, queries), F32),
            shape_of((rank, p_dev), F32),
        ),
        (adapter, adapter_far, query_raw, query_in, passage_in, embed, side_row),
        work * rank,
    )
    query_embed, weight, dots, onehot, message = run(
        functools.partial(score_kernel, group),
        (
            shape_of((queries, width), BF16),
            shape_of((p_dev, queries), F32),
            shape_of((p_dev, queries), F32),
            shape_of((slots, p_dev), F32),
            shape_of((HEAD_ROWS + rank, queries), F32),
        ),
        (
            *[blocks[k] for k in range(group)],
            embed,
            side,
            positive_row,
            query_low,
            slot_base,
        ),
        work * queries,
        [pltpu.VMEM((queries, 2 * ids.shape[1]), F32)],
    )
    near_stats = stack(message, *[exchange(message, "dp", k) for k in range(2, group, 2)])
    far_stats = exchange(near_stats, "dp", 1)
    back_query, *row_blocks = run(
        functools.partial(request_kernel, group),
        (
            shape_of((rank, queries), F32),
            *[shape_of((2 * CAP, width), BF16)] * (group // 2),
        ),
        (embed, query_embed, adapter_full, onehot),
        work * slots,
    )
    final, *terms = run(
        functools.partial(terms_kernel, group, shards),
        (
            shape_of((p_dev, queries), F32),
            shape_of((2 * rank, part), F32),
            *[shape_of((2 * rank, part), BF16)] * (shards - 1),
        ),
        (
            near_stats,
            far_stats,
            weight,
            dots,
            positive_row,
            query_embed,
            embed,
            back_query,
            slot_base,
            passage_low,
            side_row,
            own_side,
            passage_in,
            query_in,
        ),
        work * rank * 4,
        [pltpu.VMEM((2 * rank, width), F32)],
    )
    arrived = [exchange(terms[k], "fsdp", k) for k in range(1, shards)]
    final, *row_blocks = lax.optimization_barrier((final, *row_blocks))
    near = [exchange(row_blocks[k // 2], "dp", k) for k in range(2, group, 2)]
    total = run(sum_kernel, (shape_of((2 * rank, part), F32),), (terms[0], *arrived), 1)[0]
    sent = run(
        sum_two_kernel,
        (shape_of((2 * rank, part), BF16),),
        (total, exchange(total, "dp", 1)),
        1,
    )[0]
    arrived = [exchange(sent, "dp", k) for k in range(2, group, 2)]
    *arrived, near = lax.optimization_barrier((*arrived, near))
    down_total, up_total = run(
        sum_split_kernel, (shape_of((rank, part), F32),) * 2, (sent, *arrived), 1
    )

    to_sibling = run(
        forward_kernel,
        (shape_of((group // 2 * CAP, width), BF16),),
        (row_blocks[0], *near),
        1,
    )[0]
    forwarded = exchange(to_sibling, "dp", 1)
    grad_passage = run(
        passage_kernel,
        (shape_of((p_dev, width), BF16),),
        (final, query_embed, passage_raw, side),
        2 * work * queries,
        [pltpu.VMEM((p_dev, width), F32)],
    )[0]
    grad_query = run(
        functools.partial(query_kernel, group),
        (shape_of((q_dev, width), BF16),),
        (near_stats, far_stats, *near, forwarded, final, embed, query_raw),
        4 * q_dev * width * (p_dev + slots),
        [pltpu.VMEM((q_dev, width), F32)],
    )[0]
    return (grad_query[None], grad_passage[None], down_total, up_total)


def solution(mesh):
    in_specs = (
        P("fsdp", "dp", None),
        P("fsdp", "dp", None),
        P("fsdp", "dp", None),
        P("fsdp", "dp", None),
        P("fsdp", "dp"),
        P("fsdp", "dp", None),
        P("fsdp", None),
        P(None, "fsdp"),
        P(None, "fsdp"),
    )
    out_specs = (P("fsdp", "dp", None), P("fsdp", "dp", None), P(None, "fsdp"), P(None, "fsdp"))
    return jax.shard_map(
        per_device, mesh=mesh, in_specs=in_specs, out_specs=out_specs, check_vma=False
    )
```

```python
import functools

import jax
import jax.numpy as jnp
from jax import lax
from jax.experimental import pallas as pl
from jax.experimental.pallas import tpu as pltpu
from jax.sharding import PartitionSpec as P

CAP = 8
SOFTMAX_HEAT = 0.01
ADAPTER_SCALE = 2.0
EPSILON = 1e-06
LOWEST = -1e30
ID_BASE = 256
TOP_ROW, SUM_ROW, DOT_ROW, HEAD_ROWS = 8, 9, 10, 16
VMEM_BYTES = 16 * 1024 * 1024
ALL_VMEM_BYTES = 60 * 1024 * 1024
F32 = jnp.float32
BF16 = jnp.bfloat16
HIGHEST = lax.Precision.HIGHEST


def dot_nn(a, b, precision=None):
    return lax.dot_general(
        a, b, (((1,), (0,)), ((), ())), precision=precision, preferred_element_type=F32
    )


def dot_nt(a, b, precision=None):
    return lax.dot_general(
        a, b, (((1,), (1,)), ((), ())), precision=precision, preferred_element_type=F32
    )


def split_two(values):
    high = values.astype(BF16)
    low = (values - high.astype(F32)).astype(BF16)
    return high, low


def iota(shape, dim):
    return lax.broadcasted_iota(jnp.int32, shape, dim)


def shape_of(dims, kind):
    return jax.ShapeDtypeStruct(dims, kind)


def run(body, out_shape, args, flops, scratch=(), in_hbm=False):
    grant = ALL_VMEM_BYTES if in_hbm else VMEM_BYTES * max(1, size_ratio(args))
    vmem = pl.BlockSpec(memory_space=pltpu.VMEM)
    hbm = pl.BlockSpec(memory_space=pltpu.HBM)
    moved = sum(a.size * a.dtype.itemsize for a in (*args, *out_shape))
    return pl.pallas_call(
        body,
        out_shape=out_shape,
        in_specs=[hbm if in_hbm else vmem] * len(args),
        out_specs=tuple(vmem for _ in out_shape),
        scratch_shapes=list(scratch),
        compiler_params=pltpu.CompilerParams(vmem_limit_bytes=grant),
        cost_estimate=pl.CostEstimate(flops=flops, bytes_accessed=moved, transcendentals=0),
    )(*args)


def size_ratio(args):
    moved = sum(a.size * a.dtype.itemsize for a in args)
    return -(-moved * 3 // VMEM_BYTES)


def inverse_length(raw_ref, width):
    chunk = min(width, 512)
    total = jnp.zeros((raw_ref.shape[0], 1), F32)
    for at in range(0, width, chunk):
        part = raw_ref[:, at : at + chunk].astype(F32)
        total = total + jnp.sum(part * part, axis=-1, keepdims=True)
    return 1.0 / jnp.sqrt(total + EPSILON)


def pack_kernel(raw_ref, ids_ref, down_ref, up_ref, out_ref, adapter_ref, ids_here, sems):
    width = raw_ref.shape[1]
    rank = down_ref.shape[0]
    copies = [
        pltpu.make_async_copy(src, dst, sems.at[i])
        for i, (src, dst) in enumerate(
            (
                (ids_ref, ids_here),
                (raw_ref, out_ref.at[:, pl.ds(0, width)]),
                (down_ref, adapter_ref.at[pl.ds(0, rank), :]),
                (up_ref, adapter_ref.at[pl.ds(rank, rank), :]),
            )
        )
    ]
    for copy in copies:
        copy.start()
    copies[0].wait()
    ids = ids_here[...]
    coded = jnp.concatenate([ids // ID_BASE, ids % ID_BASE], axis=1)
    out_ref[:, width:] = coded.astype(F32).astype(BF16)
    for copy in copies[1:]:
        copy.wait()


def stack_kernel(*refs):
    out_ref = refs[-1]
    rows = refs[0].shape[0]
    for i, ref in enumerate(refs[:-1]):
        out_ref[i * rows : (i + 1) * rows, :] = ref[...]


def stack(*parts):
    rows, cols = parts[0].shape
    return run(stack_kernel, (shape_of((len(parts) * rows, cols), parts[0].dtype),), parts, 1)[0]


def passage_norm_kernel(raw_ref, home_ref, embed_ref, side_ref, row_ref):
    rows, width = raw_ref.shape
    total = home_ref.shape[1]
    me = lax.axis_index("dp")
    chunk = min(width, 512)
    inverse = inverse_length(raw_ref, width)
    for at in range(0, width, chunk):
        part = raw_ref[:, at : at + chunk].astype(F32)
        embed_ref[:, at : at + chunk] = (part * inverse).astype(BF16)
    row_id = iota((rows, total), 0) + me * rows
    ids = iota((rows, total), 1)
    home = jnp.sum(jnp.where(home_ref[...] == row_id, ids, 0).astype(F32), axis=1, keepdims=True)
    side_ref[...] = jnp.where(iota(side_ref.shape, 1) == 0, inverse, home)
    row_ref[...] = jnp.broadcast_to(inverse, (rows, rows)).T[: row_ref.shape[0]]


def rank_kernel(
    shards,
    blocks_ref,
    query_ref,
    query_in_ref,
    passage_in_ref,
    embed_ref,
    row_ref,
    weights_ref,
    passage_low_ref,
    query_low_ref,
    own_ref,
    slot_base_ref,
):
    part = blocks_ref.shape[2]
    rank = blocks_ref.shape[1] // 2
    q_dev, width = query_ref.shape
    queries = own_ref.shape[1]
    for f in range(shards):
        weights_ref[:, f * part : (f + 1) * part] = blocks_ref[f]
    down, up = weights_ref[:rank, :], weights_ref[rank:, :]
    place = iota((q_dev, queries), 1) == iota((q_dev, queries), 0) + lax.axis_index("dp") * q_dev
    inverse = inverse_length(query_ref, width)
    own = jnp.sum(jnp.where(place, inverse, 0.0), axis=0, keepdims=True)
    own_ref[...] = jnp.broadcast_to(own, own_ref.shape)
    same = iota((q_dev, q_dev), 0) == iota((q_dev, q_dev), 1)
    inverse_row = jnp.sum(jnp.where(same, inverse, 0.0), axis=0, keepdims=True)
    query_low = dot_nt(down, query_in_ref[...]).astype(BF16)
    query_low_ref[...] = query_low.astype(F32) * inverse_row
    passage_low = dot_nt(down, passage_in_ref[...]).astype(BF16)
    passage_low_ref[...] = passage_low.astype(F32) * row_ref[0:1, :]
    slot_base_ref[...] = dot_nt(up, embed_ref[...])


def score_kernel(group, *refs):
    blocks = refs[:group]
    embed_ref, side_ref, positive_ref, query_low_ref, base_ref = refs[group : group + 5]
    query_ref, weight_ref, dots_ref, onehot_ref, message_ref, coded_ref = refs[group + 5 :]
    rows, width = embed_ref.shape
    queries = query_ref.shape[0]
    q_dev = queries // group
    negatives = (blocks[0].shape[1] - width) // 2
    slots = group * CAP
    rank = query_low_ref.shape[0]
    me = lax.axis_index("dp")
    chunk = min(width, 1024)
    for k in range(group):
        start = pl.multiple_of((me ^ k) * q_dev, q_dev)
        inverse = inverse_length(blocks[k], width)
        for at in range(0, width, chunk):
            part = blocks[k][:, at : at + chunk].astype(F32)
            query_ref[pl.ds(start, q_dev), at : at + chunk] = (part * inverse).astype(BF16)
        coded = blocks[k][:, width:].astype(F32)
        coded_ref[pl.ds(start, q_dev), :] = coded
    dots = dot_nt(embed_ref[...], query_ref[...])
    dots_ref[...] = dots
    scores = dots / SOFTMAX_HEAT

    coded = coded_ref[...].T
    ids = coded[:negatives] * float(ID_BASE) + coded[negatives:]
    home = jnp.broadcast_to(side_ref[:, 1:2], (rows, queries))
    count = jnp.zeros((rows, queries), F32)
    for j in range(negatives):
        count = count + jnp.where(ids[j : j + 1, :] == home, 1.0, 0.0)
    members = iota((slots, queries), 0) // CAP == iota((slots, queries), 1) // q_dev
    marked = dot_nt(members.astype(BF16), count.astype(BF16)) > 0.0
    before = (iota((rows, rows), 0) <= iota((rows, rows), 1)).astype(BF16)
    rank_in = dot_nn(marked.astype(F32).astype(BF16), before)
    wanted = (iota((slots, rows), 0) % CAP + 1).astype(F32)
    onehot = jnp.where(marked & (rank_in == wanted), 1.0, 0.0)
    onehot_ref[...] = onehot

    own = iota((rows, queries), 1) // q_dev == me
    count = count + jnp.where(own & (positive_ref[...] == iota((rows, queries), 0)), 1.0, 0.0)
    named = count > 0.0
    top = jnp.max(jnp.where(named, scores, LOWEST), axis=0, keepdims=True)
    weight = count * jnp.exp(jnp.where(named, scores - top, LOWEST))
    weight_ref[...] = weight
    total = jnp.sum(weight, axis=0, keepdims=True)
    dot_total = jnp.sum(weight * dots, axis=0, keepdims=True)
    slot_weight = dot_nn(onehot, weight, precision=HIGHEST)
    slot_base = dot_nt(base_ref[...], onehot, precision=HIGHEST)
    tail_row = iota((HEAD_ROWS - CAP, queries), 0)
    tail = jnp.where(tail_row == 0, top, jnp.where(tail_row == 1, total, dot_total))
    lane_group = iota((CAP, queries), 1) // q_dev
    compact = jnp.zeros((CAP, queries), F32)
    for peer in range(group):
        part = slot_weight[peer * CAP : (peer + 1) * CAP]
        compact = jnp.where(lane_group == peer, part, compact)
    message_ref[:CAP, :] = compact
    message_ref[CAP:HEAD_ROWS, :] = tail
    message_ref[HEAD_ROWS:, :slots] = slot_base
    message_ref[HEAD_ROWS:, slots : slots + q_dev] = query_low_ref[...]


def request_kernel(group, embed_ref, query_ref, weights_ref, onehot_ref, back_ref, *blocks):
    width = embed_ref.shape[1]
    rank = weights_ref.shape[0] // 2
    me = lax.axis_index("dp")
    back_ref[...] = dot_nt(weights_ref[rank:, :], query_ref[...])
    onehot = [
        onehot_ref[pl.ds(pl.multiple_of((me ^ k) * CAP, CAP), CAP), :] for k in range(group)
    ]
    onehot = jnp.concatenate(onehot, axis=0).astype(BF16)
    chunk = min(width, 1024)
    for at in range(0, width, chunk):
        part = dot_nn(onehot, embed_ref[:, at : at + chunk]).astype(BF16)
        for i, block in enumerate(blocks):
            block[:, at : at + chunk] = part[2 * i * CAP : 2 * (i + 1) * CAP]


def forward_kernel(*refs):
    out_ref = refs[-1]
    for i, ref in enumerate(refs[:-1]):
        out_ref[i * CAP : (i + 1) * CAP, :] = ref[CAP:, :]


def message_parts(near_ref, far_ref, group):
    rows = near_ref.shape[0] // (group // 2)
    return [((near_ref, far_ref)[k % 2], k // 2 * rows) for k in range(group)]


def combine(parts):
    tops = [ref[at + TOP_ROW : at + TOP_ROW + 1, :] for ref, at in parts]
    sums = [ref[at + SUM_ROW : at + SUM_ROW + 1, :] for ref, at in parts]
    top = functools.reduce(jnp.maximum, tops)
    scales = [jnp.exp(t - top) for t in tops]
    inverse_total = 1.0 / sum(t * s for t, s in zip(scales, sums))
    return [scale * inverse_total for scale in scales]


def own_target(positive_ref, rows, queries, q_dev, me):
    own = iota((rows, queries), 1) // q_dev == me
    return jnp.where(own & (positive_ref[...] == iota((rows, queries), 0)), 1.0, 0.0)


def terms_kernel(group, shards, near_ref, far_ref, *refs):
    parts = message_parts(near_ref, far_ref, group)
    (
        weight_ref,
        dots_ref,
        positive_ref,
        query_ref,
        embed_ref,
        back_query_ref,
        back_passage_ref,
        passage_low_ref,
        row_ref,
        own_ref,
        passage_in_ref,
        query_in_ref,
    ) = refs[:12]
    final_ref = refs[12]
    blocks = refs[13 : 13 + shards]
    (sum_ref,) = refs[13 + shards :]
    rows, queries = weight_ref.shape
    q_dev = queries // group
    rank = passage_low_ref.shape[0]
    width = query_ref.shape[1]
    me = lax.axis_index("dp")

    scales = combine(parts)
    target = own_target(positive_ref, rows, queries, q_dev, me)
    weight = (weight_ref[...] * scales[0] - target) / SOFTMAX_HEAT
    final_ref[...] = weight
    dots = dots_ref[...]
    weighted = weight * dots
    share = jnp.sum(weighted, axis=0, keepdims=True)
    ones = jnp.ones((8, queries), F32)
    inner = dot_nt(ones, weighted, precision=HIGHEST)[0:1, :]

    inner_query = -jnp.sum(target * dots, axis=0, keepdims=True)
    slots = group * CAP
    bases, query_low = [], []
    for (ref, at), scale in zip(parts, scales):
        inner_query = inner_query + scale * ref[at + DOT_ROW : at + DOT_ROW + 1, :]
        bases.append(ref[at + HEAD_ROWS : at + HEAD_ROWS + rank, :slots])
        query_low.append(ref[at + HEAD_ROWS : at + HEAD_ROWS + rank, slots : slots + q_dev])
    sent_by = me ^ (iota((queries, queries), 0) // q_dev)
    place = iota((queries, queries), 1) == sent_by * q_dev + iota((queries, queries), 0) % q_dev
    query_low = dot_nn(
        jnp.concatenate(query_low, axis=1), place.astype(F32), precision=HIGHEST
    )
    pick_slots = (iota((slots, CAP), 0) == iota((slots, CAP), 1) + me * CAP).astype(F32)
    bases = dot_nn(jnp.concatenate(bases[1:], axis=0), pick_slots, precision=HIGHEST)
    far_base = [bases[k * rank : (k + 1) * rank] for k in range(group - 1)]
    far_weight = [
        ref[at : at + CAP, :] * (scale / SOFTMAX_HEAT)
        for (ref, at), scale in zip(parts[1:], scales[1:])
    ]
    inner_query = inner_query / SOFTMAX_HEAT

    passage_low = passage_low_ref[...]
    from_query = dot_nn(passage_low, weight, precision=HIGHEST) - query_low * share
    from_passage = dot_nt(query_low, weight, precision=HIGHEST) - passage_low * inner
    query_parts = jnp.concatenate(split_two(from_query), axis=0)
    passage_parts = jnp.concatenate(split_two(from_passage), axis=0)

    back_passage = dot_nt(back_query_ref[...], weight, precision=HIGHEST)
    back_passage = (back_passage - back_passage_ref[...] * inner) * row_ref[0:1, :]
    back_passage = back_passage.astype(BF16)
    back_query = dot_nn(back_passage_ref[...], weight, precision=HIGHEST)
    back_query = back_query + dot_nn(
        jnp.concatenate(far_base, axis=1),
        jnp.concatenate(far_weight, axis=0),
        precision=HIGHEST,
    )
    back_query = (back_query - back_query_ref[...] * inner_query) * own_ref[0:1, :]
    pick = (iota((q_dev, queries), 1) == iota((q_dev, queries), 0) + me * q_dev).astype(BF16)
    back_query = dot_nt(back_query.astype(BF16), pick).astype(BF16)

    chunk = min(width, 512)
    for at in range(0, width, chunk):
        cols = slice(at, at + chunk)
        both = dot_nn(query_parts, query_ref[:, cols]) + dot_nn(passage_parts, embed_ref[:, cols])
        sum_ref[rank:, cols] = ADAPTER_SCALE * (both[:rank] + both[rank:])
        sum_ref[:rank, cols] = ADAPTER_SCALE * (
            dot_nn(back_passage, passage_in_ref[:, cols])
            + dot_nn(back_query, query_in_ref[:, cols])
        )
    part = width // shards
    home = lax.axis_index("fsdp")
    for k in range(shards):
        start = pl.multiple_of((home ^ k) * part, part)
        blocks[k][...] = sum_ref[:, pl.ds(start, part)].astype(blocks[k].dtype)


def backward(upstream_of, raw_ref, inverse, grad_ref, up_ref):
    rows, width = raw_ref.shape
    chunk = min(width, 512)
    inner = jnp.zeros((rows, 1), F32)
    for at in range(0, width, chunk):
        upstream = upstream_of(at, chunk)
        up_ref[:, at : at + chunk] = upstream
        unit = raw_ref[:, at : at + chunk].astype(F32) * inverse
        inner = inner + jnp.sum(unit * upstream, axis=-1, keepdims=True)
    for at in range(0, width, chunk):
        unit = raw_ref[:, at : at + chunk].astype(F32) * inverse
        grad = (up_ref[:, at : at + chunk] - unit * inner) * inverse
        grad_ref[:, at : at + chunk] = grad.astype(BF16)


def passage_kernel(final_ref, query_ref, raw_ref, side_ref, grad_ref, up_ref):
    high, low = split_two(final_ref[...])

    def upstream_of(at, chunk):
        embed = query_ref[:, at : at + chunk]
        return dot_nn(high, embed) + dot_nn(low, embed)

    backward(upstream_of, raw_ref, side_ref[:, 0:1], grad_ref, up_ref)


def query_kernel(group, near_ref, far_ref, *refs):
    parts = message_parts(near_ref, far_ref, group)
    near = refs[: group // 2 - 1]
    forwarded_ref, final_ref, embed_ref, raw_ref, grad_ref, up_ref = refs[group // 2 - 1 :]
    q_dev, width = raw_ref.shape
    queries = final_ref.shape[1]
    me = lax.axis_index("dp")
    scales = combine(parts)
    pick = (iota((q_dev, queries), 1) == iota((q_dev, queries), 0) + me * q_dev).astype(F32)
    far = [
        ref[at : at + CAP, :] * (scale / SOFTMAX_HEAT) for (ref, at), scale in zip(parts, scales)
    ]
    far = far[2::2] + far[1::2] + [jnp.zeros((CAP, queries), F32)]
    own_parts = split_two(dot_nt(pick, final_ref[...], precision=HIGHEST))
    far_parts = split_two(dot_nt(pick, jnp.concatenate(far, axis=0), precision=HIGHEST))
    own_parts = jnp.concatenate(own_parts, axis=0)
    far_parts = jnp.concatenate(far_parts, axis=0)

    def upstream_of(at, chunk):
        rows = [ref[:, at : at + chunk].astype(F32)[:CAP] for ref in near]
        rows.append(forwarded_ref[:, at : at + chunk].astype(F32))
        rows.append(jnp.zeros((CAP, chunk), F32))
        both = dot_nn(own_parts, embed_ref[:, at : at + chunk])
        both = both + dot_nn(far_parts, jnp.concatenate(rows, axis=0).astype(BF16))
        return both[:q_dev] + both[q_dev:]

    backward(upstream_of, raw_ref, inverse_length(raw_ref, width), grad_ref, up_ref)


def sum_kernel(*refs):
    total = refs[0][...].astype(F32)
    for ref in refs[1:-1]:
        total = total + ref[...].astype(F32)
    refs[-1][...] = total


def sum_two_kernel(left_ref, right_ref, sent_ref):
    sent_ref[...] = (left_ref[...] + right_ref[...]).astype(BF16)


def sum_split_kernel(*refs):
    terms = [ref[...].astype(F32) for ref in refs[:-2]]
    while len(terms) > 1:
        terms = [a + b for a, b in zip(terms[::2], terms[1::2])]
    rank = refs[-1].shape[0]
    refs[-2][...] = terms[0][:rank]
    refs[-1][...] = terms[0][rank:]


def exchange(values, axis, k):
    size = lax.axis_size(axis)
    return lax.ppermute(values, axis, [(i, i ^ k) for i in range(size)])


def per_device(
    query_pooled_states,
    passage_pooled_states,
    query_attention_output,
    passage_attention_output,
    positive_passage_row,
    hard_negative_ids,
    passage_home_row,
    adapter_down_weight,
    adapter_up_weight,
):
    group = lax.axis_size("dp")
    shards = lax.axis_size("fsdp")
    query_raw = query_pooled_states[0]
    passage_raw = passage_pooled_states[0]
    query_in = query_attention_output[0]
    passage_in = passage_attention_output[0]
    ids = hard_negative_ids[0]
    q_dev, width = query_raw.shape
    p_dev = passage_raw.shape[0]
    rank, part = adapter_down_weight.shape
    queries = group * q_dev
    slots = group * CAP
    work = 2 * p_dev * width

    packed, adapter = run(
        pack_kernel,
        (
            shape_of((q_dev, width + 2 * ids.shape[1]), BF16),
            shape_of((2 * rank, part), BF16),
        ),
        (query_raw, ids, adapter_down_weight, adapter_up_weight),
        1,
        [pltpu.VMEM(ids.shape, jnp.int32), pltpu.SemaphoreType.DMA((4,))],
        in_hbm=True,
    )
    blocks = {0: packed}
    for k in range(2, group, 2):
        blocks[k] = exchange(packed, "dp", k)
    blocks[1] = exchange(packed, "dp", 1)
    adapter = lax.all_gather(adapter, "fsdp", axis=0, tiled=False)
    positive_row = jnp.tile(positive_passage_row, (1, group))

    embed, side, side_row = run(
        passage_norm_kernel,
        (
            shape_of((p_dev, width), BF16),
            shape_of((p_dev, 128), F32),
            shape_of((8, p_dev), F32),
        ),
        (passage_raw, passage_home_row),
        work,
    )
    for k in range(2, group, 2):
        blocks[k], side_row = lax.optimization_barrier((blocks[k], side_row))
        blocks[k ^ 1] = exchange(blocks[k], "dp", 1)
    adapter_full, passage_low, query_low, own_side, slot_base = run(
        functools.partial(rank_kernel, shards),
        (
            shape_of((2 * rank, width), BF16),
            shape_of((rank, p_dev), F32),
            shape_of((rank, q_dev), F32),
            shape_of((8, queries), F32),
            shape_of((rank, p_dev), F32),
        ),
        (adapter, query_raw, query_in, passage_in, embed, side_row),
        work * rank,
    )
    query_embed, weight, dots, onehot, message = run(
        functools.partial(score_kernel, group),
        (
            shape_of((queries, width), BF16),
            shape_of((p_dev, queries), F32),
            shape_of((p_dev, queries), F32),
            shape_of((slots, p_dev), F32),
            shape_of((HEAD_ROWS + rank, queries), F32),
        ),
        (
            *[blocks[k] for k in range(group)],
            embed,
            side,
            positive_row,
            query_low,
            slot_base,
        ),
        work * queries,
        [pltpu.VMEM((queries, 2 * ids.shape[1]), F32)],
    )
    back_query, *row_blocks = run(
        functools.partial(request_kernel, group),
        (
            shape_of((rank, queries), F32),
            *[shape_of((2 * CAP, width), BF16)] * (group // 2),
        ),
        (embed, query_embed, adapter_full, onehot),
        work * slots,
    )
    stats = [message] + [exchange(message, "dp", k) for k in range(2, group, 2)]
    stats, row_blocks = lax.optimization_barrier((stats, row_blocks))
    near_stats = stack(*stats)
    far_stats = exchange(near_stats, "dp", 1)
    final, *terms = run(
        functools.partial(terms_kernel, group, shards),
        (
            shape_of((p_dev, queries), F32),
            shape_of((2 * rank, part), F32),
            *[shape_of((2 * rank, part), BF16)] * (shards - 1),
        ),
        (
            near_stats,
            far_stats,
            weight,
            dots,
            positive_row,
            query_embed,
            embed,
            back_query,
            slot_base,
            passage_low,
            side_row,
            own_side,
            passage_in,
            query_in,
        ),
        work * rank * 4,
        [pltpu.VMEM((2 * rank, width), F32)],
    )
    arrived = [exchange(terms[k], "fsdp", k) for k in range(1, shards)]
    near = [exchange(row_blocks[k // 2], "dp", k) for k in range(2, group, 2)]
    grad_passage = run(
        passage_kernel,
        (shape_of((p_dev, width), BF16),),
        (final, query_embed, passage_raw, side),
        2 * work * queries,
        [pltpu.VMEM((p_dev, width), F32)],
    )[0]
    terms[0], grad_passage = lax.optimization_barrier((terms[0], grad_passage))
    total = run(sum_kernel, (shape_of((2 * rank, part), F32),), (terms[0], *arrived), 1)[0]
    total, near = lax.optimization_barrier((total, near))
    to_sibling = run(
        forward_kernel,
        (shape_of((group // 2 * CAP, width), BF16),),
        (row_blocks[0], *near),
        1,
    )[0]
    forwarded = exchange(to_sibling, "dp", 1)
    sent = run(
        sum_two_kernel,
        (shape_of((2 * rank, part), BF16),),
        (total, exchange(total, "dp", 1)),
        1,
    )[0]
    arrived = [exchange(sent, "dp", k) for k in range(2, group, 2)]
    grad_query = run(
        functools.partial(query_kernel, group),
        (shape_of((q_dev, width), BF16),),
        (near_stats, far_stats, *near, forwarded, final, embed, query_raw),
        4 * q_dev * width * (p_dev + slots),
        [pltpu.VMEM((q_dev, width), F32)],
    )[0]
    sent, grad_query = lax.optimization_barrier((sent, grad_query))
    down_total, up_total = run(
        sum_split_kernel, (shape_of((rank, part), F32),) * 2, (sent, *arrived), 1
    )
    return (grad_query[None], grad_passage[None], down_total, up_total)


def solution(mesh):
    in_specs = (
        P("fsdp", "dp", None),
        P("fsdp", "dp", None),
        P("fsdp", "dp", None),
        P("fsdp", "dp", None),
        P("fsdp", "dp"),
        P("fsdp", "dp", None),
        P("fsdp", None),
        P(None, "fsdp"),
        P(None, "fsdp"),
    )
    out_specs = (P("fsdp", "dp", None), P("fsdp", "dp", None), P(None, "fsdp"), P(None, "fsdp"))
    return jax.shard_map(
        per_device, mesh=mesh, in_specs=in_specs, out_specs=out_specs, check_vma=False
    )
```

```python
import functools

import jax
import jax.numpy as jnp
from jax import lax
from jax.experimental import pallas as pl
from jax.experimental.pallas import tpu as pltpu
from jax.sharding import PartitionSpec as P

CAP = 8
SOFTMAX_HEAT = 0.01
ADAPTER_SCALE = 2.0
EPSILON = 1e-06
LOWEST = -1e30
ID_BASE = 256
TOP_ROW, SUM_ROW, DOT_ROW, HEAD_ROWS = 8, 9, 10, 16
VMEM_BYTES = 16 * 1024 * 1024
ALL_VMEM_BYTES = 60 * 1024 * 1024
F32 = jnp.float32
BF16 = jnp.bfloat16
HIGHEST = lax.Precision.HIGHEST


def dot_nn(a, b, precision=None):
    return lax.dot_general(
        a, b, (((1,), (0,)), ((), ())), precision=precision, preferred_element_type=F32
    )


def dot_nt(a, b, precision=None):
    return lax.dot_general(
        a, b, (((1,), (1,)), ((), ())), precision=precision, preferred_element_type=F32
    )


def split_two(values):
    high = values.astype(BF16)
    low = (values - high.astype(F32)).astype(BF16)
    return high, low


def iota(shape, dim):
    return lax.broadcasted_iota(jnp.int32, shape, dim)


def shape_of(dims, kind):
    return jax.ShapeDtypeStruct(dims, kind)


def run(body, out_shape, args, flops, scratch=(), in_hbm=False):
    grant = ALL_VMEM_BYTES if in_hbm else VMEM_BYTES * max(1, size_ratio(args))
    vmem = pl.BlockSpec(memory_space=pltpu.VMEM)
    hbm = pl.BlockSpec(memory_space=pltpu.HBM)
    moved = sum(a.size * a.dtype.itemsize for a in (*args, *out_shape))
    return pl.pallas_call(
        body,
        out_shape=out_shape,
        in_specs=[hbm if in_hbm else vmem] * len(args),
        out_specs=tuple(vmem for _ in out_shape),
        scratch_shapes=list(scratch),
        compiler_params=pltpu.CompilerParams(vmem_limit_bytes=grant),
        cost_estimate=pl.CostEstimate(flops=flops, bytes_accessed=moved, transcendentals=0),
    )(*args)


def size_ratio(args):
    moved = sum(a.size * a.dtype.itemsize for a in args)
    return -(-moved * 3 // VMEM_BYTES)


def inverse_length(raw_ref, width):
    chunk = min(width, 512)
    total = jnp.zeros((raw_ref.shape[0], 1), F32)
    for at in range(0, width, chunk):
        part = raw_ref[:, at : at + chunk].astype(F32)
        total = total + jnp.sum(part * part, axis=-1, keepdims=True)
    return 1.0 / jnp.sqrt(total + EPSILON)


def pack_kernel(raw_ref, ids_ref, down_ref, up_ref, out_ref, adapter_ref, ids_here, sems):
    width = raw_ref.shape[1]
    core = lax.axis_index("dp") % 2
    copies = [
        pltpu.make_async_copy(ids_ref, ids_here, sems.at[0]),
        pltpu.make_async_copy(raw_ref, out_ref.at[:, pl.ds(0, width)], sems.at[1]),
    ]
    own_down = pltpu.make_async_copy(down_ref, adapter_ref, sems.at[2])
    own_up = pltpu.make_async_copy(up_ref, adapter_ref, sems.at[2])
    for copy in copies:
        copy.start()
    pl.when(core == 0)(own_down.start)
    pl.when(core == 1)(own_up.start)
    copies[0].wait()
    ids = ids_here[...]
    coded = jnp.concatenate([ids // ID_BASE, ids % ID_BASE], axis=1)
    out_ref[:, width:] = coded.astype(F32).astype(BF16)
    copies[1].wait()
    pl.when(core == 0)(own_down.wait)
    pl.when(core == 1)(own_up.wait)


def stack_kernel(*refs):
    out_ref = refs[-1]
    rows = refs[0].shape[0]
    for i, ref in enumerate(refs[:-1]):
        out_ref[i * rows : (i + 1) * rows, :] = ref[...]


def stack(*parts):
    rows, cols = parts[0].shape
    return run(stack_kernel, (shape_of((len(parts) * rows, cols), parts[0].dtype),), parts, 1)[0]


def passage_norm_kernel(raw_ref, home_ref, embed_ref, side_ref, row_ref):
    rows, width = raw_ref.shape
    total = home_ref.shape[1]
    me = lax.axis_index("dp")
    chunk = min(width, 512)
    inverse = inverse_length(raw_ref, width)
    for at in range(0, width, chunk):
        part = raw_ref[:, at : at + chunk].astype(F32)
        embed_ref[:, at : at + chunk] = (part * inverse).astype(BF16)
    row_id = iota((rows, total), 0) + me * rows
    ids = iota((rows, total), 1)
    home = jnp.sum(jnp.where(home_ref[...] == row_id, ids, 0).astype(F32), axis=1, keepdims=True)
    side_ref[...] = jnp.where(iota(side_ref.shape, 1) == 0, inverse, home)
    row_ref[...] = jnp.broadcast_to(inverse, (rows, rows)).T[: row_ref.shape[0]]


def rank_kernel(
    shards,
    near_ref,
    far_ref,
    query_ref,
    query_in_ref,
    passage_in_ref,
    embed_ref,
    row_ref,
    weights_ref,
    passage_low_ref,
    query_low_ref,
    own_ref,
    slot_base_ref,
):
    part = near_ref.shape[1]
    rank = near_ref.shape[0] // shards
    q_dev, width = query_ref.shape
    queries = own_ref.shape[1]
    me = lax.axis_index("fsdp")
    even = lax.axis_index("dp") % 2 == 0
    for k in range(shards):
        cols = pl.ds(pl.multiple_of((me ^ k) * part, part), part)
        near = near_ref[k * rank : (k + 1) * rank, :]
        far = far_ref[k * rank : (k + 1) * rank, :]
        weights_ref[:rank, cols] = jnp.where(even, near, far)
        weights_ref[rank:, cols] = jnp.where(even, far, near)
    down, up = weights_ref[:rank, :], weights_ref[rank:, :]
    place = iota((q_dev, queries), 1) == iota((q_dev, queries), 0) + lax.axis_index("dp") * q_dev
    inverse = inverse_length(query_ref, width)
    own = jnp.sum(jnp.where(place, inverse, 0.0), axis=0, keepdims=True)
    own_ref[...] = jnp.broadcast_to(own, own_ref.shape)
    same = iota((q_dev, q_dev), 0) == iota((q_dev, q_dev), 1)
    inverse_row = jnp.sum(jnp.where(same, inverse, 0.0), axis=0, keepdims=True)
    query_low = dot_nt(down, query_in_ref[...]).astype(BF16)
    query_low_ref[...] = query_low.astype(F32) * inverse_row
    passage_low = dot_nt(down, passage_in_ref[...]).astype(BF16)
    passage_low_ref[...] = passage_low.astype(F32) * row_ref[0:1, :]
    slot_base_ref[...] = dot_nt(up, embed_ref[...])


def score_kernel(group, *refs):
    blocks = refs[:group]
    embed_ref, side_ref, positive_ref, query_low_ref, base_ref = refs[group : group + 5]
    query_ref, weight_ref, dots_ref, onehot_ref, message_ref, coded_ref = refs[group + 5 :]
    rows, width = embed_ref.shape
    queries = query_ref.shape[0]
    q_dev = queries // group
    negatives = (blocks[0].shape[1] - width) // 2
    slots = group * CAP
    rank = query_low_ref.shape[0]
    me = lax.axis_index("dp")
    chunk = min(width, 1024)
    for k in range(group):
        start = pl.multiple_of((me ^ k) * q_dev, q_dev)
        inverse = inverse_length(blocks[k], width)
        for at in range(0, width, chunk):
            part = blocks[k][:, at : at + chunk].astype(F32)
            query_ref[pl.ds(start, q_dev), at : at + chunk] = (part * inverse).astype(BF16)
        coded = blocks[k][:, width:].astype(F32)
        coded_ref[pl.ds(start, q_dev), :] = coded
    dots = dot_nt(embed_ref[...], query_ref[...])
    dots_ref[...] = dots
    scores = dots / SOFTMAX_HEAT

    coded = coded_ref[...].T
    ids = coded[:negatives] * float(ID_BASE) + coded[negatives:]
    home = jnp.broadcast_to(side_ref[:, 1:2], (rows, queries))
    count = jnp.zeros((rows, queries), F32)
    for j in range(negatives):
        count = count + jnp.where(ids[j : j + 1, :] == home, 1.0, 0.0)
    members = iota((slots, queries), 0) // CAP == iota((slots, queries), 1) // q_dev
    marked = dot_nt(members.astype(BF16), count.astype(BF16)) > 0.0
    before = (iota((rows, rows), 0) <= iota((rows, rows), 1)).astype(BF16)
    rank_in = dot_nn(marked.astype(F32).astype(BF16), before)
    wanted = (iota((slots, rows), 0) % CAP + 1).astype(F32)
    onehot = jnp.where(marked & (rank_in == wanted), 1.0, 0.0)
    onehot_ref[...] = onehot

    own = iota((rows, queries), 1) // q_dev == me
    count = count + jnp.where(own & (positive_ref[...] == iota((rows, queries), 0)), 1.0, 0.0)
    named = count > 0.0
    top = jnp.max(jnp.where(named, scores, LOWEST), axis=0, keepdims=True)
    weight = count * jnp.exp(jnp.where(named, scores - top, LOWEST))
    weight_ref[...] = weight
    total = jnp.sum(weight, axis=0, keepdims=True)
    dot_total = jnp.sum(weight * dots, axis=0, keepdims=True)
    slot_weight = dot_nn(onehot, weight, precision=HIGHEST)
    slot_base = dot_nt(base_ref[...], onehot, precision=HIGHEST)
    tail_row = iota((HEAD_ROWS - CAP, queries), 0)
    tail = jnp.where(tail_row == 0, top, jnp.where(tail_row == 1, total, dot_total))
    lane_group = iota((CAP, queries), 1) // q_dev
    compact = jnp.zeros((CAP, queries), F32)
    for peer in range(group):
        part = slot_weight[peer * CAP : (peer + 1) * CAP]
        compact = jnp.where(lane_group == peer, part, compact)
    message_ref[:CAP, :] = compact
    message_ref[CAP:HEAD_ROWS, :] = tail
    message_ref[HEAD_ROWS:, :slots] = slot_base
    message_ref[HEAD_ROWS:, slots : slots + q_dev] = query_low_ref[...]


def back_kernel(query_ref, weights_ref, back_ref):
    back_ref[...] = dot_nt(weights_ref[weights_ref.shape[0] // 2 :, :], query_ref[...])


def request_kernel(first, embed_ref, onehot_ref, *blocks):
    width = embed_ref.shape[1]
    me = lax.axis_index("dp")
    onehot = [
        onehot_ref[pl.ds(pl.multiple_of((me ^ k) * CAP, CAP), CAP), :]
        for k in range(2 * first, 2 * (first + len(blocks)))
    ]
    onehot = jnp.concatenate(onehot, axis=0).astype(BF16)
    chunk = min(width, 1024)
    for at in range(0, width, chunk):
        part = dot_nn(onehot, embed_ref[:, at : at + chunk]).astype(BF16)
        for i, block in enumerate(blocks):
            block[:, at : at + chunk] = part[2 * i * CAP : 2 * (i + 1) * CAP]


def request(first, count, embed, onehot):
    width = embed.shape[1]
    return run(
        functools.partial(request_kernel, first),
        (shape_of((2 * CAP, width), BF16),) * count,
        (embed, onehot),
        2 * embed.size * 2 * CAP * count,
    )


def forward_kernel(*refs):
    out_ref = refs[-1]
    for i, ref in enumerate(refs[:-1]):
        out_ref[i * CAP : (i + 1) * CAP, :] = ref[CAP:, :]


def message_parts(near_ref, far_ref, group):
    rows = near_ref.shape[0] // (group // 2)
    return [((near_ref, far_ref)[k % 2], k // 2 * rows) for k in range(group)]


def combine(parts):
    tops = [ref[at + TOP_ROW : at + TOP_ROW + 1, :] for ref, at in parts]
    sums = [ref[at + SUM_ROW : at + SUM_ROW + 1, :] for ref, at in parts]
    top = functools.reduce(jnp.maximum, tops)
    scales = [jnp.exp(t - top) for t in tops]
    inverse_total = 1.0 / sum(t * s for t, s in zip(scales, sums))
    return [scale * inverse_total for scale in scales]


def own_target(positive_ref, rows, queries, q_dev, me):
    own = iota((rows, queries), 1) // q_dev == me
    return jnp.where(own & (positive_ref[...] == iota((rows, queries), 0)), 1.0, 0.0)


def terms_kernel(group, shards, near_ref, far_ref, *refs):
    parts = message_parts(near_ref, far_ref, group)
    (
        weight_ref,
        dots_ref,
        positive_ref,
        query_ref,
        embed_ref,
        back_query_ref,
        back_passage_ref,
        passage_low_ref,
        row_ref,
        own_ref,
        passage_in_ref,
        query_in_ref,
    ) = refs[:12]
    final_ref = refs[12]
    blocks = refs[13 : 13 + shards]
    (sum_ref,) = refs[13 + shards :]
    rows, queries = weight_ref.shape
    q_dev = queries // group
    rank = passage_low_ref.shape[0]
    width = query_ref.shape[1]
    me = lax.axis_index("dp")

    scales = combine(parts)
    target = own_target(positive_ref, rows, queries, q_dev, me)
    weight = (weight_ref[...] * scales[0] - target) / SOFTMAX_HEAT
    final_ref[...] = weight
    dots = dots_ref[...]
    weighted = weight * dots
    share = jnp.sum(weighted, axis=0, keepdims=True)
    ones = jnp.ones((8, queries), F32)
    inner = dot_nt(ones, weighted, precision=HIGHEST)[0:1, :]

    inner_query = -jnp.sum(target * dots, axis=0, keepdims=True)
    slots = group * CAP
    bases, query_low = [], []
    for (ref, at), scale in zip(parts, scales):
        inner_query = inner_query + scale * ref[at + DOT_ROW : at + DOT_ROW + 1, :]
        bases.append(ref[at + HEAD_ROWS : at + HEAD_ROWS + rank, :slots])
        query_low.append(ref[at + HEAD_ROWS : at + HEAD_ROWS + rank, slots : slots + q_dev])
    sent_by = me ^ (iota((queries, queries), 0) // q_dev)
    place = iota((queries, queries), 1) == sent_by * q_dev + iota((queries, queries), 0) % q_dev
    query_low = dot_nn(
        jnp.concatenate(query_low, axis=1), place.astype(F32), precision=HIGHEST
    )
    pick_slots = (iota((slots, CAP), 0) == iota((slots, CAP), 1) + me * CAP).astype(F32)
    bases = dot_nn(jnp.concatenate(bases[1:], axis=0), pick_slots, precision=HIGHEST)
    far_base = [bases[k * rank : (k + 1) * rank] for k in range(group - 1)]
    far_weight = [
        ref[at : at + CAP, :] * (scale / SOFTMAX_HEAT)
        for (ref, at), scale in zip(parts[1:], scales[1:])
    ]
    inner_query = inner_query / SOFTMAX_HEAT

    passage_low = passage_low_ref[...]
    from_query = dot_nn(passage_low, weight, precision=HIGHEST) - query_low * share
    from_passage = dot_nt(query_low, weight, precision=HIGHEST) - passage_low * inner
    query_parts = jnp.concatenate(split_two(from_query), axis=0)
    passage_parts = jnp.concatenate(split_two(from_passage), axis=0)

    back_passage = dot_nt(back_query_ref[...], weight, precision=HIGHEST)
    back_passage = (back_passage - back_passage_ref[...] * inner) * row_ref[0:1, :]
    back_passage = back_passage.astype(BF16)
    back_query = dot_nn(back_passage_ref[...], weight, precision=HIGHEST)
    back_query = back_query + dot_nn(
        jnp.concatenate(far_base, axis=1),
        jnp.concatenate(far_weight, axis=0),
        precision=HIGHEST,
    )
    back_query = (back_query - back_query_ref[...] * inner_query) * own_ref[0:1, :]
    pick = (iota((q_dev, queries), 1) == iota((q_dev, queries), 0) + me * q_dev).astype(BF16)
    back_query = dot_nt(back_query.astype(BF16), pick).astype(BF16)

    chunk = min(width, 512)
    for at in range(0, width, chunk):
        cols = slice(at, at + chunk)
        both = dot_nn(query_parts, query_ref[:, cols]) + dot_nn(passage_parts, embed_ref[:, cols])
        sum_ref[rank:, cols] = ADAPTER_SCALE * (both[:rank] + both[rank:])
        sum_ref[:rank, cols] = ADAPTER_SCALE * (
            dot_nn(back_passage, passage_in_ref[:, cols])
            + dot_nn(back_query, query_in_ref[:, cols])
        )
    part = width // shards
    home = lax.axis_index("fsdp")
    for k in range(shards):
        start = pl.multiple_of((home ^ k) * part, part)
        blocks[k][...] = sum_ref[:, pl.ds(start, part)].astype(blocks[k].dtype)


def backward(upstream_of, raw_ref, inverse, grad_ref, up_ref):
    rows, width = raw_ref.shape
    chunk = min(width, 512)
    inner = jnp.zeros((rows, 1), F32)
    for at in range(0, width, chunk):
        upstream = upstream_of(at, chunk)
        up_ref[:, at : at + chunk] = upstream
        unit = raw_ref[:, at : at + chunk].astype(F32) * inverse
        inner = inner + jnp.sum(unit * upstream, axis=-1, keepdims=True)
    for at in range(0, width, chunk):
        unit = raw_ref[:, at : at + chunk].astype(F32) * inverse
        grad = (up_ref[:, at : at + chunk] - unit * inner) * inverse
        grad_ref[:, at : at + chunk] = grad.astype(BF16)


def passage_kernel(final_ref, query_ref, raw_ref, side_ref, grad_ref, up_ref):
    high, low = split_two(final_ref[...])

    def upstream_of(at, chunk):
        embed = query_ref[:, at : at + chunk]
        return dot_nn(high, embed) + dot_nn(low, embed)

    backward(upstream_of, raw_ref, side_ref[:, 0:1], grad_ref, up_ref)


def query_kernel(group, near_ref, far_ref, *refs):
    parts = message_parts(near_ref, far_ref, group)
    near = refs[: group // 2 - 1]
    forwarded_ref, final_ref, embed_ref, raw_ref, grad_ref, up_ref = refs[group // 2 - 1 :]
    q_dev, width = raw_ref.shape
    queries = final_ref.shape[1]
    me = lax.axis_index("dp")
    scales = combine(parts)
    pick = (iota((q_dev, queries), 1) == iota((q_dev, queries), 0) + me * q_dev).astype(F32)
    far = [
        ref[at : at + CAP, :] * (scale / SOFTMAX_HEAT) for (ref, at), scale in zip(parts, scales)
    ]
    far = far[2::2] + far[1::2] + [jnp.zeros((CAP, queries), F32)]
    own_parts = split_two(dot_nt(pick, final_ref[...], precision=HIGHEST))
    far_parts = split_two(dot_nt(pick, jnp.concatenate(far, axis=0), precision=HIGHEST))
    own_parts = jnp.concatenate(own_parts, axis=0)
    far_parts = jnp.concatenate(far_parts, axis=0)

    def upstream_of(at, chunk):
        rows = [ref[:, at : at + chunk].astype(F32)[:CAP] for ref in near]
        rows.append(forwarded_ref[:, at : at + chunk].astype(F32))
        rows.append(jnp.zeros((CAP, chunk), F32))
        both = dot_nn(own_parts, embed_ref[:, at : at + chunk])
        both = both + dot_nn(far_parts, jnp.concatenate(rows, axis=0).astype(BF16))
        return both[:q_dev] + both[q_dev:]

    backward(upstream_of, raw_ref, inverse_length(raw_ref, width), grad_ref, up_ref)


def sum_kernel(*refs):
    total = refs[0][...].astype(F32)
    for ref in refs[1:-1]:
        total = total + ref[...].astype(F32)
    refs[-1][...] = total


def sum_two_kernel(left_ref, right_ref, sent_ref):
    sent_ref[...] = (left_ref[...] + right_ref[...]).astype(BF16)


def sum_split_kernel(*refs):
    terms = [ref[...].astype(F32) for ref in refs[:-2]]
    while len(terms) > 1:
        terms = [a + b for a, b in zip(terms[::2], terms[1::2])]
    rank = refs[-1].shape[0]
    refs[-2][...] = terms[0][:rank]
    refs[-1][...] = terms[0][rank:]


def exchange(values, axis, k):
    size = lax.axis_size(axis)
    return lax.ppermute(values, axis, [(i, i ^ k) for i in range(size)])


def per_device(
    query_pooled_states,
    passage_pooled_states,
    query_attention_output,
    passage_attention_output,
    positive_passage_row,
    hard_negative_ids,
    passage_home_row,
    adapter_down_weight,
    adapter_up_weight,
):
    group = lax.axis_size("dp")
    shards = lax.axis_size("fsdp")
    query_raw = query_pooled_states[0]
    passage_raw = passage_pooled_states[0]
    query_in = query_attention_output[0]
    passage_in = passage_attention_output[0]
    ids = hard_negative_ids[0]
    q_dev, width = query_raw.shape
    p_dev = passage_raw.shape[0]
    rank, part = adapter_down_weight.shape
    queries = group * q_dev
    slots = group * CAP
    work = 2 * p_dev * width

    packed, adapter = run(
        pack_kernel,
        (
            shape_of((q_dev, width + 2 * ids.shape[1]), BF16),
            shape_of((rank, part), BF16),
        ),
        (query_raw, ids, adapter_down_weight, adapter_up_weight),
        1,
        [pltpu.VMEM(ids.shape, jnp.int32), pltpu.SemaphoreType.DMA((3,))],
        in_hbm=True,
    )
    blocks = {0: packed}
    for k in range(2, group, 2):
        blocks[k] = exchange(packed, "dp", k)
    blocks[1] = exchange(packed, "dp", 1)
    adapter_blocks = [adapter] + [exchange(adapter, "fsdp", k) for k in range(1, shards)]
    positive_row = jnp.tile(positive_passage_row, (1, group))

    embed, side, side_row = run(
        passage_norm_kernel,
        (
            shape_of((p_dev, width), BF16),
            shape_of((p_dev, 128), F32),
            shape_of((8, p_dev), F32),
        ),
        (passage_raw, passage_home_row),
        work,
    )
    for k in range(2, group, 2):
        blocks[k], side_row = lax.optimization_barrier((blocks[k], side_row))
        blocks[k ^ 1] = exchange(blocks[k], "dp", 1)
    adapter_near = stack(*adapter_blocks)
    adapter_far = exchange(adapter_near, "dp", 1)
    adapter_full, passage_low, query_low, own_side, slot_base = run(
        functools.partial(rank_kernel, shards),
        (
            shape_of((2 * rank, width), BF16),
            shape_of((rank, p_dev), F32),
            shape_of((rank, q_dev), F32),
            shape_of((8, queries), F32),
            shape_of((rank, p_dev), F32),
        ),
        (adapter_near, adapter_far, query_raw, query_in, passage_in, embed, side_row),
        work * rank,
    )
    query_embed, weight, dots, onehot, message = run(
        functools.partial(score_kernel, group),
        (
            shape_of((queries, width), BF16),
            shape_of((p_dev, queries), F32),
            shape_of((p_dev, queries), F32),
            shape_of((slots, p_dev), F32),
            shape_of((HEAD_ROWS + rank, queries), F32),
        ),
        (
            *[blocks[k] for k in range(group)],
            embed,
            side,
            positive_row,
            query_low,
            slot_base,
        ),
        work * queries,
        [pltpu.VMEM((queries, 2 * ids.shape[1]), F32)],
    )
    back_query = run(
        back_kernel,
        (shape_of((rank, queries), F32),),
        (query_embed, adapter_full),
        work * rank,
    )[0]
    stats = [message] + [exchange(message, "dp", k) for k in range(2, group, 2)]
    chips = group // 2
    row_blocks = request(0, chips, embed, onehot)
    stats, row_blocks = lax.optimization_barrier((stats, row_blocks))
    near = [exchange(row_blocks[i], "dp", 2 * i) for i in range(1, chips)]
    near_stats = stack(*stats)
    far_stats = exchange(near_stats, "dp", 1)
    final, *terms = run(
        functools.partial(terms_kernel, group, shards),
        (
            shape_of((p_dev, queries), F32),
            shape_of((2 * rank, part), F32),
            *[shape_of((2 * rank, part), BF16)] * (shards - 1),
        ),
        (
            near_stats,
            far_stats,
            weight,
            dots,
            positive_row,
            query_embed,
            embed,
            back_query,
            slot_base,
            passage_low,
            side_row,
            own_side,
            passage_in,
            query_in,
        ),
        work * rank * 4,
        [pltpu.VMEM((2 * rank, width), F32)],
    )
    arrived = [exchange(terms[k], "fsdp", k) for k in range(1, shards)]
    final, near[0] = lax.optimization_barrier((final, near[0]))
    grad_passage = run(
        passage_kernel,
        (shape_of((p_dev, width), BF16),),
        (final, query_embed, passage_raw, side),
        2 * work * queries,
        [pltpu.VMEM((p_dev, width), F32)],
    )[0]
    terms[0], grad_passage = lax.optimization_barrier((terms[0], grad_passage))
    total = run(sum_kernel, (shape_of((2 * rank, part), F32),), (terms[0], *arrived), 1)[0]
    total, near = lax.optimization_barrier((total, near))
    to_sibling = run(
        forward_kernel,
        (shape_of((group // 2 * CAP, width), BF16),),
        (row_blocks[0], *near),
        1,
    )[0]
    forwarded = exchange(to_sibling, "dp", 1)
    sent = run(
        sum_two_kernel,
        (shape_of((2 * rank, part), BF16),),
        (total, exchange(total, "dp", 1)),
        1,
    )[0]
    arrived = [exchange(sent, "dp", k) for k in range(2, group, 2)]
    grad_query = run(
        functools.partial(query_kernel, group),
        (shape_of((q_dev, width), BF16),),
        (near_stats, far_stats, *near, forwarded, final, embed, query_raw),
        4 * q_dev * width * (p_dev + slots),
        [pltpu.VMEM((q_dev, width), F32)],
    )[0]
    sent, grad_query = lax.optimization_barrier((sent, grad_query))
    down_total, up_total = run(
        sum_split_kernel, (shape_of((rank, part), F32),) * 2, (sent, *arrived), 1
    )
    return (grad_query[None], grad_passage[None], down_total, up_total)


def solution(mesh):
    in_specs = (
        P("fsdp", "dp", None),
        P("fsdp", "dp", None),
        P("fsdp", "dp", None),
        P("fsdp", "dp", None),
        P("fsdp", "dp"),
        P("fsdp", "dp", None),
        P("fsdp", None),
        P(None, "fsdp"),
        P(None, "fsdp"),
    )
    out_specs = (P("fsdp", "dp", None), P("fsdp", "dp", None), P(None, "fsdp"), P(None, "fsdp"))
    return jax.shard_map(
        per_device, mesh=mesh, in_specs=in_specs, out_specs=out_specs, check_vma=False
    )
```

```python
import functools

import jax
import jax.numpy as jnp
from jax import lax
from jax.experimental import pallas as pl
from jax.experimental.pallas import tpu as pltpu
from jax.sharding import PartitionSpec as P

CAP = 8
SOFTMAX_HEAT = 0.01
ADAPTER_SCALE = 2.0
EPSILON = 1e-06
LOWEST = -1e30
ID_BASE = 256
TOP_ROW, SUM_ROW, DOT_ROW, HEAD_ROWS = 8, 9, 10, 16
VMEM_BYTES = 16 * 1024 * 1024
PASSAGE_CHUNKS = 4
F32 = jnp.float32
BF16 = jnp.bfloat16
HIGHEST = lax.Precision.HIGHEST


def dot_nn(a, b, precision=None):
    return lax.dot_general(
        a, b, (((1,), (0,)), ((), ())), precision=precision, preferred_element_type=F32
    )


def dot_nt(a, b, precision=None):
    return lax.dot_general(
        a, b, (((1,), (1,)), ((), ())), precision=precision, preferred_element_type=F32
    )


def split_two(values):
    high = values.astype(BF16)
    low = (values - high.astype(F32)).astype(BF16)
    return high, low


def iota(shape, dim):
    return lax.broadcasted_iota(jnp.int32, shape, dim)


def shape_of(dims, kind):
    return jax.ShapeDtypeStruct(dims, kind)


def run(body, out_shape, args, flops, scratch=(), in_hbm=False):
    grant = VMEM_BYTES * max(1, size_ratio(args))
    if in_hbm:
        args = [pltpu.with_memory_space_constraint(a, pltpu.HBM) for a in args]
    vmem = pl.BlockSpec(memory_space=pltpu.VMEM)
    hbm = pl.BlockSpec(memory_space=pltpu.HBM)
    moved = sum(a.size * a.dtype.itemsize for a in (*args, *out_shape))
    return pl.pallas_call(
        body,
        out_shape=out_shape,
        in_specs=[hbm if in_hbm else vmem] * len(args),
        out_specs=tuple(vmem for _ in out_shape),
        scratch_shapes=list(scratch),
        compiler_params=pltpu.CompilerParams(vmem_limit_bytes=grant),
        cost_estimate=pl.CostEstimate(flops=flops, bytes_accessed=moved, transcendentals=0),
    )(*args)


def size_ratio(args):
    moved = sum(a.size * a.dtype.itemsize for a in args)
    return -(-moved * 3 // VMEM_BYTES)


def inverse_length(raw_ref, width):
    chunk = min(width, 512)
    total = jnp.zeros((raw_ref.shape[0], 1), F32)
    for at in range(0, width, chunk):
        part = raw_ref[:, at : at + chunk].astype(F32)
        total = total + jnp.sum(part * part, axis=-1, keepdims=True)
    return 1.0 / jnp.sqrt(total + EPSILON)


def front_kernel(
    query_ref,
    ids_ref,
    down_ref,
    up_ref,
    passage_ref,
    home_ref,
    out_ref,
    adapter_ref,
    embed_ref,
    side_ref,
    row_ref,
    ids_here,
    passage_here,
    home_here,
    sems,
):
    rows, width = passage_ref.shape
    total = home_ref.shape[1]
    me = lax.axis_index("dp")
    part = rows // PASSAGE_CHUNKS
    copies = [
        pltpu.make_async_copy(ids_ref, ids_here, sems.at[0]),
        pltpu.make_async_copy(query_ref, out_ref.at[:, pl.ds(0, width)], sems.at[1]),
        pltpu.make_async_copy(home_ref, home_here, sems.at[2]),
    ]
    for copy in copies:
        copy.start()
    own_down = pltpu.make_async_copy(down_ref, adapter_ref, sems.at[3])
    own_up = pltpu.make_async_copy(up_ref, adapter_ref, sems.at[3])
    pl.when(me % 2 == 0)(own_down.start)
    pl.when(me % 2 == 1)(own_up.start)
    passage_copies = []
    for c in range(PASSAGE_CHUNKS):
        here = pl.ds(c * part, part)
        passage_copies.append(
            pltpu.make_async_copy(
                passage_ref.at[here, :], passage_here.at[here, :], sems.at[4 + c]
            )
        )
        passage_copies[c].start()

    copies[0].wait()
    ids = ids_here[...]
    coded = jnp.concatenate([ids // ID_BASE, ids % ID_BASE], axis=1)
    out_ref[:, width:] = coded.astype(F32).astype(BF16)
    copies[2].wait()
    row_id = iota((rows, total), 0) + me * rows
    number = iota((rows, total), 1)
    home = jnp.where(home_here[...] == row_id, number, 0).astype(F32)
    home = jnp.sum(home, axis=1, keepdims=True)

    chunk = min(width, 512)
    inverses = []
    for c in range(PASSAGE_CHUNKS):
        passage_copies[c].wait()
        here = slice(c * part, (c + 1) * part)
        inverse = inverse_length(passage_here.at[here, :], width)
        for at in range(0, width, chunk):
            values = passage_here[here, at : at + chunk].astype(F32)
            embed_ref[here, at : at + chunk] = (values * inverse).astype(BF16)
        inverses.append(inverse)
    inverse = jnp.concatenate(inverses, axis=0)
    side_ref[...] = jnp.where(iota(side_ref.shape, 1) == 0, inverse, home)
    row_ref[...] = jnp.broadcast_to(inverse, (rows, rows)).T[: row_ref.shape[0]]
    copies[1].wait()
    pl.when(me % 2 == 0)(own_down.wait)
    pl.when(me % 2 == 1)(own_up.wait)


def stack_kernel(*refs):
    out_ref = refs[-1]
    rows = refs[0].shape[0]
    for i, ref in enumerate(refs[:-1]):
        out_ref[i * rows : (i + 1) * rows, :] = ref[...]


def stack(*parts):
    rows, cols = parts[0].shape
    return run(stack_kernel, (shape_of((len(parts) * rows, cols), parts[0].dtype),), parts, 1)[0]


def rank_kernel(
    shards,
    near_ref,
    far_ref,
    query_ref,
    query_in_ref,
    passage_in_ref,
    embed_ref,
    row_ref,
    weights_ref,
    passage_low_ref,
    query_low_ref,
    own_ref,
    slot_base_ref,
):
    part = near_ref.shape[1]
    rank = near_ref.shape[0] // shards
    q_dev, width = query_ref.shape
    queries = own_ref.shape[1]
    me = lax.axis_index("fsdp")
    core = lax.axis_index("dp") % 2

    def place_halves(first_ref, second_ref):
        for k in range(shards):
            cols = pl.ds(pl.multiple_of((me ^ k) * part, part), part)
            weights_ref[:rank, cols] = first_ref[k * rank : (k + 1) * rank, :]
            weights_ref[rank:, cols] = second_ref[k * rank : (k + 1) * rank, :]

    pl.when(core == 0)(functools.partial(place_halves, near_ref, far_ref))
    pl.when(core == 1)(functools.partial(place_halves, far_ref, near_ref))
    down, up = weights_ref[:rank, :], weights_ref[rank:, :]
    place = iota((q_dev, queries), 1) == iota((q_dev, queries), 0) + lax.axis_index("dp") * q_dev
    inverse = inverse_length(query_ref, width)
    own = jnp.sum(jnp.where(place, inverse, 0.0), axis=0, keepdims=True)
    own_ref[...] = jnp.broadcast_to(own, own_ref.shape)
    same = iota((q_dev, q_dev), 0) == iota((q_dev, q_dev), 1)
    inverse_row = jnp.sum(jnp.where(same, inverse, 0.0), axis=0, keepdims=True)
    query_low = dot_nt(down, query_in_ref[...]).astype(BF16)
    query_low_ref[...] = query_low.astype(F32) * inverse_row
    passage_low = dot_nt(down, passage_in_ref[...]).astype(BF16)
    passage_low_ref[...] = passage_low.astype(F32) * row_ref[0:1, :]
    slot_base_ref[...] = dot_nt(up, embed_ref[...])


def score_kernel(group, *refs):
    blocks = refs[:group]
    embed_ref, side_ref, positive_ref, query_low_ref, base_ref = refs[group : group + 5]
    query_ref, weight_ref, dots_ref, onehot_ref, message_ref, coded_ref = refs[group + 5 :]
    rows, width = embed_ref.shape
    queries = query_ref.shape[0]
    q_dev = queries // group
    negatives = (blocks[0].shape[1] - width) // 2
    slots = group * CAP
    rank = query_low_ref.shape[0]
    me = lax.axis_index("dp")
    chunk = min(width, 1024)
    for k in range(group):
        start = pl.multiple_of((me ^ k) * q_dev, q_dev)
        inverse = inverse_length(blocks[k], width)
        for at in range(0, width, chunk):
            part = blocks[k][:, at : at + chunk].astype(F32)
            query_ref[pl.ds(start, q_dev), at : at + chunk] = (part * inverse).astype(BF16)
        coded = blocks[k][:, width:].astype(F32)
        coded_ref[pl.ds(start, q_dev), :] = coded
    dots = dot_nt(embed_ref[...], query_ref[...])
    dots_ref[...] = dots
    scores = dots / SOFTMAX_HEAT

    coded = coded_ref[...].T
    ids = coded[:negatives] * float(ID_BASE) + coded[negatives:]
    home = jnp.broadcast_to(side_ref[:, 1:2], (rows, queries))
    count = jnp.zeros((rows, queries), F32)
    for j in range(negatives):
        count = count + jnp.where(ids[j : j + 1, :] == home, 1.0, 0.0)
    members = iota((slots, queries), 0) // CAP == iota((slots, queries), 1) // q_dev
    marked = dot_nt(members.astype(BF16), count.astype(BF16)) > 0.0
    before = (iota((rows, rows), 0) <= iota((rows, rows), 1)).astype(BF16)
    rank_in = dot_nn(marked.astype(F32).astype(BF16), before)
    wanted = (iota((slots, rows), 0) % CAP + 1).astype(F32)
    onehot = jnp.where(marked & (rank_in == wanted), 1.0, 0.0)
    onehot_ref[...] = onehot

    own = iota((rows, queries), 1) // q_dev == me
    count = count + jnp.where(own & (positive_ref[...] == iota((rows, queries), 0)), 1.0, 0.0)
    named = count > 0.0
    top = jnp.max(jnp.where(named, scores, LOWEST), axis=0, keepdims=True)
    weight = count * jnp.exp(jnp.where(named, scores - top, LOWEST))
    weight_ref[...] = weight
    total = jnp.sum(weight, axis=0, keepdims=True)
    dot_total = jnp.sum(weight * dots, axis=0, keepdims=True)
    slot_weight = dot_nn(onehot, weight, precision=HIGHEST)
    slot_base = dot_nt(base_ref[...], onehot, precision=HIGHEST)
    tail_row = iota((HEAD_ROWS - CAP, queries), 0)
    tail = jnp.where(tail_row == 0, top, jnp.where(tail_row == 1, total, dot_total))
    lane_group = iota((CAP, queries), 1) // q_dev
    compact = jnp.zeros((CAP, queries), F32)
    for peer in range(group):
        part = slot_weight[peer * CAP : (peer + 1) * CAP]
        compact = jnp.where(lane_group == peer, part, compact)
    message_ref[:CAP, :] = compact
    message_ref[CAP:HEAD_ROWS, :] = tail
    message_ref[HEAD_ROWS:, :slots] = slot_base
    message_ref[HEAD_ROWS:, slots : slots + q_dev] = query_low_ref[...]


def back_kernel(query_ref, weights_ref, back_ref):
    back_ref[...] = dot_nt(weights_ref[weights_ref.shape[0] // 2 :, :], query_ref[...])


def request_kernel(first, embed_ref, onehot_ref, *blocks):
    width = embed_ref.shape[1]
    me = lax.axis_index("dp")
    onehot = [
        onehot_ref[pl.ds(pl.multiple_of((me ^ k) * CAP, CAP), CAP), :]
        for k in range(2 * first, 2 * (first + len(blocks)))
    ]
    onehot = jnp.concatenate(onehot, axis=0).astype(BF16)
    chunk = min(width, 1024)
    for at in range(0, width, chunk):
        part = dot_nn(onehot, embed_ref[:, at : at + chunk]).astype(BF16)
        for i, block in enumerate(blocks):
            block[:, at : at + chunk] = part[2 * i * CAP : 2 * (i + 1) * CAP]


def request(first, count, embed, onehot):
    width = embed.shape[1]
    return run(
        functools.partial(request_kernel, first),
        (shape_of((2 * CAP, width), BF16),) * count,
        (embed, onehot),
        2 * embed.size * 2 * CAP * count,
    )


def forward_kernel(*refs):
    out_ref = refs[-1]
    for i, ref in enumerate(refs[:-1]):
        out_ref[i * CAP : (i + 1) * CAP, :] = ref[CAP:, :]


def message_parts(near_ref, far_ref, group):
    rows = near_ref.shape[0] // (group // 2)
    return [((near_ref, far_ref)[k % 2], k // 2 * rows) for k in range(group)]


def combine(parts):
    tops = [ref[at + TOP_ROW : at + TOP_ROW + 1, :] for ref, at in parts]
    sums = [ref[at + SUM_ROW : at + SUM_ROW + 1, :] for ref, at in parts]
    top = functools.reduce(jnp.maximum, tops)
    scales = [jnp.exp(t - top) for t in tops]
    inverse_total = 1.0 / sum(t * s for t, s in zip(scales, sums))
    return [scale * inverse_total for scale in scales]


def own_target(positive_ref, rows, queries, q_dev, me):
    own = iota((rows, queries), 1) // q_dev == me
    return jnp.where(own & (positive_ref[...] == iota((rows, queries), 0)), 1.0, 0.0)


def terms_kernel(group, shards, near_ref, far_ref, *refs):
    parts = message_parts(near_ref, far_ref, group)
    (
        weight_ref,
        dots_ref,
        positive_ref,
        query_ref,
        embed_ref,
        back_query_ref,
        back_passage_ref,
        passage_low_ref,
        row_ref,
        own_ref,
        passage_in_ref,
        query_in_ref,
    ) = refs[:12]
    final_ref = refs[12]
    blocks = refs[13 : 13 + shards]
    (sum_ref,) = refs[13 + shards :]
    rows, queries = weight_ref.shape
    q_dev = queries // group
    rank = passage_low_ref.shape[0]
    width = query_ref.shape[1]
    me = lax.axis_index("dp")

    scales = combine(parts)
    target = own_target(positive_ref, rows, queries, q_dev, me)
    weight = (weight_ref[...] * scales[0] - target) / SOFTMAX_HEAT
    final_ref[...] = weight
    dots = dots_ref[...]
    weighted = weight * dots
    share = jnp.sum(weighted, axis=0, keepdims=True)
    ones = jnp.ones((8, queries), F32)
    inner = dot_nt(ones, weighted, precision=HIGHEST)[0:1, :]

    inner_query = -jnp.sum(target * dots, axis=0, keepdims=True)
    slots = group * CAP
    bases, query_low = [], []
    for (ref, at), scale in zip(parts, scales):
        inner_query = inner_query + scale * ref[at + DOT_ROW : at + DOT_ROW + 1, :]
        bases.append(ref[at + HEAD_ROWS : at + HEAD_ROWS + rank, :slots])
        query_low.append(ref[at + HEAD_ROWS : at + HEAD_ROWS + rank, slots : slots + q_dev])
    sent_by = me ^ (iota((queries, queries), 0) // q_dev)
    place = iota((queries, queries), 1) == sent_by * q_dev + iota((queries, queries), 0) % q_dev
    query_low = dot_nn(
        jnp.concatenate(query_low, axis=1), place.astype(F32), precision=HIGHEST
    )
    pick_slots = (iota((slots, CAP), 0) == iota((slots, CAP), 1) + me * CAP).astype(F32)
    bases = dot_nn(jnp.concatenate(bases[1:], axis=0), pick_slots, precision=HIGHEST)
    far_base = [bases[k * rank : (k + 1) * rank] for k in range(group - 1)]
    far_weight = [
        ref[at : at + CAP, :] * (scale / SOFTMAX_HEAT)
        for (ref, at), scale in zip(parts[1:], scales[1:])
    ]
    inner_query = inner_query / SOFTMAX_HEAT

    passage_low = passage_low_ref[...]
    from_query = dot_nn(passage_low, weight, precision=HIGHEST) - query_low * share
    from_passage = dot_nt(query_low, weight, precision=HIGHEST) - passage_low * inner
    query_parts = jnp.concatenate(split_two(from_query), axis=0)
    passage_parts = jnp.concatenate(split_two(from_passage), axis=0)

    back_passage = dot_nt(back_query_ref[...], weight, precision=HIGHEST)
    back_passage = (back_passage - back_passage_ref[...] * inner) * row_ref[0:1, :]
    back_passage = back_passage.astype(BF16)
    back_query = dot_nn(back_passage_ref[...], weight, precision=HIGHEST)
    back_query = back_query + dot_nn(
        jnp.concatenate(far_base, axis=1),
        jnp.concatenate(far_weight, axis=0),
        precision=HIGHEST,
    )
    back_query = (back_query - back_query_ref[...] * inner_query) * own_ref[0:1, :]
    pick = (iota((q_dev, queries), 1) == iota((q_dev, queries), 0) + me * q_dev).astype(BF16)
    back_query = dot_nt(back_query.astype(BF16), pick).astype(BF16)

    chunk = min(width, 512)
    for at in range(0, width, chunk):
        cols = slice(at, at + chunk)
        both = dot_nn(query_parts, query_ref[:, cols]) + dot_nn(passage_parts, embed_ref[:, cols])
        sum_ref[rank:, cols] = ADAPTER_SCALE * (both[:rank] + both[rank:])
        sum_ref[:rank, cols] = ADAPTER_SCALE * (
            dot_nn(back_passage, passage_in_ref[:, cols])
            + dot_nn(back_query, query_in_ref[:, cols])
        )
    part = width // shards
    home = lax.axis_index("fsdp")
    for k in range(shards):
        start = pl.multiple_of((home ^ k) * part, part)
        blocks[k][...] = sum_ref[:, pl.ds(start, part)].astype(blocks[k].dtype)


def backward(upstream_of, raw_ref, inverse, grad_ref, up_ref):
    rows, width = raw_ref.shape
    chunk = min(width, 512)
    inner = jnp.zeros((rows, 1), F32)
    for at in range(0, width, chunk):
        upstream = upstream_of(at, chunk)
        up_ref[:, at : at + chunk] = upstream
        unit = raw_ref[:, at : at + chunk].astype(F32) * inverse
        inner = inner + jnp.sum(unit * upstream, axis=-1, keepdims=True)
    for at in range(0, width, chunk):
        unit = raw_ref[:, at : at + chunk].astype(F32) * inverse
        grad = (up_ref[:, at : at + chunk] - unit * inner) * inverse
        grad_ref[:, at : at + chunk] = grad.astype(BF16)


def passage_kernel(final_ref, query_ref, raw_ref, side_ref, grad_ref, up_ref):
    high, low = split_two(final_ref[...])

    def upstream_of(at, chunk):
        embed = query_ref[:, at : at + chunk]
        return dot_nn(high, embed) + dot_nn(low, embed)

    backward(upstream_of, raw_ref, side_ref[:, 0:1], grad_ref, up_ref)


def query_kernel(group, near_ref, far_ref, *refs):
    parts = message_parts(near_ref, far_ref, group)
    near = refs[: group // 2 - 1]
    forwarded_ref, final_ref, embed_ref, raw_ref, grad_ref, up_ref = refs[group // 2 - 1 :]
    q_dev, width = raw_ref.shape
    queries = final_ref.shape[1]
    me = lax.axis_index("dp")
    scales = combine(parts)
    pick = (iota((q_dev, queries), 1) == iota((q_dev, queries), 0) + me * q_dev).astype(F32)
    far = [
        ref[at : at + CAP, :] * (scale / SOFTMAX_HEAT) for (ref, at), scale in zip(parts, scales)
    ]
    far = far[2::2] + far[1::2] + [jnp.zeros((CAP, queries), F32)]
    own_parts = split_two(dot_nt(pick, final_ref[...], precision=HIGHEST))
    far_parts = split_two(dot_nt(pick, jnp.concatenate(far, axis=0), precision=HIGHEST))
    own_parts = jnp.concatenate(own_parts, axis=0)
    far_parts = jnp.concatenate(far_parts, axis=0)

    def upstream_of(at, chunk):
        rows = [ref[:, at : at + chunk].astype(F32)[:CAP] for ref in near]
        rows.append(forwarded_ref[:, at : at + chunk].astype(F32))
        rows.append(jnp.zeros((CAP, chunk), F32))
        both = dot_nn(own_parts, embed_ref[:, at : at + chunk])
        both = both + dot_nn(far_parts, jnp.concatenate(rows, axis=0).astype(BF16))
        return both[:q_dev] + both[q_dev:]

    backward(upstream_of, raw_ref, inverse_length(raw_ref, width), grad_ref, up_ref)


def sum_kernel(*refs):
    total = refs[0][...].astype(F32)
    for ref in refs[1:-1]:
        total = total + ref[...].astype(F32)
    refs[-1][...] = total


def sum_two_kernel(left_ref, right_ref, sent_ref):
    sent_ref[...] = (left_ref[...] + right_ref[...]).astype(BF16)


def sum_split_kernel(*refs):
    terms = [ref[...].astype(F32) for ref in refs[:-2]]
    while len(terms) > 1:
        terms = [a + b for a, b in zip(terms[::2], terms[1::2])]
    rank = refs[-1].shape[0]
    refs[-2][...] = terms[0][:rank]
    refs[-1][...] = terms[0][rank:]


def exchange(values, axis, k):
    size = lax.axis_size(axis)
    return lax.ppermute(values, axis, [(i, i ^ k) for i in range(size)])


def per_device(
    query_pooled_states,
    passage_pooled_states,
    query_attention_output,
    passage_attention_output,
    positive_passage_row,
    hard_negative_ids,
    passage_home_row,
    adapter_down_weight,
    adapter_up_weight,
):
    group = lax.axis_size("dp")
    shards = lax.axis_size("fsdp")
    query_raw = query_pooled_states[0]
    passage_raw = passage_pooled_states[0]
    query_in = query_attention_output[0]
    passage_in = passage_attention_output[0]
    ids = hard_negative_ids[0]
    q_dev, width = query_raw.shape
    p_dev = passage_raw.shape[0]
    rank, part = adapter_down_weight.shape
    queries = group * q_dev
    slots = group * CAP
    work = 2 * p_dev * width

    packed, adapter, embed, side, side_row = run(
        front_kernel,
        (
            shape_of((q_dev, width + 2 * ids.shape[1]), BF16),
            shape_of((rank, part), BF16),
            shape_of((p_dev, width), BF16),
            shape_of((p_dev, 128), F32),
            shape_of((8, p_dev), F32),
        ),
        (
            query_raw,
            ids,
            adapter_down_weight,
            adapter_up_weight,
            passage_raw,
            passage_home_row,
        ),
        work,
        [
            pltpu.VMEM(ids.shape, jnp.int32),
            pltpu.VMEM(passage_raw.shape, BF16),
            pltpu.VMEM(passage_home_row.shape, jnp.int32),
            pltpu.SemaphoreType.DMA((4 + PASSAGE_CHUNKS,)),
        ],
        in_hbm=True,
    )
    blocks = {0: packed}
    for k in range(2, group, 2):
        blocks[k] = exchange(packed, "dp", k)
    blocks[1] = exchange(packed, "dp", 1)
    adapter_blocks = [adapter] + [exchange(adapter, "fsdp", k) for k in range(1, shards)]
    positive_row = jnp.tile(positive_passage_row, (1, group))

    for k in range(2, group, 2):
        blocks[k ^ 1] = exchange(blocks[k], "dp", 1)
    adapter_near = stack(*adapter_blocks)
    adapter_far = exchange(adapter_near, "dp", 1)
    adapter_full, passage_low, query_low, own_side, slot_base = run(
        functools.partial(rank_kernel, shards),
        (
            shape_of((2 * rank, width), BF16),
            shape_of((rank, p_dev), F32),
            shape_of((rank, q_dev), F32),
            shape_of((8, queries), F32),
            shape_of((rank, p_dev), F32),
        ),
        (adapter_near, adapter_far, query_raw, query_in, passage_in, embed, side_row),
        work * rank,
    )
    query_embed, weight, dots, onehot, message = run(
        functools.partial(score_kernel, group),
        (
            shape_of((queries, width), BF16),
            shape_of((p_dev, queries), F32),
            shape_of((p_dev, queries), F32),
            shape_of((slots, p_dev), F32),
            shape_of((HEAD_ROWS + rank, queries), F32),
        ),
        (
            *[blocks[k] for k in range(group)],
            embed,
            side,
            positive_row,
            query_low,
            slot_base,
        ),
        work * queries,
        [pltpu.VMEM((queries, 2 * ids.shape[1]), F32)],
    )
    back_query = run(
        back_kernel,
        (shape_of((rank, queries), F32),),
        (query_embed, adapter_full),
        work * rank,
    )[0]
    stats = [message] + [exchange(message, "dp", k) for k in range(2, group, 2)]
    chips = group // 2
    row_blocks = request(0, chips, embed, onehot)
    stats, row_blocks = lax.optimization_barrier((stats, row_blocks))
    near = [exchange(row_blocks[i], "dp", 2 * i) for i in range(1, chips)]
    near_stats = stack(*stats)
    far_stats = exchange(near_stats, "dp", 1)
    final, *terms = run(
        functools.partial(terms_kernel, group, shards),
        (
            shape_of((p_dev, queries), F32),
            shape_of((2 * rank, part), F32),
            *[shape_of((2 * rank, part), BF16)] * (shards - 1),
        ),
        (
            near_stats,
            far_stats,
            weight,
            dots,
            positive_row,
            query_embed,
            embed,
            back_query,
            slot_base,
            passage_low,
            side_row,
            own_side,
            passage_in,
            query_in,
        ),
        work * rank * 4,
        [pltpu.VMEM((2 * rank, width), F32)],
    )
    arrived = [exchange(terms[k], "fsdp", k) for k in range(1, shards)]
    final, near[0] = lax.optimization_barrier((final, near[0]))
    grad_passage = run(
        passage_kernel,
        (shape_of((p_dev, width), BF16),),
        (final, query_embed, passage_raw, side),
        2 * work * queries,
        [pltpu.VMEM((p_dev, width), F32)],
    )[0]
    terms[0], grad_passage = lax.optimization_barrier((terms[0], grad_passage))
    total = run(sum_kernel, (shape_of((2 * rank, part), F32),), (terms[0], *arrived), 1)[0]
    total, near = lax.optimization_barrier((total, near))
    to_sibling = run(
        forward_kernel,
        (shape_of((group // 2 * CAP, width), BF16),),
        (row_blocks[0], *near),
        1,
    )[0]
    forwarded = exchange(to_sibling, "dp", 1)
    sent = run(
        sum_two_kernel,
        (shape_of((2 * rank, part), BF16),),
        (total, exchange(total, "dp", 1)),
        1,
    )[0]
    arrived = [exchange(sent, "dp", k) for k in range(2, group, 2)]
    grad_query = run(
        functools.partial(query_kernel, group),
        (shape_of((q_dev, width), BF16),),
        (near_stats, far_stats, *near, forwarded, final, embed, query_raw),
        4 * q_dev * width * (p_dev + slots),
        [pltpu.VMEM((q_dev, width), F32)],
    )[0]
    sent, grad_query = lax.optimization_barrier((sent, grad_query))
    down_total, up_total = run(
        sum_split_kernel, (shape_of((rank, part), F32),) * 2, (sent, *arrived), 1
    )
    return (grad_query[None], grad_passage[None], down_total, up_total)


def solution(mesh):
    in_specs = (
        P("fsdp", "dp", None),
        P("fsdp", "dp", None),
        P("fsdp", "dp", None),
        P("fsdp", "dp", None),
        P("fsdp", "dp"),
        P("fsdp", "dp", None),
        P("fsdp", None),
        P(None, "fsdp"),
        P(None, "fsdp"),
    )
    out_specs = (P("fsdp", "dp", None), P("fsdp", "dp", None), P(None, "fsdp"), P(None, "fsdp"))
    return jax.shard_map(
        per_device, mesh=mesh, in_specs=in_specs, out_specs=out_specs, check_vma=False
    )
```

```python
import functools

import jax
import jax.numpy as jnp
from jax import lax
from jax.experimental import pallas as pl
from jax.experimental.pallas import tpu as pltpu
from jax.sharding import PartitionSpec as P

CAP = 8
SOFTMAX_HEAT = 0.01
ADAPTER_SCALE = 2.0
EPSILON = 1e-06
LOWEST = -1e30
ID_BASE = 256
TOP_ROW, SUM_ROW, DOT_ROW, HEAD_ROWS = 8, 9, 10, 16
VMEM_BYTES = 16 * 1024 * 1024
PASSAGE_CHUNKS = 4
F32 = jnp.float32
BF16 = jnp.bfloat16
HIGHEST = lax.Precision.HIGHEST


def dot_nn(a, b, precision=None):
    return lax.dot_general(
        a, b, (((1,), (0,)), ((), ())), precision=precision, preferred_element_type=F32
    )


def dot_nt(a, b, precision=None):
    return lax.dot_general(
        a, b, (((1,), (1,)), ((), ())), precision=precision, preferred_element_type=F32
    )


def split_two(values):
    high = values.astype(BF16)
    low = (values - high.astype(F32)).astype(BF16)
    return high, low


def iota(shape, dim):
    return lax.broadcasted_iota(jnp.int32, shape, dim)


def shape_of(dims, kind):
    return jax.ShapeDtypeStruct(dims, kind)


def run(body, out_shape, args, flops, scratch=(), in_hbm=False):
    grant = VMEM_BYTES * max(1, size_ratio(args))
    if in_hbm:
        args = [pltpu.with_memory_space_constraint(a, pltpu.HBM) for a in args]
    vmem = pl.BlockSpec(memory_space=pltpu.VMEM)
    hbm = pl.BlockSpec(memory_space=pltpu.HBM)
    moved = sum(a.size * a.dtype.itemsize for a in (*args, *out_shape))
    return pl.pallas_call(
        body,
        out_shape=out_shape,
        in_specs=[hbm if in_hbm else vmem] * len(args),
        out_specs=tuple(vmem for _ in out_shape),
        scratch_shapes=list(scratch),
        compiler_params=pltpu.CompilerParams(vmem_limit_bytes=grant),
        cost_estimate=pl.CostEstimate(flops=flops, bytes_accessed=moved, transcendentals=0),
    )(*args)


def size_ratio(args):
    moved = sum(a.size * a.dtype.itemsize for a in args)
    return -(-moved * 3 // VMEM_BYTES)


def near_core(values):
    return pltpu.with_memory_space_constraint(values, pltpu.VMEM)


def inverse_length(raw_ref, width):
    chunk = min(width, 512)
    total = jnp.zeros((raw_ref.shape[0], 1), F32)
    for at in range(0, width, chunk):
        part = raw_ref[:, at : at + chunk].astype(F32)
        total = total + jnp.sum(part * part, axis=-1, keepdims=True)
    return 1.0 / jnp.sqrt(total + EPSILON)


def front_kernel(
    query_ref,
    ids_ref,
    down_ref,
    up_ref,
    passage_ref,
    home_ref,
    out_ref,
    adapter_ref,
    embed_ref,
    side_ref,
    row_ref,
    ids_here,
    passage_here,
    home_here,
    sems,
):
    rows, width = passage_ref.shape
    total = home_ref.shape[1]
    me = lax.axis_index("dp")
    part = rows // PASSAGE_CHUNKS
    copies = [
        pltpu.make_async_copy(ids_ref, ids_here, sems.at[0]),
        pltpu.make_async_copy(query_ref, out_ref.at[:, pl.ds(0, width)], sems.at[1]),
        pltpu.make_async_copy(home_ref, home_here, sems.at[2]),
    ]
    for copy in copies:
        copy.start()
    own_down = pltpu.make_async_copy(down_ref, adapter_ref, sems.at[3])
    own_up = pltpu.make_async_copy(up_ref, adapter_ref, sems.at[3])
    pl.when(me % 2 == 0)(own_down.start)
    pl.when(me % 2 == 1)(own_up.start)
    passage_copies = []
    for c in range(PASSAGE_CHUNKS):
        here = pl.ds(c * part, part)
        passage_copies.append(
            pltpu.make_async_copy(
                passage_ref.at[here, :], passage_here.at[here, :], sems.at[4 + c]
            )
        )
        passage_copies[c].start()

    copies[0].wait()
    ids = ids_here[...]
    coded = jnp.concatenate([ids // ID_BASE, ids % ID_BASE], axis=1)
    out_ref[:, width:] = coded.astype(F32).astype(BF16)
    copies[2].wait()
    row_id = iota((rows, total), 0) + me * rows
    number = iota((rows, total), 1)
    home = jnp.where(home_here[...] == row_id, number, 0).astype(F32)
    home = jnp.sum(home, axis=1, keepdims=True)

    chunk = min(width, 512)
    inverses = []
    for c in range(PASSAGE_CHUNKS):
        passage_copies[c].wait()
        here = slice(c * part, (c + 1) * part)
        inverse = inverse_length(passage_here.at[here, :], width)
        for at in range(0, width, chunk):
            values = passage_here[here, at : at + chunk].astype(F32)
            embed_ref[here, at : at + chunk] = (values * inverse).astype(BF16)
        inverses.append(inverse)
    inverse = jnp.concatenate(inverses, axis=0)
    side_ref[...] = jnp.where(iota(side_ref.shape, 1) == 0, inverse, home)
    row_ref[...] = jnp.broadcast_to(inverse, (rows, rows)).T[: row_ref.shape[0]]
    copies[1].wait()
    pl.when(me % 2 == 0)(own_down.wait)
    pl.when(me % 2 == 1)(own_up.wait)


def stack_kernel(*refs):
    out_ref = refs[-1]
    rows = refs[0].shape[0]
    for i, ref in enumerate(refs[:-1]):
        out_ref[i * rows : (i + 1) * rows, :] = ref[...]


def stack(*parts):
    rows, cols = parts[0].shape
    return run(stack_kernel, (shape_of((len(parts) * rows, cols), parts[0].dtype),), parts, 1)[0]


def rank_kernel(
    shards,
    near_ref,
    far_ref,
    query_ref,
    query_in_ref,
    passage_in_ref,
    embed_ref,
    row_ref,
    weights_ref,
    passage_low_ref,
    query_low_ref,
    own_ref,
    slot_base_ref,
):
    part = near_ref.shape[1]
    rank = near_ref.shape[0] // shards
    q_dev, width = query_ref.shape
    queries = own_ref.shape[1]
    me = lax.axis_index("fsdp")
    core = lax.axis_index("dp") % 2

    def place_halves(first_ref, second_ref):
        for k in range(shards):
            cols = pl.ds(pl.multiple_of((me ^ k) * part, part), part)
            weights_ref[:rank, cols] = first_ref[k * rank : (k + 1) * rank, :]
            weights_ref[rank:, cols] = second_ref[k * rank : (k + 1) * rank, :]

    pl.when(core == 0)(functools.partial(place_halves, near_ref, far_ref))
    pl.when(core == 1)(functools.partial(place_halves, far_ref, near_ref))
    down, up = weights_ref[:rank, :], weights_ref[rank:, :]
    place = iota((q_dev, queries), 1) == iota((q_dev, queries), 0) + lax.axis_index("dp") * q_dev
    inverse = inverse_length(query_ref, width)
    own = jnp.sum(jnp.where(place, inverse, 0.0), axis=0, keepdims=True)
    own_ref[...] = jnp.broadcast_to(own, own_ref.shape)
    same = iota((q_dev, q_dev), 0) == iota((q_dev, q_dev), 1)
    inverse_row = jnp.sum(jnp.where(same, inverse, 0.0), axis=0, keepdims=True)
    query_low = dot_nt(down, query_in_ref[...]).astype(BF16)
    query_low_ref[...] = query_low.astype(F32) * inverse_row
    passage_low = dot_nt(down, passage_in_ref[...]).astype(BF16)
    passage_low_ref[...] = passage_low.astype(F32) * row_ref[0:1, :]
    slot_base_ref[...] = dot_nt(up, embed_ref[...])


def score_kernel(group, *refs):
    blocks = refs[:group]
    embed_ref, side_ref, positive_ref, query_low_ref, base_ref = refs[group : group + 5]
    query_ref, weight_ref, dots_ref, onehot_ref, message_ref, coded_ref = refs[group + 5 :]
    rows, width = embed_ref.shape
    queries = query_ref.shape[0]
    q_dev = queries // group
    negatives = (blocks[0].shape[1] - width) // 2
    slots = group * CAP
    rank = query_low_ref.shape[0]
    me = lax.axis_index("dp")
    chunk = min(width, 1024)
    for k in range(group):
        start = pl.multiple_of((me ^ k) * q_dev, q_dev)
        inverse = inverse_length(blocks[k], width)
        for at in range(0, width, chunk):
            part = blocks[k][:, at : at + chunk].astype(F32)
            query_ref[pl.ds(start, q_dev), at : at + chunk] = (part * inverse).astype(BF16)
        coded = blocks[k][:, width:].astype(F32)
        coded_ref[pl.ds(start, q_dev), :] = coded
    dots = dot_nt(embed_ref[...], query_ref[...])
    dots_ref[...] = dots
    scores = dots / SOFTMAX_HEAT

    coded = coded_ref[...].T
    ids = coded[:negatives] * float(ID_BASE) + coded[negatives:]
    home = jnp.broadcast_to(side_ref[:, 1:2], (rows, queries))
    count = jnp.zeros((rows, queries), F32)
    for j in range(negatives):
        count = count + jnp.where(ids[j : j + 1, :] == home, 1.0, 0.0)
    members = iota((slots, queries), 0) // CAP == iota((slots, queries), 1) // q_dev
    marked = dot_nt(members.astype(BF16), count.astype(BF16)) > 0.0
    before = (iota((rows, rows), 0) <= iota((rows, rows), 1)).astype(BF16)
    rank_in = dot_nn(marked.astype(F32).astype(BF16), before)
    wanted = (iota((slots, rows), 0) % CAP + 1).astype(F32)
    onehot = jnp.where(marked & (rank_in == wanted), 1.0, 0.0)
    onehot_ref[...] = onehot

    own = iota((rows, queries), 1) // q_dev == me
    count = count + jnp.where(own & (positive_ref[...] == iota((rows, queries), 0)), 1.0, 0.0)
    named = count > 0.0
    top = jnp.max(jnp.where(named, scores, LOWEST), axis=0, keepdims=True)
    weight = count * jnp.exp(jnp.where(named, scores - top, LOWEST))
    weight_ref[...] = weight
    total = jnp.sum(weight, axis=0, keepdims=True)
    dot_total = jnp.sum(weight * dots, axis=0, keepdims=True)
    slot_weight = dot_nn(onehot, weight, precision=HIGHEST)
    slot_base = dot_nt(base_ref[...], onehot, precision=HIGHEST)
    tail_row = iota((HEAD_ROWS - CAP, queries), 0)
    tail = jnp.where(tail_row == 0, top, jnp.where(tail_row == 1, total, dot_total))
    lane_group = iota((CAP, queries), 1) // q_dev
    compact = jnp.zeros((CAP, queries), F32)
    for peer in range(group):
        part = slot_weight[peer * CAP : (peer + 1) * CAP]
        compact = jnp.where(lane_group == peer, part, compact)
    message_ref[:CAP, :] = compact
    message_ref[CAP:HEAD_ROWS, :] = tail
    message_ref[HEAD_ROWS:, :slots] = slot_base
    message_ref[HEAD_ROWS:, slots : slots + q_dev] = query_low_ref[...]


def back_kernel(query_ref, weights_ref, back_ref):
    back_ref[...] = dot_nt(weights_ref[weights_ref.shape[0] // 2 :, :], query_ref[...])


def request_kernel(first, embed_ref, onehot_ref, *blocks):
    width = embed_ref.shape[1]
    me = lax.axis_index("dp")
    onehot = [
        onehot_ref[pl.ds(pl.multiple_of((me ^ k) * CAP, CAP), CAP), :]
        for k in range(2 * first, 2 * (first + len(blocks)))
    ]
    onehot = jnp.concatenate(onehot, axis=0).astype(BF16)
    chunk = min(width, 1024)
    for at in range(0, width, chunk):
        part = dot_nn(onehot, embed_ref[:, at : at + chunk]).astype(BF16)
        for i, block in enumerate(blocks):
            block[:, at : at + chunk] = part[2 * i * CAP : 2 * (i + 1) * CAP]


def request(first, count, embed, onehot):
    width = embed.shape[1]
    return run(
        functools.partial(request_kernel, first),
        (shape_of((2 * CAP, width), BF16),) * count,
        (embed, onehot),
        2 * embed.size * 2 * CAP * count,
    )


def forward_kernel(*refs):
    out_ref = refs[-1]
    for i, ref in enumerate(refs[:-1]):
        out_ref[i * CAP : (i + 1) * CAP, :] = ref[CAP:, :]


def message_parts(near_ref, far_ref, group):
    rows = near_ref.shape[0] // (group // 2)
    return [((near_ref, far_ref)[k % 2], k // 2 * rows) for k in range(group)]


def combine(parts):
    tops = [ref[at + TOP_ROW : at + TOP_ROW + 1, :] for ref, at in parts]
    sums = [ref[at + SUM_ROW : at + SUM_ROW + 1, :] for ref, at in parts]
    top = functools.reduce(jnp.maximum, tops)
    scales = [jnp.exp(t - top) for t in tops]
    inverse_total = 1.0 / sum(t * s for t, s in zip(scales, sums))
    return [scale * inverse_total for scale in scales]


def own_target(positive_ref, rows, queries, q_dev, me):
    own = iota((rows, queries), 1) // q_dev == me
    return jnp.where(own & (positive_ref[...] == iota((rows, queries), 0)), 1.0, 0.0)


def terms_kernel(group, shards, near_ref, far_ref, *refs):
    parts = message_parts(near_ref, far_ref, group)
    (
        weight_ref,
        dots_ref,
        positive_ref,
        query_ref,
        embed_ref,
        back_query_ref,
        back_passage_ref,
        passage_low_ref,
        row_ref,
        own_ref,
        passage_in_ref,
        query_in_ref,
    ) = refs[:12]
    final_ref = refs[12]
    blocks = refs[13 : 13 + shards]
    (sum_ref,) = refs[13 + shards :]
    rows, queries = weight_ref.shape
    q_dev = queries // group
    rank = passage_low_ref.shape[0]
    width = query_ref.shape[1]
    me = lax.axis_index("dp")

    scales = combine(parts)
    target = own_target(positive_ref, rows, queries, q_dev, me)
    weight = (weight_ref[...] * scales[0] - target) / SOFTMAX_HEAT
    final_ref[...] = weight
    dots = dots_ref[...]
    weighted = weight * dots
    share = jnp.sum(weighted, axis=0, keepdims=True)
    ones = jnp.ones((8, queries), F32)
    inner = dot_nt(ones, weighted, precision=HIGHEST)[0:1, :]

    inner_query = -jnp.sum(target * dots, axis=0, keepdims=True)
    slots = group * CAP
    bases, query_low = [], []
    for (ref, at), scale in zip(parts, scales):
        inner_query = inner_query + scale * ref[at + DOT_ROW : at + DOT_ROW + 1, :]
        bases.append(ref[at + HEAD_ROWS : at + HEAD_ROWS + rank, :slots])
        query_low.append(ref[at + HEAD_ROWS : at + HEAD_ROWS + rank, slots : slots + q_dev])
    sent_by = me ^ (iota((queries, queries), 0) // q_dev)
    place = iota((queries, queries), 1) == sent_by * q_dev + iota((queries, queries), 0) % q_dev
    query_low = dot_nn(
        jnp.concatenate(query_low, axis=1), place.astype(F32), precision=HIGHEST
    )
    pick_slots = (iota((slots, CAP), 0) == iota((slots, CAP), 1) + me * CAP).astype(F32)
    bases = dot_nn(jnp.concatenate(bases[1:], axis=0), pick_slots, precision=HIGHEST)
    far_base = [bases[k * rank : (k + 1) * rank] for k in range(group - 1)]
    far_weight = [
        ref[at : at + CAP, :] * (scale / SOFTMAX_HEAT)
        for (ref, at), scale in zip(parts[1:], scales[1:])
    ]
    inner_query = inner_query / SOFTMAX_HEAT

    passage_low = passage_low_ref[...]
    from_query = dot_nn(passage_low, weight, precision=HIGHEST) - query_low * share
    from_passage = dot_nt(query_low, weight, precision=HIGHEST) - passage_low * inner
    query_parts = jnp.concatenate(split_two(from_query), axis=0)
    passage_parts = jnp.concatenate(split_two(from_passage), axis=0)

    back_passage = dot_nt(back_query_ref[...], weight, precision=HIGHEST)
    back_passage = (back_passage - back_passage_ref[...] * inner) * row_ref[0:1, :]
    back_passage = back_passage.astype(BF16)
    back_query = dot_nn(back_passage_ref[...], weight, precision=HIGHEST)
    back_query = back_query + dot_nn(
        jnp.concatenate(far_base, axis=1),
        jnp.concatenate(far_weight, axis=0),
        precision=HIGHEST,
    )
    back_query = (back_query - back_query_ref[...] * inner_query) * own_ref[0:1, :]
    pick = (iota((q_dev, queries), 1) == iota((q_dev, queries), 0) + me * q_dev).astype(BF16)
    back_query = dot_nt(back_query.astype(BF16), pick).astype(BF16)

    chunk = min(width, 512)
    for at in range(0, width, chunk):
        cols = slice(at, at + chunk)
        both = dot_nn(query_parts, query_ref[:, cols]) + dot_nn(passage_parts, embed_ref[:, cols])
        sum_ref[rank:, cols] = ADAPTER_SCALE * (both[:rank] + both[rank:])
        sum_ref[:rank, cols] = ADAPTER_SCALE * (
            dot_nn(back_passage, passage_in_ref[:, cols])
            + dot_nn(back_query, query_in_ref[:, cols])
        )
    part = width // shards
    home = lax.axis_index("fsdp")
    for k in range(shards):
        start = pl.multiple_of((home ^ k) * part, part)
        blocks[k][...] = sum_ref[:, pl.ds(start, part)].astype(blocks[k].dtype)


def backward(upstream_of, raw_ref, inverse, grad_ref, up_ref):
    rows, width = raw_ref.shape
    chunk = min(width, 512)
    inner = jnp.zeros((rows, 1), F32)
    for at in range(0, width, chunk):
        upstream = upstream_of(at, chunk)
        up_ref[:, at : at + chunk] = upstream
        unit = raw_ref[:, at : at + chunk].astype(F32) * inverse
        inner = inner + jnp.sum(unit * upstream, axis=-1, keepdims=True)
    for at in range(0, width, chunk):
        unit = raw_ref[:, at : at + chunk].astype(F32) * inverse
        grad = (up_ref[:, at : at + chunk] - unit * inner) * inverse
        grad_ref[:, at : at + chunk] = grad.astype(BF16)


def passage_kernel(final_ref, query_ref, raw_ref, side_ref, grad_ref, up_ref):
    high, low = split_two(final_ref[...])

    def upstream_of(at, chunk):
        embed = query_ref[:, at : at + chunk]
        return dot_nn(high, embed) + dot_nn(low, embed)

    backward(upstream_of, raw_ref, side_ref[:, 0:1], grad_ref, up_ref)


def query_kernel(group, near_ref, far_ref, *refs):
    parts = message_parts(near_ref, far_ref, group)
    near = refs[: group // 2 - 1]
    forwarded_ref, final_ref, embed_ref, raw_ref, grad_ref, up_ref = refs[group // 2 - 1 :]
    q_dev, width = raw_ref.shape
    queries = final_ref.shape[1]
    me = lax.axis_index("dp")
    scales = combine(parts)
    pick = (iota((q_dev, queries), 1) == iota((q_dev, queries), 0) + me * q_dev).astype(F32)
    far = [
        ref[at : at + CAP, :] * (scale / SOFTMAX_HEAT) for (ref, at), scale in zip(parts, scales)
    ]
    far = far[2::2] + far[1::2] + [jnp.zeros((CAP, queries), F32)]
    own_parts = split_two(dot_nt(pick, final_ref[...], precision=HIGHEST))
    far_parts = split_two(dot_nt(pick, jnp.concatenate(far, axis=0), precision=HIGHEST))
    own_parts = jnp.concatenate(own_parts, axis=0)
    far_parts = jnp.concatenate(far_parts, axis=0)

    def upstream_of(at, chunk):
        rows = [ref[:, at : at + chunk].astype(F32)[:CAP] for ref in near]
        rows.append(forwarded_ref[:, at : at + chunk].astype(F32))
        rows.append(jnp.zeros((CAP, chunk), F32))
        both = dot_nn(own_parts, embed_ref[:, at : at + chunk])
        both = both + dot_nn(far_parts, jnp.concatenate(rows, axis=0).astype(BF16))
        return both[:q_dev] + both[q_dev:]

    backward(upstream_of, raw_ref, inverse_length(raw_ref, width), grad_ref, up_ref)


def sum_kernel(*refs):
    total = refs[0][...].astype(F32)
    for ref in refs[1:-1]:
        total = total + ref[...].astype(F32)
    refs[-1][...] = total


def sum_two_kernel(left_ref, right_ref, sent_ref):
    sent_ref[...] = (left_ref[...] + right_ref[...]).astype(BF16)


def sum_split_kernel(*refs):
    terms = [ref[...].astype(F32) for ref in refs[:-2]]
    while len(terms) > 1:
        terms = [a + b for a, b in zip(terms[::2], terms[1::2])]
    rank = refs[-1].shape[0]
    refs[-2][...] = terms[0][:rank]
    refs[-1][...] = terms[0][rank:]


def exchange(values, axis, k):
    size = lax.axis_size(axis)
    return lax.ppermute(values, axis, [(i, i ^ k) for i in range(size)])


def per_device(
    query_pooled_states,
    passage_pooled_states,
    query_attention_output,
    passage_attention_output,
    positive_passage_row,
    hard_negative_ids,
    passage_home_row,
    adapter_down_weight,
    adapter_up_weight,
):
    group = lax.axis_size("dp")
    shards = lax.axis_size("fsdp")
    query_raw = query_pooled_states[0]
    passage_raw = passage_pooled_states[0]
    query_in = query_attention_output[0]
    passage_in = passage_attention_output[0]
    ids = hard_negative_ids[0]
    q_dev, width = query_raw.shape
    p_dev = passage_raw.shape[0]
    rank, part = adapter_down_weight.shape
    queries = group * q_dev
    slots = group * CAP
    work = 2 * p_dev * width

    packed, adapter, embed, side, side_row = run(
        front_kernel,
        (
            shape_of((q_dev, width + 2 * ids.shape[1]), BF16),
            shape_of((rank, part), BF16),
            shape_of((p_dev, width), BF16),
            shape_of((p_dev, 128), F32),
            shape_of((8, p_dev), F32),
        ),
        (
            query_raw,
            ids,
            adapter_down_weight,
            adapter_up_weight,
            passage_raw,
            passage_home_row,
        ),
        work,
        [
            pltpu.VMEM(ids.shape, jnp.int32),
            pltpu.VMEM(passage_raw.shape, BF16),
            pltpu.VMEM(passage_home_row.shape, jnp.int32),
            pltpu.SemaphoreType.DMA((4 + PASSAGE_CHUNKS,)),
        ],
        in_hbm=True,
    )
    blocks = {0: packed}
    for k in range(2, group, 2):
        blocks[k] = exchange(packed, "dp", k)
    blocks[1] = exchange(packed, "dp", 1)
    adapter_blocks = [adapter] + [exchange(adapter, "fsdp", k) for k in range(1, shards)]
    positive_row = jnp.tile(positive_passage_row, (1, group))

    for k in range(2, group, 2):
        blocks[k ^ 1] = exchange(blocks[k], "dp", 1)
    adapter_near = stack(*adapter_blocks)
    adapter_far = exchange(adapter_near, "dp", 1)
    adapter_full, passage_low, query_low, own_side, slot_base = run(
        functools.partial(rank_kernel, shards),
        (
            shape_of((2 * rank, width), BF16),
            shape_of((rank, p_dev), F32),
            shape_of((rank, q_dev), F32),
            shape_of((8, queries), F32),
            shape_of((rank, p_dev), F32),
        ),
        (adapter_near, near_core(adapter_far), query_raw, query_in, passage_in, embed, side_row),
        work * rank,
    )
    query_embed, weight, dots, onehot, message = run(
        functools.partial(score_kernel, group),
        (
            shape_of((queries, width), BF16),
            shape_of((p_dev, queries), F32),
            shape_of((p_dev, queries), F32),
            shape_of((slots, p_dev), F32),
            shape_of((HEAD_ROWS + rank, queries), F32),
        ),
        (
            *[near_core(blocks[k]) for k in range(group)],
            embed,
            side,
            positive_row,
            query_low,
            slot_base,
        ),
        work * queries,
        [pltpu.VMEM((queries, 2 * ids.shape[1]), F32)],
    )
    back_query = run(
        back_kernel,
        (shape_of((rank, queries), F32),),
        (query_embed, adapter_full),
        work * rank,
    )[0]
    stats = [message] + [exchange(message, "dp", k) for k in range(2, group, 2)]
    chips = group // 2
    row_blocks = request(0, chips, embed, onehot)
    stats, row_blocks = lax.optimization_barrier((stats, row_blocks))
    near = [exchange(row_blocks[i], "dp", 2 * i) for i in range(1, chips)]
    near_stats = stack(*stats)
    far_stats = exchange(near_stats, "dp", 1)
    final, *terms = run(
        functools.partial(terms_kernel, group, shards),
        (
            shape_of((p_dev, queries), F32),
            shape_of((2 * rank, part), F32),
            *[shape_of((2 * rank, part), BF16)] * (shards - 1),
        ),
        (
            near_stats,
            far_stats,
            weight,
            dots,
            positive_row,
            query_embed,
            embed,
            back_query,
            slot_base,
            passage_low,
            side_row,
            own_side,
            passage_in,
            query_in,
        ),
        work * rank * 4,
        [pltpu.VMEM((2 * rank, width), F32)],
    )
    arrived = [exchange(terms[k], "fsdp", k) for k in range(1, shards)]
    final, near[0] = lax.optimization_barrier((final, near[0]))
    grad_passage = run(
        passage_kernel,
        (shape_of((p_dev, width), BF16),),
        (final, query_embed, passage_raw, side),
        2 * work * queries,
        [pltpu.VMEM((p_dev, width), F32)],
    )[0]
    terms[0], grad_passage = lax.optimization_barrier((terms[0], grad_passage))
    total = run(sum_kernel, (shape_of((2 * rank, part), F32),), (terms[0], *arrived), 1)[0]
    total, near = lax.optimization_barrier((total, near))
    to_sibling = run(
        forward_kernel,
        (shape_of((group // 2 * CAP, width), BF16),),
        (row_blocks[0], *near),
        1,
    )[0]
    forwarded = exchange(to_sibling, "dp", 1)
    sent = run(
        sum_two_kernel,
        (shape_of((2 * rank, part), BF16),),
        (total, exchange(total, "dp", 1)),
        1,
    )[0]
    arrived = [exchange(sent, "dp", k) for k in range(2, group, 2)]
    grad_query = run(
        functools.partial(query_kernel, group),
        (shape_of((q_dev, width), BF16),),
        (near_stats, far_stats, *near, forwarded, final, embed, query_raw),
        4 * q_dev * width * (p_dev + slots),
        [pltpu.VMEM((q_dev, width), F32)],
    )[0]
    sent, grad_query = lax.optimization_barrier((sent, grad_query))
    down_total, up_total = run(
        sum_split_kernel, (shape_of((rank, part), F32),) * 2, (sent, *arrived), 1
    )
    return (grad_query[None], grad_passage[None], down_total, up_total)


def solution(mesh):
    in_specs = (
        P("fsdp", "dp", None),
        P("fsdp", "dp", None),
        P("fsdp", "dp", None),
        P("fsdp", "dp", None),
        P("fsdp", "dp"),
        P("fsdp", "dp", None),
        P("fsdp", None),
        P(None, "fsdp"),
        P(None, "fsdp"),
    )
    out_specs = (P("fsdp", "dp", None), P("fsdp", "dp", None), P(None, "fsdp"), P(None, "fsdp"))
    return jax.shard_map(
        per_device, mesh=mesh, in_specs=in_specs, out_specs=out_specs, check_vma=False
    )
```

```python
import functools

import jax
import jax.numpy as jnp
from jax import lax
from jax.experimental import pallas as pl
from jax.experimental.pallas import tpu as pltpu
from jax.sharding import PartitionSpec as P

CAP = 8
SOFTMAX_HEAT = 0.01
ADAPTER_SCALE = 2.0
EPSILON = 1e-06
LOWEST = -1e30
ID_BASE = 256
TOP_ROW, SUM_ROW, DOT_ROW, HEAD_ROWS = 8, 9, 10, 16
VMEM_BYTES = 16 * 1024 * 1024
PASSAGE_CHUNKS = 4
F32 = jnp.float32
BF16 = jnp.bfloat16
HIGHEST = lax.Precision.HIGHEST


def dot_nn(a, b, precision=None):
    return lax.dot_general(
        a, b, (((1,), (0,)), ((), ())), precision=precision, preferred_element_type=F32
    )


def dot_nt(a, b, precision=None):
    return lax.dot_general(
        a, b, (((1,), (1,)), ((), ())), precision=precision, preferred_element_type=F32
    )


def split_two(values):
    high = values.astype(BF16)
    low = (values - high.astype(F32)).astype(BF16)
    return high, low


def iota(shape, dim):
    return lax.broadcasted_iota(jnp.int32, shape, dim)


def shape_of(dims, kind):
    return jax.ShapeDtypeStruct(dims, kind)


def run(body, out_shape, args, flops, scratch=(), in_hbm=False):
    grant = VMEM_BYTES * max(1, size_ratio(args))
    if in_hbm:
        args = [pltpu.with_memory_space_constraint(a, pltpu.HBM) for a in args]
    vmem = pl.BlockSpec(memory_space=pltpu.VMEM)
    hbm = pl.BlockSpec(memory_space=pltpu.HBM)
    moved = sum(a.size * a.dtype.itemsize for a in (*args, *out_shape))
    return pl.pallas_call(
        body,
        out_shape=out_shape,
        in_specs=[hbm if in_hbm else vmem] * len(args),
        out_specs=tuple(vmem for _ in out_shape),
        scratch_shapes=list(scratch),
        compiler_params=pltpu.CompilerParams(vmem_limit_bytes=grant),
        cost_estimate=pl.CostEstimate(flops=flops, bytes_accessed=moved, transcendentals=0),
    )(*args)


def size_ratio(args):
    moved = sum(a.size * a.dtype.itemsize for a in args)
    return -(-moved * 3 // VMEM_BYTES)


def inverse_length(raw_ref, width):
    chunk = min(width, 512)
    total = jnp.zeros((raw_ref.shape[0], 1), F32)
    for at in range(0, width, chunk):
        part = raw_ref[:, at : at + chunk].astype(F32)
        total = total + jnp.sum(part * part, axis=-1, keepdims=True)
    return 1.0 / jnp.sqrt(total + EPSILON)


def front_kernel(
    query_ref,
    ids_ref,
    down_ref,
    up_ref,
    passage_ref,
    home_ref,
    positive_ref,
    out_ref,
    adapter_ref,
    embed_ref,
    side_ref,
    row_ref,
    tiled_ref,
    ids_here,
    passage_here,
    home_here,
    positive_here,
    adapter_here,
    sems,
):
    rows, width = passage_ref.shape
    total = home_ref.shape[1]
    me = lax.axis_index("dp")
    part = rows // PASSAGE_CHUNKS
    copies = [
        pltpu.make_async_copy(ids_ref, ids_here, sems.at[0]),
        pltpu.make_async_copy(query_ref, out_ref.at[:, pl.ds(0, width)], sems.at[1]),
        pltpu.make_async_copy(home_ref, home_here, sems.at[2]),
        pltpu.make_async_copy(positive_ref, positive_here, sems.at[3]),
    ]
    for copy in copies:
        copy.start()
    own_down = pltpu.make_async_copy(down_ref, adapter_here, sems.at[4])
    own_up = pltpu.make_async_copy(up_ref, adapter_here, sems.at[4])
    pl.when(me % 2 == 0)(own_down.start)
    pl.when(me % 2 == 1)(own_up.start)
    passage_copies = []
    for c in range(PASSAGE_CHUNKS):
        here = pl.ds(c * part, part)
        passage_copies.append(
            pltpu.make_async_copy(
                passage_ref.at[here, :], passage_here.at[here, :], sems.at[5 + c]
            )
        )
        passage_copies[c].start()

    copies[0].wait()
    ids = ids_here[...]
    coded = jnp.concatenate([ids // ID_BASE, ids % ID_BASE], axis=1)
    out_ref[:, width:] = coded.astype(F32).astype(BF16)
    copies[2].wait()
    row_id = iota((rows, total), 0) + me * rows
    number = iota((rows, total), 1)
    home = jnp.where(home_here[...] == row_id, number, 0).astype(F32)
    home = jnp.sum(home, axis=1, keepdims=True)
    copies[3].wait()
    q_dev = positive_here.shape[1]
    queries = tiled_ref.shape[1]
    repeat = iota((q_dev, queries), 1) % q_dev == iota((q_dev, queries), 0)
    positives = jnp.broadcast_to(positive_here[...].astype(F32), (8, q_dev))
    tiled = dot_nn(positives, repeat.astype(F32), precision=HIGHEST)
    tiled_ref[...] = tiled[0:1, :].astype(jnp.int32)

    chunk = min(width, 512)
    inverses = []
    for c in range(PASSAGE_CHUNKS):
        passage_copies[c].wait()
        here = slice(c * part, (c + 1) * part)
        inverse = inverse_length(passage_here.at[here, :], width)
        for at in range(0, width, chunk):
            values = passage_here[here, at : at + chunk].astype(F32)
            embed_ref[here, at : at + chunk] = (values * inverse).astype(BF16)
        inverses.append(inverse)
    inverse = jnp.concatenate(inverses, axis=0)
    side_ref[...] = jnp.where(iota(side_ref.shape, 1) == 0, inverse, home)
    row_ref[...] = jnp.broadcast_to(inverse, (rows, rows)).T[: row_ref.shape[0]]
    copies[1].wait()
    pl.when(me % 2 == 0)(own_down.wait)
    pl.when(me % 2 == 1)(own_up.wait)
    for f in range(adapter_ref.shape[0]):
        adapter_ref[f] = adapter_here[...]


def stack_kernel(*refs):
    out_ref = refs[-1]
    rows = refs[0].shape[0]
    for i, ref in enumerate(refs[:-1]):
        out_ref[i * rows : (i + 1) * rows, :] = ref[...]


def stack(*parts):
    rows, cols = parts[0].shape
    return run(stack_kernel, (shape_of((len(parts) * rows, cols), parts[0].dtype),), parts, 1)[0]


def rank_kernel(
    shards,
    near_ref,
    far_ref,
    query_ref,
    query_in_ref,
    passage_in_ref,
    embed_ref,
    row_ref,
    weights_ref,
    passage_low_ref,
    query_low_ref,
    own_ref,
    slot_base_ref,
):
    part = near_ref.shape[1]
    rank = near_ref.shape[0] // shards
    q_dev, width = query_ref.shape
    queries = own_ref.shape[1]
    core = lax.axis_index("dp") % 2

    def place_halves(first_ref, second_ref):
        for k in range(shards):
            cols = slice(k * part, (k + 1) * part)
            weights_ref[:rank, cols] = first_ref[k * rank : (k + 1) * rank, :]
            weights_ref[rank:, cols] = second_ref[k * rank : (k + 1) * rank, :]

    pl.when(core == 0)(functools.partial(place_halves, near_ref, far_ref))
    pl.when(core == 1)(functools.partial(place_halves, far_ref, near_ref))
    down, up = weights_ref[:rank, :], weights_ref[rank:, :]
    place = iota((q_dev, queries), 1) == iota((q_dev, queries), 0) + lax.axis_index("dp") * q_dev
    inverse = inverse_length(query_ref, width)
    own = jnp.sum(jnp.where(place, inverse, 0.0), axis=0, keepdims=True)
    own_ref[...] = jnp.broadcast_to(own, own_ref.shape)
    same = iota((q_dev, q_dev), 0) == iota((q_dev, q_dev), 1)
    inverse_row = jnp.sum(jnp.where(same, inverse, 0.0), axis=0, keepdims=True)
    query_low = dot_nt(down, query_in_ref[...]).astype(BF16)
    query_low_ref[...] = query_low.astype(F32) * inverse_row
    passage_low = dot_nt(down, passage_in_ref[...]).astype(BF16)
    passage_low_ref[...] = passage_low.astype(F32) * row_ref[0:1, :]
    slot_base_ref[...] = dot_nt(up, embed_ref[...])


def score_kernel(group, *refs):
    blocks = refs[:group]
    embed_ref, side_ref, positive_ref, query_low_ref, base_ref = refs[group : group + 5]
    query_ref, weight_ref, dots_ref, onehot_ref, message_ref, coded_ref = refs[group + 5 :]
    rows, width = embed_ref.shape
    queries = query_ref.shape[0]
    q_dev = queries // group
    negatives = (blocks[0].shape[1] - width) // 2
    slots = group * CAP
    rank = query_low_ref.shape[0]
    me = lax.axis_index("dp")
    chunk = min(width, 1024)
    for k in range(group):
        start = pl.multiple_of((me ^ k) * q_dev, q_dev)
        inverse = inverse_length(blocks[k], width)
        for at in range(0, width, chunk):
            part = blocks[k][:, at : at + chunk].astype(F32)
            query_ref[pl.ds(start, q_dev), at : at + chunk] = (part * inverse).astype(BF16)
        coded = blocks[k][:, width:].astype(F32)
        coded_ref[pl.ds(start, q_dev), :] = coded
    dots = dot_nt(embed_ref[...], query_ref[...])
    dots_ref[...] = dots
    scores = dots / SOFTMAX_HEAT

    coded = coded_ref[...].T
    ids = coded[:negatives] * float(ID_BASE) + coded[negatives:]
    home = jnp.broadcast_to(side_ref[:, 1:2], (rows, queries))
    count = jnp.zeros((rows, queries), F32)
    for j in range(negatives):
        count = count + jnp.where(ids[j : j + 1, :] == home, 1.0, 0.0)
    members = iota((slots, queries), 0) // CAP == iota((slots, queries), 1) // q_dev
    marked = dot_nt(members.astype(BF16), count.astype(BF16)) > 0.0
    before = (iota((rows, rows), 0) <= iota((rows, rows), 1)).astype(BF16)
    rank_in = dot_nn(marked.astype(F32).astype(BF16), before)
    wanted = (iota((slots, rows), 0) % CAP + 1).astype(F32)
    onehot = jnp.where(marked & (rank_in == wanted), 1.0, 0.0)
    onehot_ref[...] = onehot

    own = iota((rows, queries), 1) // q_dev == me
    count = count + jnp.where(own & (positive_ref[...] == iota((rows, queries), 0)), 1.0, 0.0)
    named = count > 0.0
    top = jnp.max(jnp.where(named, scores, LOWEST), axis=0, keepdims=True)
    weight = count * jnp.exp(jnp.where(named, scores - top, LOWEST))
    weight_ref[...] = weight
    total = jnp.sum(weight, axis=0, keepdims=True)
    dot_total = jnp.sum(weight * dots, axis=0, keepdims=True)
    slot_weight = dot_nn(onehot, weight, precision=HIGHEST)
    slot_base = dot_nt(base_ref[...], onehot, precision=HIGHEST)
    tail_row = iota((HEAD_ROWS - CAP, queries), 0)
    tail = jnp.where(tail_row == 0, top, jnp.where(tail_row == 1, total, dot_total))
    lane_group = iota((CAP, queries), 1) // q_dev
    compact = jnp.zeros((CAP, queries), F32)
    for peer in range(group):
        part = slot_weight[peer * CAP : (peer + 1) * CAP]
        compact = jnp.where(lane_group == peer, part, compact)
    message_ref[:CAP, :] = compact
    message_ref[CAP:HEAD_ROWS, :] = tail
    message_ref[HEAD_ROWS:, :slots] = slot_base
    message_ref[HEAD_ROWS:, slots : slots + q_dev] = query_low_ref[...]


def back_kernel(query_ref, weights_ref, back_ref):
    back_ref[...] = dot_nt(weights_ref[weights_ref.shape[0] // 2 :, :], query_ref[...])


def request_kernel(first, embed_ref, onehot_ref, *blocks):
    width = embed_ref.shape[1]
    me = lax.axis_index("dp")
    onehot = [
        onehot_ref[pl.ds(pl.multiple_of((me ^ k) * CAP, CAP), CAP), :]
        for k in range(2 * first, 2 * (first + len(blocks)))
    ]
    onehot = jnp.concatenate(onehot, axis=0).astype(BF16)
    chunk = min(width, 1024)
    for at in range(0, width, chunk):
        part = dot_nn(onehot, embed_ref[:, at : at + chunk]).astype(BF16)
        for i, block in enumerate(blocks):
            block[:, at : at + chunk] = part[2 * i * CAP : 2 * (i + 1) * CAP]


def request(first, count, embed, onehot):
    width = embed.shape[1]
    return run(
        functools.partial(request_kernel, first),
        (shape_of((2 * CAP, width), BF16),) * count,
        (embed, onehot),
        2 * embed.size * 2 * CAP * count,
    )


def forward_kernel(*refs):
    out_ref = refs[-1]
    for i, ref in enumerate(refs[:-1]):
        out_ref[i * CAP : (i + 1) * CAP, :] = ref[CAP:, :]


def message_parts(near_ref, far_ref, group):
    rows = near_ref.shape[0] // (group // 2)
    return [((near_ref, far_ref)[k % 2], k // 2 * rows) for k in range(group)]


def combine(parts):
    tops = [ref[at + TOP_ROW : at + TOP_ROW + 1, :] for ref, at in parts]
    sums = [ref[at + SUM_ROW : at + SUM_ROW + 1, :] for ref, at in parts]
    top = functools.reduce(jnp.maximum, tops)
    scales = [jnp.exp(t - top) for t in tops]
    inverse_total = 1.0 / sum(t * s for t, s in zip(scales, sums))
    return [scale * inverse_total for scale in scales]


def own_target(positive_ref, rows, queries, q_dev, me):
    own = iota((rows, queries), 1) // q_dev == me
    return jnp.where(own & (positive_ref[...] == iota((rows, queries), 0)), 1.0, 0.0)


def terms_kernel(group, shards, near_ref, far_ref, *refs):
    parts = message_parts(near_ref, far_ref, group)
    (
        weight_ref,
        dots_ref,
        positive_ref,
        query_ref,
        embed_ref,
        back_query_ref,
        back_passage_ref,
        passage_low_ref,
        row_ref,
        own_ref,
        passage_in_ref,
        query_in_ref,
    ) = refs[:12]
    final_ref = refs[12]
    blocks = refs[13 : 13 + shards]
    (sum_ref,) = refs[13 + shards :]
    rows, queries = weight_ref.shape
    q_dev = queries // group
    rank = passage_low_ref.shape[0]
    width = query_ref.shape[1]
    me = lax.axis_index("dp")

    scales = combine(parts)
    target = own_target(positive_ref, rows, queries, q_dev, me)
    weight = (weight_ref[...] * scales[0] - target) / SOFTMAX_HEAT
    final_ref[...] = weight
    dots = dots_ref[...]
    weighted = weight * dots
    share = jnp.sum(weighted, axis=0, keepdims=True)
    ones = jnp.ones((8, queries), F32)
    inner = dot_nt(ones, weighted, precision=HIGHEST)[0:1, :]

    inner_query = -jnp.sum(target * dots, axis=0, keepdims=True)
    slots = group * CAP
    bases, query_low = [], []
    for (ref, at), scale in zip(parts, scales):
        inner_query = inner_query + scale * ref[at + DOT_ROW : at + DOT_ROW + 1, :]
        bases.append(ref[at + HEAD_ROWS : at + HEAD_ROWS + rank, :slots])
        query_low.append(ref[at + HEAD_ROWS : at + HEAD_ROWS + rank, slots : slots + q_dev])
    sent_by = me ^ (iota((queries, queries), 0) // q_dev)
    place = iota((queries, queries), 1) == sent_by * q_dev + iota((queries, queries), 0) % q_dev
    query_low = dot_nn(
        jnp.concatenate(query_low, axis=1), place.astype(F32), precision=HIGHEST
    )
    pick_slots = (iota((slots, CAP), 0) == iota((slots, CAP), 1) + me * CAP).astype(F32)
    bases = dot_nn(jnp.concatenate(bases[1:], axis=0), pick_slots, precision=HIGHEST)
    far_base = [bases[k * rank : (k + 1) * rank] for k in range(group - 1)]
    far_weight = [
        ref[at : at + CAP, :] * (scale / SOFTMAX_HEAT)
        for (ref, at), scale in zip(parts[1:], scales[1:])
    ]
    inner_query = inner_query / SOFTMAX_HEAT

    passage_low = passage_low_ref[...]
    from_query = dot_nn(passage_low, weight, precision=HIGHEST) - query_low * share
    from_passage = dot_nt(query_low, weight, precision=HIGHEST) - passage_low * inner
    query_parts = jnp.concatenate(split_two(from_query), axis=0)
    passage_parts = jnp.concatenate(split_two(from_passage), axis=0)

    back_passage = dot_nt(back_query_ref[...], weight, precision=HIGHEST)
    back_passage = (back_passage - back_passage_ref[...] * inner) * row_ref[0:1, :]
    back_passage = back_passage.astype(BF16)
    back_query = dot_nn(back_passage_ref[...], weight, precision=HIGHEST)
    back_query = back_query + dot_nn(
        jnp.concatenate(far_base, axis=1),
        jnp.concatenate(far_weight, axis=0),
        precision=HIGHEST,
    )
    back_query = (back_query - back_query_ref[...] * inner_query) * own_ref[0:1, :]
    pick = (iota((q_dev, queries), 1) == iota((q_dev, queries), 0) + me * q_dev).astype(BF16)
    back_query = dot_nt(back_query.astype(BF16), pick).astype(BF16)

    chunk = min(width, 512)
    for at in range(0, width, chunk):
        cols = slice(at, at + chunk)
        both = dot_nn(query_parts, query_ref[:, cols]) + dot_nn(passage_parts, embed_ref[:, cols])
        sum_ref[rank:, cols] = ADAPTER_SCALE * (both[:rank] + both[rank:])
        sum_ref[:rank, cols] = ADAPTER_SCALE * (
            dot_nn(back_passage, passage_in_ref[:, cols])
            + dot_nn(back_query, query_in_ref[:, cols])
        )
    part = width // shards
    home = lax.axis_index("fsdp")
    for k in range(shards):
        start = pl.multiple_of((home ^ k) * part, part)
        blocks[k][...] = sum_ref[:, pl.ds(start, part)].astype(blocks[k].dtype)


def backward(upstream_of, raw_ref, inverse, grad_ref, up_ref):
    rows, width = raw_ref.shape
    chunk = min(width, 512)
    inner = jnp.zeros((rows, 1), F32)
    for at in range(0, width, chunk):
        upstream = upstream_of(at, chunk)
        up_ref[:, at : at + chunk] = upstream
        unit = raw_ref[:, at : at + chunk].astype(F32) * inverse
        inner = inner + jnp.sum(unit * upstream, axis=-1, keepdims=True)
    for at in range(0, width, chunk):
        unit = raw_ref[:, at : at + chunk].astype(F32) * inverse
        grad = (up_ref[:, at : at + chunk] - unit * inner) * inverse
        grad_ref[:, at : at + chunk] = grad.astype(BF16)


def passage_kernel(final_ref, query_ref, raw_ref, side_ref, grad_ref, up_ref):
    high, low = split_two(final_ref[...])

    def upstream_of(at, chunk):
        embed = query_ref[:, at : at + chunk]
        return dot_nn(high, embed) + dot_nn(low, embed)

    backward(upstream_of, raw_ref, side_ref[:, 0:1], grad_ref, up_ref)


def query_kernel(group, near_ref, far_ref, *refs):
    parts = message_parts(near_ref, far_ref, group)
    near = refs[: group // 2 - 1]
    forwarded_ref, final_ref, embed_ref, raw_ref, grad_ref, up_ref = refs[group // 2 - 1 :]
    q_dev, width = raw_ref.shape
    queries = final_ref.shape[1]
    me = lax.axis_index("dp")
    scales = combine(parts)
    pick = (iota((q_dev, queries), 1) == iota((q_dev, queries), 0) + me * q_dev).astype(F32)
    far = [
        ref[at : at + CAP, :] * (scale / SOFTMAX_HEAT) for (ref, at), scale in zip(parts, scales)
    ]
    far = far[2::2] + far[1::2] + [jnp.zeros((CAP, queries), F32)]
    own_parts = split_two(dot_nt(pick, final_ref[...], precision=HIGHEST))
    far_parts = split_two(dot_nt(pick, jnp.concatenate(far, axis=0), precision=HIGHEST))
    own_parts = jnp.concatenate(own_parts, axis=0)
    far_parts = jnp.concatenate(far_parts, axis=0)

    def upstream_of(at, chunk):
        rows = [ref[:, at : at + chunk].astype(F32)[:CAP] for ref in near]
        rows.append(forwarded_ref[:, at : at + chunk].astype(F32))
        rows.append(jnp.zeros((CAP, chunk), F32))
        both = dot_nn(own_parts, embed_ref[:, at : at + chunk])
        both = both + dot_nn(far_parts, jnp.concatenate(rows, axis=0).astype(BF16))
        return both[:q_dev] + both[q_dev:]

    backward(upstream_of, raw_ref, inverse_length(raw_ref, width), grad_ref, up_ref)


def sum_kernel(*refs):
    total = refs[0][...].astype(F32)
    for ref in refs[1:-1]:
        total = total + ref[...].astype(F32)
    refs[-1][...] = total


def sum_two_kernel(left_ref, right_ref, sent_ref):
    sent_ref[...] = (left_ref[...] + right_ref[...]).astype(BF16)


def sum_split_kernel(*refs):
    terms = [ref[...].astype(F32) for ref in refs[:-2]]
    while len(terms) > 1:
        terms = [a + b for a, b in zip(terms[::2], terms[1::2])]
    rank = refs[-1].shape[0]
    refs[-2][...] = terms[0][:rank]
    refs[-1][...] = terms[0][rank:]


def exchange(values, axis, k):
    size = lax.axis_size(axis)
    return lax.ppermute(values, axis, [(i, i ^ k) for i in range(size)])


def per_device(
    query_pooled_states,
    passage_pooled_states,
    query_attention_output,
    passage_attention_output,
    positive_passage_row,
    hard_negative_ids,
    passage_home_row,
    adapter_down_weight,
    adapter_up_weight,
):
    group = lax.axis_size("dp")
    shards = lax.axis_size("fsdp")
    query_raw = query_pooled_states[0]
    passage_raw = passage_pooled_states[0]
    query_in = query_attention_output[0]
    passage_in = passage_attention_output[0]
    ids = hard_negative_ids[0]
    q_dev, width = query_raw.shape
    p_dev = passage_raw.shape[0]
    rank, part = adapter_down_weight.shape
    queries = group * q_dev
    slots = group * CAP
    work = 2 * p_dev * width

    packed, adapter, embed, side, side_row, positive_row = run(
        front_kernel,
        (
            shape_of((q_dev, width + 2 * ids.shape[1]), BF16),
            shape_of((shards, rank, part), BF16),
            shape_of((p_dev, width), BF16),
            shape_of((p_dev, 128), F32),
            shape_of((8, p_dev), F32),
            shape_of((1, queries), jnp.int32),
        ),
        (
            query_raw,
            ids,
            adapter_down_weight,
            adapter_up_weight,
            passage_raw,
            passage_home_row,
            positive_passage_row,
        ),
        work,
        [
            pltpu.VMEM(ids.shape, jnp.int32),
            pltpu.VMEM(passage_raw.shape, BF16),
            pltpu.VMEM(passage_home_row.shape, jnp.int32),
            pltpu.VMEM(positive_passage_row.shape, jnp.int32),
            pltpu.VMEM((rank, part), BF16),
            pltpu.SemaphoreType.DMA((5 + PASSAGE_CHUNKS,)),
        ],
        in_hbm=True,
    )
    blocks = {0: packed}
    for k in range(2, group, 2):
        blocks[k] = exchange(packed, "dp", k)
    adapter = lax.all_to_all(adapter, "fsdp", split_axis=0, concat_axis=0, tiled=True)
    adapter_near = adapter.reshape(shards * rank, part)
    for k in range(0, group, 2):
        adapter_near, blocks[k] = lax.optimization_barrier((adapter_near, blocks[k]))
    adapter_far = exchange(adapter_near, "dp", 1)
    for k in range(0, group, 2):
        blocks[k ^ 1] = exchange(blocks[k], "dp", 1)
    adapter_full, passage_low, query_low, own_side, slot_base = run(
        functools.partial(rank_kernel, shards),
        (
            shape_of((2 * rank, width), BF16),
            shape_of((rank, p_dev), F32),
            shape_of((rank, q_dev), F32),
            shape_of((8, queries), F32),
            shape_of((rank, p_dev), F32),
        ),
        (adapter_near, adapter_far, query_raw, query_in, passage_in, embed, side_row),
        work * rank,
    )
    query_embed, weight, dots, onehot, message = run(
        functools.partial(score_kernel, group),
        (
            shape_of((queries, width), BF16),
            shape_of((p_dev, queries), F32),
            shape_of((p_dev, queries), F32),
            shape_of((slots, p_dev), F32),
            shape_of((HEAD_ROWS + rank, queries), F32),
        ),
        (
            *[blocks[k] for k in range(group)],
            embed,
            side,
            positive_row,
            query_low,
            slot_base,
        ),
        work * queries,
        [pltpu.VMEM((queries, 2 * ids.shape[1]), F32)],
    )
    back_query = run(
        back_kernel,
        (shape_of((rank, queries), F32),),
        (query_embed, adapter_full),
        work * rank,
    )[0]
    stats = [message] + [exchange(message, "dp", k) for k in range(2, group, 2)]
    chips = group // 2
    row_blocks = request(0, chips, embed, onehot)
    stats, row_blocks = lax.optimization_barrier((stats, row_blocks))
    near = [exchange(row_blocks[i], "dp", 2 * i) for i in range(1, chips)]
    near_stats = stack(*stats)
    far_stats = exchange(near_stats, "dp", 1)
    final, *terms = run(
        functools.partial(terms_kernel, group, shards),
        (
            shape_of((p_dev, queries), F32),
            shape_of((2 * rank, part), F32),
            *[shape_of((2 * rank, part), BF16)] * (shards - 1),
        ),
        (
            near_stats,
            far_stats,
            weight,
            dots,
            positive_row,
            query_embed,
            embed,
            back_query,
            slot_base,
            passage_low,
            side_row,
            own_side,
            passage_in,
            query_in,
        ),
        work * rank * 4,
        [pltpu.VMEM((2 * rank, width), F32)],
    )
    arrived = [exchange(terms[k], "fsdp", k) for k in range(1, shards)]
    final, near[0] = lax.optimization_barrier((final, near[0]))
    grad_passage = run(
        passage_kernel,
        (shape_of((p_dev, width), BF16),),
        (final, query_embed, passage_raw, side),
        2 * work * queries,
        [pltpu.VMEM((p_dev, width), F32)],
    )[0]
    terms[0], grad_passage = lax.optimization_barrier((terms[0], grad_passage))
    total = run(sum_kernel, (shape_of((2 * rank, part), F32),), (terms[0], *arrived), 1)[0]
    total, near = lax.optimization_barrier((total, near))
    to_sibling = run(
        forward_kernel,
        (shape_of((group // 2 * CAP, width), BF16),),
        (row_blocks[0], *near),
        1,
    )[0]
    forwarded = exchange(to_sibling, "dp", 1)
    sent = run(
        sum_two_kernel,
        (shape_of((2 * rank, part), BF16),),
        (total, exchange(total, "dp", 1)),
        1,
    )[0]
    arrived = [exchange(sent, "dp", k) for k in range(2, group, 2)]
    grad_query = run(
        functools.partial(query_kernel, group),
        (shape_of((q_dev, width), BF16),),
        (near_stats, far_stats, *near, forwarded, final, embed, query_raw),
        4 * q_dev * width * (p_dev + slots),
        [pltpu.VMEM((q_dev, width), F32)],
    )[0]
    sent, grad_query = lax.optimization_barrier((sent, grad_query))
    down_total, up_total = run(
        sum_split_kernel, (shape_of((rank, part), F32),) * 2, (sent, *arrived), 1
    )
    return (grad_query[None], grad_passage[None], down_total, up_total)


def solution(mesh):
    in_specs = (
        P("fsdp", "dp", None),
        P("fsdp", "dp", None),
        P("fsdp", "dp", None),
        P("fsdp", "dp", None),
        P("fsdp", "dp"),
        P("fsdp", "dp", None),
        P("fsdp", None),
        P(None, "fsdp"),
        P(None, "fsdp"),
    )
    out_specs = (P("fsdp", "dp", None), P("fsdp", "dp", None), P(None, "fsdp"), P(None, "fsdp"))
    return jax.shard_map(
        per_device, mesh=mesh, in_specs=in_specs, out_specs=out_specs, check_vma=False
    )
```

```python
import functools

import jax
import jax.numpy as jnp
from jax import lax
from jax.experimental import pallas as pl
from jax.experimental.pallas import tpu as pltpu
from jax.sharding import PartitionSpec as P

CAP = 8
SOFTMAX_HEAT = 0.01
ADAPTER_SCALE = 2.0
EPSILON = 1e-06
LOWEST = -1e30
ID_BASE = 256
TOP_ROW, SUM_ROW, DOT_ROW, HEAD_ROWS = 8, 9, 10, 16
VMEM_BYTES = 16 * 1024 * 1024
PASSAGE_CHUNKS = 4
F32 = jnp.float32
BF16 = jnp.bfloat16


def dot_nn(a, b, precision=None):
    return lax.dot_general(
        a, b, (((1,), (0,)), ((), ())), precision=precision, preferred_element_type=F32
    )


def dot_nt(a, b, precision=None):
    return lax.dot_general(
        a, b, (((1,), (1,)), ((), ())), precision=precision, preferred_element_type=F32
    )


def split_two(values):
    high = values.astype(BF16)
    low = (values - high.astype(F32)).astype(BF16)
    return high, low


def dot_pieces(dot, a, b):
    rows = a.shape[0]
    a_high, a_low = split_two(a)
    b_high, b_low = split_two(b)
    both = dot(jnp.concatenate([a_high, a_low], axis=0), b_high)
    return both[:rows] + both[rows:] + dot(a_high, b_low)


def iota(shape, dim):
    return lax.broadcasted_iota(jnp.int32, shape, dim)


def shape_of(dims, kind):
    return jax.ShapeDtypeStruct(dims, kind)


def run(body, out_shape, args, flops, scratch=(), in_hbm=False):
    grant = VMEM_BYTES * max(1, size_ratio(args))
    if in_hbm:
        args = [pltpu.with_memory_space_constraint(a, pltpu.HBM) for a in args]
    vmem = pl.BlockSpec(memory_space=pltpu.VMEM)
    hbm = pl.BlockSpec(memory_space=pltpu.HBM)
    moved = sum(a.size * a.dtype.itemsize for a in (*args, *out_shape))
    return pl.pallas_call(
        body,
        out_shape=out_shape,
        in_specs=[hbm if in_hbm else vmem] * len(args),
        out_specs=tuple(vmem for _ in out_shape),
        scratch_shapes=list(scratch),
        compiler_params=pltpu.CompilerParams(vmem_limit_bytes=grant),
        cost_estimate=pl.CostEstimate(flops=flops, bytes_accessed=moved, transcendentals=0),
    )(*args)


def size_ratio(args):
    moved = sum(a.size * a.dtype.itemsize for a in args)
    return -(-moved * 3 // VMEM_BYTES)


def inverse_length(raw_ref, width):
    chunk = min(width, 512)
    total = jnp.zeros((raw_ref.shape[0], 1), F32)
    for at in range(0, width, chunk):
        part = raw_ref[:, at : at + chunk].astype(F32)
        total = total + jnp.sum(part * part, axis=-1, keepdims=True)
    return 1.0 / jnp.sqrt(total + EPSILON)


def front_kernel(
    query_ref,
    ids_ref,
    down_ref,
    up_ref,
    passage_ref,
    home_ref,
    positive_ref,
    out_ref,
    adapter_ref,
    half_ref,
    embed_ref,
    side_ref,
    row_ref,
    tiled_ref,
    ids_here,
    passage_here,
    home_here,
    positive_here,
    sems,
):
    rows, width = passage_ref.shape
    total = home_ref.shape[1]
    me = lax.axis_index("dp")
    part = rows // PASSAGE_CHUNKS
    copies = [
        pltpu.make_async_copy(ids_ref, ids_here, sems.at[0]),
        pltpu.make_async_copy(query_ref, out_ref.at[:, pl.ds(0, width)], sems.at[1]),
        pltpu.make_async_copy(home_ref, home_here, sems.at[2]),
        pltpu.make_async_copy(positive_ref, positive_here, sems.at[3]),
    ]
    for copy in copies:
        copy.start()
    rank = down_ref.shape[0]
    own_down = pltpu.make_async_copy(down_ref, adapter_ref.at[pl.ds(0, rank), :], sems.at[4])
    own_up = pltpu.make_async_copy(up_ref, adapter_ref.at[pl.ds(rank, rank), :], sems.at[5])
    own_down.start()
    own_up.start()
    passage_copies = []
    for c in range(PASSAGE_CHUNKS):
        here = pl.ds(c * part, part)
        passage_copies.append(
            pltpu.make_async_copy(
                passage_ref.at[here, :], passage_here.at[here, :], sems.at[6 + c]
            )
        )
        passage_copies[c].start()

    copies[0].wait()
    ids = ids_here[...]
    coded = jnp.concatenate([ids // ID_BASE, ids % ID_BASE], axis=1)
    out_ref[:, width:] = coded.astype(F32).astype(BF16)
    copies[2].wait()
    row_id = iota((rows, total), 0) + me * rows
    number = iota((rows, total), 1)
    home = jnp.where(home_here[...] == row_id, number, 0).astype(F32)
    home = jnp.sum(home, axis=1, keepdims=True)
    copies[3].wait()
    q_dev = positive_here.shape[1]
    for at in range(0, tiled_ref.shape[1], q_dev):
        tiled_ref[:, at : at + q_dev] = positive_here[...]

    chunk = min(width, 512)
    inverses = []
    for c in range(PASSAGE_CHUNKS):
        passage_copies[c].wait()
        here = slice(c * part, (c + 1) * part)
        inverse = inverse_length(passage_here.at[here, :], width)
        for at in range(0, width, chunk):
            values = passage_here[here, at : at + chunk].astype(F32)
            embed_ref[here, at : at + chunk] = (values * inverse).astype(BF16)
        inverses.append(inverse)
    inverse = jnp.concatenate(inverses, axis=0)
    side_ref[...] = jnp.where(iota(side_ref.shape, 1) == 0, inverse, home)
    row_ref[...] = jnp.broadcast_to(inverse, (rows, rows)).T[: row_ref.shape[0]]
    copies[1].wait()
    own_down.wait()
    own_up.wait()

    @pl.when(me % 2 == 0)
    def _():
        half_ref[...] = adapter_ref[:rank, :]

    @pl.when(me % 2 == 1)
    def _():
        half_ref[...] = adapter_ref[rank:, :]


def stack_kernel(*refs):
    out_ref = refs[-1]
    rows = refs[0].shape[0]
    for i, ref in enumerate(refs[:-1]):
        out_ref[i * rows : (i + 1) * rows, :] = ref[...]


def stack(*parts):
    rows, cols = parts[0].shape
    return run(stack_kernel, (shape_of((len(parts) * rows, cols), parts[0].dtype),), parts, 1)[0]


def join_kernel(first_ref, second_ref, out_ref):
    rows = first_ref.shape[0]
    out_ref[:rows, :] = first_ref[...]
    out_ref[rows:, :] = second_ref[...]


def place_paired(own_ref, near_ref, far_ref, weights_ref):
    rank, part = own_ref.shape[0] // 2, own_ref.shape[1]
    me = lax.axis_index("fsdp")
    core = lax.axis_index("dp") % 2

    def columns(k):
        return pl.ds(pl.multiple_of((me ^ k) * part, part), part)

    def place(even_ref, odd_ref):
        weights_ref[:, columns(1)] = even_ref[: 2 * rank, :]
        weights_ref[:, columns(2)] = odd_ref[: 2 * rank, :]
        weights_ref[:rank, columns(3)] = even_ref[2 * rank :, :]
        weights_ref[rank:, columns(3)] = odd_ref[2 * rank :, :]

    weights_ref[:, columns(0)] = own_ref[...]
    pl.when(core == 0)(functools.partial(place, near_ref, far_ref))
    pl.when(core == 1)(functools.partial(place, far_ref, near_ref))


def place_blocks(*refs):
    part = refs[0].shape[1]
    me = lax.axis_index("fsdp")
    for k, ref in enumerate(refs[:-1]):
        refs[-1][:, pl.ds(pl.multiple_of((me ^ k) * part, part), part)] = ref[...]


def rank_kernel(shards, *refs):
    blocks = refs[:-10]
    query_ref, query_in_ref, passage_in_ref, embed_ref, row_ref = refs[-10:-5]
    weights_ref, passage_low_ref, query_low_ref, own_ref, slot_base_ref = refs[-5:]
    rank = blocks[0].shape[0] // 2
    q_dev, width = query_ref.shape
    queries = own_ref.shape[1]
    place = place_paired if shards == 4 else place_blocks
    place(*blocks, weights_ref)
    down, up = weights_ref[:rank, :], weights_ref[rank:, :]
    start = lax.axis_index("dp") * q_dev
    place = iota((q_dev, queries), 1) == iota((q_dev, queries), 0) + start
    inverse = inverse_length(query_ref, width)
    own = jnp.sum(jnp.where(place, inverse, 0.0), axis=0, keepdims=True)
    own_ref[...] = jnp.broadcast_to(own, own_ref.shape)
    same = iota((q_dev, q_dev), 0) == iota((q_dev, q_dev), 1)
    inverse_row = jnp.sum(jnp.where(same, inverse, 0.0), axis=0, keepdims=True)
    query_low = dot_nt(down, query_in_ref[...]).astype(BF16)
    query_low_ref[...] = query_low.astype(F32) * inverse_row
    passage_low = dot_nt(down, passage_in_ref[...]).astype(BF16)
    passage_low_ref[...] = passage_low.astype(F32) * row_ref[0:1, :]
    slot_base_ref[...] = dot_nt(up, embed_ref[...])


def score_kernel(group, *refs):
    blocks = refs[:group]
    embed_ref, side_ref, positive_ref, query_low_ref, base_ref = refs[group : group + 5]
    query_ref, weight_ref, dots_ref, onehot_ref, message_ref, coded_ref = refs[group + 5 :]
    rows, width = embed_ref.shape
    queries = query_ref.shape[0]
    q_dev = queries // group
    negatives = (blocks[0].shape[1] - width) // 2
    slots = group * CAP
    rank = query_low_ref.shape[0]
    me = lax.axis_index("dp")
    chunk = min(width, 1024)
    for k in range(group):
        start = pl.multiple_of((me ^ k) * q_dev, q_dev)
        inverse = inverse_length(blocks[k], width)
        for at in range(0, width, chunk):
            part = blocks[k][:, at : at + chunk].astype(F32)
            query_ref[pl.ds(start, q_dev), at : at + chunk] = (part * inverse).astype(BF16)
        coded = blocks[k][:, width:].astype(F32)
        coded_ref[pl.ds(start, q_dev), :] = coded
    dots = dot_nt(embed_ref[...], query_ref[...])
    dots_ref[...] = dots
    scores = dots / SOFTMAX_HEAT

    coded = coded_ref[...].T
    ids = coded[:negatives] * float(ID_BASE) + coded[negatives:]
    home = jnp.broadcast_to(side_ref[:, 1:2], (rows, queries))
    count = jnp.zeros((rows, queries), F32)
    for j in range(negatives):
        count = count + jnp.where(ids[j : j + 1, :] == home, 1.0, 0.0)
    members = iota((slots, queries), 0) // CAP == iota((slots, queries), 1) // q_dev
    marked = dot_nt(members.astype(BF16), count.astype(BF16)) > 0.0
    before = (iota((rows, rows), 0) <= iota((rows, rows), 1)).astype(BF16)
    rank_in = dot_nn(marked.astype(F32).astype(BF16), before)
    wanted = (iota((slots, rows), 0) % CAP + 1).astype(F32)
    onehot = jnp.where(marked & (rank_in == wanted), 1.0, 0.0)
    onehot_ref[...] = onehot

    own = iota((rows, queries), 1) // q_dev == me
    count = count + jnp.where(own & (positive_ref[...] == iota((rows, queries), 0)), 1.0, 0.0)
    named = count > 0.0
    top = jnp.max(jnp.where(named, scores, LOWEST), axis=0, keepdims=True)
    weight = count * jnp.exp(jnp.where(named, scores - top, LOWEST))
    weight_ref[...] = weight
    total = jnp.sum(weight, axis=0, keepdims=True)
    dot_total = jnp.sum(weight * dots, axis=0, keepdims=True)
    slot_weight = dot_pieces(dot_nn, onehot, weight)
    slot_base = dot_pieces(dot_nt, base_ref[...], onehot)
    tail_row = iota((HEAD_ROWS - CAP, queries), 0)
    tail = jnp.where(tail_row == 0, top, jnp.where(tail_row == 1, total, dot_total))
    lane_group = iota((CAP, queries), 1) // q_dev
    compact = jnp.zeros((CAP, queries), F32)
    for peer in range(group):
        part = slot_weight[peer * CAP : (peer + 1) * CAP]
        compact = jnp.where(lane_group == peer, part, compact)
    message_ref[:CAP, :] = compact
    message_ref[CAP:HEAD_ROWS, :] = tail
    message_ref[HEAD_ROWS:, :slots] = slot_base
    message_ref[HEAD_ROWS:, slots : slots + q_dev] = query_low_ref[...]


def back_kernel(query_ref, weights_ref, back_ref):
    back_ref[...] = dot_nt(weights_ref[weights_ref.shape[0] // 2 :, :], query_ref[...])


def request_kernel(first, embed_ref, onehot_ref, *blocks):
    width = embed_ref.shape[1]
    me = lax.axis_index("dp")
    onehot = [
        onehot_ref[pl.ds(pl.multiple_of((me ^ k) * CAP, CAP), CAP), :]
        for k in range(2 * first, 2 * (first + len(blocks)))
    ]
    onehot = jnp.concatenate(onehot, axis=0).astype(BF16)
    chunk = min(width, 1024)
    for at in range(0, width, chunk):
        part = dot_nn(onehot, embed_ref[:, at : at + chunk]).astype(BF16)
        for i, block in enumerate(blocks):
            block[:, at : at + chunk] = part[2 * i * CAP : 2 * (i + 1) * CAP]


def request(first, count, embed, onehot):
    width = embed.shape[1]
    return run(
        functools.partial(request_kernel, first),
        (shape_of((2 * CAP, width), BF16),) * count,
        (embed, onehot),
        2 * embed.size * 2 * CAP * count,
    )


def forward_kernel(*refs):
    out_ref = refs[-1]
    for i, ref in enumerate(refs[:-1]):
        out_ref[i * CAP : (i + 1) * CAP, :] = ref[CAP:, :]


def message_parts(near_ref, far_ref, group):
    rows = near_ref.shape[0] // (group // 2)
    return [((near_ref, far_ref)[k % 2], k // 2 * rows) for k in range(group)]


def combine(parts):
    tops = [ref[at + TOP_ROW : at + TOP_ROW + 1, :] for ref, at in parts]
    sums = [ref[at + SUM_ROW : at + SUM_ROW + 1, :] for ref, at in parts]
    top = functools.reduce(jnp.maximum, tops)
    scales = [jnp.exp(t - top) for t in tops]
    inverse_total = 1.0 / sum(t * s for t, s in zip(scales, sums))
    return [scale * inverse_total for scale in scales]


def own_target(positive_ref, rows, queries, q_dev, me):
    own = iota((rows, queries), 1) // q_dev == me
    return jnp.where(own & (positive_ref[...] == iota((rows, queries), 0)), 1.0, 0.0)


def terms_kernel(group, shards, near_ref, far_ref, *refs):
    parts = message_parts(near_ref, far_ref, group)
    (
        weight_ref,
        dots_ref,
        positive_ref,
        query_ref,
        embed_ref,
        back_query_ref,
        back_passage_ref,
        passage_low_ref,
        row_ref,
        own_ref,
        passage_in_ref,
        query_in_ref,
    ) = refs[:12]
    final_ref = refs[12]
    blocks = refs[13 : 13 + shards]
    (sum_ref,) = refs[13 + shards :]
    rows, queries = weight_ref.shape
    q_dev = queries // group
    rank = passage_low_ref.shape[0]
    width = query_ref.shape[1]
    me = lax.axis_index("dp")

    scales = combine(parts)
    target = own_target(positive_ref, rows, queries, q_dev, me)
    weight = (weight_ref[...] * scales[0] - target) / SOFTMAX_HEAT
    final_ref[...] = weight
    dots = dots_ref[...]
    weighted = weight * dots
    share = jnp.sum(weighted, axis=0, keepdims=True)
    ones = jnp.ones((8, queries), F32)
    inner = dot_pieces(dot_nt, ones, weighted)[0:1, :]

    inner_query = -jnp.sum(target * dots, axis=0, keepdims=True)
    slots = group * CAP
    bases, query_low = [], []
    for (ref, at), scale in zip(parts, scales):
        inner_query = inner_query + scale * ref[at + DOT_ROW : at + DOT_ROW + 1, :]
        bases.append(ref[at + HEAD_ROWS : at + HEAD_ROWS + rank, :slots])
        query_low.append(ref[at + HEAD_ROWS : at + HEAD_ROWS + rank, slots : slots + q_dev])
    sent_by = me ^ (iota((queries, queries), 0) // q_dev)
    place = iota((queries, queries), 1) == sent_by * q_dev + iota((queries, queries), 0) % q_dev
    query_low = dot_pieces(dot_nn, jnp.concatenate(query_low, axis=1), place.astype(F32))
    pick_slots = (iota((slots, CAP), 0) == iota((slots, CAP), 1) + me * CAP).astype(F32)
    bases = dot_pieces(dot_nn, jnp.concatenate(bases[1:], axis=0), pick_slots)
    far_base = [bases[k * rank : (k + 1) * rank] for k in range(group - 1)]
    far_weight = [
        ref[at : at + CAP, :] * (scale / SOFTMAX_HEAT)
        for (ref, at), scale in zip(parts[1:], scales[1:])
    ]
    inner_query = inner_query / SOFTMAX_HEAT

    passage_low = passage_low_ref[...]
    from_query = dot_pieces(dot_nn, passage_low, weight) - query_low * share
    from_passage = dot_pieces(dot_nt, query_low, weight) - passage_low * inner
    query_parts = jnp.concatenate(split_two(from_query), axis=0)
    passage_parts = jnp.concatenate(split_two(from_passage), axis=0)

    back_passage = dot_pieces(dot_nt, back_query_ref[...], weight)
    back_passage = (back_passage - back_passage_ref[...] * inner) * row_ref[0:1, :]
    back_passage = back_passage.astype(BF16)
    back_query = dot_pieces(dot_nn, back_passage_ref[...], weight)
    back_query = back_query + dot_pieces(
        dot_nn, jnp.concatenate(far_base, axis=1), jnp.concatenate(far_weight, axis=0)
    )
    back_query = (back_query - back_query_ref[...] * inner_query) * own_ref[0:1, :]
    pick = (iota((q_dev, queries), 1) == iota((q_dev, queries), 0) + me * q_dev).astype(BF16)
    back_query = dot_nt(back_query.astype(BF16), pick).astype(BF16)

    chunk = min(width, 512)
    for at in range(0, width, chunk):
        cols = slice(at, at + chunk)
        both = dot_nn(query_parts, query_ref[:, cols]) + dot_nn(passage_parts, embed_ref[:, cols])
        sum_ref[rank:, cols] = ADAPTER_SCALE * (both[:rank] + both[rank:])
        sum_ref[:rank, cols] = ADAPTER_SCALE * (
            dot_nn(back_passage, passage_in_ref[:, cols])
            + dot_nn(back_query, query_in_ref[:, cols])
        )
    part = width // shards
    home = lax.axis_index("fsdp")
    for k in range(shards):
        start = pl.multiple_of((home ^ k) * part, part)
        blocks[k][...] = sum_ref[:, pl.ds(start, part)].astype(blocks[k].dtype)


def backward(upstream_of, raw_ref, inverse, grad_ref, up_ref):
    rows, width = raw_ref.shape
    chunk = min(width, 512)
    inner = jnp.zeros((rows, 1), F32)
    for at in range(0, width, chunk):
        upstream = upstream_of(at, chunk)
        up_ref[:, at : at + chunk] = upstream
        unit = raw_ref[:, at : at + chunk].astype(F32) * inverse
        inner = inner + jnp.sum(unit * upstream, axis=-1, keepdims=True)
    for at in range(0, width, chunk):
        unit = raw_ref[:, at : at + chunk].astype(F32) * inverse
        grad = (up_ref[:, at : at + chunk] - unit * inner) * inverse
        grad_ref[:, at : at + chunk] = grad.astype(BF16)


def passage_kernel(final_ref, query_ref, raw_ref, side_ref, grad_ref, up_ref):
    high, low = split_two(final_ref[...])

    def upstream_of(at, chunk):
        embed = query_ref[:, at : at + chunk]
        return dot_nn(high, embed) + dot_nn(low, embed)

    backward(upstream_of, raw_ref, side_ref[:, 0:1], grad_ref, up_ref)


def query_kernel(group, near_ref, far_ref, *refs):
    parts = message_parts(near_ref, far_ref, group)
    near = refs[: group // 2 - 1]
    forwarded_ref, final_ref, embed_ref, raw_ref, grad_ref, up_ref = refs[group // 2 - 1 :]
    q_dev, width = raw_ref.shape
    queries = final_ref.shape[1]
    me = lax.axis_index("dp")
    scales = combine(parts)
    pick = (iota((q_dev, queries), 1) == iota((q_dev, queries), 0) + me * q_dev).astype(F32)
    far = [
        ref[at : at + CAP, :] * (scale / SOFTMAX_HEAT) for (ref, at), scale in zip(parts, scales)
    ]
    far = far[2::2] + far[1::2] + [jnp.zeros((CAP, queries), F32)]
    own_parts = split_two(dot_pieces(dot_nt, pick, final_ref[...]))
    far_parts = split_two(dot_pieces(dot_nt, pick, jnp.concatenate(far, axis=0)))
    own_parts = jnp.concatenate(own_parts, axis=0)
    far_parts = jnp.concatenate(far_parts, axis=0)

    def upstream_of(at, chunk):
        rows = [ref[:, at : at + chunk].astype(F32)[:CAP] for ref in near]
        rows.append(forwarded_ref[:, at : at + chunk].astype(F32))
        rows.append(jnp.zeros((CAP, chunk), F32))
        both = dot_nn(own_parts, embed_ref[:, at : at + chunk])
        both = both + dot_nn(far_parts, jnp.concatenate(rows, axis=0).astype(BF16))
        return both[:q_dev] + both[q_dev:]

    backward(upstream_of, raw_ref, inverse_length(raw_ref, width), grad_ref, up_ref)


def sum_kernel(*refs):
    total = refs[0][...].astype(F32)
    for ref in refs[1:-1]:
        total = total + ref[...].astype(F32)
    refs[-1][...] = total


def sum_two_kernel(left_ref, right_ref, sent_ref):
    sent_ref[...] = (left_ref[...] + right_ref[...]).astype(BF16)


def sum_split_kernel(*refs):
    terms = [ref[...].astype(F32) for ref in refs[:-2]]
    while len(terms) > 1:
        terms = [a + b for a, b in zip(terms[::2], terms[1::2])]
    rank = refs[-1].shape[0]
    refs[-2][...] = terms[0][:rank]
    refs[-1][...] = terms[0][rank:]


def exchange(values, axis, k):
    size = lax.axis_size(axis)
    return lax.ppermute(values, axis, [(i, i ^ k) for i in range(size)])


def core_step(values, even_step, odd_step):
    outer, inner = lax.axis_size("dp"), lax.axis_size("fsdp")
    pairs = []
    for d in range(outer):
        step = odd_step if d % 2 else even_step
        pairs += [(d * inner + f, d * inner + (f ^ step)) for f in range(inner)]
    return lax.ppermute(values, ("dp", "fsdp"), pairs)


def per_device(
    query_pooled_states,
    passage_pooled_states,
    query_attention_output,
    passage_attention_output,
    positive_passage_row,
    hard_negative_ids,
    passage_home_row,
    adapter_down_weight,
    adapter_up_weight,
):
    group = lax.axis_size("dp")
    shards = lax.axis_size("fsdp")
    query_raw = query_pooled_states[0]
    passage_raw = passage_pooled_states[0]
    query_in = query_attention_output[0]
    passage_in = passage_attention_output[0]
    ids = hard_negative_ids[0]
    q_dev, width = query_raw.shape
    p_dev = passage_raw.shape[0]
    rank, part = adapter_down_weight.shape
    queries = group * q_dev
    slots = group * CAP
    work = 2 * p_dev * width

    packed, adapter, half, embed, side, side_row, positive_row = run(
        front_kernel,
        (
            shape_of((q_dev, width + 2 * ids.shape[1]), BF16),
            shape_of((2 * rank, part), BF16),
            shape_of((rank, part), BF16),
            shape_of((p_dev, width), BF16),
            shape_of((p_dev, 128), F32),
            shape_of((8, p_dev), F32),
            shape_of((1, queries), jnp.int32),
        ),
        (
            query_raw,
            ids,
            adapter_down_weight,
            adapter_up_weight,
            passage_raw,
            passage_home_row,
            positive_passage_row,
        ),
        work,
        [
            pltpu.VMEM(ids.shape, jnp.int32),
            pltpu.VMEM(passage_raw.shape, BF16),
            pltpu.VMEM(passage_home_row.shape, jnp.int32),
            pltpu.VMEM(positive_passage_row.shape, jnp.int32),
            pltpu.SemaphoreType.DMA((6 + PASSAGE_CHUNKS,)),
        ],
        in_hbm=True,
    )
    blocks = {0: packed}
    for k in range(2, group, 2):
        blocks[k] = exchange(packed, "dp", k)
    blocks[1] = exchange(packed, "dp", 1)
    for k in range(2, group, 2):
        blocks[k ^ 1] = exchange(blocks[k], "dp", 1)
    if shards == 4:
        whole_block = core_step(adapter, 1, 2)
        half_block = exchange(half, "fsdp", 3)
        adapter_near = run(
            join_kernel,
            (shape_of((3 * rank, part), BF16),),
            (whole_block, half_block),
            1,
        )[0]
        adapter_blocks = [adapter, adapter_near, exchange(adapter_near, "dp", 1)]
    else:
        adapter_blocks = [adapter] + [exchange(adapter, "fsdp", k) for k in range(1, shards)]
    adapter_full, passage_low, query_low, own_side, slot_base = run(
        functools.partial(rank_kernel, shards),
        (
            shape_of((2 * rank, width), BF16),
            shape_of((rank, p_dev), F32),
            shape_of((rank, q_dev), F32),
            shape_of((8, queries), F32),
            shape_of((rank, p_dev), F32),
        ),
        (*adapter_blocks, query_raw, query_in, passage_in, embed, side_row),
        work * rank,
    )
    query_embed, weight, dots, onehot, message = run(
        functools.partial(score_kernel, group),
        (
            shape_of((queries, width), BF16),
            shape_of((p_dev, queries), F32),
            shape_of((p_dev, queries), F32),
            shape_of((slots, p_dev), F32),
            shape_of((HEAD_ROWS + rank, queries), F32),
        ),
        (
            *[blocks[k] for k in range(group)],
            embed,
            side,
            positive_row,
            query_low,
            slot_base,
        ),
        work * queries,
        [pltpu.VMEM((queries, 2 * ids.shape[1]), F32)],
    )
    back_query = run(
        back_kernel,
        (shape_of((rank, queries), F32),),
        (query_embed, adapter_full),
        work * rank,
    )[0]
    stats = [message] + [exchange(message, "dp", k) for k in range(2, group, 2)]
    chips = group // 2
    row_blocks = request(0, chips, embed, onehot)
    stats, row_blocks = lax.optimization_barrier((stats, row_blocks))
    near = [exchange(row_blocks[i], "dp", 2 * i) for i in range(1, chips)]
    near_stats = stack(*stats)
    far_stats = exchange(near_stats, "dp", 1)
    final, *terms = run(
        functools.partial(terms_kernel, group, shards),
        (
            shape_of((p_dev, queries), F32),
            shape_of((2 * rank, part), F32),
            *[shape_of((2 * rank, part), BF16)] * (shards - 1),
        ),
        (
            near_stats,
            far_stats,
            weight,
            dots,
            positive_row,
            query_embed,
            embed,
            back_query,
            slot_base,
            passage_low,
            side_row,
            own_side,
            passage_in,
            query_in,
        ),
        work * rank * 4,
        [pltpu.VMEM((2 * rank, width), F32)],
    )
    arrived = [exchange(terms[k], "fsdp", k) for k in range(1, shards)]
    final, near[0] = lax.optimization_barrier((final, near[0]))
    grad_passage = run(
        passage_kernel,
        (shape_of((p_dev, width), BF16),),
        (final, query_embed, passage_raw, side),
        2 * work * queries,
        [pltpu.VMEM((p_dev, width), F32)],
    )[0]
    terms[0], grad_passage = lax.optimization_barrier((terms[0], grad_passage))
    total = run(sum_kernel, (shape_of((2 * rank, part), F32),), (terms[0], *arrived), 1)[0]
    total, near = lax.optimization_barrier((total, near))
    to_sibling = run(
        forward_kernel,
        (shape_of((group // 2 * CAP, width), BF16),),
        (row_blocks[0], *near),
        1,
    )[0]
    forwarded = exchange(to_sibling, "dp", 1)
    sent = run(
        sum_two_kernel,
        (shape_of((2 * rank, part), BF16),),
        (total, exchange(total, "dp", 1)),
        1,
    )[0]
    arrived = [exchange(sent, "dp", k) for k in range(2, group, 2)]
    grad_query = run(
        functools.partial(query_kernel, group),
        (shape_of((q_dev, width), BF16),),
        (near_stats, far_stats, *near, forwarded, final, embed, query_raw),
        4 * q_dev * width * (p_dev + slots),
        [pltpu.VMEM((q_dev, width), F32)],
    )[0]
    sent, grad_query = lax.optimization_barrier((sent, grad_query))
    down_total, up_total = run(
        sum_split_kernel, (shape_of((rank, part), F32),) * 2, (sent, *arrived), 1
    )
    return (grad_query[None], grad_passage[None], down_total, up_total)


def solution(mesh):
    in_specs = (
        P("fsdp", "dp", None),
        P("fsdp", "dp", None),
        P("fsdp", "dp", None),
        P("fsdp", "dp", None),
        P("fsdp", "dp"),
        P("fsdp", "dp", None),
        P("fsdp", None),
        P(None, "fsdp"),
        P(None, "fsdp"),
    )
    out_specs = (P("fsdp", "dp", None), P("fsdp", "dp", None), P(None, "fsdp"), P(None, "fsdp"))
    return jax.shard_map(
        per_device, mesh=mesh, in_specs=in_specs, out_specs=out_specs, check_vma=False
    )
```

```python
import functools

import jax
import jax.numpy as jnp
from jax import lax
from jax.experimental import pallas as pl
from jax.experimental.pallas import tpu as pltpu
from jax.sharding import PartitionSpec as P

CAP = 8
SOFTMAX_HEAT = 0.01
ADAPTER_SCALE = 2.0
EPSILON = 1e-06
LOWEST = -1e30
ID_BASE = 256
TOP_ROW, SUM_ROW, DOT_ROW, HEAD_ROWS = 8, 9, 10, 16
VMEM_BYTES = 16 * 1024 * 1024
PASSAGE_CHUNKS = 4
F32 = jnp.float32
BF16 = jnp.bfloat16


def dot_nn(a, b, precision=None):
    return lax.dot_general(
        a, b, (((1,), (0,)), ((), ())), precision=precision, preferred_element_type=F32
    )


def dot_nt(a, b, precision=None):
    return lax.dot_general(
        a, b, (((1,), (1,)), ((), ())), precision=precision, preferred_element_type=F32
    )


def split_two(values):
    high = values.astype(BF16)
    low = (values - high.astype(F32)).astype(BF16)
    return high, low


def dot_pieces(dot, a, b):
    rows = a.shape[0]
    a_high, a_low = split_two(a)
    b_high, b_low = split_two(b)
    both = dot(jnp.concatenate([a_high, a_low], axis=0), b_high)
    return both[:rows] + both[rows:] + dot(a_high, b_low)


def iota(shape, dim):
    return lax.broadcasted_iota(jnp.int32, shape, dim)


def shape_of(dims, kind):
    return jax.ShapeDtypeStruct(dims, kind)


def run(body, out_shape, args, flops, scratch=(), in_hbm=False):
    grant = VMEM_BYTES * max(1, size_ratio(args))
    if in_hbm:
        args = [pltpu.with_memory_space_constraint(a, pltpu.HBM) for a in args]
    vmem = pl.BlockSpec(memory_space=pltpu.VMEM)
    hbm = pl.BlockSpec(memory_space=pltpu.HBM)
    moved = sum(a.size * a.dtype.itemsize for a in (*args, *out_shape))
    return pl.pallas_call(
        body,
        out_shape=out_shape,
        in_specs=[hbm if in_hbm else vmem] * len(args),
        out_specs=tuple(vmem for _ in out_shape),
        scratch_shapes=list(scratch),
        compiler_params=pltpu.CompilerParams(vmem_limit_bytes=grant),
        cost_estimate=pl.CostEstimate(flops=flops, bytes_accessed=moved, transcendentals=0),
    )(*args)


def size_ratio(args):
    moved = sum(a.size * a.dtype.itemsize for a in args)
    return -(-moved * 3 // VMEM_BYTES)


def inverse_length(raw_ref, width):
    chunk = min(width, 512)
    total = jnp.zeros((raw_ref.shape[0], 1), F32)
    for at in range(0, width, chunk):
        part = raw_ref[:, at : at + chunk].astype(F32)
        total = total + jnp.sum(part * part, axis=-1, keepdims=True)
    return 1.0 / jnp.sqrt(total + EPSILON)


def front_kernel(
    query_ref,
    ids_ref,
    down_ref,
    up_ref,
    positive_ref,
    out_ref,
    adapter_ref,
    half_ref,
    tiled_ref,
    ids_here,
    positive_here,
    sems,
):
    width = query_ref.shape[1]
    rank = down_ref.shape[0]
    me = lax.axis_index("dp")
    pairs = (
        (ids_ref, ids_here),
        (query_ref, out_ref.at[:, pl.ds(0, width)]),
        (positive_ref, positive_here),
        (down_ref, adapter_ref.at[pl.ds(0, rank), :]),
        (up_ref, adapter_ref.at[pl.ds(rank, rank), :]),
    )
    copies = [pltpu.make_async_copy(a, b, sems.at[i]) for i, (a, b) in enumerate(pairs)]
    for copy in copies:
        copy.start()
    copies[0].wait()
    ids = ids_here[...]
    coded = jnp.concatenate([ids // ID_BASE, ids % ID_BASE], axis=1)
    out_ref[:, width:] = coded.astype(F32).astype(BF16)
    copies[2].wait()
    q_dev = positive_here.shape[1]
    for at in range(0, tiled_ref.shape[1], q_dev):
        tiled_ref[:, at : at + q_dev] = positive_here[...]
    copies[3].wait()
    copies[4].wait()

    @pl.when(me % 2 == 0)
    def _():
        half_ref[...] = adapter_ref[:rank, :]

    @pl.when(me % 2 == 1)
    def _():
        half_ref[...] = adapter_ref[rank:, :]

    copies[1].wait()


def passage_norm_kernel(
    passage_ref, home_ref, embed_ref, side_ref, row_ref, passage_here, home_here, sems
):
    rows, width = passage_ref.shape
    total = home_ref.shape[1]
    me = lax.axis_index("dp")
    part = rows // PASSAGE_CHUNKS
    home_copy = pltpu.make_async_copy(home_ref, home_here, sems.at[0])
    home_copy.start()
    passage_copies = []
    for c in range(PASSAGE_CHUNKS):
        here = pl.ds(c * part, part)
        passage_copies.append(
            pltpu.make_async_copy(
                passage_ref.at[here, :], passage_here.at[here, :], sems.at[1 + c]
            )
        )
        passage_copies[c].start()

    home_copy.wait()
    row_id = iota((rows, total), 0) + me * rows
    number = iota((rows, total), 1)
    home = jnp.where(home_here[...] == row_id, number, 0).astype(F32)
    home = jnp.sum(home, axis=1, keepdims=True)

    chunk = min(width, 512)
    inverses = []
    for c in range(PASSAGE_CHUNKS):
        passage_copies[c].wait()
        here = slice(c * part, (c + 1) * part)
        inverse = inverse_length(passage_here.at[here, :], width)
        for at in range(0, width, chunk):
            values = passage_here[here, at : at + chunk].astype(F32)
            embed_ref[here, at : at + chunk] = (values * inverse).astype(BF16)
        inverses.append(inverse)
    inverse = jnp.concatenate(inverses, axis=0)
    side_ref[...] = jnp.where(iota(side_ref.shape, 1) == 0, inverse, home)
    row_ref[...] = jnp.broadcast_to(inverse, (rows, rows)).T[: row_ref.shape[0]]


def stack_kernel(*refs):
    out_ref = refs[-1]
    rows = refs[0].shape[0]
    for i, ref in enumerate(refs[:-1]):
        out_ref[i * rows : (i + 1) * rows, :] = ref[...]


def stack(*parts):
    rows, cols = parts[0].shape
    return run(stack_kernel, (shape_of((len(parts) * rows, cols), parts[0].dtype),), parts, 1)[0]


def join_kernel(first_ref, second_ref, out_ref):
    rows = first_ref.shape[0]
    out_ref[:rows, :] = first_ref[...]
    out_ref[rows:, :] = second_ref[...]


def place_paired(own_ref, near_ref, far_ref, weights_ref):
    rank, part = own_ref.shape[0] // 2, own_ref.shape[1]
    me = lax.axis_index("fsdp")
    core = lax.axis_index("dp") % 2

    def columns(k):
        return pl.ds(pl.multiple_of((me ^ k) * part, part), part)

    def place(even_ref, odd_ref):
        weights_ref[:, columns(1)] = even_ref[: 2 * rank, :]
        weights_ref[:, columns(2)] = odd_ref[: 2 * rank, :]
        weights_ref[:rank, columns(3)] = even_ref[2 * rank :, :]
        weights_ref[rank:, columns(3)] = odd_ref[2 * rank :, :]

    weights_ref[:, columns(0)] = own_ref[...]
    pl.when(core == 0)(functools.partial(place, near_ref, far_ref))
    pl.when(core == 1)(functools.partial(place, far_ref, near_ref))


def place_blocks(*refs):
    part = refs[0].shape[1]
    me = lax.axis_index("fsdp")
    for k, ref in enumerate(refs[:-1]):
        refs[-1][:, pl.ds(pl.multiple_of((me ^ k) * part, part), part)] = ref[...]


def rank_kernel(shards, *refs):
    blocks = refs[:-10]
    query_ref, query_in_ref, passage_in_ref, embed_ref, row_ref = refs[-10:-5]
    weights_ref, passage_low_ref, query_low_ref, own_ref, slot_base_ref = refs[-5:]
    rank = blocks[0].shape[0] // 2
    q_dev, width = query_ref.shape
    queries = own_ref.shape[1]
    place = place_paired if shards == 4 else place_blocks
    place(*blocks, weights_ref)
    down, up = weights_ref[:rank, :], weights_ref[rank:, :]
    start = lax.axis_index("dp") * q_dev
    place = iota((q_dev, queries), 1) == iota((q_dev, queries), 0) + start
    inverse = inverse_length(query_ref, width)
    own = jnp.sum(jnp.where(place, inverse, 0.0), axis=0, keepdims=True)
    own_ref[...] = jnp.broadcast_to(own, own_ref.shape)
    same = iota((q_dev, q_dev), 0) == iota((q_dev, q_dev), 1)
    inverse_row = jnp.sum(jnp.where(same, inverse, 0.0), axis=0, keepdims=True)
    query_low = dot_nt(down, query_in_ref[...]).astype(BF16)
    query_low_ref[...] = query_low.astype(F32) * inverse_row
    passage_low = dot_nt(down, passage_in_ref[...]).astype(BF16)
    passage_low_ref[...] = passage_low.astype(F32) * row_ref[0:1, :]
    slot_base_ref[...] = dot_nt(up, embed_ref[...])


def score_kernel(group, *refs):
    blocks = refs[:group]
    embed_ref, side_ref, positive_ref, query_low_ref, base_ref = refs[group : group + 5]
    query_ref, weight_ref, dots_ref, onehot_ref, message_ref, coded_ref = refs[group + 5 :]
    rows, width = embed_ref.shape
    queries = query_ref.shape[0]
    q_dev = queries // group
    negatives = (blocks[0].shape[1] - width) // 2
    slots = group * CAP
    rank = query_low_ref.shape[0]
    me = lax.axis_index("dp")
    chunk = min(width, 1024)
    for k in range(group):
        start = pl.multiple_of((me ^ k) * q_dev, q_dev)
        inverse = inverse_length(blocks[k], width)
        for at in range(0, width, chunk):
            part = blocks[k][:, at : at + chunk].astype(F32)
            query_ref[pl.ds(start, q_dev), at : at + chunk] = (part * inverse).astype(BF16)
        coded = blocks[k][:, width:].astype(F32)
        coded_ref[pl.ds(start, q_dev), :] = coded
    dots = dot_nt(embed_ref[...], query_ref[...])
    dots_ref[...] = dots
    scores = dots / SOFTMAX_HEAT

    coded = coded_ref[...].T
    ids = coded[:negatives] * float(ID_BASE) + coded[negatives:]
    home = jnp.broadcast_to(side_ref[:, 1:2], (rows, queries))
    count = jnp.zeros((rows, queries), F32)
    for j in range(negatives):
        count = count + jnp.where(ids[j : j + 1, :] == home, 1.0, 0.0)
    members = iota((slots, queries), 0) // CAP == iota((slots, queries), 1) // q_dev
    marked = dot_nt(members.astype(BF16), count.astype(BF16)) > 0.0
    before = (iota((rows, rows), 0) <= iota((rows, rows), 1)).astype(BF16)
    rank_in = dot_nn(marked.astype(F32).astype(BF16), before)
    wanted = (iota((slots, rows), 0) % CAP + 1).astype(F32)
    onehot = jnp.where(marked & (rank_in == wanted), 1.0, 0.0)
    onehot_ref[...] = onehot

    own = iota((rows, queries), 1) // q_dev == me
    count = count + jnp.where(own & (positive_ref[...] == iota((rows, queries), 0)), 1.0, 0.0)
    named = count > 0.0
    top = jnp.max(jnp.where(named, scores, LOWEST), axis=0, keepdims=True)
    weight = count * jnp.exp(jnp.where(named, scores - top, LOWEST))
    weight_ref[...] = weight
    total = jnp.sum(weight, axis=0, keepdims=True)
    dot_total = jnp.sum(weight * dots, axis=0, keepdims=True)
    slot_weight = dot_pieces(dot_nn, onehot, weight)
    slot_base = dot_pieces(dot_nt, base_ref[...], onehot)
    tail_row = iota((HEAD_ROWS - CAP, queries), 0)
    tail = jnp.where(tail_row == 0, top, jnp.where(tail_row == 1, total, dot_total))
    lane_group = iota((CAP, queries), 1) // q_dev
    compact = jnp.zeros((CAP, queries), F32)
    for peer in range(group):
        part = slot_weight[peer * CAP : (peer + 1) * CAP]
        compact = jnp.where(lane_group == peer, part, compact)
    message_ref[:CAP, :] = compact
    message_ref[CAP:HEAD_ROWS, :] = tail
    message_ref[HEAD_ROWS:, :slots] = slot_base
    message_ref[HEAD_ROWS:, slots : slots + q_dev] = query_low_ref[...]


def back_kernel(query_ref, weights_ref, back_ref):
    back_ref[...] = dot_nt(weights_ref[weights_ref.shape[0] // 2 :, :], query_ref[...])


def request_kernel(first, embed_ref, onehot_ref, *blocks):
    width = embed_ref.shape[1]
    me = lax.axis_index("dp")
    onehot = [
        onehot_ref[pl.ds(pl.multiple_of((me ^ k) * CAP, CAP), CAP), :]
        for k in range(2 * first, 2 * (first + len(blocks)))
    ]
    onehot = jnp.concatenate(onehot, axis=0).astype(BF16)
    chunk = min(width, 1024)
    for at in range(0, width, chunk):
        part = dot_nn(onehot, embed_ref[:, at : at + chunk]).astype(BF16)
        for i, block in enumerate(blocks):
            block[:, at : at + chunk] = part[2 * i * CAP : 2 * (i + 1) * CAP]


def request(first, count, embed, onehot):
    width = embed.shape[1]
    return run(
        functools.partial(request_kernel, first),
        (shape_of((2 * CAP, width), BF16),) * count,
        (embed, onehot),
        2 * embed.size * 2 * CAP * count,
    )


def forward_kernel(*refs):
    out_ref = refs[-1]
    for i, ref in enumerate(refs[:-1]):
        out_ref[i * CAP : (i + 1) * CAP, :] = ref[CAP:, :]


def message_parts(near_ref, far_ref, group):
    rows = near_ref.shape[0] // (group // 2)
    return [((near_ref, far_ref)[k % 2], k // 2 * rows) for k in range(group)]


def combine(parts):
    tops = [ref[at + TOP_ROW : at + TOP_ROW + 1, :] for ref, at in parts]
    sums = [ref[at + SUM_ROW : at + SUM_ROW + 1, :] for ref, at in parts]
    top = functools.reduce(jnp.maximum, tops)
    scales = [jnp.exp(t - top) for t in tops]
    inverse_total = 1.0 / sum(t * s for t, s in zip(scales, sums))
    return [scale * inverse_total for scale in scales]


def own_target(positive_ref, rows, queries, q_dev, me):
    own = iota((rows, queries), 1) // q_dev == me
    return jnp.where(own & (positive_ref[...] == iota((rows, queries), 0)), 1.0, 0.0)


def terms_kernel(group, shards, near_ref, far_ref, *refs):
    parts = message_parts(near_ref, far_ref, group)
    (
        weight_ref,
        dots_ref,
        positive_ref,
        query_ref,
        embed_ref,
        back_query_ref,
        back_passage_ref,
        passage_low_ref,
        row_ref,
        own_ref,
        passage_in_ref,
        query_in_ref,
    ) = refs[:12]
    final_ref = refs[12]
    blocks = refs[13 : 13 + shards]
    (sum_ref,) = refs[13 + shards :]
    rows, queries = weight_ref.shape
    q_dev = queries // group
    rank = passage_low_ref.shape[0]
    width = query_ref.shape[1]
    me = lax.axis_index("dp")

    scales = combine(parts)
    target = own_target(positive_ref, rows, queries, q_dev, me)
    weight = (weight_ref[...] * scales[0] - target) / SOFTMAX_HEAT
    final_ref[...] = weight
    dots = dots_ref[...]
    weighted = weight * dots
    share = jnp.sum(weighted, axis=0, keepdims=True)
    ones = jnp.ones((8, queries), F32)
    inner = dot_pieces(dot_nt, ones, weighted)[0:1, :]

    inner_query = -jnp.sum(target * dots, axis=0, keepdims=True)
    slots = group * CAP
    bases, query_low = [], []
    for (ref, at), scale in zip(parts, scales):
        inner_query = inner_query + scale * ref[at + DOT_ROW : at + DOT_ROW + 1, :]
        bases.append(ref[at + HEAD_ROWS : at + HEAD_ROWS + rank, :slots])
        query_low.append(ref[at + HEAD_ROWS : at + HEAD_ROWS + rank, slots : slots + q_dev])
    sent_by = me ^ (iota((queries, queries), 0) // q_dev)
    place = iota((queries, queries), 1) == sent_by * q_dev + iota((queries, queries), 0) % q_dev
    query_low = dot_pieces(dot_nn, jnp.concatenate(query_low, axis=1), place.astype(F32))
    pick_slots = (iota((slots, CAP), 0) == iota((slots, CAP), 1) + me * CAP).astype(F32)
    bases = dot_pieces(dot_nn, jnp.concatenate(bases[1:], axis=0), pick_slots)
    far_base = [bases[k * rank : (k + 1) * rank] for k in range(group - 1)]
    far_weight = [
        ref[at : at + CAP, :] * (scale / SOFTMAX_HEAT)
        for (ref, at), scale in zip(parts[1:], scales[1:])
    ]
    inner_query = inner_query / SOFTMAX_HEAT

    passage_low = passage_low_ref[...]
    from_query = dot_pieces(dot_nn, passage_low, weight) - query_low * share
    from_passage = dot_pieces(dot_nt, query_low, weight) - passage_low * inner
    query_parts = jnp.concatenate(split_two(from_query), axis=0)
    passage_parts = jnp.concatenate(split_two(from_passage), axis=0)

    back_passage = dot_pieces(dot_nt, back_query_ref[...], weight)
    back_passage = (back_passage - back_passage_ref[...] * inner) * row_ref[0:1, :]
    back_passage = back_passage.astype(BF16)
    back_query = dot_pieces(dot_nn, back_passage_ref[...], weight)
    back_query = back_query + dot_pieces(
        dot_nn, jnp.concatenate(far_base, axis=1), jnp.concatenate(far_weight, axis=0)
    )
    back_query = (back_query - back_query_ref[...] * inner_query) * own_ref[0:1, :]
    pick = (iota((q_dev, queries), 1) == iota((q_dev, queries), 0) + me * q_dev).astype(BF16)
    back_query = dot_nt(back_query.astype(BF16), pick).astype(BF16)

    chunk = min(width, 512)
    for at in range(0, width, chunk):
        cols = slice(at, at + chunk)
        both = dot_nn(query_parts, query_ref[:, cols]) + dot_nn(passage_parts, embed_ref[:, cols])
        sum_ref[rank:, cols] = ADAPTER_SCALE * (both[:rank] + both[rank:])
        sum_ref[:rank, cols] = ADAPTER_SCALE * (
            dot_nn(back_passage, passage_in_ref[:, cols])
            + dot_nn(back_query, query_in_ref[:, cols])
        )
    part = width // shards
    home = lax.axis_index("fsdp")
    for k in range(shards):
        start = pl.multiple_of((home ^ k) * part, part)
        blocks[k][...] = sum_ref[:, pl.ds(start, part)].astype(blocks[k].dtype)


def backward(upstream_of, raw_ref, inverse, grad_ref, up_ref):
    rows, width = raw_ref.shape
    chunk = min(width, 512)
    inner = jnp.zeros((rows, 1), F32)
    for at in range(0, width, chunk):
        upstream = upstream_of(at, chunk)
        up_ref[:, at : at + chunk] = upstream
        unit = raw_ref[:, at : at + chunk].astype(F32) * inverse
        inner = inner + jnp.sum(unit * upstream, axis=-1, keepdims=True)
    for at in range(0, width, chunk):
        unit = raw_ref[:, at : at + chunk].astype(F32) * inverse
        grad = (up_ref[:, at : at + chunk] - unit * inner) * inverse
        grad_ref[:, at : at + chunk] = grad.astype(BF16)


def passage_kernel(final_ref, query_ref, raw_ref, side_ref, grad_ref, up_ref):
    high, low = split_two(final_ref[...])

    def upstream_of(at, chunk):
        embed = query_ref[:, at : at + chunk]
        return dot_nn(high, embed) + dot_nn(low, embed)

    backward(upstream_of, raw_ref, side_ref[:, 0:1], grad_ref, up_ref)


def query_kernel(group, near_ref, far_ref, *refs):
    parts = message_parts(near_ref, far_ref, group)
    near = refs[: group // 2 - 1]
    forwarded_ref, final_ref, embed_ref, raw_ref, grad_ref, up_ref = refs[group // 2 - 1 :]
    q_dev, width = raw_ref.shape
    queries = final_ref.shape[1]
    me = lax.axis_index("dp")
    scales = combine(parts)
    pick = (iota((q_dev, queries), 1) == iota((q_dev, queries), 0) + me * q_dev).astype(F32)
    far = [
        ref[at : at + CAP, :] * (scale / SOFTMAX_HEAT) for (ref, at), scale in zip(parts, scales)
    ]
    far = far[2::2] + far[1::2] + [jnp.zeros((CAP, queries), F32)]
    own_parts = split_two(dot_pieces(dot_nt, pick, final_ref[...]))
    far_parts = split_two(dot_pieces(dot_nt, pick, jnp.concatenate(far, axis=0)))
    own_parts = jnp.concatenate(own_parts, axis=0)
    far_parts = jnp.concatenate(far_parts, axis=0)

    def upstream_of(at, chunk):
        rows = [ref[:, at : at + chunk].astype(F32)[:CAP] for ref in near]
        rows.append(forwarded_ref[:, at : at + chunk].astype(F32))
        rows.append(jnp.zeros((CAP, chunk), F32))
        both = dot_nn(own_parts, embed_ref[:, at : at + chunk])
        both = both + dot_nn(far_parts, jnp.concatenate(rows, axis=0).astype(BF16))
        return both[:q_dev] + both[q_dev:]

    backward(upstream_of, raw_ref, inverse_length(raw_ref, width), grad_ref, up_ref)


def sum_kernel(*refs):
    total = refs[0][...].astype(F32)
    for ref in refs[1:-1]:
        total = total + ref[...].astype(F32)
    refs[-1][...] = total


def sum_two_kernel(left_ref, right_ref, sent_ref):
    sent_ref[...] = (left_ref[...] + right_ref[...]).astype(BF16)


def sum_split_kernel(*refs):
    terms = [ref[...].astype(F32) for ref in refs[:-2]]
    while len(terms) > 1:
        terms = [a + b for a, b in zip(terms[::2], terms[1::2])]
    rank = refs[-1].shape[0]
    refs[-2][...] = terms[0][:rank]
    refs[-1][...] = terms[0][rank:]


def exchange(values, axis, k):
    size = lax.axis_size(axis)
    return lax.ppermute(values, axis, [(i, i ^ k) for i in range(size)])


def core_step(values, even_step, odd_step):
    outer, inner = lax.axis_size("dp"), lax.axis_size("fsdp")
    pairs = []
    for d in range(outer):
        step = odd_step if d % 2 else even_step
        pairs += [(d * inner + f, d * inner + (f ^ step)) for f in range(inner)]
    return lax.ppermute(values, ("dp", "fsdp"), pairs)


def per_device(
    query_pooled_states,
    passage_pooled_states,
    query_attention_output,
    passage_attention_output,
    positive_passage_row,
    hard_negative_ids,
    passage_home_row,
    adapter_down_weight,
    adapter_up_weight,
):
    group = lax.axis_size("dp")
    shards = lax.axis_size("fsdp")
    query_raw = query_pooled_states[0]
    passage_raw = passage_pooled_states[0]
    query_in = query_attention_output[0]
    passage_in = passage_attention_output[0]
    ids = hard_negative_ids[0]
    q_dev, width = query_raw.shape
    p_dev = passage_raw.shape[0]
    rank, part = adapter_down_weight.shape
    queries = group * q_dev
    slots = group * CAP
    work = 2 * p_dev * width

    packed, adapter, half, positive_row = run(
        front_kernel,
        (
            shape_of((q_dev, width + 2 * ids.shape[1]), BF16),
            shape_of((2 * rank, part), BF16),
            shape_of((rank, part), BF16),
            shape_of((1, queries), jnp.int32),
        ),
        (query_raw, ids, adapter_down_weight, adapter_up_weight, positive_passage_row),
        1,
        [
            pltpu.VMEM(ids.shape, jnp.int32),
            pltpu.VMEM(positive_passage_row.shape, jnp.int32),
            pltpu.SemaphoreType.DMA((5,)),
        ],
        in_hbm=True,
    )
    embed, side, side_row = run(
        passage_norm_kernel,
        (
            shape_of((p_dev, width), BF16),
            shape_of((p_dev, 128), F32),
            shape_of((8, p_dev), F32),
        ),
        (passage_raw, passage_home_row),
        work,
        [
            pltpu.VMEM(passage_raw.shape, BF16),
            pltpu.VMEM(passage_home_row.shape, jnp.int32),
            pltpu.SemaphoreType.DMA((1 + PASSAGE_CHUNKS,)),
        ],
        in_hbm=True,
    )
    blocks = {0: packed}
    for k in range(2, group, 2):
        blocks[k] = exchange(packed, "dp", k)
    blocks[1] = exchange(packed, "dp", 1)
    for k in range(2, group, 2):
        blocks[k], embed = lax.optimization_barrier((blocks[k], embed))
        blocks[k ^ 1] = exchange(blocks[k], "dp", 1)
    if shards == 4:
        whole_block = core_step(adapter, 1, 2)
        half_block = exchange(half, "fsdp", 3)
        adapter_near = run(
            join_kernel,
            (shape_of((3 * rank, part), BF16),),
            (whole_block, half_block),
            1,
        )[0]
        adapter_blocks = [adapter, adapter_near, exchange(adapter_near, "dp", 1)]
    else:
        adapter_blocks = [adapter] + [exchange(adapter, "fsdp", k) for k in range(1, shards)]
    adapter_full, passage_low, query_low, own_side, slot_base = run(
        functools.partial(rank_kernel, shards),
        (
            shape_of((2 * rank, width), BF16),
            shape_of((rank, p_dev), F32),
            shape_of((rank, q_dev), F32),
            shape_of((8, queries), F32),
            shape_of((rank, p_dev), F32),
        ),
        (*adapter_blocks, query_raw, query_in, passage_in, embed, side_row),
        work * rank,
    )
    query_embed, weight, dots, onehot, message = run(
        functools.partial(score_kernel, group),
        (
            shape_of((queries, width), BF16),
            shape_of((p_dev, queries), F32),
            shape_of((p_dev, queries), F32),
            shape_of((slots, p_dev), F32),
            shape_of((HEAD_ROWS + rank, queries), F32),
        ),
        (
            *[blocks[k] for k in range(group)],
            embed,
            side,
            positive_row,
            query_low,
            slot_base,
        ),
        work * queries,
        [pltpu.VMEM((queries, 2 * ids.shape[1]), F32)],
    )
    back_query = run(
        back_kernel,
        (shape_of((rank, queries), F32),),
        (query_embed, adapter_full),
        work * rank,
    )[0]
    stats = [message] + [exchange(message, "dp", k) for k in range(2, group, 2)]
    chips = group // 2
    row_blocks = request(0, chips, embed, onehot)
    stats, row_blocks = lax.optimization_barrier((stats, row_blocks))
    near = [exchange(row_blocks[i], "dp", 2 * i) for i in range(1, chips)]
    near_stats = stack(*stats)
    far_stats = exchange(near_stats, "dp", 1)
    final, *terms = run(
        functools.partial(terms_kernel, group, shards),
        (
            shape_of((p_dev, queries), F32),
            shape_of((2 * rank, part), F32),
            *[shape_of((2 * rank, part), BF16)] * (shards - 1),
        ),
        (
            near_stats,
            far_stats,
            weight,
            dots,
            positive_row,
            query_embed,
            embed,
            back_query,
            slot_base,
            passage_low,
            side_row,
            own_side,
            passage_in,
            query_in,
        ),
        work * rank * 4,
        [pltpu.VMEM((2 * rank, width), F32)],
    )
    arrived = [exchange(terms[k], "fsdp", k) for k in range(1, shards)]
    final, near[0] = lax.optimization_barrier((final, near[0]))
    grad_passage = run(
        passage_kernel,
        (shape_of((p_dev, width), BF16),),
        (final, query_embed, passage_raw, side),
        2 * work * queries,
        [pltpu.VMEM((p_dev, width), F32)],
    )[0]
    terms[0], grad_passage = lax.optimization_barrier((terms[0], grad_passage))
    total = run(sum_kernel, (shape_of((2 * rank, part), F32),), (terms[0], *arrived), 1)[0]
    total, near = lax.optimization_barrier((total, near))
    to_sibling = run(
        forward_kernel,
        (shape_of((group // 2 * CAP, width), BF16),),
        (row_blocks[0], *near),
        1,
    )[0]
    forwarded = exchange(to_sibling, "dp", 1)
    sent = run(
        sum_two_kernel,
        (shape_of((2 * rank, part), BF16),),
        (total, exchange(total, "dp", 1)),
        1,
    )[0]
    arrived = [exchange(sent, "dp", k) for k in range(2, group, 2)]
    grad_query = run(
        functools.partial(query_kernel, group),
        (shape_of((q_dev, width), BF16),),
        (near_stats, far_stats, *near, forwarded, final, embed, query_raw),
        4 * q_dev * width * (p_dev + slots),
        [pltpu.VMEM((q_dev, width), F32)],
    )[0]
    sent, grad_query = lax.optimization_barrier((sent, grad_query))
    down_total, up_total = run(
        sum_split_kernel, (shape_of((rank, part), F32),) * 2, (sent, *arrived), 1
    )
    return (grad_query[None], grad_passage[None], down_total, up_total)


def solution(mesh):
    in_specs = (
        P("fsdp", "dp", None),
        P("fsdp", "dp", None),
        P("fsdp", "dp", None),
        P("fsdp", "dp", None),
        P("fsdp", "dp"),
        P("fsdp", "dp", None),
        P("fsdp", None),
        P(None, "fsdp"),
        P(None, "fsdp"),
    )
    out_specs = (P("fsdp", "dp", None), P("fsdp", "dp", None), P(None, "fsdp"), P(None, "fsdp"))
    return jax.shard_map(
        per_device, mesh=mesh, in_specs=in_specs, out_specs=out_specs, check_vma=False
    )
```

```python
import functools

import jax
import jax.numpy as jnp
from jax import lax
from jax.experimental import pallas as pl
from jax.experimental.pallas import tpu as pltpu
from jax.sharding import PartitionSpec as P

CAP = 8
SOFTMAX_HEAT = 0.01
ADAPTER_SCALE = 2.0
EPSILON = 1e-06
LOWEST = -1e30
ID_BASE = 256
TOP_ROW, SUM_ROW, DOT_ROW, HEAD_ROWS = 8, 9, 10, 16
VMEM_BYTES = 16 * 1024 * 1024
PASSAGE_CHUNKS = 4
F32 = jnp.float32
BF16 = jnp.bfloat16


def dot_nn(a, b, precision=None):
    return lax.dot_general(
        a, b, (((1,), (0,)), ((), ())), precision=precision, preferred_element_type=F32
    )


def dot_nt(a, b, precision=None):
    return lax.dot_general(
        a, b, (((1,), (1,)), ((), ())), precision=precision, preferred_element_type=F32
    )


def split_two(values):
    high = values.astype(BF16)
    low = (values - high.astype(F32)).astype(BF16)
    return high, low


def dot_pieces(dot, a, b):
    rows = a.shape[0]
    a_high, a_low = split_two(a)
    b_high, b_low = split_two(b)
    both = dot(jnp.concatenate([a_high, a_low], axis=0), b_high)
    return both[:rows] + both[rows:] + dot(a_high, b_low)


def iota(shape, dim):
    return lax.broadcasted_iota(jnp.int32, shape, dim)


def shape_of(dims, kind):
    return jax.ShapeDtypeStruct(dims, kind)


def run(body, out_shape, args, flops, scratch=(), in_hbm=False):
    grant = VMEM_BYTES * max(1, size_ratio(args))
    if in_hbm:
        args = [pltpu.with_memory_space_constraint(a, pltpu.HBM) for a in args]
    vmem = pl.BlockSpec(memory_space=pltpu.VMEM)
    hbm = pl.BlockSpec(memory_space=pltpu.HBM)
    moved = sum(a.size * a.dtype.itemsize for a in (*args, *out_shape))
    return pl.pallas_call(
        body,
        out_shape=out_shape,
        in_specs=[hbm if in_hbm else vmem] * len(args),
        out_specs=tuple(vmem for _ in out_shape),
        scratch_shapes=list(scratch),
        compiler_params=pltpu.CompilerParams(vmem_limit_bytes=grant),
        cost_estimate=pl.CostEstimate(flops=flops, bytes_accessed=moved, transcendentals=0),
    )(*args)


def size_ratio(args):
    moved = sum(a.size * a.dtype.itemsize for a in args)
    return -(-moved * 3 // VMEM_BYTES)


def inverse_length(raw_ref, width):
    chunk = min(width, 512)
    total = jnp.zeros((raw_ref.shape[0], 1), F32)
    for at in range(0, width, chunk):
        part = raw_ref[:, at : at + chunk].astype(F32)
        total = total + jnp.sum(part * part, axis=-1, keepdims=True)
    return 1.0 / jnp.sqrt(total + EPSILON)


def front_kernel(
    query_ref,
    ids_ref,
    down_ref,
    up_ref,
    positive_ref,
    out_ref,
    adapter_ref,
    half_ref,
    tiled_ref,
    ids_here,
    positive_here,
    sems,
):
    width = query_ref.shape[1]
    rank = down_ref.shape[0]
    me = lax.axis_index("dp")
    pairs = (
        (ids_ref, ids_here),
        (query_ref, out_ref.at[:, pl.ds(0, width)]),
        (positive_ref, positive_here),
        (down_ref, adapter_ref.at[pl.ds(0, rank), :]),
        (up_ref, adapter_ref.at[pl.ds(rank, rank), :]),
    )
    copies = [pltpu.make_async_copy(a, b, sems.at[i]) for i, (a, b) in enumerate(pairs)]
    for copy in copies:
        copy.start()
    copies[0].wait()
    ids = ids_here[...]
    coded = jnp.concatenate([ids // ID_BASE, ids % ID_BASE], axis=1)
    out_ref[:, width:] = coded.astype(F32).astype(BF16)
    copies[2].wait()
    q_dev = positive_here.shape[1]
    for at in range(0, tiled_ref.shape[1], q_dev):
        tiled_ref[:, at : at + q_dev] = positive_here[...]
    copies[3].wait()
    copies[4].wait()

    @pl.when(me % 2 == 0)
    def _():
        half_ref[...] = adapter_ref[:rank, :]

    @pl.when(me % 2 == 1)
    def _():
        half_ref[...] = adapter_ref[rank:, :]

    copies[1].wait()


def passage_norm_kernel(
    passage_ref, home_ref, embed_ref, side_ref, row_ref, passage_here, home_here, sems
):
    rows, width = passage_ref.shape
    total = home_ref.shape[1]
    me = lax.axis_index("dp")
    part = rows // PASSAGE_CHUNKS
    home_copy = pltpu.make_async_copy(home_ref, home_here, sems.at[0])
    home_copy.start()
    passage_copies = []
    for c in range(PASSAGE_CHUNKS):
        here = pl.ds(c * part, part)
        passage_copies.append(
            pltpu.make_async_copy(
                passage_ref.at[here, :], passage_here.at[here, :], sems.at[1 + c]
            )
        )
        passage_copies[c].start()

    home_copy.wait()
    row_id = iota((rows, total), 0) + me * rows
    number = iota((rows, total), 1)
    home = jnp.where(home_here[...] == row_id, number, 0).astype(F32)
    home = jnp.sum(home, axis=1, keepdims=True)

    chunk = min(width, 512)
    inverses = []
    for c in range(PASSAGE_CHUNKS):
        passage_copies[c].wait()
        here = slice(c * part, (c + 1) * part)
        inverse = inverse_length(passage_here.at[here, :], width)
        for at in range(0, width, chunk):
            values = passage_here[here, at : at + chunk].astype(F32)
            embed_ref[here, at : at + chunk] = (values * inverse).astype(BF16)
        inverses.append(inverse)
    inverse = jnp.concatenate(inverses, axis=0)
    side_ref[...] = jnp.where(iota(side_ref.shape, 1) == 0, inverse, home)
    row_ref[...] = jnp.broadcast_to(inverse, (rows, rows)).T[: row_ref.shape[0]]


def stack_kernel(*refs):
    out_ref = refs[-1]
    rows = refs[0].shape[0]
    for i, ref in enumerate(refs[:-1]):
        out_ref[i * rows : (i + 1) * rows, :] = ref[...]


def stack(*parts):
    rows, cols = parts[0].shape
    return run(stack_kernel, (shape_of((len(parts) * rows, cols), parts[0].dtype),), parts, 1)[0]


def join_kernel(first_ref, second_ref, out_ref):
    rows = first_ref.shape[0]
    out_ref[:rows, :] = first_ref[...]
    out_ref[rows:, :] = second_ref[...]


def place_paired(own_ref, near_ref, far_ref, weights_ref):
    rank, part = own_ref.shape[0] // 2, own_ref.shape[1]
    me = lax.axis_index("fsdp")
    core = lax.axis_index("dp") % 2

    def columns(k):
        return pl.ds(pl.multiple_of((me ^ k) * part, part), part)

    def place(even_ref, odd_ref):
        weights_ref[:, columns(1)] = even_ref[: 2 * rank, :]
        weights_ref[:, columns(2)] = odd_ref[: 2 * rank, :]
        weights_ref[:rank, columns(3)] = even_ref[2 * rank :, :]
        weights_ref[rank:, columns(3)] = odd_ref[2 * rank :, :]

    weights_ref[:, columns(0)] = own_ref[...]
    pl.when(core == 0)(functools.partial(place, near_ref, far_ref))
    pl.when(core == 1)(functools.partial(place, far_ref, near_ref))


def place_blocks(*refs):
    part = refs[0].shape[1]
    me = lax.axis_index("fsdp")
    for k, ref in enumerate(refs[:-1]):
        refs[-1][:, pl.ds(pl.multiple_of((me ^ k) * part, part), part)] = ref[...]


def rank_kernel(shards, *refs):
    blocks = refs[:-12]
    query_ref, query_in_ref, passage_in_ref, embed_ref, row_ref = refs[-12:-7]
    onehot_ref, head_ref = refs[-7:-5]
    weights_ref, passage_low_ref, message_ref, own_ref, base_ref = refs[-5:]
    slots = onehot_ref.shape[0]
    rank = blocks[0].shape[0] // 2
    q_dev, width = query_ref.shape
    queries = own_ref.shape[1]
    place = place_paired if shards == 4 else place_blocks
    place(*blocks, weights_ref)
    down, up = weights_ref[:rank, :], weights_ref[rank:, :]
    start = lax.axis_index("dp") * q_dev
    place = iota((q_dev, queries), 1) == iota((q_dev, queries), 0) + start
    inverse = inverse_length(query_ref, width)
    own = jnp.sum(jnp.where(place, inverse, 0.0), axis=0, keepdims=True)
    own_ref[...] = jnp.broadcast_to(own, own_ref.shape)
    same = iota((q_dev, q_dev), 0) == iota((q_dev, q_dev), 1)
    inverse_row = jnp.sum(jnp.where(same, inverse, 0.0), axis=0, keepdims=True)
    query_low = dot_nt(down, query_in_ref[...]).astype(BF16)
    message_ref[HEAD_ROWS:, slots : slots + q_dev] = query_low.astype(F32) * inverse_row
    passage_low = dot_nt(down, passage_in_ref[...]).astype(BF16)
    passage_low_ref[...] = passage_low.astype(F32) * row_ref[0:1, :]
    base = dot_nt(up, embed_ref[...])
    base_ref[...] = base
    message_ref[:HEAD_ROWS, :] = head_ref[...]
    message_ref[HEAD_ROWS:, :slots] = dot_pieces(dot_nt, base, onehot_ref[...])


def score_kernel(group, *refs):
    blocks = refs[:group]
    embed_ref, side_ref, positive_ref = refs[group : group + 3]
    query_ref, weight_ref, dots_ref, onehot_ref, head_ref, coded_ref = refs[group + 3 :]
    rows, width = embed_ref.shape
    queries = query_ref.shape[0]
    q_dev = queries // group
    negatives = (blocks[0].shape[1] - width) // 2
    slots = group * CAP
    me = lax.axis_index("dp")
    chunk = min(width, 1024)
    for k in range(group):
        start = pl.multiple_of((me ^ k) * q_dev, q_dev)
        inverse = inverse_length(blocks[k], width)
        for at in range(0, width, chunk):
            part = blocks[k][:, at : at + chunk].astype(F32)
            query_ref[pl.ds(start, q_dev), at : at + chunk] = (part * inverse).astype(BF16)
        coded = blocks[k][:, width:].astype(F32)
        coded_ref[pl.ds(start, q_dev), :] = coded
    dots = dot_nt(embed_ref[...], query_ref[...])
    dots_ref[...] = dots
    scores = dots / SOFTMAX_HEAT

    coded = coded_ref[...].T
    ids = coded[:negatives] * float(ID_BASE) + coded[negatives:]
    home = jnp.broadcast_to(side_ref[:, 1:2], (rows, queries))
    count = jnp.zeros((rows, queries), F32)
    for j in range(negatives):
        count = count + jnp.where(ids[j : j + 1, :] == home, 1.0, 0.0)
    members = iota((slots, queries), 0) // CAP == iota((slots, queries), 1) // q_dev
    marked = dot_nt(members.astype(BF16), count.astype(BF16)) > 0.0
    before = (iota((rows, rows), 0) <= iota((rows, rows), 1)).astype(BF16)
    rank_in = dot_nn(marked.astype(F32).astype(BF16), before)
    wanted = (iota((slots, rows), 0) % CAP + 1).astype(F32)
    onehot = jnp.where(marked & (rank_in == wanted), 1.0, 0.0)
    onehot_ref[...] = onehot

    own = iota((rows, queries), 1) // q_dev == me
    count = count + jnp.where(own & (positive_ref[...] == iota((rows, queries), 0)), 1.0, 0.0)
    named = count > 0.0
    top = jnp.max(jnp.where(named, scores, LOWEST), axis=0, keepdims=True)
    weight = count * jnp.exp(jnp.where(named, scores - top, LOWEST))
    weight_ref[...] = weight
    total = jnp.sum(weight, axis=0, keepdims=True)
    dot_total = jnp.sum(weight * dots, axis=0, keepdims=True)
    slot_weight = dot_pieces(dot_nn, onehot, weight)
    tail_row = iota((HEAD_ROWS - CAP, queries), 0)
    tail = jnp.where(tail_row == 0, top, jnp.where(tail_row == 1, total, dot_total))
    lane_group = iota((CAP, queries), 1) // q_dev
    compact = jnp.zeros((CAP, queries), F32)
    for peer in range(group):
        part = slot_weight[peer * CAP : (peer + 1) * CAP]
        compact = jnp.where(lane_group == peer, part, compact)
    head_ref[:CAP, :] = compact
    head_ref[CAP:, :] = tail


def request_kernel(group, *refs):
    (
        embed_ref,
        onehot_ref,
        query_ref,
        weights_ref,
        low_ref,
        base_ref,
        weight_ref,
        positive_ref,
        back_ref,
        local_ref,
        target_ref,
    ) = refs[:11]
    blocks = refs[11:]
    width = embed_ref.shape[1]
    rows, queries = weight_ref.shape
    me = lax.axis_index("dp")
    onehot = [
        onehot_ref[pl.ds(pl.multiple_of((me ^ k) * CAP, CAP), CAP), :] for k in range(group)
    ]
    onehot = jnp.concatenate(onehot, axis=0).astype(BF16)
    chunk = min(width, 1024)
    for at in range(0, width, chunk):
        part = dot_nn(onehot, embed_ref[:, at : at + chunk]).astype(BF16)
        for i, block in enumerate(blocks):
            block[:, at : at + chunk] = part[2 * i * CAP : 2 * (i + 1) * CAP]
    back_ref[...] = dot_nt(weights_ref[weights_ref.shape[0] // 2 :, :], query_ref[...])
    both = jnp.concatenate([low_ref[...], base_ref[...]], axis=0)
    local_ref[...] = dot_pieces(dot_nn, both, weight_ref[...])
    target = own_target(positive_ref, rows, queries, queries // group, me)
    target_ref[...] = dot_pieces(dot_nn, both, target)


def forward_kernel(*refs):
    out_ref = refs[-1]
    for i, ref in enumerate(refs[:-1]):
        out_ref[i * CAP : (i + 1) * CAP, :] = ref[CAP:, :]


def message_parts(near_ref, far_ref, group):
    rows = near_ref.shape[0] // (group // 2)
    return [((near_ref, far_ref)[k % 2], k // 2 * rows) for k in range(group)]


def combine(parts):
    tops = [ref[at + TOP_ROW : at + TOP_ROW + 1, :] for ref, at in parts]
    sums = [ref[at + SUM_ROW : at + SUM_ROW + 1, :] for ref, at in parts]
    top = functools.reduce(jnp.maximum, tops)
    scales = [jnp.exp(t - top) for t in tops]
    inverse_total = 1.0 / sum(t * s for t, s in zip(scales, sums))
    return [scale * inverse_total for scale in scales]


def own_target(positive_ref, rows, queries, q_dev, me):
    own = iota((rows, queries), 1) // q_dev == me
    return jnp.where(own & (positive_ref[...] == iota((rows, queries), 0)), 1.0, 0.0)


def terms_kernel(group, shards, near_ref, far_ref, *refs):
    parts = message_parts(near_ref, far_ref, group)
    (
        weight_ref,
        dots_ref,
        positive_ref,
        query_ref,
        embed_ref,
        back_query_ref,
        back_passage_ref,
        passage_low_ref,
        row_ref,
        own_ref,
        passage_in_ref,
        query_in_ref,
        local_ref,
        target_ref,
    ) = refs[:14]
    final_ref = refs[14]
    blocks = refs[15 : 15 + shards]
    (sum_ref,) = refs[15 + shards :]
    rows, queries = weight_ref.shape
    q_dev = queries // group
    rank = passage_low_ref.shape[0]
    width = query_ref.shape[1]
    me = lax.axis_index("dp")

    scales = combine(parts)
    target = own_target(positive_ref, rows, queries, q_dev, me)
    weight = (weight_ref[...] * scales[0] - target) / SOFTMAX_HEAT
    final_ref[...] = weight
    dots = dots_ref[...]
    ones = jnp.ones((8, queries), F32)
    inner = dot_pieces(dot_nt, ones, weight * dots)[0:1, :]

    inner_query = -jnp.sum(target * dots, axis=0, keepdims=True)
    own_dots = near_ref[DOT_ROW : DOT_ROW + 1, :]
    share = (scales[0] * own_dots + inner_query) / SOFTMAX_HEAT
    slots = group * CAP
    bases, query_low = [], []
    for (ref, at), scale in zip(parts, scales):
        inner_query = inner_query + scale * ref[at + DOT_ROW : at + DOT_ROW + 1, :]
        bases.append(ref[at + HEAD_ROWS : at + HEAD_ROWS + rank, :slots])
        query_low.append(ref[at + HEAD_ROWS : at + HEAD_ROWS + rank, slots : slots + q_dev])
    sent_by = me ^ (iota((queries, queries), 0) // q_dev)
    place = iota((queries, queries), 1) == sent_by * q_dev + iota((queries, queries), 0) % q_dev
    query_low = dot_pieces(dot_nn, jnp.concatenate(query_low, axis=1), place.astype(F32))
    pick_slots = (iota((slots, CAP), 0) == iota((slots, CAP), 1) + me * CAP).astype(F32)
    bases = dot_pieces(dot_nn, jnp.concatenate(bases[1:], axis=0), pick_slots)
    far_base = [bases[k * rank : (k + 1) * rank] for k in range(group - 1)]
    far_weight = [
        ref[at : at + CAP, :] * (scale / SOFTMAX_HEAT)
        for (ref, at), scale in zip(parts[1:], scales[1:])
    ]
    inner_query = inner_query / SOFTMAX_HEAT

    passage_low = passage_low_ref[...]
    local = (local_ref[...] * scales[0] - target_ref[...]) / SOFTMAX_HEAT
    from_query = local[:rank] - query_low * share
    from_passage = dot_pieces(dot_nt, query_low, weight) - passage_low * inner
    query_parts = jnp.concatenate(split_two(from_query), axis=0)
    passage_parts = jnp.concatenate(split_two(from_passage), axis=0)

    back_passage = dot_pieces(dot_nt, back_query_ref[...], weight)
    back_passage = (back_passage - back_passage_ref[...] * inner) * row_ref[0:1, :]
    back_passage = back_passage.astype(BF16)
    back_query = local[rank:] + dot_pieces(
        dot_nn, jnp.concatenate(far_base, axis=1), jnp.concatenate(far_weight, axis=0)
    )
    back_query = (back_query - back_query_ref[...] * inner_query) * own_ref[0:1, :]
    pick = (iota((q_dev, queries), 1) == iota((q_dev, queries), 0) + me * q_dev).astype(BF16)
    back_query = dot_nt(back_query.astype(BF16), pick).astype(BF16)

    chunk = min(width, 512)
    for at in range(0, width, chunk):
        cols = slice(at, at + chunk)
        both = dot_nn(query_parts, query_ref[:, cols]) + dot_nn(passage_parts, embed_ref[:, cols])
        sum_ref[rank:, cols] = ADAPTER_SCALE * (both[:rank] + both[rank:])
        sum_ref[:rank, cols] = ADAPTER_SCALE * (
            dot_nn(back_passage, passage_in_ref[:, cols])
            + dot_nn(back_query, query_in_ref[:, cols])
        )
    part = width // shards
    home = lax.axis_index("fsdp")
    for k in range(shards):
        start = pl.multiple_of((home ^ k) * part, part)
        blocks[k][...] = sum_ref[:, pl.ds(start, part)].astype(blocks[k].dtype)


def backward(upstream_of, raw_ref, inverse, grad_ref, up_ref):
    rows, width = raw_ref.shape
    chunk = min(width, 512)
    inner = jnp.zeros((rows, 1), F32)
    for at in range(0, width, chunk):
        upstream = upstream_of(at, chunk)
        up_ref[:, at : at + chunk] = upstream
        unit = raw_ref[:, at : at + chunk].astype(F32) * inverse
        inner = inner + jnp.sum(unit * upstream, axis=-1, keepdims=True)
    for at in range(0, width, chunk):
        unit = raw_ref[:, at : at + chunk].astype(F32) * inverse
        grad = (up_ref[:, at : at + chunk] - unit * inner) * inverse
        grad_ref[:, at : at + chunk] = grad.astype(BF16)


def passage_kernel(final_ref, query_ref, raw_ref, side_ref, grad_ref, up_ref):
    high, low = split_two(final_ref[...])

    def upstream_of(at, chunk):
        embed = query_ref[:, at : at + chunk]
        return dot_nn(high, embed) + dot_nn(low, embed)

    backward(upstream_of, raw_ref, side_ref[:, 0:1], grad_ref, up_ref)


def query_kernel(group, near_ref, far_ref, *refs):
    parts = message_parts(near_ref, far_ref, group)
    near = refs[: group // 2 - 1]
    forwarded_ref, final_ref, embed_ref, raw_ref, grad_ref, up_ref = refs[group // 2 - 1 :]
    q_dev, width = raw_ref.shape
    queries = final_ref.shape[1]
    me = lax.axis_index("dp")
    scales = combine(parts)
    pick = (iota((q_dev, queries), 1) == iota((q_dev, queries), 0) + me * q_dev).astype(F32)
    far = [
        ref[at : at + CAP, :] * (scale / SOFTMAX_HEAT) for (ref, at), scale in zip(parts, scales)
    ]
    far = far[2::2] + far[1::2] + [jnp.zeros((CAP, queries), F32)]
    own_parts = split_two(dot_pieces(dot_nt, pick, final_ref[...]))
    far_parts = split_two(dot_pieces(dot_nt, pick, jnp.concatenate(far, axis=0)))
    own_parts = jnp.concatenate(own_parts, axis=0)
    far_parts = jnp.concatenate(far_parts, axis=0)

    def upstream_of(at, chunk):
        rows = [ref[:, at : at + chunk].astype(F32)[:CAP] for ref in near]
        rows.append(forwarded_ref[:, at : at + chunk].astype(F32))
        rows.append(jnp.zeros((CAP, chunk), F32))
        both = dot_nn(own_parts, embed_ref[:, at : at + chunk])
        both = both + dot_nn(far_parts, jnp.concatenate(rows, axis=0).astype(BF16))
        return both[:q_dev] + both[q_dev:]

    backward(upstream_of, raw_ref, inverse_length(raw_ref, width), grad_ref, up_ref)


def sum_kernel(*refs):
    total = refs[0][...].astype(F32)
    for ref in refs[1:-1]:
        total = total + ref[...].astype(F32)
    refs[-1][...] = total


def sum_two_kernel(left_ref, right_ref, sent_ref):
    sent_ref[...] = (left_ref[...] + right_ref[...]).astype(BF16)


def sum_split_kernel(*refs):
    terms = [ref[...].astype(F32) for ref in refs[:-2]]
    while len(terms) > 1:
        terms = [a + b for a, b in zip(terms[::2], terms[1::2])]
    rank = refs[-1].shape[0]
    refs[-2][...] = terms[0][:rank]
    refs[-1][...] = terms[0][rank:]


def exchange(values, axis, k):
    size = lax.axis_size(axis)
    return lax.ppermute(values, axis, [(i, i ^ k) for i in range(size)])


def core_step(values, even_step, odd_step):
    outer, inner = lax.axis_size("dp"), lax.axis_size("fsdp")
    pairs = []
    for d in range(outer):
        step = odd_step if d % 2 else even_step
        pairs += [(d * inner + f, d * inner + (f ^ step)) for f in range(inner)]
    return lax.ppermute(values, ("dp", "fsdp"), pairs)


def per_device(
    query_pooled_states,
    passage_pooled_states,
    query_attention_output,
    passage_attention_output,
    positive_passage_row,
    hard_negative_ids,
    passage_home_row,
    adapter_down_weight,
    adapter_up_weight,
):
    group = lax.axis_size("dp")
    shards = lax.axis_size("fsdp")
    query_raw = query_pooled_states[0]
    passage_raw = passage_pooled_states[0]
    query_in = query_attention_output[0]
    passage_in = passage_attention_output[0]
    ids = hard_negative_ids[0]
    q_dev, width = query_raw.shape
    p_dev = passage_raw.shape[0]
    rank, part = adapter_down_weight.shape
    queries = group * q_dev
    slots = group * CAP
    work = 2 * p_dev * width

    packed, adapter, half, positive_row = run(
        front_kernel,
        (
            shape_of((q_dev, width + 2 * ids.shape[1]), BF16),
            shape_of((2 * rank, part), BF16),
            shape_of((rank, part), BF16),
            shape_of((1, queries), jnp.int32),
        ),
        (query_raw, ids, adapter_down_weight, adapter_up_weight, positive_passage_row),
        1,
        [
            pltpu.VMEM(ids.shape, jnp.int32),
            pltpu.VMEM(positive_passage_row.shape, jnp.int32),
            pltpu.SemaphoreType.DMA((5,)),
        ],
        in_hbm=True,
    )
    embed, side, side_row = run(
        passage_norm_kernel,
        (
            shape_of((p_dev, width), BF16),
            shape_of((p_dev, 128), F32),
            shape_of((8, p_dev), F32),
        ),
        (passage_raw, passage_home_row),
        work,
        [
            pltpu.VMEM(passage_raw.shape, BF16),
            pltpu.VMEM(passage_home_row.shape, jnp.int32),
            pltpu.SemaphoreType.DMA((1 + PASSAGE_CHUNKS,)),
        ],
        in_hbm=True,
    )
    blocks = {0: packed}
    for k in range(2, group, 2):
        blocks[k] = exchange(packed, "dp", k)
    blocks[1] = exchange(packed, "dp", 1)
    for k in range(2, group, 2):
        blocks[k], embed = lax.optimization_barrier((blocks[k], embed))
        blocks[k ^ 1] = exchange(blocks[k], "dp", 1)
    if shards == 4:
        half_block = exchange(half, "fsdp", 3)
        whole_block = core_step(adapter, 1, 2)
        adapter_near = run(
            join_kernel,
            (shape_of((3 * rank, part), BF16),),
            (whole_block, half_block),
            1,
        )[0]
        adapter_blocks = [adapter, adapter_near, exchange(adapter_near, "dp", 1)]
    else:
        adapter_blocks = [adapter] + [exchange(adapter, "fsdp", k) for k in range(1, shards)]
    query_embed, weight, dots, onehot, head = run(
        functools.partial(score_kernel, group),
        (
            shape_of((queries, width), BF16),
            shape_of((p_dev, queries), F32),
            shape_of((p_dev, queries), F32),
            shape_of((slots, p_dev), F32),
            shape_of((HEAD_ROWS, queries), F32),
        ),
        (
            *[blocks[k] for k in range(group)],
            embed,
            side,
            positive_row,
        ),
        work * queries,
        [pltpu.VMEM((queries, 2 * ids.shape[1]), F32)],
    )
    adapter_full, passage_low, message, own_side, slot_base = run(
        functools.partial(rank_kernel, shards),
        (
            shape_of((2 * rank, width), BF16),
            shape_of((rank, p_dev), F32),
            shape_of((HEAD_ROWS + rank, queries), F32),
            shape_of((8, queries), F32),
            shape_of((rank, p_dev), F32),
        ),
        (
            *adapter_blocks,
            query_raw,
            query_in,
            passage_in,
            embed,
            side_row,
            onehot,
            head,
        ),
        work * rank,
    )
    stats = [message] + [exchange(message, "dp", k) for k in range(2, group, 2)]
    chips = group // 2
    back_query, local, targets, *row_blocks = run(
        functools.partial(request_kernel, group),
        (
            shape_of((rank, queries), F32),
            shape_of((2 * rank, queries), F32),
            shape_of((2 * rank, queries), F32),
            *[shape_of((2 * CAP, width), BF16)] * chips,
        ),
        (
            embed,
            onehot,
            query_embed,
            adapter_full,
            passage_low,
            slot_base,
            weight,
            positive_row,
        ),
        work * slots,
    )
    stats, row_blocks = lax.optimization_barrier((stats, row_blocks))
    near = [exchange(row_blocks[i], "dp", 2 * i) for i in range(1, chips)]
    near_stats = stack(*stats)
    far_stats = exchange(near_stats, "dp", 1)
    final, *terms = run(
        functools.partial(terms_kernel, group, shards),
        (
            shape_of((p_dev, queries), F32),
            shape_of((2 * rank, part), F32),
            *[shape_of((2 * rank, part), BF16)] * (shards - 1),
        ),
        (
            near_stats,
            far_stats,
            weight,
            dots,
            positive_row,
            query_embed,
            embed,
            back_query,
            slot_base,
            passage_low,
            side_row,
            own_side,
            passage_in,
            query_in,
            local,
            targets,
        ),
        work * rank * 4,
        [pltpu.VMEM((2 * rank, width), F32)],
    )
    arrived = [exchange(terms[k], "fsdp", k) for k in range(1, shards)]
    final, near[0] = lax.optimization_barrier((final, near[0]))
    grad_passage = run(
        passage_kernel,
        (shape_of((p_dev, width), BF16),),
        (final, query_embed, passage_raw, side),
        2 * work * queries,
        [pltpu.VMEM((p_dev, width), F32)],
    )[0]
    terms[0], grad_passage = lax.optimization_barrier((terms[0], grad_passage))
    total = run(sum_kernel, (shape_of((2 * rank, part), F32),), (terms[0], *arrived), 1)[0]
    total, near = lax.optimization_barrier((total, near))
    to_sibling = run(
        forward_kernel,
        (shape_of((group // 2 * CAP, width), BF16),),
        (row_blocks[0], *near),
        1,
    )[0]
    forwarded = exchange(to_sibling, "dp", 1)
    sent = run(
        sum_two_kernel,
        (shape_of((2 * rank, part), BF16),),
        (total, exchange(total, "dp", 1)),
        1,
    )[0]
    arrived = [exchange(sent, "dp", k) for k in range(2, group, 2)]
    grad_query = run(
        functools.partial(query_kernel, group),
        (shape_of((q_dev, width), BF16),),
        (near_stats, far_stats, *near, forwarded, final, embed, query_raw),
        4 * q_dev * width * (p_dev + slots),
        [pltpu.VMEM((q_dev, width), F32)],
    )[0]
    sent, grad_query = lax.optimization_barrier((sent, grad_query))
    down_total, up_total = run(
        sum_split_kernel, (shape_of((rank, part), F32),) * 2, (sent, *arrived), 1
    )
    return (grad_query[None], grad_passage[None], down_total, up_total)


def solution(mesh):
    in_specs = (
        P("fsdp", "dp", None),
        P("fsdp", "dp", None),
        P("fsdp", "dp", None),
        P("fsdp", "dp", None),
        P("fsdp", "dp"),
        P("fsdp", "dp", None),
        P("fsdp", None),
        P(None, "fsdp"),
        P(None, "fsdp"),
    )
    out_specs = (P("fsdp", "dp", None), P("fsdp", "dp", None), P(None, "fsdp"), P(None, "fsdp"))
    return jax.shard_map(
        per_device, mesh=mesh, in_specs=in_specs, out_specs=out_specs, check_vma=False
    )
```

```python
import functools

import jax
import jax.numpy as jnp
from jax import lax
from jax.experimental import pallas as pl
from jax.experimental.pallas import tpu as pltpu
from jax.sharding import PartitionSpec as P

CAP = 8
SOFTMAX_HEAT = 0.01
ADAPTER_SCALE = 2.0
EPSILON = 1e-06
LOWEST = -1e30
ID_BASE = 256
TOP_ROW, SUM_ROW, DOT_ROW, HEAD_ROWS = 8, 9, 10, 16
VMEM_BYTES = 16 * 1024 * 1024
PASSAGE_CHUNKS = 4
F32 = jnp.float32
BF16 = jnp.bfloat16


def dot_nn(a, b, precision=None):
    return lax.dot_general(
        a, b, (((1,), (0,)), ((), ())), precision=precision, preferred_element_type=F32
    )


def dot_nt(a, b, precision=None):
    return lax.dot_general(
        a, b, (((1,), (1,)), ((), ())), precision=precision, preferred_element_type=F32
    )


def split_two(values):
    high = values.astype(BF16)
    low = (values - high.astype(F32)).astype(BF16)
    return high, low


def dot_pieces(dot, a, b):
    rows = a.shape[0]
    a_high, a_low = split_two(a)
    b_high, b_low = split_two(b)
    both = dot(jnp.concatenate([a_high, a_low], axis=0), b_high)
    return both[:rows] + both[rows:] + dot(a_high, b_low)


def iota(shape, dim):
    return lax.broadcasted_iota(jnp.int32, shape, dim)


def shape_of(dims, kind):
    return jax.ShapeDtypeStruct(dims, kind)


def run(body, out_shape, args, flops, scratch=(), in_hbm=False):
    grant = VMEM_BYTES * max(1, size_ratio(args))
    if in_hbm:
        args = [pltpu.with_memory_space_constraint(a, pltpu.HBM) for a in args]
    vmem = pl.BlockSpec(memory_space=pltpu.VMEM)
    hbm = pl.BlockSpec(memory_space=pltpu.HBM)
    moved = sum(a.size * a.dtype.itemsize for a in (*args, *out_shape))
    return pl.pallas_call(
        body,
        out_shape=out_shape,
        in_specs=[hbm if in_hbm else vmem] * len(args),
        out_specs=tuple(vmem for _ in out_shape),
        scratch_shapes=list(scratch),
        compiler_params=pltpu.CompilerParams(vmem_limit_bytes=grant),
        cost_estimate=pl.CostEstimate(flops=flops, bytes_accessed=moved, transcendentals=0),
    )(*args)


def size_ratio(args):
    moved = sum(a.size * a.dtype.itemsize for a in args)
    return -(-moved * 3 // VMEM_BYTES)


def inverse_length(raw_ref, width):
    chunk = min(width, 512)
    total = jnp.zeros((raw_ref.shape[0], 1), F32)
    for at in range(0, width, chunk):
        part = raw_ref[:, at : at + chunk].astype(F32)
        total = total + jnp.sum(part * part, axis=-1, keepdims=True)
    return 1.0 / jnp.sqrt(total + EPSILON)


def front_kernel(
    query_ref,
    ids_ref,
    down_ref,
    up_ref,
    positive_ref,
    out_ref,
    adapter_ref,
    half_ref,
    tiled_ref,
    ids_here,
    positive_here,
    sems,
):
    width = query_ref.shape[1]
    rank = down_ref.shape[0]
    me = lax.axis_index("dp")
    pairs = (
        (ids_ref, ids_here),
        (query_ref, out_ref.at[:, pl.ds(0, width)]),
        (positive_ref, positive_here),
        (down_ref, adapter_ref.at[pl.ds(0, rank), :]),
        (up_ref, adapter_ref.at[pl.ds(rank, rank), :]),
    )
    copies = [pltpu.make_async_copy(a, b, sems.at[i]) for i, (a, b) in enumerate(pairs)]
    for copy in copies:
        copy.start()
    copies[0].wait()
    ids = ids_here[...]
    coded = jnp.concatenate([ids // ID_BASE, ids % ID_BASE], axis=1)
    out_ref[:, width:] = coded.astype(F32).astype(BF16)
    copies[2].wait()
    q_dev = positive_here.shape[1]
    for at in range(0, tiled_ref.shape[1], q_dev):
        tiled_ref[:, at : at + q_dev] = positive_here[...]
    copies[3].wait()
    copies[4].wait()

    @pl.when(me % 2 == 0)
    def _():
        half_ref[...] = adapter_ref[:rank, :]

    @pl.when(me % 2 == 1)
    def _():
        half_ref[...] = adapter_ref[rank:, :]

    copies[1].wait()


def passage_norm_kernel(
    query_ref,
    passage_ref,
    home_ref,
    embed_ref,
    side_ref,
    row_ref,
    own_ref,
    low_scale_ref,
    passage_here,
    home_here,
    query_here,
    sems,
):
    rows, width = passage_ref.shape
    total = home_ref.shape[1]
    me = lax.axis_index("dp")
    part = rows // PASSAGE_CHUNKS
    home_copy = pltpu.make_async_copy(home_ref, home_here, sems.at[0])
    home_copy.start()
    query_copy = pltpu.make_async_copy(query_ref, query_here, sems.at[1 + PASSAGE_CHUNKS])
    query_copy.start()
    passage_copies = []
    for c in range(PASSAGE_CHUNKS):
        here = pl.ds(c * part, part)
        passage_copies.append(
            pltpu.make_async_copy(
                passage_ref.at[here, :], passage_here.at[here, :], sems.at[1 + c]
            )
        )
        passage_copies[c].start()

    home_copy.wait()
    row_id = iota((rows, total), 0) + me * rows
    number = iota((rows, total), 1)
    home = jnp.where(home_here[...] == row_id, number, 0).astype(F32)
    home = jnp.sum(home, axis=1, keepdims=True)
    query_copy.wait()
    q_dev = query_here.shape[0]
    queries = own_ref.shape[1]
    inverse = inverse_length(query_here, width)
    place = iota((q_dev, queries), 1) == iota((q_dev, queries), 0) + me * q_dev
    own = jnp.sum(jnp.where(place, inverse, 0.0), axis=0, keepdims=True)
    own_ref[...] = jnp.broadcast_to(own, own_ref.shape)
    same = iota((q_dev, q_dev), 0) == iota((q_dev, q_dev), 1)
    low_scale = jnp.sum(jnp.where(same, inverse, 0.0), axis=0, keepdims=True)
    low_scale_ref[...] = jnp.broadcast_to(low_scale, low_scale_ref.shape)

    chunk = min(width, 512)
    inverses = []
    for c in range(PASSAGE_CHUNKS):
        passage_copies[c].wait()
        here = slice(c * part, (c + 1) * part)
        inverse = inverse_length(passage_here.at[here, :], width)
        for at in range(0, width, chunk):
            values = passage_here[here, at : at + chunk].astype(F32)
            embed_ref[here, at : at + chunk] = (values * inverse).astype(BF16)
        inverses.append(inverse)
    inverse = jnp.concatenate(inverses, axis=0)
    side_ref[...] = jnp.where(iota(side_ref.shape, 1) == 0, inverse, home)
    row_ref[...] = jnp.broadcast_to(inverse, (rows, rows)).T[: row_ref.shape[0]]


def stack_kernel(*refs):
    out_ref = refs[-1]
    rows = refs[0].shape[0]
    for i, ref in enumerate(refs[:-1]):
        out_ref[i * rows : (i + 1) * rows, :] = ref[...]


def stack(*parts):
    rows, cols = parts[0].shape
    return run(stack_kernel, (shape_of((len(parts) * rows, cols), parts[0].dtype),), parts, 1)[0]


def join_kernel(first_ref, second_ref, out_ref):
    rows = first_ref.shape[0]
    out_ref[:rows, :] = first_ref[...]
    out_ref[rows:, :] = second_ref[...]


def place_paired(own_ref, near_ref, far_ref, weights_ref):
    rank, part = own_ref.shape[0] // 2, own_ref.shape[1]
    me = lax.axis_index("fsdp")
    core = lax.axis_index("dp") % 2

    def columns(k):
        return pl.ds(pl.multiple_of((me ^ k) * part, part), part)

    def place(even_ref, odd_ref):
        weights_ref[:, columns(1)] = even_ref[: 2 * rank, :]
        weights_ref[:, columns(2)] = odd_ref[: 2 * rank, :]
        weights_ref[:rank, columns(3)] = even_ref[2 * rank :, :]
        weights_ref[rank:, columns(3)] = odd_ref[2 * rank :, :]

    weights_ref[:, columns(0)] = own_ref[...]
    pl.when(core == 0)(functools.partial(place, near_ref, far_ref))
    pl.when(core == 1)(functools.partial(place, far_ref, near_ref))


def place_blocks(*refs):
    part = refs[0].shape[1]
    me = lax.axis_index("fsdp")
    for k, ref in enumerate(refs[:-1]):
        refs[-1][:, pl.ds(pl.multiple_of((me ^ k) * part, part), part)] = ref[...]


def rank_kernel(shards, *refs):
    blocks = refs[:-11]
    query_in_ref, passage_in_ref, embed_ref, row_ref, low_scale_ref = refs[-11:-6]
    onehot_ref, head_ref = refs[-6:-4]
    weights_ref, passage_low_ref, message_ref, base_ref = refs[-4:]
    rank = blocks[0].shape[0] // 2
    q_dev = query_in_ref.shape[0]
    slots = onehot_ref.shape[0]
    queries = message_ref.shape[1]
    place = place_paired if shards == 4 else place_blocks
    place(*blocks, weights_ref)
    down, up = weights_ref[:rank, :], weights_ref[rank:, :]
    query_low = dot_nt(down, query_in_ref[...]).astype(BF16)
    message_ref[HEAD_ROWS:, slots : slots + q_dev] = query_low.astype(F32) * low_scale_ref[0:1, :]
    passage_low = dot_nt(down, passage_in_ref[...]).astype(BF16)
    passage_low_ref[...] = passage_low.astype(F32) * row_ref[0:1, :]
    base = dot_nt(up, embed_ref[...])
    base_ref[...] = base
    message_ref[:HEAD_ROWS, :] = head_ref[...]
    message_ref[HEAD_ROWS:, :slots] = dot_pieces(dot_nt, base, onehot_ref[...])
    unused = jnp.zeros((rank, queries - slots - q_dev), F32)
    message_ref[HEAD_ROWS:, slots + q_dev :] = unused


def score_kernel(group, *refs):
    blocks = refs[:group]
    embed_ref, side_ref, positive_ref = refs[group : group + 3]
    query_ref, weight_ref, dots_ref, onehot_ref, head_ref, coded_ref = refs[group + 3 :]
    rows, width = embed_ref.shape
    queries = query_ref.shape[0]
    q_dev = queries // group
    negatives = (blocks[0].shape[1] - width) // 2
    slots = group * CAP
    me = lax.axis_index("dp")
    chunk = min(width, 1024)
    for k in range(group):
        start = pl.multiple_of((me ^ k) * q_dev, q_dev)
        inverse = inverse_length(blocks[k], width)
        for at in range(0, width, chunk):
            part = blocks[k][:, at : at + chunk].astype(F32)
            query_ref[pl.ds(start, q_dev), at : at + chunk] = (part * inverse).astype(BF16)
        coded = blocks[k][:, width:].astype(F32)
        coded_ref[pl.ds(start, q_dev), :] = coded
    dots = dot_nt(embed_ref[...], query_ref[...])
    dots_ref[...] = dots
    scores = dots / SOFTMAX_HEAT

    coded = coded_ref[...].T
    ids = coded[:negatives] * float(ID_BASE) + coded[negatives:]
    home = jnp.broadcast_to(side_ref[:, 1:2], (rows, queries))
    count = jnp.zeros((rows, queries), F32)
    for j in range(negatives):
        count = count + jnp.where(ids[j : j + 1, :] == home, 1.0, 0.0)
    members = iota((slots, queries), 0) // CAP == iota((slots, queries), 1) // q_dev
    marked = dot_nt(members.astype(BF16), count.astype(BF16)) > 0.0
    before = (iota((rows, rows), 0) <= iota((rows, rows), 1)).astype(BF16)
    rank_in = dot_nn(marked.astype(F32).astype(BF16), before)
    wanted = (iota((slots, rows), 0) % CAP + 1).astype(F32)
    onehot = jnp.where(marked & (rank_in == wanted), 1.0, 0.0)
    onehot_ref[...] = onehot

    own = iota((rows, queries), 1) // q_dev == me
    count = count + jnp.where(own & (positive_ref[...] == iota((rows, queries), 0)), 1.0, 0.0)
    named = count > 0.0
    top = jnp.max(jnp.where(named, scores, LOWEST), axis=0, keepdims=True)
    weight = count * jnp.exp(jnp.where(named, scores - top, LOWEST))
    weight_ref[...] = weight
    total = jnp.sum(weight, axis=0, keepdims=True)
    dot_total = jnp.sum(weight * dots, axis=0, keepdims=True)
    slot_weight = dot_pieces(dot_nn, onehot, weight)
    tail_row = iota((HEAD_ROWS - CAP, queries), 0)
    tail = jnp.where(tail_row == 0, top, jnp.where(tail_row == 1, total, dot_total))
    lane_group = iota((CAP, queries), 1) // q_dev
    compact = jnp.zeros((CAP, queries), F32)
    for peer in range(group):
        part = slot_weight[peer * CAP : (peer + 1) * CAP]
        compact = jnp.where(lane_group == peer, part, compact)
    head_ref[:CAP, :] = compact
    head_ref[CAP:, :] = tail


def request_kernel(group, *refs):
    (
        embed_ref,
        onehot_ref,
        query_ref,
        weights_ref,
        low_ref,
        base_ref,
        weight_ref,
        positive_ref,
        back_ref,
        local_ref,
        target_ref,
    ) = refs[:11]
    blocks = refs[11:]
    width = embed_ref.shape[1]
    rows, queries = weight_ref.shape
    me = lax.axis_index("dp")
    onehot = [
        onehot_ref[pl.ds(pl.multiple_of((me ^ k) * CAP, CAP), CAP), :] for k in range(group)
    ]
    onehot = jnp.concatenate(onehot, axis=0).astype(BF16)
    chunk = min(width, 1024)
    for at in range(0, width, chunk):
        part = dot_nn(onehot, embed_ref[:, at : at + chunk]).astype(BF16)
        for i, block in enumerate(blocks):
            block[:, at : at + chunk] = part[2 * i * CAP : 2 * (i + 1) * CAP]
    back_ref[...] = dot_nt(weights_ref[weights_ref.shape[0] // 2 :, :], query_ref[...])
    both = jnp.concatenate([low_ref[...], base_ref[...]], axis=0)
    local_ref[...] = dot_pieces(dot_nn, both, weight_ref[...])
    target = own_target(positive_ref, rows, queries, queries // group, me)
    target_ref[...] = dot_pieces(dot_nn, both, target)


def forward_kernel(*refs):
    out_ref = refs[-1]
    for i, ref in enumerate(refs[:-1]):
        out_ref[i * CAP : (i + 1) * CAP, :] = ref[CAP:, :]


def message_parts(near_ref, far_ref, group):
    rows = near_ref.shape[0] // (group // 2)
    return [((near_ref, far_ref)[k % 2], k // 2 * rows) for k in range(group)]


def combine(parts):
    tops = [ref[at + TOP_ROW : at + TOP_ROW + 1, :] for ref, at in parts]
    sums = [ref[at + SUM_ROW : at + SUM_ROW + 1, :] for ref, at in parts]
    top = functools.reduce(jnp.maximum, tops)
    scales = [jnp.exp(t - top) for t in tops]
    inverse_total = 1.0 / sum(t * s for t, s in zip(scales, sums))
    return [scale * inverse_total for scale in scales]


def own_target(positive_ref, rows, queries, q_dev, me):
    own = iota((rows, queries), 1) // q_dev == me
    return jnp.where(own & (positive_ref[...] == iota((rows, queries), 0)), 1.0, 0.0)


def terms_kernel(group, shards, near_ref, far_ref, *refs):
    parts = message_parts(near_ref, far_ref, group)
    (
        weight_ref,
        dots_ref,
        positive_ref,
        query_ref,
        embed_ref,
        back_query_ref,
        back_passage_ref,
        passage_low_ref,
        row_ref,
        own_ref,
        passage_in_ref,
        query_in_ref,
        local_ref,
        target_ref,
    ) = refs[:14]
    final_ref = refs[14]
    blocks = refs[15 : 15 + shards]
    (sum_ref,) = refs[15 + shards :]
    rows, queries = weight_ref.shape
    q_dev = queries // group
    rank = passage_low_ref.shape[0]
    width = query_ref.shape[1]
    me = lax.axis_index("dp")

    scales = combine(parts)
    target = own_target(positive_ref, rows, queries, q_dev, me)
    weight = (weight_ref[...] * scales[0] - target) / SOFTMAX_HEAT
    final_ref[...] = weight
    dots = dots_ref[...]
    ones = jnp.ones((8, queries), F32)
    inner = dot_pieces(dot_nt, ones, weight * dots)[0:1, :]

    inner_query = -jnp.sum(target * dots, axis=0, keepdims=True)
    own_dots = near_ref[DOT_ROW : DOT_ROW + 1, :]
    share = (scales[0] * own_dots + inner_query) / SOFTMAX_HEAT
    slots = group * CAP
    bases, query_low = [], []
    for (ref, at), scale in zip(parts, scales):
        inner_query = inner_query + scale * ref[at + DOT_ROW : at + DOT_ROW + 1, :]
        bases.append(ref[at + HEAD_ROWS : at + HEAD_ROWS + rank, :])
        query_low.append(ref[at + HEAD_ROWS : at + HEAD_ROWS + rank, :])
    low_total = jnp.zeros((rank, queries), F32)
    lane_group = iota((rank, queries), 1) // q_dev
    for k, rows_at in enumerate(query_low):
        shift = lax.rem((me ^ k) * q_dev + queries - slots, queries)
        rolled = pltpu.roll(rows_at, shift, 1)
        low_total = low_total + jnp.where(lane_group == (me ^ k), rolled, 0.0)
    query_low = low_total
    shift = lax.rem(queries - me * CAP, queries)
    bases = pltpu.roll(jnp.concatenate(bases[1:], axis=0), shift, 1)[:, :CAP]
    far_base = [bases[k * rank : (k + 1) * rank] for k in range(group - 1)]
    far_weight = [
        ref[at : at + CAP, :] * (scale / SOFTMAX_HEAT)
        for (ref, at), scale in zip(parts[1:], scales[1:])
    ]
    inner_query = inner_query / SOFTMAX_HEAT

    passage_low = passage_low_ref[...]
    local = (local_ref[...] * scales[0] - target_ref[...]) / SOFTMAX_HEAT
    from_query = local[:rank] - query_low * share
    from_passage = dot_pieces(dot_nt, query_low, weight) - passage_low * inner
    query_parts = jnp.concatenate(split_two(from_query), axis=0)
    passage_parts = jnp.concatenate(split_two(from_passage), axis=0)

    back_passage = dot_pieces(dot_nt, back_query_ref[...], weight)
    back_passage = (back_passage - back_passage_ref[...] * inner) * row_ref[0:1, :]
    back_passage = back_passage.astype(BF16)
    back_query = local[rank:] + dot_pieces(
        dot_nn, jnp.concatenate(far_base, axis=1), jnp.concatenate(far_weight, axis=0)
    )
    back_query = (back_query - back_query_ref[...] * inner_query) * own_ref[0:1, :]
    pick = (iota((q_dev, queries), 1) == iota((q_dev, queries), 0) + me * q_dev).astype(BF16)
    back_query = dot_nt(back_query.astype(BF16), pick).astype(BF16)

    chunk = min(width, 512)
    for at in range(0, width, chunk):
        cols = slice(at, at + chunk)
        both = dot_nn(query_parts, query_ref[:, cols]) + dot_nn(passage_parts, embed_ref[:, cols])
        sum_ref[rank:, cols] = ADAPTER_SCALE * (both[:rank] + both[rank:])
        sum_ref[:rank, cols] = ADAPTER_SCALE * (
            dot_nn(back_passage, passage_in_ref[:, cols])
            + dot_nn(back_query, query_in_ref[:, cols])
        )
    part = width // shards
    home = lax.axis_index("fsdp")
    for k in range(shards):
        start = pl.multiple_of((home ^ k) * part, part)
        blocks[k][...] = sum_ref[:, pl.ds(start, part)].astype(blocks[k].dtype)


def backward(upstream_of, raw_ref, inverse, grad_ref, up_ref):
    rows, width = raw_ref.shape
    chunk = min(width, 512)
    inner = jnp.zeros((rows, 1), F32)
    for at in range(0, width, chunk):
        upstream = upstream_of(at, chunk)
        up_ref[:, at : at + chunk] = upstream
        unit = raw_ref[:, at : at + chunk].astype(F32) * inverse
        inner = inner + jnp.sum(unit * upstream, axis=-1, keepdims=True)
    for at in range(0, width, chunk):
        unit = raw_ref[:, at : at + chunk].astype(F32) * inverse
        grad = (up_ref[:, at : at + chunk] - unit * inner) * inverse
        grad_ref[:, at : at + chunk] = grad.astype(BF16)


def passage_kernel(final_ref, query_ref, raw_ref, side_ref, grad_ref, up_ref):
    high, low = split_two(final_ref[...])

    def upstream_of(at, chunk):
        embed = query_ref[:, at : at + chunk]
        return dot_nn(high, embed) + dot_nn(low, embed)

    backward(upstream_of, raw_ref, side_ref[:, 0:1], grad_ref, up_ref)


def query_kernel(group, near_ref, far_ref, *refs):
    parts = message_parts(near_ref, far_ref, group)
    near = refs[: group // 2 - 1]
    forwarded_ref, final_ref, embed_ref, raw_ref, grad_ref, up_ref = refs[group // 2 - 1 :]
    q_dev, width = raw_ref.shape
    queries = final_ref.shape[1]
    me = lax.axis_index("dp")
    scales = combine(parts)
    pick = (iota((q_dev, queries), 1) == iota((q_dev, queries), 0) + me * q_dev).astype(F32)
    far = [
        ref[at : at + CAP, :] * (scale / SOFTMAX_HEAT) for (ref, at), scale in zip(parts, scales)
    ]
    far = far[2::2] + far[1::2] + [jnp.zeros((CAP, queries), F32)]
    own_parts = split_two(dot_pieces(dot_nt, pick, final_ref[...]))
    far_parts = split_two(dot_pieces(dot_nt, pick, jnp.concatenate(far, axis=0)))
    own_parts = jnp.concatenate(own_parts, axis=0)
    far_parts = jnp.concatenate(far_parts, axis=0)

    def upstream_of(at, chunk):
        rows = [ref[:, at : at + chunk].astype(F32)[:CAP] for ref in near]
        rows.append(forwarded_ref[:, at : at + chunk].astype(F32))
        rows.append(jnp.zeros((CAP, chunk), F32))
        both = dot_nn(own_parts, embed_ref[:, at : at + chunk])
        both = both + dot_nn(far_parts, jnp.concatenate(rows, axis=0).astype(BF16))
        return both[:q_dev] + both[q_dev:]

    backward(upstream_of, raw_ref, inverse_length(raw_ref, width), grad_ref, up_ref)


def sum_kernel(*refs):
    total = refs[0][...].astype(F32)
    for ref in refs[1:-1]:
        total = total + ref[...].astype(F32)
    refs[-1][...] = total


def sum_two_kernel(left_ref, right_ref, sent_ref):
    sent_ref[...] = (left_ref[...] + right_ref[...]).astype(BF16)


def sum_split_kernel(*refs):
    terms = [ref[...].astype(F32) for ref in refs[:-2]]
    while len(terms) > 1:
        terms = [a + b for a, b in zip(terms[::2], terms[1::2])]
    rank = refs[-1].shape[0]
    refs[-2][...] = terms[0][:rank]
    refs[-1][...] = terms[0][rank:]


def exchange(values, axis, k):
    size = lax.axis_size(axis)
    return lax.ppermute(values, axis, [(i, i ^ k) for i in range(size)])


def core_step(values, even_step, odd_step):
    outer, inner = lax.axis_size("dp"), lax.axis_size("fsdp")
    pairs = []
    for d in range(outer):
        step = odd_step if d % 2 else even_step
        pairs += [(d * inner + f, d * inner + (f ^ step)) for f in range(inner)]
    return lax.ppermute(values, ("dp", "fsdp"), pairs)


def per_device(
    query_pooled_states,
    passage_pooled_states,
    query_attention_output,
    passage_attention_output,
    positive_passage_row,
    hard_negative_ids,
    passage_home_row,
    adapter_down_weight,
    adapter_up_weight,
):
    group = lax.axis_size("dp")
    shards = lax.axis_size("fsdp")
    query_raw = query_pooled_states[0]
    passage_raw = passage_pooled_states[0]
    query_in = query_attention_output[0]
    passage_in = passage_attention_output[0]
    ids = hard_negative_ids[0]
    q_dev, width = query_raw.shape
    p_dev = passage_raw.shape[0]
    rank, part = adapter_down_weight.shape
    queries = group * q_dev
    slots = group * CAP
    work = 2 * p_dev * width

    packed, adapter, half, positive_row = run(
        front_kernel,
        (
            shape_of((q_dev, width + 2 * ids.shape[1]), BF16),
            shape_of((2 * rank, part), BF16),
            shape_of((rank, part), BF16),
            shape_of((1, queries), jnp.int32),
        ),
        (query_raw, ids, adapter_down_weight, adapter_up_weight, positive_passage_row),
        1,
        [
            pltpu.VMEM(ids.shape, jnp.int32),
            pltpu.VMEM(positive_passage_row.shape, jnp.int32),
            pltpu.SemaphoreType.DMA((5,)),
        ],
        in_hbm=True,
    )
    embed, side, side_row, own_side, low_scale = run(
        passage_norm_kernel,
        (
            shape_of((p_dev, width), BF16),
            shape_of((p_dev, 128), F32),
            shape_of((8, p_dev), F32),
            shape_of((8, queries), F32),
            shape_of((8, q_dev), F32),
        ),
        (query_raw, passage_raw, passage_home_row),
        work,
        [
            pltpu.VMEM(passage_raw.shape, BF16),
            pltpu.VMEM(passage_home_row.shape, jnp.int32),
            pltpu.VMEM(query_raw.shape, BF16),
            pltpu.SemaphoreType.DMA((2 + PASSAGE_CHUNKS,)),
        ],
        in_hbm=True,
    )
    blocks = {0: packed}
    for k in range(2, group, 2):
        blocks[k] = exchange(packed, "dp", k)
    blocks[1] = exchange(packed, "dp", 1)
    for k in range(2, group, 2):
        blocks[k], embed = lax.optimization_barrier((blocks[k], embed))
        blocks[k ^ 1] = exchange(blocks[k], "dp", 1)
    if shards == 4:
        half_block = exchange(half, "fsdp", 3)
        whole_block = core_step(adapter, 1, 2)
        adapter_near = run(
            join_kernel,
            (shape_of((3 * rank, part), BF16),),
            (whole_block, half_block),
            1,
        )[0]
        adapter_blocks = [adapter, adapter_near, exchange(adapter_near, "dp", 1)]
    else:
        adapter_blocks = [adapter] + [exchange(adapter, "fsdp", k) for k in range(1, shards)]
    query_embed, weight, dots, onehot, head = run(
        functools.partial(score_kernel, group),
        (
            shape_of((queries, width), BF16),
            shape_of((p_dev, queries), F32),
            shape_of((p_dev, queries), F32),
            shape_of((slots, p_dev), F32),
            shape_of((HEAD_ROWS, queries), F32),
        ),
        (
            *[blocks[k] for k in range(group)],
            embed,
            side,
            positive_row,
        ),
        work * queries,
        [pltpu.VMEM((queries, 2 * ids.shape[1]), F32)],
    )
    adapter_full, passage_low, message, slot_base = run(
        functools.partial(rank_kernel, shards),
        (
            shape_of((2 * rank, width), BF16),
            shape_of((rank, p_dev), F32),
            shape_of((HEAD_ROWS + rank, queries), F32),
            shape_of((rank, p_dev), F32),
        ),
        (
            *adapter_blocks,
            query_in,
            passage_in,
            embed,
            side_row,
            low_scale,
            onehot,
            head,
        ),
        work * rank,
    )
    stats = [message] + [exchange(message, "dp", k) for k in range(2, group, 2)]
    chips = group // 2
    back_query, local, targets, *row_blocks = run(
        functools.partial(request_kernel, group),
        (
            shape_of((rank, queries), F32),
            shape_of((2 * rank, queries), F32),
            shape_of((2 * rank, queries), F32),
            *[shape_of((2 * CAP, width), BF16)] * chips,
        ),
        (
            embed,
            onehot,
            query_embed,
            adapter_full,
            passage_low,
            slot_base,
            weight,
            positive_row,
        ),
        work * slots,
    )
    stats, row_blocks = lax.optimization_barrier((stats, row_blocks))
    near = [exchange(row_blocks[i], "dp", 2 * i) for i in range(1, chips)]
    near_stats = stack(*stats)
    far_stats = exchange(near_stats, "dp", 1)
    final, *terms = run(
        functools.partial(terms_kernel, group, shards),
        (
            shape_of((p_dev, queries), F32),
            shape_of((2 * rank, part), F32),
            *[shape_of((2 * rank, part), BF16)] * (shards - 1),
        ),
        (
            near_stats,
            far_stats,
            weight,
            dots,
            positive_row,
            query_embed,
            embed,
            back_query,
            slot_base,
            passage_low,
            side_row,
            own_side,
            passage_in,
            query_in,
            local,
            targets,
        ),
        work * rank * 4,
        [pltpu.VMEM((2 * rank, width), F32)],
    )
    arrived = [exchange(terms[k], "fsdp", k) for k in range(1, shards)]
    final, near[0] = lax.optimization_barrier((final, near[0]))
    grad_passage = run(
        passage_kernel,
        (shape_of((p_dev, width), BF16),),
        (final, query_embed, passage_raw, side),
        2 * work * queries,
        [pltpu.VMEM((p_dev, width), F32)],
    )[0]
    terms[0], grad_passage = lax.optimization_barrier((terms[0], grad_passage))
    total = run(sum_kernel, (shape_of((2 * rank, part), F32),), (terms[0], *arrived), 1)[0]
    total, near = lax.optimization_barrier((total, near))
    to_sibling = run(
        forward_kernel,
        (shape_of((group // 2 * CAP, width), BF16),),
        (row_blocks[0], *near),
        1,
    )[0]
    forwarded = exchange(to_sibling, "dp", 1)
    sent = run(
        sum_two_kernel,
        (shape_of((2 * rank, part), BF16),),
        (total, exchange(total, "dp", 1)),
        1,
    )[0]
    arrived = [exchange(sent, "dp", k) for k in range(2, group, 2)]
    grad_query = run(
        functools.partial(query_kernel, group),
        (shape_of((q_dev, width), BF16),),
        (near_stats, far_stats, *near, forwarded, final, embed, query_raw),
        4 * q_dev * width * (p_dev + slots),
        [pltpu.VMEM((q_dev, width), F32)],
    )[0]
    sent, grad_query = lax.optimization_barrier((sent, grad_query))
    down_total, up_total = run(
        sum_split_kernel, (shape_of((rank, part), F32),) * 2, (sent, *arrived), 1
    )
    return (grad_query[None], grad_passage[None], down_total, up_total)


def solution(mesh):
    in_specs = (
        P("fsdp", "dp", None),
        P("fsdp", "dp", None),
        P("fsdp", "dp", None),
        P("fsdp", "dp", None),
        P("fsdp", "dp"),
        P("fsdp", "dp", None),
        P("fsdp", None),
        P(None, "fsdp"),
        P(None, "fsdp"),
    )
    out_specs = (P("fsdp", "dp", None), P("fsdp", "dp", None), P(None, "fsdp"), P(None, "fsdp"))
    return jax.shard_map(
        per_device, mesh=mesh, in_specs=in_specs, out_specs=out_specs, check_vma=False
    )
```

```python
import functools

import jax
import jax.numpy as jnp
from jax import lax
from jax.experimental import pallas as pl
from jax.experimental.pallas import tpu as pltpu
from jax.sharding import PartitionSpec as P

CAP = 8
SOFTMAX_HEAT = 0.01
ADAPTER_SCALE = 2.0
EPSILON = 1e-06
LOWEST = -1e30
ID_BASE = 256
TOP_ROW, SUM_ROW, DOT_ROW, HEAD_ROWS = 8, 9, 10, 16
VMEM_BYTES = 16 * 1024 * 1024
PASSAGE_CHUNKS = 4
F32 = jnp.float32
BF16 = jnp.bfloat16


def dot_nn(a, b, precision=None):
    return lax.dot_general(
        a, b, (((1,), (0,)), ((), ())), precision=precision, preferred_element_type=F32
    )


def dot_nt(a, b, precision=None):
    return lax.dot_general(
        a, b, (((1,), (1,)), ((), ())), precision=precision, preferred_element_type=F32
    )


def split_two(values):
    high = values.astype(BF16)
    low = (values - high.astype(F32)).astype(BF16)
    return high, low


def dot_pieces(dot, a, b):
    rows = a.shape[0]
    a_high, a_low = split_two(a)
    b_high, b_low = split_two(b)
    both = dot(jnp.concatenate([a_high, a_low], axis=0), b_high)
    return both[:rows] + both[rows:] + dot(a_high, b_low)


def iota(shape, dim):
    return lax.broadcasted_iota(jnp.int32, shape, dim)


def shape_of(dims, kind):
    return jax.ShapeDtypeStruct(dims, kind)


def run(body, out_shape, args, flops, scratch=(), in_hbm=False):
    grant = VMEM_BYTES * max(1, size_ratio(args))
    if in_hbm:
        args = [pltpu.with_memory_space_constraint(a, pltpu.HBM) for a in args]
    vmem = pl.BlockSpec(memory_space=pltpu.VMEM)
    hbm = pl.BlockSpec(memory_space=pltpu.HBM)
    moved = sum(a.size * a.dtype.itemsize for a in (*args, *out_shape))
    return pl.pallas_call(
        body,
        out_shape=out_shape,
        in_specs=[hbm if in_hbm else vmem] * len(args),
        out_specs=tuple(vmem for _ in out_shape),
        scratch_shapes=list(scratch),
        compiler_params=pltpu.CompilerParams(vmem_limit_bytes=grant),
        cost_estimate=pl.CostEstimate(flops=flops, bytes_accessed=moved, transcendentals=0),
    )(*args)


def size_ratio(args):
    moved = sum(a.size * a.dtype.itemsize for a in args)
    return -(-moved * 3 // VMEM_BYTES)


def inverse_length(raw_ref, width):
    chunk = min(width, 512)
    total = jnp.zeros((raw_ref.shape[0], 1), F32)
    for at in range(0, width, chunk):
        part = raw_ref[:, at : at + chunk].astype(F32)
        total = total + jnp.sum(part * part, axis=-1, keepdims=True)
    return 1.0 / jnp.sqrt(total + EPSILON)


def front_kernel(
    query_ref,
    ids_ref,
    down_ref,
    up_ref,
    positive_ref,
    out_ref,
    adapter_ref,
    half_ref,
    tiled_ref,
    ids_here,
    positive_here,
    sems,
):
    width = query_ref.shape[1]
    rank = down_ref.shape[0]
    me = lax.axis_index("dp")
    pairs = (
        (ids_ref, ids_here),
        (query_ref, out_ref.at[:, pl.ds(0, width)]),
        (positive_ref, positive_here),
        (down_ref, adapter_ref.at[pl.ds(0, rank), :]),
        (up_ref, adapter_ref.at[pl.ds(rank, rank), :]),
    )
    copies = [pltpu.make_async_copy(a, b, sems.at[i]) for i, (a, b) in enumerate(pairs)]
    for copy in copies:
        copy.start()
    copies[0].wait()
    ids = ids_here[...]
    coded = jnp.concatenate([ids // ID_BASE, ids % ID_BASE], axis=1)
    out_ref[:, width:] = coded.astype(F32).astype(BF16)
    copies[2].wait()
    q_dev = positive_here.shape[1]
    for at in range(0, tiled_ref.shape[1], q_dev):
        tiled_ref[:, at : at + q_dev] = positive_here[...]
    copies[3].wait()
    copies[4].wait()

    @pl.when(me % 2 == 0)
    def _():
        half_ref[...] = adapter_ref[:rank, :]

    @pl.when(me % 2 == 1)
    def _():
        half_ref[...] = adapter_ref[rank:, :]

    copies[1].wait()


def passage_norm_kernel(
    query_ref,
    passage_ref,
    home_ref,
    embed_ref,
    side_ref,
    row_ref,
    own_ref,
    low_scale_ref,
    passage_here,
    home_here,
    query_here,
    sems,
):
    rows, width = passage_ref.shape
    total = home_ref.shape[1]
    me = lax.axis_index("dp")
    part = rows // PASSAGE_CHUNKS
    home_copy = pltpu.make_async_copy(home_ref, home_here, sems.at[0])
    home_copy.start()
    query_copy = pltpu.make_async_copy(query_ref, query_here, sems.at[1 + PASSAGE_CHUNKS])
    query_copy.start()
    passage_copies = []
    for c in range(PASSAGE_CHUNKS):
        here = pl.ds(c * part, part)
        passage_copies.append(
            pltpu.make_async_copy(
                passage_ref.at[here, :], passage_here.at[here, :], sems.at[1 + c]
            )
        )
        passage_copies[c].start()

    home_copy.wait()
    row_id = iota((rows, total), 0) + me * rows
    number = iota((rows, total), 1)
    home = jnp.where(home_here[...] == row_id, number, 0).astype(F32)
    home = jnp.sum(home, axis=1, keepdims=True)
    query_copy.wait()
    q_dev = query_here.shape[0]
    queries = own_ref.shape[1]
    inverse = inverse_length(query_here, width)
    place = iota((q_dev, queries), 1) == iota((q_dev, queries), 0) + me * q_dev
    own = jnp.sum(jnp.where(place, inverse, 0.0), axis=0, keepdims=True)
    own_ref[...] = jnp.broadcast_to(own, own_ref.shape)
    same = iota((q_dev, q_dev), 0) == iota((q_dev, q_dev), 1)
    low_scale = jnp.sum(jnp.where(same, inverse, 0.0), axis=0, keepdims=True)
    low_scale_ref[...] = jnp.broadcast_to(low_scale, low_scale_ref.shape)

    chunk = min(width, 512)
    inverses = []
    for c in range(PASSAGE_CHUNKS):
        passage_copies[c].wait()
        here = slice(c * part, (c + 1) * part)
        inverse = inverse_length(passage_here.at[here, :], width)
        for at in range(0, width, chunk):
            values = passage_here[here, at : at + chunk].astype(F32)
            embed_ref[here, at : at + chunk] = (values * inverse).astype(BF16)
        inverses.append(inverse)
    inverse = jnp.concatenate(inverses, axis=0)
    side_ref[...] = jnp.where(iota(side_ref.shape, 1) == 0, inverse, home)
    row_ref[...] = jnp.broadcast_to(inverse, (rows, rows)).T[: row_ref.shape[0]]


def stack_kernel(*refs):
    out_ref = refs[-1]
    rows = refs[0].shape[0]
    for i, ref in enumerate(refs[:-1]):
        out_ref[i * rows : (i + 1) * rows, :] = ref[...]


def stack(*parts):
    rows, cols = parts[0].shape
    return run(stack_kernel, (shape_of((len(parts) * rows, cols), parts[0].dtype),), parts, 1)[0]


def join_kernel(first_ref, second_ref, out_ref):
    rows = first_ref.shape[0]
    out_ref[:rows, :] = first_ref[...]
    out_ref[rows:, :] = second_ref[...]


def place_paired(own_ref, near_ref, far_ref, weights_ref):
    rank, part = own_ref.shape[0] // 2, own_ref.shape[1]
    me = lax.axis_index("fsdp")
    core = lax.axis_index("dp") % 2

    def columns(k):
        return pl.ds(pl.multiple_of((me ^ k) * part, part), part)

    def place(even_ref, odd_ref):
        weights_ref[:, columns(1)] = even_ref[: 2 * rank, :]
        weights_ref[:, columns(2)] = odd_ref[: 2 * rank, :]
        weights_ref[:rank, columns(3)] = even_ref[2 * rank :, :]
        weights_ref[rank:, columns(3)] = odd_ref[2 * rank :, :]

    weights_ref[:, columns(0)] = own_ref[...]
    pl.when(core == 0)(functools.partial(place, near_ref, far_ref))
    pl.when(core == 1)(functools.partial(place, far_ref, near_ref))


def place_blocks(*refs):
    part = refs[0].shape[1]
    me = lax.axis_index("fsdp")
    for k, ref in enumerate(refs[:-1]):
        refs[-1][:, pl.ds(pl.multiple_of((me ^ k) * part, part), part)] = ref[...]


def rank_kernel(shards, *refs):
    blocks = refs[:-11]
    query_in_ref, passage_in_ref, embed_ref, row_ref, low_scale_ref = refs[-11:-6]
    onehot_ref, head_ref = refs[-6:-4]
    weights_ref, passage_low_ref, message_ref, base_ref = refs[-4:]
    rank = blocks[0].shape[0] // 2
    q_dev = query_in_ref.shape[0]
    slots = onehot_ref.shape[0]
    queries = message_ref.shape[1]
    place = place_paired if shards == 4 else place_blocks
    place(*blocks, weights_ref)
    down, up = weights_ref[:rank, :], weights_ref[rank:, :]
    query_low = dot_nt(down, query_in_ref[...]).astype(BF16)
    message_ref[HEAD_ROWS:, slots : slots + q_dev] = query_low.astype(F32) * low_scale_ref[0:1, :]
    passage_low = dot_nt(down, passage_in_ref[...]).astype(BF16)
    passage_low_ref[...] = passage_low.astype(F32) * row_ref[0:1, :]
    base = dot_nt(up, embed_ref[...])
    base_ref[...] = base
    message_ref[:HEAD_ROWS, :] = head_ref[...]
    message_ref[HEAD_ROWS:, :slots] = dot_pieces(dot_nt, base, onehot_ref[...])
    unused = jnp.zeros((rank, queries - slots - q_dev), F32)
    message_ref[HEAD_ROWS:, slots + q_dev :] = unused


def score_kernel(group, *refs):
    blocks = refs[:group]
    embed_ref, side_ref, positive_ref = refs[group : group + 3]
    query_ref, weight_ref, dots_ref, onehot_ref, head_ref, coded_ref = refs[group + 3 :]
    rows, width = embed_ref.shape
    queries = query_ref.shape[0]
    q_dev = queries // group
    negatives = (blocks[0].shape[1] - width) // 2
    slots = group * CAP
    me = lax.axis_index("dp")
    chunk = min(width, 1024)
    for k in range(group):
        start = pl.multiple_of((me ^ k) * q_dev, q_dev)
        inverse = inverse_length(blocks[k], width)
        for at in range(0, width, chunk):
            part = blocks[k][:, at : at + chunk].astype(F32)
            query_ref[pl.ds(start, q_dev), at : at + chunk] = (part * inverse).astype(BF16)
        coded = blocks[k][:, width:].astype(F32)
        coded_ref[pl.ds(start, q_dev), :] = coded
    dots = dot_nt(embed_ref[...], query_ref[...])
    dots_ref[...] = dots
    scores = dots / SOFTMAX_HEAT

    coded = coded_ref[...].T
    ids = coded[:negatives] * float(ID_BASE) + coded[negatives:]
    home = jnp.broadcast_to(side_ref[:, 1:2], (rows, queries))
    count = jnp.zeros((rows, queries), F32)
    for j in range(negatives):
        count = count + jnp.where(ids[j : j + 1, :] == home, 1.0, 0.0)
    members = iota((slots, queries), 0) // CAP == iota((slots, queries), 1) // q_dev
    marked = dot_nt(members.astype(BF16), count.astype(BF16)) > 0.0
    before = (iota((rows, rows), 0) <= iota((rows, rows), 1)).astype(BF16)
    rank_in = dot_nn(marked.astype(F32).astype(BF16), before)
    wanted = (iota((slots, rows), 0) % CAP + 1).astype(F32)
    onehot = jnp.where(marked & (rank_in == wanted), 1.0, 0.0)
    onehot_ref[...] = onehot

    own = iota((rows, queries), 1) // q_dev == me
    count = count + jnp.where(own & (positive_ref[...] == iota((rows, queries), 0)), 1.0, 0.0)
    named = count > 0.0
    top = jnp.max(jnp.where(named, scores, LOWEST), axis=0, keepdims=True)
    weight = count * jnp.exp(jnp.where(named, scores - top, LOWEST))
    weight_ref[...] = weight
    total = jnp.sum(weight, axis=0, keepdims=True)
    dot_total = jnp.sum(weight * dots, axis=0, keepdims=True)
    slot_weight = dot_pieces(dot_nn, onehot, weight)
    tail_row = iota((HEAD_ROWS - CAP, queries), 0)
    tail = jnp.where(tail_row == 0, top, jnp.where(tail_row == 1, total, dot_total))
    lane_group = iota((CAP, queries), 1) // q_dev
    compact = jnp.zeros((CAP, queries), F32)
    for peer in range(group):
        part = slot_weight[peer * CAP : (peer + 1) * CAP]
        compact = jnp.where(lane_group == peer, part, compact)
    head_ref[:CAP, :] = compact
    head_ref[CAP:, :] = tail


def request_kernel(group, *refs):
    (
        embed_ref,
        onehot_ref,
        query_ref,
        weights_ref,
        low_ref,
        base_ref,
        weight_ref,
        positive_ref,
        back_ref,
        local_ref,
        target_ref,
    ) = refs[:11]
    blocks = refs[11:]
    width = embed_ref.shape[1]
    rows, queries = weight_ref.shape
    me = lax.axis_index("dp")
    onehot = [
        onehot_ref[pl.ds(pl.multiple_of((me ^ k) * CAP, CAP), CAP), :] for k in range(group)
    ]
    onehot = jnp.concatenate(onehot, axis=0).astype(BF16)
    chunk = min(width, 1024)
    for at in range(0, width, chunk):
        part = dot_nn(onehot, embed_ref[:, at : at + chunk]).astype(BF16)
        for i, block in enumerate(blocks):
            block[:, at : at + chunk] = part[2 * i * CAP : 2 * (i + 1) * CAP]
    back_ref[...] = dot_nt(weights_ref[weights_ref.shape[0] // 2 :, :], query_ref[...])
    both = jnp.concatenate([low_ref[...], base_ref[...]], axis=0)
    local_ref[...] = dot_pieces(dot_nn, both, weight_ref[...])
    target = own_target(positive_ref, rows, queries, queries // group, me)
    target_ref[...] = dot_pieces(dot_nn, both, target)


def forward_kernel(*refs):
    out_ref = refs[-1]
    for i, ref in enumerate(refs[:-1]):
        out_ref[i * CAP : (i + 1) * CAP, :] = ref[CAP:, :]


def message_parts(near_ref, far_ref, group):
    rows = near_ref.shape[0] // (group // 2)
    return [((near_ref, far_ref)[k % 2], k // 2 * rows) for k in range(group)]


def combine(parts):
    tops = [ref[at + TOP_ROW : at + TOP_ROW + 1, :] for ref, at in parts]
    sums = [ref[at + SUM_ROW : at + SUM_ROW + 1, :] for ref, at in parts]
    top = functools.reduce(jnp.maximum, tops)
    scales = [jnp.exp(t - top) for t in tops]
    inverse_total = 1.0 / sum(t * s for t, s in zip(scales, sums))
    return [scale * inverse_total for scale in scales]


def own_target(positive_ref, rows, queries, q_dev, me):
    own = iota((rows, queries), 1) // q_dev == me
    return jnp.where(own & (positive_ref[...] == iota((rows, queries), 0)), 1.0, 0.0)


def terms_kernel(group, near_ref, far_ref, *refs):
    parts = message_parts(near_ref, far_ref, group)
    (
        weight_ref,
        dots_ref,
        positive_ref,
        query_ref,
        embed_ref,
        back_query_ref,
        back_passage_ref,
        passage_low_ref,
        row_ref,
        own_ref,
        passage_in_ref,
        query_in_ref,
        local_ref,
        target_ref,
    ) = refs[:14]
    final_ref, mine_ref, theirs_ref, sum_ref = refs[14:]
    rows, queries = weight_ref.shape
    q_dev = queries // group
    rank = passage_low_ref.shape[0]
    width = query_ref.shape[1]
    me = lax.axis_index("dp")

    scales = combine(parts)
    target = own_target(positive_ref, rows, queries, q_dev, me)
    weight = (weight_ref[...] * scales[0] - target) / SOFTMAX_HEAT
    final_ref[...] = weight
    dots = dots_ref[...]
    ones = jnp.ones((8, queries), F32)
    inner = dot_pieces(dot_nt, ones, weight * dots)[0:1, :]

    inner_query = -jnp.sum(target * dots, axis=0, keepdims=True)
    own_dots = near_ref[DOT_ROW : DOT_ROW + 1, :]
    share = (scales[0] * own_dots + inner_query) / SOFTMAX_HEAT
    slots = group * CAP
    bases, query_low = [], []
    for (ref, at), scale in zip(parts, scales):
        inner_query = inner_query + scale * ref[at + DOT_ROW : at + DOT_ROW + 1, :]
        bases.append(ref[at + HEAD_ROWS : at + HEAD_ROWS + rank, :])
        query_low.append(ref[at + HEAD_ROWS : at + HEAD_ROWS + rank, :])
    low_total = jnp.zeros((rank, queries), F32)
    lane_group = iota((rank, queries), 1) // q_dev
    for k, rows_at in enumerate(query_low):
        shift = lax.rem((me ^ k) * q_dev + queries - slots, queries)
        rolled = pltpu.roll(rows_at, shift, 1)
        low_total = low_total + jnp.where(lane_group == (me ^ k), rolled, 0.0)
    query_low = low_total
    shift = lax.rem(queries - me * CAP, queries)
    bases = pltpu.roll(jnp.concatenate(bases[1:], axis=0), shift, 1)[:, :CAP]
    far_base = [bases[k * rank : (k + 1) * rank] for k in range(group - 1)]
    far_weight = [
        ref[at : at + CAP, :] * (scale / SOFTMAX_HEAT)
        for (ref, at), scale in zip(parts[1:], scales[1:])
    ]
    inner_query = inner_query / SOFTMAX_HEAT

    passage_low = passage_low_ref[...]
    local = (local_ref[...] * scales[0] - target_ref[...]) / SOFTMAX_HEAT
    from_query = local[:rank] - query_low * share
    from_passage = dot_pieces(dot_nt, query_low, weight) - passage_low * inner
    query_parts = jnp.concatenate(split_two(from_query), axis=0)
    passage_parts = jnp.concatenate(split_two(from_passage), axis=0)

    back_passage = dot_pieces(dot_nt, back_query_ref[...], weight)
    back_passage = (back_passage - back_passage_ref[...] * inner) * row_ref[0:1, :]
    back_passage = back_passage.astype(BF16)
    back_query = local[rank:] + dot_pieces(
        dot_nn, jnp.concatenate(far_base, axis=1), jnp.concatenate(far_weight, axis=0)
    )
    back_query = (back_query - back_query_ref[...] * inner_query) * own_ref[0:1, :]
    pick = (iota((q_dev, queries), 1) == iota((q_dev, queries), 0) + me * q_dev).astype(BF16)
    back_query = dot_nt(back_query.astype(BF16), pick).astype(BF16)

    chunk = min(width, 512)
    for at in range(0, width, chunk):
        cols = slice(at, at + chunk)
        both = dot_nn(query_parts, query_ref[:, cols]) + dot_nn(passage_parts, embed_ref[:, cols])
        sum_ref[rank:, cols] = ADAPTER_SCALE * (both[:rank] + both[rank:])
        sum_ref[:rank, cols] = ADAPTER_SCALE * (
            dot_nn(back_passage, passage_in_ref[:, cols])
            + dot_nn(back_query, query_in_ref[:, cols])
        )
    @pl.when(me % 2 == 0)
    def _():
        mine_ref[...] = sum_ref[:rank, :]
        theirs_ref[...] = sum_ref[rank:, :]

    @pl.when(me % 2 == 1)
    def _():
        mine_ref[...] = sum_ref[rank:, :]
        theirs_ref[...] = sum_ref[:rank, :]


def halves_kernel(mine_ref, arrived_ref, *blocks):
    shards = len(blocks)
    part = mine_ref.shape[1] // shards
    home = lax.axis_index("fsdp")
    for k, block in enumerate(blocks):
        cols = pl.ds(pl.multiple_of((home ^ k) * part, part), part)
        block[...] = (mine_ref[:, cols] + arrived_ref[:, cols]).astype(block.dtype)


def backward(upstream_of, raw_ref, inverse, grad_ref, up_ref):
    rows, width = raw_ref.shape
    chunk = min(width, 512)
    inner = jnp.zeros((rows, 1), F32)
    for at in range(0, width, chunk):
        upstream = upstream_of(at, chunk)
        up_ref[:, at : at + chunk] = upstream
        unit = raw_ref[:, at : at + chunk].astype(F32) * inverse
        inner = inner + jnp.sum(unit * upstream, axis=-1, keepdims=True)
    for at in range(0, width, chunk):
        unit = raw_ref[:, at : at + chunk].astype(F32) * inverse
        grad = (up_ref[:, at : at + chunk] - unit * inner) * inverse
        grad_ref[:, at : at + chunk] = grad.astype(BF16)


def passage_kernel(final_ref, query_ref, raw_ref, side_ref, grad_ref, up_ref):
    high, low = split_two(final_ref[...])

    def upstream_of(at, chunk):
        embed = query_ref[:, at : at + chunk]
        return dot_nn(high, embed) + dot_nn(low, embed)

    backward(upstream_of, raw_ref, side_ref[:, 0:1], grad_ref, up_ref)


def query_kernel(group, near_ref, far_ref, *refs):
    parts = message_parts(near_ref, far_ref, group)
    near = refs[: group // 2 - 1]
    forwarded_ref, final_ref, embed_ref, raw_ref, grad_ref, up_ref = refs[group // 2 - 1 :]
    q_dev, width = raw_ref.shape
    queries = final_ref.shape[1]
    me = lax.axis_index("dp")
    scales = combine(parts)
    pick = (iota((q_dev, queries), 1) == iota((q_dev, queries), 0) + me * q_dev).astype(F32)
    far = [
        ref[at : at + CAP, :] * (scale / SOFTMAX_HEAT) for (ref, at), scale in zip(parts, scales)
    ]
    far = far[2::2] + far[1::2] + [jnp.zeros((CAP, queries), F32)]
    own_parts = split_two(dot_pieces(dot_nt, pick, final_ref[...]))
    far_parts = split_two(dot_pieces(dot_nt, pick, jnp.concatenate(far, axis=0)))
    own_parts = jnp.concatenate(own_parts, axis=0)
    far_parts = jnp.concatenate(far_parts, axis=0)

    def upstream_of(at, chunk):
        rows = [ref[:, at : at + chunk].astype(F32)[:CAP] for ref in near]
        rows.append(forwarded_ref[:, at : at + chunk].astype(F32))
        rows.append(jnp.zeros((CAP, chunk), F32))
        both = dot_nn(own_parts, embed_ref[:, at : at + chunk])
        both = both + dot_nn(far_parts, jnp.concatenate(rows, axis=0).astype(BF16))
        return both[:q_dev] + both[q_dev:]

    backward(upstream_of, raw_ref, inverse_length(raw_ref, width), grad_ref, up_ref)


def sum_kernel(*refs):
    total = refs[0][...].astype(F32)
    for ref in refs[1:-1]:
        total = total + ref[...].astype(F32)
    refs[-1][...] = total.astype(refs[-1].dtype)


def pair_sum_kernel(*refs):
    terms = [ref[...].astype(F32) for ref in refs[:-1]]
    while len(terms) > 1:
        terms = [a + b for a, b in zip(terms[::2], terms[1::2])]
    refs[-1][...] = terms[0]


def both_halves_kernel(mine_ref, theirs_ref, down_ref, up_ref):
    core = lax.axis_index("dp") % 2

    @pl.when(core == 0)
    def _():
        down_ref[...] = mine_ref[...]
        up_ref[...] = theirs_ref[...]

    @pl.when(core == 1)
    def _():
        down_ref[...] = theirs_ref[...]
        up_ref[...] = mine_ref[...]


def exchange(values, axis, k):
    size = lax.axis_size(axis)
    return lax.ppermute(values, axis, [(i, i ^ k) for i in range(size)])


def core_step(values, even_step, odd_step):
    outer, inner = lax.axis_size("dp"), lax.axis_size("fsdp")
    pairs = []
    for d in range(outer):
        step = odd_step if d % 2 else even_step
        pairs += [(d * inner + f, d * inner + (f ^ step)) for f in range(inner)]
    return lax.ppermute(values, ("dp", "fsdp"), pairs)


def per_device(
    query_pooled_states,
    passage_pooled_states,
    query_attention_output,
    passage_attention_output,
    positive_passage_row,
    hard_negative_ids,
    passage_home_row,
    adapter_down_weight,
    adapter_up_weight,
):
    group = lax.axis_size("dp")
    shards = lax.axis_size("fsdp")
    query_raw = query_pooled_states[0]
    passage_raw = passage_pooled_states[0]
    query_in = query_attention_output[0]
    passage_in = passage_attention_output[0]
    ids = hard_negative_ids[0]
    q_dev, width = query_raw.shape
    p_dev = passage_raw.shape[0]
    rank, part = adapter_down_weight.shape
    queries = group * q_dev
    slots = group * CAP
    work = 2 * p_dev * width

    packed, adapter, half, positive_row = run(
        front_kernel,
        (
            shape_of((q_dev, width + 2 * ids.shape[1]), BF16),
            shape_of((2 * rank, part), BF16),
            shape_of((rank, part), BF16),
            shape_of((1, queries), jnp.int32),
        ),
        (query_raw, ids, adapter_down_weight, adapter_up_weight, positive_passage_row),
        1,
        [
            pltpu.VMEM(ids.shape, jnp.int32),
            pltpu.VMEM(positive_passage_row.shape, jnp.int32),
            pltpu.SemaphoreType.DMA((5,)),
        ],
        in_hbm=True,
    )
    embed, side, side_row, own_side, low_scale = run(
        passage_norm_kernel,
        (
            shape_of((p_dev, width), BF16),
            shape_of((p_dev, 128), F32),
            shape_of((8, p_dev), F32),
            shape_of((8, queries), F32),
            shape_of((8, q_dev), F32),
        ),
        (query_raw, passage_raw, passage_home_row),
        work,
        [
            pltpu.VMEM(passage_raw.shape, BF16),
            pltpu.VMEM(passage_home_row.shape, jnp.int32),
            pltpu.VMEM(query_raw.shape, BF16),
            pltpu.SemaphoreType.DMA((2 + PASSAGE_CHUNKS,)),
        ],
        in_hbm=True,
    )
    blocks = {0: packed}
    for k in range(2, group, 2):
        blocks[k] = exchange(packed, "dp", k)
    blocks[1] = exchange(packed, "dp", 1)
    for k in range(2, group, 2):
        blocks[k], embed = lax.optimization_barrier((blocks[k], embed))
        blocks[k ^ 1] = exchange(blocks[k], "dp", 1)
    if shards == 4:
        half_block = exchange(half, "fsdp", 3)
        whole_block = core_step(adapter, 1, 2)
        adapter_near = run(
            join_kernel,
            (shape_of((3 * rank, part), BF16),),
            (whole_block, half_block),
            1,
        )[0]
        adapter_blocks = [adapter, adapter_near, exchange(adapter_near, "dp", 1)]
    else:
        adapter_blocks = [adapter] + [exchange(adapter, "fsdp", k) for k in range(1, shards)]
    query_embed, weight, dots, onehot, head = run(
        functools.partial(score_kernel, group),
        (
            shape_of((queries, width), BF16),
            shape_of((p_dev, queries), F32),
            shape_of((p_dev, queries), F32),
            shape_of((slots, p_dev), F32),
            shape_of((HEAD_ROWS, queries), F32),
        ),
        (
            *[blocks[k] for k in range(group)],
            embed,
            side,
            positive_row,
        ),
        work * queries,
        [pltpu.VMEM((queries, 2 * ids.shape[1]), F32)],
    )
    adapter_full, passage_low, message, slot_base = run(
        functools.partial(rank_kernel, shards),
        (
            shape_of((2 * rank, width), BF16),
            shape_of((rank, p_dev), F32),
            shape_of((HEAD_ROWS + rank, queries), F32),
            shape_of((rank, p_dev), F32),
        ),
        (
            *adapter_blocks,
            query_in,
            passage_in,
            embed,
            side_row,
            low_scale,
            onehot,
            head,
        ),
        work * rank,
    )
    stats = [message] + [exchange(message, "dp", k) for k in range(2, group, 2)]
    chips = group // 2
    back_query, local, targets, *row_blocks = run(
        functools.partial(request_kernel, group),
        (
            shape_of((rank, queries), F32),
            shape_of((2 * rank, queries), F32),
            shape_of((2 * rank, queries), F32),
            *[shape_of((2 * CAP, width), BF16)] * chips,
        ),
        (
            embed,
            onehot,
            query_embed,
            adapter_full,
            passage_low,
            slot_base,
            weight,
            positive_row,
        ),
        work * slots,
    )
    stats, row_blocks = lax.optimization_barrier((stats, row_blocks))
    near = [exchange(row_blocks[i], "dp", 2 * i) for i in range(1, chips)]
    near_stats = stack(*stats)
    far_stats = exchange(near_stats, "dp", 1)
    final, mine, theirs = run(
        functools.partial(terms_kernel, group),
        (
            shape_of((p_dev, queries), F32),
            shape_of((rank, width), F32),
            shape_of((rank, width), F32),
        ),
        (
            near_stats,
            far_stats,
            weight,
            dots,
            positive_row,
            query_embed,
            embed,
            back_query,
            slot_base,
            passage_low,
            side_row,
            own_side,
            passage_in,
            query_in,
            local,
            targets,
        ),
        work * rank * 4,
        [pltpu.VMEM((2 * rank, width), F32)],
    )
    terms = run(
        halves_kernel,
        (
            shape_of((rank, part), F32),
            *[shape_of((rank, part), BF16)] * (shards - 1),
        ),
        (mine, exchange(theirs, "dp", 1)),
        1,
    )
    terms = list(terms)
    arrived = [exchange(terms[k], "fsdp", k) for k in range(1, shards)]
    final, near[0] = lax.optimization_barrier((final, near[0]))
    grad_passage = run(
        passage_kernel,
        (shape_of((p_dev, width), BF16),),
        (final, query_embed, passage_raw, side),
        2 * work * queries,
        [pltpu.VMEM((p_dev, width), F32)],
    )[0]
    terms[0], grad_passage = lax.optimization_barrier((terms[0], grad_passage))
    sent = run(sum_kernel, (shape_of((rank, part), BF16),), (terms[0], *arrived), 1)[0]
    sent, near = lax.optimization_barrier((sent, near))
    to_sibling = run(
        forward_kernel,
        (shape_of((group // 2 * CAP, width), BF16),),
        (row_blocks[0], *near),
        1,
    )[0]
    forwarded = exchange(to_sibling, "dp", 1)
    arrived = [exchange(sent, "dp", k) for k in range(2, group, 2)]
    grad_query = run(
        functools.partial(query_kernel, group),
        (shape_of((q_dev, width), BF16),),
        (near_stats, far_stats, *near, forwarded, final, embed, query_raw),
        4 * q_dev * width * (p_dev + slots),
        [pltpu.VMEM((q_dev, width), F32)],
    )[0]
    half_total = run(pair_sum_kernel, (shape_of((rank, part), F32),), (sent, *arrived), 1)[0]
    other_half = exchange(half_total, "dp", 1)
    half_total, grad_query = lax.optimization_barrier((half_total, grad_query))
    down_total, up_total = run(
        both_halves_kernel, (shape_of((rank, part), F32),) * 2, (half_total, other_half), 1
    )
    return (grad_query[None], grad_passage[None], down_total, up_total)


def solution(mesh):
    in_specs = (
        P("fsdp", "dp", None),
        P("fsdp", "dp", None),
        P("fsdp", "dp", None),
        P("fsdp", "dp", None),
        P("fsdp", "dp"),
        P("fsdp", "dp", None),
        P("fsdp", None),
        P(None, "fsdp"),
        P(None, "fsdp"),
    )
    out_specs = (P("fsdp", "dp", None), P("fsdp", "dp", None), P(None, "fsdp"), P(None, "fsdp"))
    return jax.shard_map(
        per_device, mesh=mesh, in_specs=in_specs, out_specs=out_specs, check_vma=False
    )
```

```python
import functools

import jax
import jax.numpy as jnp
from jax import lax
from jax.experimental import pallas as pl
from jax.experimental.pallas import tpu as pltpu
from jax.sharding import PartitionSpec as P

CAP = 8
SOFTMAX_HEAT = 0.01
ADAPTER_SCALE = 2.0
EPSILON = 1e-06
LOWEST = -1e30
ID_BASE = 256
TOP_ROW, SUM_ROW, DOT_ROW, HEAD_ROWS = 8, 9, 10, 16
VMEM_BYTES = 16 * 1024 * 1024
PASSAGE_CHUNKS = 4
F32 = jnp.float32
BF16 = jnp.bfloat16


def dot_nn(a, b, precision=None):
    return lax.dot_general(
        a, b, (((1,), (0,)), ((), ())), precision=precision, preferred_element_type=F32
    )


def dot_nt(a, b, precision=None):
    return lax.dot_general(
        a, b, (((1,), (1,)), ((), ())), precision=precision, preferred_element_type=F32
    )


def split_two(values):
    high = values.astype(BF16)
    low = (values - high.astype(F32)).astype(BF16)
    return high, low


def dot_pieces(dot, a, b):
    rows = a.shape[0]
    a_high, a_low = split_two(a)
    b_high, b_low = split_two(b)
    both = dot(jnp.concatenate([a_high, a_low], axis=0), b_high)
    return both[:rows] + both[rows:] + dot(a_high, b_low)


def iota(shape, dim):
    return lax.broadcasted_iota(jnp.int32, shape, dim)


def shape_of(dims, kind):
    return jax.ShapeDtypeStruct(dims, kind)


def run(body, out_shape, args, flops, scratch=(), in_hbm=False):
    grant = VMEM_BYTES * max(1, size_ratio(args))
    if in_hbm:
        args = [pltpu.with_memory_space_constraint(a, pltpu.HBM) for a in args]
    vmem = pl.BlockSpec(memory_space=pltpu.VMEM)
    hbm = pl.BlockSpec(memory_space=pltpu.HBM)
    moved = sum(a.size * a.dtype.itemsize for a in (*args, *out_shape))
    return pl.pallas_call(
        body,
        out_shape=out_shape,
        in_specs=[hbm if in_hbm else vmem] * len(args),
        out_specs=tuple(vmem for _ in out_shape),
        scratch_shapes=list(scratch),
        compiler_params=pltpu.CompilerParams(vmem_limit_bytes=grant),
        cost_estimate=pl.CostEstimate(flops=flops, bytes_accessed=moved, transcendentals=0),
    )(*args)


def size_ratio(args):
    moved = sum(a.size * a.dtype.itemsize for a in args)
    return -(-moved * 3 // VMEM_BYTES)


def inverse_length(raw_ref, width):
    chunk = min(width, 512)
    total = jnp.zeros((raw_ref.shape[0], 1), F32)
    for at in range(0, width, chunk):
        part = raw_ref[:, at : at + chunk].astype(F32)
        total = total + jnp.sum(part * part, axis=-1, keepdims=True)
    return 1.0 / jnp.sqrt(total + EPSILON)


def front_kernel(
    query_ref,
    ids_ref,
    down_ref,
    up_ref,
    positive_ref,
    out_ref,
    adapter_ref,
    half_ref,
    tiled_ref,
    ids_here,
    positive_here,
    sems,
):
    width = query_ref.shape[1]
    rank = down_ref.shape[0]
    me = lax.axis_index("dp")
    pairs = (
        (ids_ref, ids_here),
        (query_ref, out_ref.at[:, pl.ds(0, width)]),
        (positive_ref, positive_here),
        (down_ref, adapter_ref.at[pl.ds(0, rank), :]),
        (up_ref, adapter_ref.at[pl.ds(rank, rank), :]),
    )
    copies = [pltpu.make_async_copy(a, b, sems.at[i]) for i, (a, b) in enumerate(pairs)]
    for copy in copies:
        copy.start()
    copies[0].wait()
    ids = ids_here[...]
    coded = jnp.concatenate([ids // ID_BASE, ids % ID_BASE], axis=1)
    out_ref[:, width:] = coded.astype(F32).astype(BF16)
    copies[2].wait()
    q_dev = positive_here.shape[1]
    for at in range(0, tiled_ref.shape[1], q_dev):
        tiled_ref[:, at : at + q_dev] = positive_here[...]
    copies[3].wait()
    copies[4].wait()

    @pl.when(me % 2 == 0)
    def _():
        half_ref[...] = adapter_ref[:rank, :]

    @pl.when(me % 2 == 1)
    def _():
        half_ref[...] = adapter_ref[rank:, :]

    copies[1].wait()


def passage_norm_kernel(
    query_ref,
    passage_ref,
    home_ref,
    embed_ref,
    side_ref,
    row_ref,
    own_ref,
    low_scale_ref,
    passage_here,
    home_here,
    query_here,
    sems,
):
    rows, width = passage_ref.shape
    total = home_ref.shape[1]
    me = lax.axis_index("dp")
    part = rows // PASSAGE_CHUNKS
    home_copy = pltpu.make_async_copy(home_ref, home_here, sems.at[0])
    home_copy.start()
    query_copy = pltpu.make_async_copy(query_ref, query_here, sems.at[1 + PASSAGE_CHUNKS])
    query_copy.start()
    passage_copies = []
    for c in range(PASSAGE_CHUNKS):
        here = pl.ds(c * part, part)
        passage_copies.append(
            pltpu.make_async_copy(
                passage_ref.at[here, :], passage_here.at[here, :], sems.at[1 + c]
            )
        )
        passage_copies[c].start()

    home_copy.wait()
    row_id = iota((rows, total), 0) + me * rows
    number = iota((rows, total), 1)
    home = jnp.where(home_here[...] == row_id, number, 0).astype(F32)
    home = jnp.sum(home, axis=1, keepdims=True)
    query_copy.wait()
    q_dev = query_here.shape[0]
    queries = own_ref.shape[1]
    inverse = inverse_length(query_here, width)
    place = iota((q_dev, queries), 1) == iota((q_dev, queries), 0) + me * q_dev
    own = jnp.sum(jnp.where(place, inverse, 0.0), axis=0, keepdims=True)
    own_ref[...] = jnp.broadcast_to(own, own_ref.shape)
    same = iota((q_dev, q_dev), 0) == iota((q_dev, q_dev), 1)
    low_scale = jnp.sum(jnp.where(same, inverse, 0.0), axis=0, keepdims=True)
    low_scale_ref[...] = jnp.broadcast_to(low_scale, low_scale_ref.shape)

    chunk = min(width, 512)
    inverses = []
    for c in range(PASSAGE_CHUNKS):
        passage_copies[c].wait()
        here = slice(c * part, (c + 1) * part)
        inverse = inverse_length(passage_here.at[here, :], width)
        for at in range(0, width, chunk):
            values = passage_here[here, at : at + chunk].astype(F32)
            embed_ref[here, at : at + chunk] = (values * inverse).astype(BF16)
        inverses.append(inverse)
    inverse = jnp.concatenate(inverses, axis=0)
    side_ref[...] = jnp.where(iota(side_ref.shape, 1) == 0, inverse, home)
    row_ref[...] = jnp.broadcast_to(inverse, (rows, rows)).T[: row_ref.shape[0]]


def stack_kernel(*refs):
    out_ref = refs[-1]
    rows = refs[0].shape[0]
    for i, ref in enumerate(refs[:-1]):
        out_ref[i * rows : (i + 1) * rows, :] = ref[...]


def stack(*parts):
    rows, cols = parts[0].shape
    return run(stack_kernel, (shape_of((len(parts) * rows, cols), parts[0].dtype),), parts, 1)[0]


def join_kernel(first_ref, second_ref, out_ref):
    rows = first_ref.shape[0]
    out_ref[:rows, :] = first_ref[...]
    out_ref[rows:, :] = second_ref[...]


def place_paired(own_ref, near_ref, far_ref, weights_ref):
    rank, part = own_ref.shape[0] // 2, own_ref.shape[1]
    me = lax.axis_index("fsdp")
    core = lax.axis_index("dp") % 2

    def columns(k):
        return pl.ds(pl.multiple_of((me ^ k) * part, part), part)

    def place(even_ref, odd_ref):
        weights_ref[:, columns(1)] = even_ref[: 2 * rank, :]
        weights_ref[:, columns(2)] = odd_ref[: 2 * rank, :]
        weights_ref[:rank, columns(3)] = even_ref[2 * rank :, :]
        weights_ref[rank:, columns(3)] = odd_ref[2 * rank :, :]

    weights_ref[:, columns(0)] = own_ref[...]
    pl.when(core == 0)(functools.partial(place, near_ref, far_ref))
    pl.when(core == 1)(functools.partial(place, far_ref, near_ref))


def place_blocks(*refs):
    part = refs[0].shape[1]
    me = lax.axis_index("fsdp")
    for k, ref in enumerate(refs[:-1]):
        refs[-1][:, pl.ds(pl.multiple_of((me ^ k) * part, part), part)] = ref[...]


def rank_kernel(shards, *refs):
    blocks = refs[:-11]
    query_in_ref, passage_in_ref, embed_ref, row_ref, low_scale_ref = refs[-11:-6]
    onehot_ref, head_ref = refs[-6:-4]
    weights_ref, passage_low_ref, message_ref, base_ref = refs[-4:]
    rank = blocks[0].shape[0] // 2
    q_dev = query_in_ref.shape[0]
    slots = onehot_ref.shape[0]
    queries = message_ref.shape[1]
    place = place_paired if shards == 4 else place_blocks
    place(*blocks, weights_ref)
    down, up = weights_ref[:rank, :], weights_ref[rank:, :]
    query_low = dot_nt(down, query_in_ref[...]).astype(BF16)
    message_ref[HEAD_ROWS:, slots : slots + q_dev] = query_low.astype(F32) * low_scale_ref[0:1, :]
    passage_low = dot_nt(down, passage_in_ref[...]).astype(BF16)
    passage_low_ref[...] = passage_low.astype(F32) * row_ref[0:1, :]
    base = dot_nt(up, embed_ref[...])
    base_ref[...] = base
    message_ref[:HEAD_ROWS, :] = head_ref[...]
    message_ref[HEAD_ROWS:, :slots] = dot_pieces(dot_nt, base, onehot_ref[...])
    unused = jnp.zeros((rank, queries - slots - q_dev), F32)
    message_ref[HEAD_ROWS:, slots + q_dev :] = unused


def score_kernel(group, *refs):
    blocks = refs[:group]
    embed_ref, side_ref, positive_ref = refs[group : group + 3]
    query_ref, weight_ref, dots_ref, onehot_ref, head_ref, coded_ref = refs[group + 3 :]
    rows, width = embed_ref.shape
    queries = query_ref.shape[0]
    q_dev = queries // group
    negatives = (blocks[0].shape[1] - width) // 2
    slots = group * CAP
    me = lax.axis_index("dp")
    chunk = min(width, 1024)
    for k in range(group):
        start = pl.multiple_of((me ^ k) * q_dev, q_dev)
        inverse = inverse_length(blocks[k], width)
        for at in range(0, width, chunk):
            part = blocks[k][:, at : at + chunk].astype(F32)
            query_ref[pl.ds(start, q_dev), at : at + chunk] = (part * inverse).astype(BF16)
        coded = blocks[k][:, width:].astype(F32)
        coded_ref[pl.ds(start, q_dev), :] = coded
    dots = dot_nt(embed_ref[...], query_ref[...])
    dots_ref[...] = dots
    scores = dots / SOFTMAX_HEAT

    coded = coded_ref[...].T
    ids = coded[:negatives] * float(ID_BASE) + coded[negatives:]
    home = jnp.broadcast_to(side_ref[:, 1:2], (rows, queries))
    count = jnp.zeros((rows, queries), F32)
    for j in range(negatives):
        count = count + jnp.where(ids[j : j + 1, :] == home, 1.0, 0.0)
    members = iota((slots, queries), 0) // CAP == iota((slots, queries), 1) // q_dev
    marked = dot_nt(members.astype(BF16), count.astype(BF16)) > 0.0
    before = (iota((rows, rows), 0) <= iota((rows, rows), 1)).astype(BF16)
    rank_in = dot_nn(marked.astype(F32).astype(BF16), before)
    wanted = (iota((slots, rows), 0) % CAP + 1).astype(F32)
    onehot = jnp.where(marked & (rank_in == wanted), 1.0, 0.0)
    onehot_ref[...] = onehot

    own = iota((rows, queries), 1) // q_dev == me
    count = count + jnp.where(own & (positive_ref[...] == iota((rows, queries), 0)), 1.0, 0.0)
    named = count > 0.0
    top = jnp.max(jnp.where(named, scores, LOWEST), axis=0, keepdims=True)
    weight = count * jnp.exp(jnp.where(named, scores - top, LOWEST))
    weight_ref[...] = weight
    total = jnp.sum(weight, axis=0, keepdims=True)
    dot_total = jnp.sum(weight * dots, axis=0, keepdims=True)
    slot_weight = dot_pieces(dot_nn, onehot, weight)
    tail_row = iota((HEAD_ROWS - CAP, queries), 0)
    tail = jnp.where(tail_row == 0, top, jnp.where(tail_row == 1, total, dot_total))
    lane_group = iota((CAP, queries), 1) // q_dev
    compact = jnp.zeros((CAP, queries), F32)
    for peer in range(group):
        part = slot_weight[peer * CAP : (peer + 1) * CAP]
        compact = jnp.where(lane_group == peer, part, compact)
    head_ref[:CAP, :] = compact
    head_ref[CAP:, :] = tail


def request_kernel(group, *refs):
    (
        embed_ref,
        onehot_ref,
        query_ref,
        weights_ref,
        low_ref,
        base_ref,
        weight_ref,
        positive_ref,
        back_ref,
        local_ref,
        target_ref,
    ) = refs[:11]
    blocks = refs[11:]
    width = embed_ref.shape[1]
    rows, queries = weight_ref.shape
    me = lax.axis_index("dp")
    onehot = [
        onehot_ref[pl.ds(pl.multiple_of((me ^ k) * CAP, CAP), CAP), :] for k in range(group)
    ]
    onehot = jnp.concatenate(onehot, axis=0).astype(BF16)
    chunk = min(width, 1024)
    for at in range(0, width, chunk):
        part = dot_nn(onehot, embed_ref[:, at : at + chunk]).astype(BF16)
        for i, block in enumerate(blocks):
            block[:, at : at + chunk] = part[2 * i * CAP : 2 * (i + 1) * CAP]
    back_ref[...] = dot_nt(weights_ref[weights_ref.shape[0] // 2 :, :], query_ref[...])
    both = jnp.concatenate([low_ref[...], base_ref[...]], axis=0)
    local_ref[...] = dot_pieces(dot_nn, both, weight_ref[...])
    target = own_target(positive_ref, rows, queries, queries // group, me)
    target_ref[...] = dot_pieces(dot_nn, both, target)


def forward_kernel(*refs):
    halves = [ref[...].astype(F32)[CAP:] for ref in refs[:-1]]
    refs[-1][...] = jnp.concatenate(halves, axis=0).astype(BF16)


def message_parts(near_ref, far_ref, group):
    rows = near_ref.shape[0] // (group // 2)
    return [((near_ref, far_ref)[k % 2], k // 2 * rows) for k in range(group)]


def combine(parts):
    tops = [ref[at + TOP_ROW : at + TOP_ROW + 1, :] for ref, at in parts]
    sums = [ref[at + SUM_ROW : at + SUM_ROW + 1, :] for ref, at in parts]
    top = functools.reduce(jnp.maximum, tops)
    scales = [jnp.exp(t - top) for t in tops]
    inverse_total = 1.0 / sum(t * s for t, s in zip(scales, sums))
    return [scale * inverse_total for scale in scales]


def own_target(positive_ref, rows, queries, q_dev, me):
    own = iota((rows, queries), 1) // q_dev == me
    return jnp.where(own & (positive_ref[...] == iota((rows, queries), 0)), 1.0, 0.0)


def terms_kernel(group, shards, near_ref, far_ref, *refs):
    parts = message_parts(near_ref, far_ref, group)
    (
        weight_ref,
        dots_ref,
        positive_ref,
        query_ref,
        embed_ref,
        back_query_ref,
        back_passage_ref,
        passage_low_ref,
        row_ref,
        own_ref,
        passage_in_ref,
        query_in_ref,
        local_ref,
        target_ref,
    ) = refs[:14]
    final_ref = refs[14]
    blocks = refs[15 : 15 + shards]
    (sum_ref,) = refs[15 + shards :]
    rows, queries = weight_ref.shape
    q_dev = queries // group
    rank = passage_low_ref.shape[0]
    width = query_ref.shape[1]
    me = lax.axis_index("dp")

    scales = combine(parts)
    target = own_target(positive_ref, rows, queries, q_dev, me)
    weight = (weight_ref[...] * scales[0] - target) / SOFTMAX_HEAT
    final_ref[...] = weight
    dots = dots_ref[...]
    ones = jnp.ones((16, queries), F32)
    inner = dot_pieces(dot_nt, ones, weight * dots)[0:1, :]

    inner_query = -jnp.sum(target * dots, axis=0, keepdims=True)
    own_dots = near_ref[DOT_ROW : DOT_ROW + 1, :]
    share = (scales[0] * own_dots + inner_query) / SOFTMAX_HEAT
    slots = group * CAP
    bases, query_low = [], []
    for (ref, at), scale in zip(parts, scales):
        inner_query = inner_query + scale * ref[at + DOT_ROW : at + DOT_ROW + 1, :]
        bases.append(ref[at + HEAD_ROWS : at + HEAD_ROWS + rank, :])
        query_low.append(ref[at + HEAD_ROWS : at + HEAD_ROWS + rank, :])
    low_total = jnp.zeros((rank, queries), F32)
    lane_group = iota((rank, queries), 1) // q_dev
    for k, rows_at in enumerate(query_low):
        shift = lax.rem((me ^ k) * q_dev + queries - slots, queries)
        rolled = pltpu.roll(rows_at, shift, 1)
        low_total = low_total + jnp.where(lane_group == (me ^ k), rolled, 0.0)
    query_low = low_total
    shift = lax.rem(queries - me * CAP, queries)
    bases = pltpu.roll(jnp.concatenate(bases[1:], axis=0), shift, 1)[:, :CAP]
    far_base = [bases[k * rank : (k + 1) * rank] for k in range(group - 1)]
    far_weight = [
        ref[at : at + CAP, :] * (scale / SOFTMAX_HEAT)
        for (ref, at), scale in zip(parts[1:], scales[1:])
    ]
    inner_query = inner_query / SOFTMAX_HEAT

    passage_low = passage_low_ref[...]
    local = (local_ref[...] * scales[0] - target_ref[...]) / SOFTMAX_HEAT
    from_query = local[:rank] - query_low * share
    from_passage = dot_pieces(dot_nt, query_low, weight) - passage_low * inner
    query_parts = jnp.concatenate(split_two(from_query), axis=0)
    passage_parts = jnp.concatenate(split_two(from_passage), axis=0)

    back_passage = dot_pieces(dot_nt, back_query_ref[...], weight)
    back_passage = (back_passage - back_passage_ref[...] * inner) * row_ref[0:1, :]
    back_passage = back_passage.astype(BF16)
    back_query = local[rank:] + dot_pieces(
        dot_nn, jnp.concatenate(far_base, axis=1), jnp.concatenate(far_weight, axis=0)
    )
    back_query = (back_query - back_query_ref[...] * inner_query) * own_ref[0:1, :]
    pick = (iota((q_dev, queries), 1) == iota((q_dev, queries), 0) + me * q_dev).astype(BF16)
    back_query = dot_nt(back_query.astype(BF16), pick).astype(BF16)

    chunk = min(width, 512)
    for at in range(0, width, chunk):
        cols = slice(at, at + chunk)
        both = dot_nn(query_parts, query_ref[:, cols]) + dot_nn(passage_parts, embed_ref[:, cols])
        sum_ref[rank:, cols] = ADAPTER_SCALE * (both[:rank] + both[rank:])
        sum_ref[:rank, cols] = ADAPTER_SCALE * (
            dot_nn(back_passage, passage_in_ref[:, cols])
            + dot_nn(back_query, query_in_ref[:, cols])
        )
    part = width // shards
    home = lax.axis_index("fsdp")
    for k in range(shards):
        start = pl.multiple_of((home ^ k) * part, part)
        blocks[k][...] = sum_ref[:, pl.ds(start, part)].astype(blocks[k].dtype)


def backward(upstream_of, raw_ref, inverse, grad_ref, up_ref):
    rows, width = raw_ref.shape
    chunk = min(width, 512)
    inner = jnp.zeros((rows, 1), F32)
    for at in range(0, width, chunk):
        upstream = upstream_of(at, chunk)
        up_ref[:, at : at + chunk] = upstream
        unit = raw_ref[:, at : at + chunk].astype(F32) * inverse
        inner = inner + jnp.sum(unit * upstream, axis=-1, keepdims=True)
    for at in range(0, width, chunk):
        unit = raw_ref[:, at : at + chunk].astype(F32) * inverse
        grad = (up_ref[:, at : at + chunk] - unit * inner) * inverse
        grad_ref[:, at : at + chunk] = grad.astype(BF16)


def passage_kernel(final_ref, query_ref, raw_ref, side_ref, grad_ref, up_ref):
    high, low = split_two(final_ref[...])

    def upstream_of(at, chunk):
        embed = query_ref[:, at : at + chunk]
        return dot_nn(high, embed) + dot_nn(low, embed)

    backward(upstream_of, raw_ref, side_ref[:, 0:1], grad_ref, up_ref)


def query_kernel(group, near_ref, far_ref, *refs):
    parts = message_parts(near_ref, far_ref, group)
    near = refs[: group // 2 - 1]
    forwarded_ref, final_ref, embed_ref, raw_ref, grad_ref, up_ref = refs[group // 2 - 1 :]
    q_dev, width = raw_ref.shape
    queries = final_ref.shape[1]
    me = lax.axis_index("dp")
    scales = combine(parts)
    pick = (iota((q_dev, queries), 1) == iota((q_dev, queries), 0) + me * q_dev).astype(F32)
    far = [
        ref[at : at + CAP, :] * (scale / SOFTMAX_HEAT) for (ref, at), scale in zip(parts, scales)
    ]
    far = far[2::2] + far[1::2] + [jnp.zeros((CAP, queries), F32)]
    own_parts = split_two(dot_pieces(dot_nt, pick, final_ref[...]))
    far_parts = split_two(dot_pieces(dot_nt, pick, jnp.concatenate(far, axis=0)))
    own_parts = jnp.concatenate(own_parts, axis=0)
    far_parts = jnp.concatenate(far_parts, axis=0)

    def upstream_of(at, chunk):
        rows = [ref[:, at : at + chunk].astype(F32)[:CAP] for ref in near]
        rows.append(forwarded_ref[:, at : at + chunk].astype(F32))
        rows.append(jnp.zeros((CAP, chunk), F32))
        both = dot_nn(own_parts, embed_ref[:, at : at + chunk])
        both = both + dot_nn(far_parts, jnp.concatenate(rows, axis=0).astype(BF16))
        return both[:q_dev] + both[q_dev:]

    backward(upstream_of, raw_ref, inverse_length(raw_ref, width), grad_ref, up_ref)


def sum_kernel(*refs):
    total = refs[0][...].astype(F32)
    for ref in refs[1:-1]:
        total = total + ref[...].astype(F32)
    refs[-1][...] = total


def sum_two_kernel(left_ref, right_ref, sent_ref):
    sent_ref[...] = (left_ref[...] + right_ref[...]).astype(BF16)


def sum_split_kernel(*refs):
    terms = [ref[...].astype(F32) for ref in refs[:-2]]
    while len(terms) > 1:
        terms = [a + b for a, b in zip(terms[::2], terms[1::2])]
    rank = refs[-1].shape[0]
    refs[-2][...] = terms[0][:rank]
    refs[-1][...] = terms[0][rank:]


def exchange(values, axis, k):
    size = lax.axis_size(axis)
    return lax.ppermute(values, axis, [(i, i ^ k) for i in range(size)])


def core_step(values, even_step, odd_step):
    outer, inner = lax.axis_size("dp"), lax.axis_size("fsdp")
    pairs = []
    for d in range(outer):
        step = odd_step if d % 2 else even_step
        pairs += [(d * inner + f, d * inner + (f ^ step)) for f in range(inner)]
    return lax.ppermute(values, ("dp", "fsdp"), pairs)


def per_device(
    query_pooled_states,
    passage_pooled_states,
    query_attention_output,
    passage_attention_output,
    positive_passage_row,
    hard_negative_ids,
    passage_home_row,
    adapter_down_weight,
    adapter_up_weight,
):
    group = lax.axis_size("dp")
    shards = lax.axis_size("fsdp")
    query_raw = query_pooled_states[0]
    passage_raw = passage_pooled_states[0]
    query_in = query_attention_output[0]
    passage_in = passage_attention_output[0]
    ids = hard_negative_ids[0]
    q_dev, width = query_raw.shape
    p_dev = passage_raw.shape[0]
    rank, part = adapter_down_weight.shape
    queries = group * q_dev
    slots = group * CAP
    work = 2 * p_dev * width

    packed, adapter, half, positive_row = run(
        front_kernel,
        (
            shape_of((q_dev, width + 2 * ids.shape[1]), BF16),
            shape_of((2 * rank, part), BF16),
            shape_of((rank, part), BF16),
            shape_of((1, queries), jnp.int32),
        ),
        (query_raw, ids, adapter_down_weight, adapter_up_weight, positive_passage_row),
        1,
        [
            pltpu.VMEM(ids.shape, jnp.int32),
            pltpu.VMEM(positive_passage_row.shape, jnp.int32),
            pltpu.SemaphoreType.DMA((5,)),
        ],
        in_hbm=True,
    )
    embed, side, side_row, own_side, low_scale = run(
        passage_norm_kernel,
        (
            shape_of((p_dev, width), BF16),
            shape_of((p_dev, 128), F32),
            shape_of((8, p_dev), F32),
            shape_of((8, queries), F32),
            shape_of((8, q_dev), F32),
        ),
        (query_raw, passage_raw, passage_home_row),
        work,
        [
            pltpu.VMEM(passage_raw.shape, BF16),
            pltpu.VMEM(passage_home_row.shape, jnp.int32),
            pltpu.VMEM(query_raw.shape, BF16),
            pltpu.SemaphoreType.DMA((2 + PASSAGE_CHUNKS,)),
        ],
        in_hbm=True,
    )
    blocks = {0: packed}
    for k in range(2, group, 2):
        blocks[k] = exchange(packed, "dp", k)
    blocks[1] = exchange(packed, "dp", 1)
    if shards == 4:
        half_block = exchange(half, "fsdp", 3)
        whole_block = core_step(adapter, 1, 2)
        whole_block, half_block, blocks[2] = lax.optimization_barrier(
            (whole_block, half_block, blocks[2])
        )
    for k in range(2, group, 2):
        blocks[k], embed = lax.optimization_barrier((blocks[k], embed))
        blocks[k ^ 1] = exchange(blocks[k], "dp", 1)
    if shards == 4:
        adapter_near = run(
            join_kernel,
            (shape_of((3 * rank, part), BF16),),
            (whole_block, half_block),
            1,
        )[0]
        adapter_blocks = [adapter, adapter_near, exchange(adapter_near, "dp", 1)]
    else:
        adapter_blocks = [adapter] + [exchange(adapter, "fsdp", k) for k in range(1, shards)]
    query_embed, weight, dots, onehot, head = run(
        functools.partial(score_kernel, group),
        (
            shape_of((queries, width), BF16),
            shape_of((p_dev, queries), F32),
            shape_of((p_dev, queries), F32),
            shape_of((slots, p_dev), F32),
            shape_of((HEAD_ROWS, queries), F32),
        ),
        (
            *[blocks[k] for k in range(group)],
            embed,
            side,
            positive_row,
        ),
        work * queries,
        [pltpu.VMEM((queries, 2 * ids.shape[1]), F32)],
    )
    adapter_full, passage_low, message, slot_base = run(
        functools.partial(rank_kernel, shards),
        (
            shape_of((2 * rank, width), BF16),
            shape_of((rank, p_dev), F32),
            shape_of((HEAD_ROWS + rank, queries), F32),
            shape_of((rank, p_dev), F32),
        ),
        (
            *adapter_blocks,
            query_in,
            passage_in,
            embed,
            side_row,
            low_scale,
            onehot,
            head,
        ),
        work * rank,
    )
    stats = [message] + [exchange(message, "dp", k) for k in range(2, group, 2)]
    chips = group // 2
    back_query, local, targets, *row_blocks = run(
        functools.partial(request_kernel, group),
        (
            shape_of((rank, queries), F32),
            shape_of((2 * rank, queries), F32),
            shape_of((2 * rank, queries), F32),
            *[shape_of((2 * CAP, width), BF16)] * chips,
        ),
        (
            embed,
            onehot,
            query_embed,
            adapter_full,
            passage_low,
            slot_base,
            weight,
            positive_row,
        ),
        work * slots,
    )
    stats, row_blocks = lax.optimization_barrier((stats, row_blocks))
    near = [exchange(row_blocks[i], "dp", 2 * i) for i in range(1, chips)]
    near_stats = stack(*stats)
    far_stats = exchange(near_stats, "dp", 1)
    final, *terms = run(
        functools.partial(terms_kernel, group, shards),
        (
            shape_of((p_dev, queries), F32),
            shape_of((2 * rank, part), F32),
            *[shape_of((2 * rank, part), BF16)] * (shards - 1),
        ),
        (
            near_stats,
            far_stats,
            weight,
            dots,
            positive_row,
            query_embed,
            embed,
            back_query,
            slot_base,
            passage_low,
            side_row,
            own_side,
            passage_in,
            query_in,
            local,
            targets,
        ),
        work * rank * 4,
        [pltpu.VMEM((2 * rank, width), F32)],
    )
    arrived = [exchange(terms[k], "fsdp", k) for k in range(1, shards)]
    final, near[0] = lax.optimization_barrier((final, near[0]))
    grad_passage = run(
        passage_kernel,
        (shape_of((p_dev, width), BF16),),
        (final, query_embed, passage_raw, side),
        2 * work * queries,
        [pltpu.VMEM((p_dev, width), F32)],
    )[0]
    terms[0], grad_passage = lax.optimization_barrier((terms[0], grad_passage))
    total = run(sum_kernel, (shape_of((2 * rank, part), F32),), (terms[0], *arrived), 1)[0]
    total, near = lax.optimization_barrier((total, near))
    to_sibling = run(
        forward_kernel,
        (shape_of((group // 2 * CAP, width), BF16),),
        (row_blocks[0], *near),
        1,
    )[0]
    forwarded = exchange(to_sibling, "dp", 1)
    sent = run(
        sum_two_kernel,
        (shape_of((2 * rank, part), BF16),),
        (total, exchange(total, "dp", 1)),
        1,
    )[0]
    arrived = [exchange(sent, "dp", k) for k in range(2, group, 2)]
    grad_query = run(
        functools.partial(query_kernel, group),
        (shape_of((q_dev, width), BF16),),
        (near_stats, far_stats, *near, forwarded, final, embed, query_raw),
        4 * q_dev * width * (p_dev + slots),
        [pltpu.VMEM((q_dev, width), F32)],
    )[0]
    sent, grad_query = lax.optimization_barrier((sent, grad_query))
    down_total, up_total = run(
        sum_split_kernel, (shape_of((rank, part), F32),) * 2, (sent, *arrived), 1
    )
    return (grad_query[None], grad_passage[None], down_total, up_total)


def solution(mesh):
    in_specs = (
        P("fsdp", "dp", None),
        P("fsdp", "dp", None),
        P("fsdp", "dp", None),
        P("fsdp", "dp", None),
        P("fsdp", "dp"),
        P("fsdp", "dp", None),
        P("fsdp", None),
        P(None, "fsdp"),
        P(None, "fsdp"),
    )
    out_specs = (P("fsdp", "dp", None), P("fsdp", "dp", None), P(None, "fsdp"), P(None, "fsdp"))
    return jax.shard_map(
        per_device, mesh=mesh, in_specs=in_specs, out_specs=out_specs, check_vma=False
    )
```

```python
import functools

import jax
import jax.numpy as jnp
from jax import lax
from jax.experimental import pallas as pl
from jax.experimental.pallas import tpu as pltpu
from jax.sharding import PartitionSpec as P

CAP = 8
SOFTMAX_HEAT = 0.01
ADAPTER_SCALE = 2.0
EPSILON = 1e-06
LOWEST = -1e30
ID_BASE = 256
TOP_ROW, SUM_ROW, DOT_ROW, HEAD_ROWS = 8, 9, 10, 16
VMEM_BYTES = 16 * 1024 * 1024
PASSAGE_CHUNKS = 4
F32 = jnp.float32
BF16 = jnp.bfloat16


def dot_nn(a, b, precision=None):
    return lax.dot_general(
        a, b, (((1,), (0,)), ((), ())), precision=precision, preferred_element_type=F32
    )


def dot_nt(a, b, precision=None):
    return lax.dot_general(
        a, b, (((1,), (1,)), ((), ())), precision=precision, preferred_element_type=F32
    )


def split_two(values):
    high = values.astype(BF16)
    low = (values - high.astype(F32)).astype(BF16)
    return high, low


def dot_pieces(dot, a, b):
    rows = a.shape[0]
    a_high, a_low = split_two(a)
    b_high, b_low = split_two(b)
    both = dot(jnp.concatenate([a_high, a_low], axis=0), b_high)
    return both[:rows] + both[rows:] + dot(a_high, b_low)


def iota(shape, dim):
    return lax.broadcasted_iota(jnp.int32, shape, dim)


def shape_of(dims, kind):
    return jax.ShapeDtypeStruct(dims, kind)


def run(body, out_shape, args, flops, scratch=(), in_hbm=False):
    grant = VMEM_BYTES * max(1, size_ratio(args))
    if in_hbm:
        args = [pltpu.with_memory_space_constraint(a, pltpu.HBM) for a in args]
    vmem = pl.BlockSpec(memory_space=pltpu.VMEM)
    hbm = pl.BlockSpec(memory_space=pltpu.HBM)
    moved = sum(a.size * a.dtype.itemsize for a in (*args, *out_shape))
    return pl.pallas_call(
        body,
        out_shape=out_shape,
        in_specs=[hbm if in_hbm else vmem] * len(args),
        out_specs=tuple(vmem for _ in out_shape),
        scratch_shapes=list(scratch),
        compiler_params=pltpu.CompilerParams(vmem_limit_bytes=grant),
        cost_estimate=pl.CostEstimate(flops=flops, bytes_accessed=moved, transcendentals=0),
    )(*args)


def size_ratio(args):
    moved = sum(a.size * a.dtype.itemsize for a in args)
    return -(-moved * 3 // VMEM_BYTES)


def inverse_length(raw_ref, width):
    chunk = min(width, 512)
    total = jnp.zeros((raw_ref.shape[0], 1), F32)
    for at in range(0, width, chunk):
        part = raw_ref[:, at : at + chunk].astype(F32)
        total = total + jnp.sum(part * part, axis=-1, keepdims=True)
    return 1.0 / jnp.sqrt(total + EPSILON)


def front_kernel(
    query_ref,
    ids_ref,
    down_ref,
    up_ref,
    positive_ref,
    out_ref,
    adapter_ref,
    half_ref,
    tiled_ref,
    ids_here,
    positive_here,
    sems,
):
    width = query_ref.shape[1]
    rank = down_ref.shape[0]
    me = lax.axis_index("dp")
    pairs = (
        (ids_ref, ids_here),
        (query_ref, out_ref.at[:, pl.ds(0, width)]),
        (positive_ref, positive_here),
        (down_ref, adapter_ref.at[pl.ds(0, rank), :]),
        (up_ref, adapter_ref.at[pl.ds(rank, rank), :]),
    )
    copies = [pltpu.make_async_copy(a, b, sems.at[i]) for i, (a, b) in enumerate(pairs)]
    for copy in copies:
        copy.start()
    copies[0].wait()
    ids = ids_here[...]
    coded = jnp.concatenate([ids // ID_BASE, ids % ID_BASE], axis=1)
    out_ref[:, width:] = coded.astype(F32).astype(BF16)
    copies[2].wait()
    q_dev = positive_here.shape[1]
    for at in range(0, tiled_ref.shape[1], q_dev):
        tiled_ref[:, at : at + q_dev] = positive_here[...]
    copies[3].wait()
    copies[4].wait()

    @pl.when(me % 2 == 0)
    def _():
        half_ref[...] = adapter_ref[:rank, :]

    @pl.when(me % 2 == 1)
    def _():
        half_ref[...] = adapter_ref[rank:, :]

    copies[1].wait()


def passage_norm_kernel(
    query_ref,
    passage_ref,
    home_ref,
    embed_ref,
    side_ref,
    row_ref,
    own_ref,
    low_scale_ref,
    passage_here,
    home_here,
    query_here,
    sems,
):
    rows, width = passage_ref.shape
    total = home_ref.shape[1]
    me = lax.axis_index("dp")
    part = rows // PASSAGE_CHUNKS
    home_copy = pltpu.make_async_copy(home_ref, home_here, sems.at[0])
    home_copy.start()
    query_copy = pltpu.make_async_copy(query_ref, query_here, sems.at[1 + PASSAGE_CHUNKS])
    query_copy.start()
    passage_copies = []
    for c in range(PASSAGE_CHUNKS):
        here = pl.ds(c * part, part)
        passage_copies.append(
            pltpu.make_async_copy(
                passage_ref.at[here, :], passage_here.at[here, :], sems.at[1 + c]
            )
        )
        passage_copies[c].start()

    home_copy.wait()
    row_id = iota((rows, total), 0) + me * rows
    number = iota((rows, total), 1)
    home = jnp.where(home_here[...] == row_id, number, 0).astype(F32)
    home = jnp.sum(home, axis=1, keepdims=True)
    query_copy.wait()
    q_dev = query_here.shape[0]
    queries = own_ref.shape[1]
    inverse = inverse_length(query_here, width)
    place = iota((q_dev, queries), 1) == iota((q_dev, queries), 0) + me * q_dev
    own = jnp.sum(jnp.where(place, inverse, 0.0), axis=0, keepdims=True)
    own_ref[...] = jnp.broadcast_to(own, own_ref.shape)
    same = iota((q_dev, q_dev), 0) == iota((q_dev, q_dev), 1)
    low_scale = jnp.sum(jnp.where(same, inverse, 0.0), axis=0, keepdims=True)
    low_scale_ref[...] = jnp.broadcast_to(low_scale, low_scale_ref.shape)

    chunk = min(width, 512)
    inverses = []
    for c in range(PASSAGE_CHUNKS):
        passage_copies[c].wait()
        here = slice(c * part, (c + 1) * part)
        inverse = inverse_length(passage_here.at[here, :], width)
        for at in range(0, width, chunk):
            values = passage_here[here, at : at + chunk].astype(F32)
            embed_ref[here, at : at + chunk] = (values * inverse).astype(BF16)
        inverses.append(inverse)
    inverse = jnp.concatenate(inverses, axis=0)
    side_ref[...] = jnp.where(iota(side_ref.shape, 1) == 0, inverse, home)
    row_ref[...] = jnp.broadcast_to(inverse, (rows, rows)).T[: row_ref.shape[0]]


def stack_kernel(*refs):
    out_ref = refs[-1]
    rows = refs[0].shape[0]
    for i, ref in enumerate(refs[:-1]):
        out_ref[i * rows : (i + 1) * rows, :] = ref[...]


def stack(*parts):
    rows, cols = parts[0].shape
    return run(stack_kernel, (shape_of((len(parts) * rows, cols), parts[0].dtype),), parts, 1)[0]


def join_kernel(first_ref, second_ref, out_ref):
    rows = first_ref.shape[0]
    out_ref[:rows, :] = first_ref[...]
    out_ref[rows:, :] = second_ref[...]


def place_paired(own_ref, near_ref, far_ref, weights_ref):
    rank, part = own_ref.shape[0] // 2, own_ref.shape[1]
    me = lax.axis_index("fsdp")
    core = lax.axis_index("dp") % 2

    def columns(k):
        return pl.ds(pl.multiple_of((me ^ k) * part, part), part)

    def place(even_ref, odd_ref):
        weights_ref[:, columns(1)] = even_ref[: 2 * rank, :]
        weights_ref[:, columns(2)] = odd_ref[: 2 * rank, :]
        weights_ref[:rank, columns(3)] = even_ref[2 * rank :, :]
        weights_ref[rank:, columns(3)] = odd_ref[2 * rank :, :]

    weights_ref[:, columns(0)] = own_ref[...]
    pl.when(core == 0)(functools.partial(place, near_ref, far_ref))
    pl.when(core == 1)(functools.partial(place, far_ref, near_ref))


def place_blocks(*refs):
    part = refs[0].shape[1]
    me = lax.axis_index("fsdp")
    for k, ref in enumerate(refs[:-1]):
        refs[-1][:, pl.ds(pl.multiple_of((me ^ k) * part, part), part)] = ref[...]


def rank_kernel(shards, *refs):
    blocks = refs[:-11]
    query_in_ref, passage_in_ref, embed_ref, row_ref, low_scale_ref = refs[-11:-6]
    onehot_ref, head_ref = refs[-6:-4]
    weights_ref, passage_low_ref, message_ref, base_ref = refs[-4:]
    rank = blocks[0].shape[0] // 2
    q_dev = query_in_ref.shape[0]
    slots = onehot_ref.shape[0]
    queries = message_ref.shape[1]
    place = place_paired if shards == 4 else place_blocks
    place(*blocks, weights_ref)
    down, up = weights_ref[:rank, :], weights_ref[rank:, :]
    query_low = dot_nt(down, query_in_ref[...]).astype(BF16)
    message_ref[HEAD_ROWS:, slots : slots + q_dev] = query_low.astype(F32) * low_scale_ref[0:1, :]
    low_columns = dot_nt(passage_in_ref[...], down).astype(BF16).astype(F32)
    base_columns = dot_nt(embed_ref[...], up)
    both = jnp.concatenate([low_columns, base_columns], axis=1).T
    passage_low_ref[...] = both[:rank] * row_ref[0:1, :]
    base = both[rank:]
    base_ref[...] = base
    message_ref[:HEAD_ROWS, :] = head_ref[...]
    message_ref[HEAD_ROWS:, :slots] = dot_pieces(dot_nt, base, onehot_ref[...])
    unused = jnp.zeros((rank, queries - slots - q_dev), F32)
    message_ref[HEAD_ROWS:, slots + q_dev :] = unused


def score_kernel(group, *refs):
    blocks = refs[:group]
    embed_ref, side_ref, positive_ref = refs[group : group + 3]
    query_ref, weight_ref, dots_ref, onehot_ref, head_ref, coded_ref = refs[group + 3 :]
    rows, width = embed_ref.shape
    queries = query_ref.shape[0]
    q_dev = queries // group
    negatives = (blocks[0].shape[1] - width) // 2
    slots = group * CAP
    me = lax.axis_index("dp")
    chunk = min(width, 1024)
    for k in range(group):
        start = pl.multiple_of((me ^ k) * q_dev, q_dev)
        inverse = inverse_length(blocks[k], width)
        for at in range(0, width, chunk):
            part = blocks[k][:, at : at + chunk].astype(F32)
            query_ref[pl.ds(start, q_dev), at : at + chunk] = (part * inverse).astype(BF16)
        coded = blocks[k][:, width:].astype(F32)
        coded_ref[pl.ds(start, q_dev), :] = coded
    dots = dot_nt(embed_ref[...], query_ref[...])
    dots_ref[...] = dots
    scores = dots / SOFTMAX_HEAT

    coded = coded_ref[...].T
    ids = coded[:negatives] * float(ID_BASE) + coded[negatives:]
    home = jnp.broadcast_to(side_ref[:, 1:2], (rows, queries))
    count = jnp.zeros((rows, queries), F32)
    for j in range(negatives):
        count = count + jnp.where(ids[j : j + 1, :] == home, 1.0, 0.0)
    members = iota((slots, queries), 0) // CAP == iota((slots, queries), 1) // q_dev
    marked = dot_nt(members.astype(BF16), count.astype(BF16)) > 0.0
    before = (iota((rows, rows), 0) <= iota((rows, rows), 1)).astype(BF16)
    rank_in = dot_nn(marked.astype(F32).astype(BF16), before)
    wanted = (iota((slots, rows), 0) % CAP + 1).astype(F32)
    onehot = jnp.where(marked & (rank_in == wanted), 1.0, 0.0)
    onehot_ref[...] = onehot

    own = iota((rows, queries), 1) // q_dev == me
    count = count + jnp.where(own & (positive_ref[...] == iota((rows, queries), 0)), 1.0, 0.0)
    named = count > 0.0
    top = jnp.max(jnp.where(named, scores, LOWEST), axis=0, keepdims=True)
    weight = count * jnp.exp(jnp.where(named, scores - top, LOWEST))
    weight_ref[...] = weight
    total = jnp.sum(weight, axis=0, keepdims=True)
    dot_total = jnp.sum(weight * dots, axis=0, keepdims=True)
    slot_weight = dot_pieces(dot_nn, onehot, weight)
    tail_row = iota((HEAD_ROWS - CAP, queries), 0)
    tail = jnp.where(tail_row == 0, top, jnp.where(tail_row == 1, total, dot_total))
    lane_group = iota((CAP, queries), 1) // q_dev
    compact = jnp.zeros((CAP, queries), F32)
    for peer in range(group):
        part = slot_weight[peer * CAP : (peer + 1) * CAP]
        compact = jnp.where(lane_group == peer, part, compact)
    head_ref[:CAP, :] = compact
    head_ref[CAP:, :] = tail


def request_kernel(group, *refs):
    (
        embed_ref,
        onehot_ref,
        query_ref,
        weights_ref,
        low_ref,
        base_ref,
        weight_ref,
        positive_ref,
        back_ref,
        local_ref,
        target_ref,
    ) = refs[:11]
    blocks = refs[11:]
    width = embed_ref.shape[1]
    rows, queries = weight_ref.shape
    me = lax.axis_index("dp")
    onehot = [
        onehot_ref[pl.ds(pl.multiple_of((me ^ k) * CAP, CAP), CAP), :] for k in range(group)
    ]
    onehot = jnp.concatenate(onehot, axis=0).astype(BF16)
    chunk = min(width, 1024)
    for at in range(0, width, chunk):
        part = dot_nn(onehot, embed_ref[:, at : at + chunk]).astype(BF16)
        for i, block in enumerate(blocks):
            block[:, at : at + chunk] = part[2 * i * CAP : 2 * (i + 1) * CAP]
    back_ref[...] = dot_nt(weights_ref[weights_ref.shape[0] // 2 :, :], query_ref[...])
    both = jnp.concatenate([low_ref[...], base_ref[...]], axis=0)
    local_ref[...] = dot_pieces(dot_nn, both, weight_ref[...])
    target = own_target(positive_ref, rows, queries, queries // group, me)
    target_ref[...] = dot_pieces(dot_nn, both, target)


def forward_kernel(*refs):
    halves = [ref[...].astype(F32)[CAP:] for ref in refs[:-1]]
    refs[-1][...] = jnp.concatenate(halves, axis=0).astype(BF16)


def message_parts(near_ref, far_ref, group):
    rows = near_ref.shape[0] // (group // 2)
    return [((near_ref, far_ref)[k % 2], k // 2 * rows) for k in range(group)]


def combine(parts):
    tops = [ref[at + TOP_ROW : at + TOP_ROW + 1, :] for ref, at in parts]
    sums = [ref[at + SUM_ROW : at + SUM_ROW + 1, :] for ref, at in parts]
    top = functools.reduce(jnp.maximum, tops)
    scales = [jnp.exp(t - top) for t in tops]
    inverse_total = 1.0 / sum(t * s for t, s in zip(scales, sums))
    return [scale * inverse_total for scale in scales]


def own_target(positive_ref, rows, queries, q_dev, me):
    own = iota((rows, queries), 1) // q_dev == me
    return jnp.where(own & (positive_ref[...] == iota((rows, queries), 0)), 1.0, 0.0)


def terms_kernel(group, shards, near_ref, far_ref, *refs):
    parts = message_parts(near_ref, far_ref, group)
    (
        weight_ref,
        dots_ref,
        positive_ref,
        query_ref,
        embed_ref,
        back_query_ref,
        back_passage_ref,
        passage_low_ref,
        row_ref,
        own_ref,
        passage_in_ref,
        query_in_ref,
        local_ref,
        target_ref,
    ) = refs[:14]
    final_ref = refs[14]
    blocks = refs[15 : 15 + shards]
    (sum_ref,) = refs[15 + shards :]
    rows, queries = weight_ref.shape
    q_dev = queries // group
    rank = passage_low_ref.shape[0]
    width = query_ref.shape[1]
    me = lax.axis_index("dp")

    scales = combine(parts)
    target = own_target(positive_ref, rows, queries, q_dev, me)
    weight = (weight_ref[...] * scales[0] - target) / SOFTMAX_HEAT
    final_ref[...] = weight
    dots = dots_ref[...]
    ones = jnp.ones((16, queries), F32)
    inner = dot_pieces(dot_nt, ones, weight * dots)[0:1, :]

    inner_query = -jnp.sum(target * dots, axis=0, keepdims=True)
    own_dots = near_ref[DOT_ROW : DOT_ROW + 1, :]
    share = (scales[0] * own_dots + inner_query) / SOFTMAX_HEAT
    slots = group * CAP
    bases, query_low = [], []
    for (ref, at), scale in zip(parts, scales):
        inner_query = inner_query + scale * ref[at + DOT_ROW : at + DOT_ROW + 1, :]
        bases.append(ref[at + HEAD_ROWS : at + HEAD_ROWS + rank, :])
        query_low.append(ref[at + HEAD_ROWS : at + HEAD_ROWS + rank, :])
    low_total = jnp.zeros((rank, queries), F32)
    lane_group = iota((rank, queries), 1) // q_dev
    for k, rows_at in enumerate(query_low):
        shift = lax.rem((me ^ k) * q_dev + queries - slots, queries)
        rolled = pltpu.roll(rows_at, shift, 1)
        low_total = low_total + jnp.where(lane_group == (me ^ k), rolled, 0.0)
    query_low = low_total
    shift = lax.rem(queries - me * CAP, queries)
    bases = pltpu.roll(jnp.concatenate(bases[1:], axis=0), shift, 1)[:, :CAP]
    far_base = [bases[k * rank : (k + 1) * rank] for k in range(group - 1)]
    far_weight = [
        ref[at : at + CAP, :] * (scale / SOFTMAX_HEAT)
        for (ref, at), scale in zip(parts[1:], scales[1:])
    ]
    inner_query = inner_query / SOFTMAX_HEAT

    passage_low = passage_low_ref[...]
    local = (local_ref[...] * scales[0] - target_ref[...]) / SOFTMAX_HEAT
    from_query = local[:rank] - query_low * share
    from_passage = dot_pieces(dot_nt, query_low, weight) - passage_low * inner
    query_parts = jnp.concatenate(split_two(from_query), axis=0)
    passage_parts = jnp.concatenate(split_two(from_passage), axis=0)

    back_passage = dot_pieces(dot_nt, back_query_ref[...], weight)
    back_passage = (back_passage - back_passage_ref[...] * inner) * row_ref[0:1, :]
    back_passage = back_passage.astype(BF16)
    back_query = local[rank:] + dot_pieces(
        dot_nn, jnp.concatenate(far_base, axis=1), jnp.concatenate(far_weight, axis=0)
    )
    back_query = (back_query - back_query_ref[...] * inner_query) * own_ref[0:1, :]
    pick = (iota((q_dev, queries), 1) == iota((q_dev, queries), 0) + me * q_dev).astype(BF16)
    back_query = dot_nt(back_query.astype(BF16), pick).astype(BF16)

    chunk = min(width, 512)
    for at in range(0, width, chunk):
        cols = slice(at, at + chunk)
        both = dot_nn(query_parts, query_ref[:, cols]) + dot_nn(passage_parts, embed_ref[:, cols])
        sum_ref[rank:, cols] = ADAPTER_SCALE * (both[:rank] + both[rank:])
        sum_ref[:rank, cols] = ADAPTER_SCALE * (
            dot_nn(back_passage, passage_in_ref[:, cols])
            + dot_nn(back_query, query_in_ref[:, cols])
        )
    part = width // shards
    home = lax.axis_index("fsdp")
    for k in range(shards):
        start = pl.multiple_of((home ^ k) * part, part)
        blocks[k][...] = sum_ref[:, pl.ds(start, part)].astype(blocks[k].dtype)


def backward(upstream_of, raw_ref, inverse, grad_ref, up_ref):
    rows, width = raw_ref.shape
    chunk = min(width, 512)
    inner = jnp.zeros((rows, 1), F32)
    for at in range(0, width, chunk):
        upstream = upstream_of(at, chunk)
        up_ref[:, at : at + chunk] = upstream
        unit = raw_ref[:, at : at + chunk].astype(F32) * inverse
        inner = inner + jnp.sum(unit * upstream, axis=-1, keepdims=True)
    for at in range(0, width, chunk):
        unit = raw_ref[:, at : at + chunk].astype(F32) * inverse
        grad = (up_ref[:, at : at + chunk] - unit * inner) * inverse
        grad_ref[:, at : at + chunk] = grad.astype(BF16)


def passage_kernel(final_ref, query_ref, raw_ref, side_ref, grad_ref, up_ref):
    high, low = split_two(final_ref[...])

    def upstream_of(at, chunk):
        embed = query_ref[:, at : at + chunk]
        return dot_nn(high, embed) + dot_nn(low, embed)

    backward(upstream_of, raw_ref, side_ref[:, 0:1], grad_ref, up_ref)


def query_kernel(group, near_ref, far_ref, *refs):
    parts = message_parts(near_ref, far_ref, group)
    near = refs[: group // 2 - 1]
    forwarded_ref, final_ref, embed_ref, raw_ref, grad_ref, up_ref = refs[group // 2 - 1 :]
    q_dev, width = raw_ref.shape
    queries = final_ref.shape[1]
    me = lax.axis_index("dp")
    scales = combine(parts)
    pick = (iota((q_dev, queries), 1) == iota((q_dev, queries), 0) + me * q_dev).astype(F32)
    far = [
        ref[at : at + CAP, :] * (scale / SOFTMAX_HEAT) for (ref, at), scale in zip(parts, scales)
    ]
    far = far[2::2] + far[1::2] + [jnp.zeros((CAP, queries), F32)]
    own_parts = split_two(dot_pieces(dot_nt, pick, final_ref[...]))
    far_parts = split_two(dot_pieces(dot_nt, pick, jnp.concatenate(far, axis=0)))
    own_parts = jnp.concatenate(own_parts, axis=0)
    far_parts = jnp.concatenate(far_parts, axis=0)

    def upstream_of(at, chunk):
        rows = [ref[:, at : at + chunk].astype(F32)[:CAP] for ref in near]
        rows.append(forwarded_ref[:, at : at + chunk].astype(F32))
        rows.append(jnp.zeros((CAP, chunk), F32))
        both = dot_nn(own_parts, embed_ref[:, at : at + chunk])
        both = both + dot_nn(far_parts, jnp.concatenate(rows, axis=0).astype(BF16))
        return both[:q_dev] + both[q_dev:]

    backward(upstream_of, raw_ref, inverse_length(raw_ref, width), grad_ref, up_ref)


def sum_kernel(*refs):
    total = refs[0][...].astype(F32)
    for ref in refs[1:-1]:
        total = total + ref[...].astype(F32)
    refs[-1][...] = total


def sum_two_kernel(left_ref, right_ref, sent_ref):
    sent_ref[...] = (left_ref[...] + right_ref[...]).astype(BF16)


def sum_split_kernel(*refs):
    terms = [ref[...].astype(F32) for ref in refs[:-2]]
    while len(terms) > 1:
        terms = [a + b for a, b in zip(terms[::2], terms[1::2])]
    rank = refs[-1].shape[0]
    refs[-2][...] = terms[0][:rank]
    refs[-1][...] = terms[0][rank:]


def exchange(values, axis, k):
    size = lax.axis_size(axis)
    return lax.ppermute(values, axis, [(i, i ^ k) for i in range(size)])


def core_step(values, even_step, odd_step):
    outer, inner = lax.axis_size("dp"), lax.axis_size("fsdp")
    pairs = []
    for d in range(outer):
        step = odd_step if d % 2 else even_step
        pairs += [(d * inner + f, d * inner + (f ^ step)) for f in range(inner)]
    return lax.ppermute(values, ("dp", "fsdp"), pairs)


def per_device(
    query_pooled_states,
    passage_pooled_states,
    query_attention_output,
    passage_attention_output,
    positive_passage_row,
    hard_negative_ids,
    passage_home_row,
    adapter_down_weight,
    adapter_up_weight,
):
    group = lax.axis_size("dp")
    shards = lax.axis_size("fsdp")
    query_raw = query_pooled_states[0]
    passage_raw = passage_pooled_states[0]
    query_in = query_attention_output[0]
    passage_in = passage_attention_output[0]
    ids = hard_negative_ids[0]
    q_dev, width = query_raw.shape
    p_dev = passage_raw.shape[0]
    rank, part = adapter_down_weight.shape
    queries = group * q_dev
    slots = group * CAP
    work = 2 * p_dev * width

    packed, adapter, half, positive_row = run(
        front_kernel,
        (
            shape_of((q_dev, width + 2 * ids.shape[1]), BF16),
            shape_of((2 * rank, part), BF16),
            shape_of((rank, part), BF16),
            shape_of((1, queries), jnp.int32),
        ),
        (query_raw, ids, adapter_down_weight, adapter_up_weight, positive_passage_row),
        1,
        [
            pltpu.VMEM(ids.shape, jnp.int32),
            pltpu.VMEM(positive_passage_row.shape, jnp.int32),
            pltpu.SemaphoreType.DMA((5,)),
        ],
        in_hbm=True,
    )
    embed, side, side_row, own_side, low_scale = run(
        passage_norm_kernel,
        (
            shape_of((p_dev, width), BF16),
            shape_of((p_dev, 128), F32),
            shape_of((8, p_dev), F32),
            shape_of((8, queries), F32),
            shape_of((8, q_dev), F32),
        ),
        (query_raw, passage_raw, passage_home_row),
        work,
        [
            pltpu.VMEM(passage_raw.shape, BF16),
            pltpu.VMEM(passage_home_row.shape, jnp.int32),
            pltpu.VMEM(query_raw.shape, BF16),
            pltpu.SemaphoreType.DMA((2 + PASSAGE_CHUNKS,)),
        ],
        in_hbm=True,
    )
    blocks = {0: packed}
    for k in range(2, group, 2):
        blocks[k] = exchange(packed, "dp", k)
    blocks[1] = exchange(packed, "dp", 1)
    for k in range(2, group, 2):
        blocks[k], embed = lax.optimization_barrier((blocks[k], embed))
        blocks[k ^ 1] = exchange(blocks[k], "dp", 1)
    if shards == 4:
        half_block = exchange(half, "fsdp", 3)
        whole_block = core_step(adapter, 1, 2)
        adapter_near = run(
            join_kernel,
            (shape_of((3 * rank, part), BF16),),
            (whole_block, half_block),
            1,
        )[0]
        adapter_blocks = [adapter, adapter_near, exchange(adapter_near, "dp", 1)]
    else:
        adapter_blocks = [adapter] + [exchange(adapter, "fsdp", k) for k in range(1, shards)]
    query_embed, weight, dots, onehot, head = run(
        functools.partial(score_kernel, group),
        (
            shape_of((queries, width), BF16),
            shape_of((p_dev, queries), F32),
            shape_of((p_dev, queries), F32),
            shape_of((slots, p_dev), F32),
            shape_of((HEAD_ROWS, queries), F32),
        ),
        (
            *[blocks[k] for k in range(group)],
            embed,
            side,
            positive_row,
        ),
        work * queries,
        [pltpu.VMEM((queries, 2 * ids.shape[1]), F32)],
    )
    adapter_full, passage_low, message, slot_base = run(
        functools.partial(rank_kernel, shards),
        (
            shape_of((2 * rank, width), BF16),
            shape_of((rank, p_dev), F32),
            shape_of((HEAD_ROWS + rank, queries), F32),
            shape_of((rank, p_dev), F32),
        ),
        (
            *adapter_blocks,
            query_in,
            passage_in,
            embed,
            side_row,
            low_scale,
            onehot,
            head,
        ),
        work * rank,
    )
    stats = [message] + [exchange(message, "dp", k) for k in range(2, group, 2)]
    chips = group // 2
    back_query, local, targets, *row_blocks = run(
        functools.partial(request_kernel, group),
        (
            shape_of((rank, queries), F32),
            shape_of((2 * rank, queries), F32),
            shape_of((2 * rank, queries), F32),
            *[shape_of((2 * CAP, width), BF16)] * chips,
        ),
        (
            embed,
            onehot,
            query_embed,
            adapter_full,
            passage_low,
            slot_base,
            weight,
            positive_row,
        ),
        work * slots,
    )
    stats, row_blocks = lax.optimization_barrier((stats, row_blocks))
    near = [exchange(row_blocks[i], "dp", 2 * i) for i in range(1, chips)]
    near_stats = stack(*stats)
    far_stats = exchange(near_stats, "dp", 1)
    final, *terms = run(
        functools.partial(terms_kernel, group, shards),
        (
            shape_of((p_dev, queries), F32),
            shape_of((2 * rank, part), F32),
            *[shape_of((2 * rank, part), BF16)] * (shards - 1),
        ),
        (
            near_stats,
            far_stats,
            weight,
            dots,
            positive_row,
            query_embed,
            embed,
            back_query,
            slot_base,
            passage_low,
            side_row,
            own_side,
            passage_in,
            query_in,
            local,
            targets,
        ),
        work * rank * 4,
        [pltpu.VMEM((2 * rank, width), F32)],
    )
    arrived = [exchange(terms[k], "fsdp", k) for k in range(1, shards)]
    final, near[0] = lax.optimization_barrier((final, near[0]))
    grad_passage = run(
        passage_kernel,
        (shape_of((p_dev, width), BF16),),
        (final, query_embed, passage_raw, side),
        2 * work * queries,
        [pltpu.VMEM((p_dev, width), F32)],
    )[0]
    terms[0], grad_passage = lax.optimization_barrier((terms[0], grad_passage))
    total = run(sum_kernel, (shape_of((2 * rank, part), F32),), (terms[0], *arrived), 1)[0]
    total, near = lax.optimization_barrier((total, near))
    to_sibling = run(
        forward_kernel,
        (shape_of((group // 2 * CAP, width), BF16),),
        (row_blocks[0], *near),
        1,
    )[0]
    forwarded = exchange(to_sibling, "dp", 1)
    sent = run(
        sum_two_kernel,
        (shape_of((2 * rank, part), BF16),),
        (total, exchange(total, "dp", 1)),
        1,
    )[0]
    arrived = [exchange(sent, "dp", k) for k in range(2, group, 2)]
    grad_query = run(
        functools.partial(query_kernel, group),
        (shape_of((q_dev, width), BF16),),
        (near_stats, far_stats, *near, forwarded, final, embed, query_raw),
        4 * q_dev * width * (p_dev + slots),
        [pltpu.VMEM((q_dev, width), F32)],
    )[0]
    sent, grad_query = lax.optimization_barrier((sent, grad_query))
    down_total, up_total = run(
        sum_split_kernel, (shape_of((rank, part), F32),) * 2, (sent, *arrived), 1
    )
    return (grad_query[None], grad_passage[None], down_total, up_total)


def solution(mesh):
    in_specs = (
        P("fsdp", "dp", None),
        P("fsdp", "dp", None),
        P("fsdp", "dp", None),
        P("fsdp", "dp", None),
        P("fsdp", "dp"),
        P("fsdp", "dp", None),
        P("fsdp", None),
        P(None, "fsdp"),
        P(None, "fsdp"),
    )
    out_specs = (P("fsdp", "dp", None), P("fsdp", "dp", None), P(None, "fsdp"), P(None, "fsdp"))
    return jax.shard_map(
        per_device, mesh=mesh, in_specs=in_specs, out_specs=out_specs, check_vma=False
    )
```

```python
import functools

import jax
import jax.numpy as jnp
from jax import lax
from jax.experimental import pallas as pl
from jax.experimental.pallas import tpu as pltpu
from jax.sharding import PartitionSpec as P

CAP = 8
SOFTMAX_HEAT = 0.01
ADAPTER_SCALE = 2.0
EPSILON = 1e-06
LOWEST = -1e30
ID_BASE = 256
TOP_ROW, SUM_ROW, DOT_ROW, HEAD_ROWS = 8, 9, 10, 16
VMEM_BYTES = 16 * 1024 * 1024
PASSAGE_CHUNKS = 4
F32 = jnp.float32
BF16 = jnp.bfloat16


def dot_nn(a, b, precision=None):
    return lax.dot_general(
        a, b, (((1,), (0,)), ((), ())), precision=precision, preferred_element_type=F32
    )


def dot_nt(a, b, precision=None):
    return lax.dot_general(
        a, b, (((1,), (1,)), ((), ())), precision=precision, preferred_element_type=F32
    )


def split_two(values):
    high = values.astype(BF16)
    low = (values - high.astype(F32)).astype(BF16)
    return high, low


def dot_pieces(dot, a, b):
    rows = a.shape[0]
    a_high, a_low = split_two(a)
    b_high, b_low = split_two(b)
    both = dot(jnp.concatenate([a_high, a_low], axis=0), b_high)
    return both[:rows] + both[rows:] + dot(a_high, b_low)


def iota(shape, dim):
    return lax.broadcasted_iota(jnp.int32, shape, dim)


def shape_of(dims, kind):
    return jax.ShapeDtypeStruct(dims, kind)


def run(body, out_shape, args, flops, scratch=(), in_hbm=False):
    grant = VMEM_BYTES * max(1, size_ratio(args))
    if in_hbm:
        args = [pltpu.with_memory_space_constraint(a, pltpu.HBM) for a in args]
    vmem = pl.BlockSpec(memory_space=pltpu.VMEM)
    hbm = pl.BlockSpec(memory_space=pltpu.HBM)
    moved = sum(a.size * a.dtype.itemsize for a in (*args, *out_shape))
    return pl.pallas_call(
        body,
        out_shape=out_shape,
        in_specs=[hbm if in_hbm else vmem] * len(args),
        out_specs=tuple(vmem for _ in out_shape),
        scratch_shapes=list(scratch),
        compiler_params=pltpu.CompilerParams(vmem_limit_bytes=grant),
        cost_estimate=pl.CostEstimate(flops=flops, bytes_accessed=moved, transcendentals=0),
    )(*args)


def size_ratio(args):
    moved = sum(a.size * a.dtype.itemsize for a in args)
    return -(-moved * 3 // VMEM_BYTES)


def inverse_length(raw_ref, width):
    chunk = min(width, 512)
    total = jnp.zeros((raw_ref.shape[0], 1), F32)
    for at in range(0, width, chunk):
        part = raw_ref[:, at : at + chunk].astype(F32)
        total = total + jnp.sum(part * part, axis=-1, keepdims=True)
    return 1.0 / jnp.sqrt(total + EPSILON)


def front_kernel(
    query_ref,
    ids_ref,
    down_ref,
    up_ref,
    positive_ref,
    out_ref,
    adapter_ref,
    half_ref,
    tiled_ref,
    ids_here,
    positive_here,
    sems,
):
    width = query_ref.shape[1]
    rank = down_ref.shape[0]
    me = lax.axis_index("dp")
    pairs = (
        (ids_ref, ids_here),
        (query_ref, out_ref.at[:, pl.ds(0, width)]),
        (positive_ref, positive_here),
        (down_ref, adapter_ref.at[pl.ds(0, rank), :]),
        (up_ref, adapter_ref.at[pl.ds(rank, rank), :]),
    )
    copies = [pltpu.make_async_copy(a, b, sems.at[i]) for i, (a, b) in enumerate(pairs)]
    for copy in copies:
        copy.start()
    copies[0].wait()
    ids = ids_here[...]
    coded = jnp.concatenate([ids // ID_BASE, ids % ID_BASE], axis=1)
    out_ref[:, width:] = coded.astype(F32).astype(BF16)
    copies[2].wait()
    q_dev = positive_here.shape[1]
    for at in range(0, tiled_ref.shape[1], q_dev):
        tiled_ref[:, at : at + q_dev] = positive_here[...]
    copies[3].wait()
    copies[4].wait()

    @pl.when(me % 2 == 0)
    def _():
        half_ref[...] = adapter_ref[:rank, :]

    @pl.when(me % 2 == 1)
    def _():
        half_ref[...] = adapter_ref[rank:, :]

    copies[1].wait()


def passage_norm_kernel(
    passage_ref, home_ref, embed_ref, side_ref, row_ref, passage_here, home_here, sems
):
    rows, width = passage_ref.shape
    total = home_ref.shape[1]
    me = lax.axis_index("dp")
    part = rows // PASSAGE_CHUNKS
    home_copy = pltpu.make_async_copy(home_ref, home_here, sems.at[0])
    home_copy.start()
    passage_copies = []
    for c in range(PASSAGE_CHUNKS):
        here = pl.ds(c * part, part)
        passage_copies.append(
            pltpu.make_async_copy(
                passage_ref.at[here, :], passage_here.at[here, :], sems.at[1 + c]
            )
        )
        passage_copies[c].start()

    home_copy.wait()
    row_id = iota((rows, total), 0) + me * rows
    number = iota((rows, total), 1)
    home = jnp.where(home_here[...] == row_id, number, 0).astype(F32)
    home = jnp.sum(home, axis=1, keepdims=True)

    chunk = min(width, 512)
    inverses = []
    for c in range(PASSAGE_CHUNKS):
        passage_copies[c].wait()
        here = slice(c * part, (c + 1) * part)
        inverse = inverse_length(passage_here.at[here, :], width)
        for at in range(0, width, chunk):
            values = passage_here[here, at : at + chunk].astype(F32)
            embed_ref[here, at : at + chunk] = (values * inverse).astype(BF16)
        inverses.append(inverse)
    inverse = jnp.concatenate(inverses, axis=0)
    side_ref[...] = jnp.where(iota(side_ref.shape, 1) == 0, inverse, home)
    row_ref[...] = jnp.broadcast_to(inverse, (rows, rows)).T[: row_ref.shape[0]]


def stack_kernel(*refs):
    out_ref = refs[-1]
    rows = refs[0].shape[0]
    for i, ref in enumerate(refs[:-1]):
        out_ref[i * rows : (i + 1) * rows, :] = ref[...]


def stack(*parts):
    rows, cols = parts[0].shape
    return run(stack_kernel, (shape_of((len(parts) * rows, cols), parts[0].dtype),), parts, 1)[0]


def join_kernel(first_ref, second_ref, out_ref):
    rows = first_ref.shape[0]
    out_ref[:rows, :] = first_ref[...]
    out_ref[rows:, :] = second_ref[...]


def place_paired(own_ref, near_ref, far_ref, weights_ref):
    rank, part = own_ref.shape[0] // 2, own_ref.shape[1]
    me = lax.axis_index("fsdp")
    core = lax.axis_index("dp") % 2

    def columns(k):
        return pl.ds(pl.multiple_of((me ^ k) * part, part), part)

    def place(even_ref, odd_ref):
        weights_ref[:, columns(1)] = even_ref[: 2 * rank, :]
        weights_ref[:, columns(2)] = odd_ref[: 2 * rank, :]
        weights_ref[:rank, columns(3)] = even_ref[2 * rank :, :]
        weights_ref[rank:, columns(3)] = odd_ref[2 * rank :, :]

    weights_ref[:, columns(0)] = own_ref[...]
    pl.when(core == 0)(functools.partial(place, near_ref, far_ref))
    pl.when(core == 1)(functools.partial(place, far_ref, near_ref))


def place_blocks(*refs):
    part = refs[0].shape[1]
    me = lax.axis_index("fsdp")
    for k, ref in enumerate(refs[:-1]):
        refs[-1][:, pl.ds(pl.multiple_of((me ^ k) * part, part), part)] = ref[...]


def rank_kernel(shards, *refs):
    blocks = refs[:-12]
    query_ref, query_in_ref, passage_in_ref, embed_ref, row_ref = refs[-12:-7]
    onehot_ref, head_ref = refs[-7:-5]
    weights_ref, passage_low_ref, message_ref, own_ref, base_ref = refs[-5:]
    slots = onehot_ref.shape[0]
    rank = blocks[0].shape[0] // 2
    q_dev, width = query_ref.shape
    queries = own_ref.shape[1]
    place = place_paired if shards == 4 else place_blocks
    place(*blocks, weights_ref)
    down, up = weights_ref[:rank, :], weights_ref[rank:, :]
    start = lax.axis_index("dp") * q_dev
    place = iota((q_dev, queries), 1) == iota((q_dev, queries), 0) + start
    inverse = inverse_length(query_ref, width)
    own = jnp.sum(jnp.where(place, inverse, 0.0), axis=0, keepdims=True)
    own_ref[...] = jnp.broadcast_to(own, own_ref.shape)
    same = iota((q_dev, q_dev), 0) == iota((q_dev, q_dev), 1)
    inverse_row = jnp.sum(jnp.where(same, inverse, 0.0), axis=0, keepdims=True)
    query_low = dot_nt(down, query_in_ref[...]).astype(BF16)
    message_ref[HEAD_ROWS:, slots : slots + q_dev] = query_low.astype(F32) * inverse_row
    passage_low = dot_nt(down, passage_in_ref[...]).astype(BF16)
    passage_low_ref[...] = passage_low.astype(F32) * row_ref[0:1, :]
    base = dot_nt(up, embed_ref[...])
    base_ref[...] = base
    message_ref[:HEAD_ROWS, :] = head_ref[...]
    message_ref[HEAD_ROWS:, :slots] = dot_pieces(dot_nt, base, onehot_ref[...])
    unused = jnp.zeros((rank, queries - slots - q_dev), F32)
    message_ref[HEAD_ROWS:, slots + q_dev :] = unused


def score_kernel(group, *refs):
    blocks = refs[:group]
    embed_ref, side_ref, positive_ref = refs[group : group + 3]
    query_ref, weight_ref, dots_ref, onehot_ref, head_ref, coded_ref = refs[group + 3 :]
    rows, width = embed_ref.shape
    queries = query_ref.shape[0]
    q_dev = queries // group
    negatives = (blocks[0].shape[1] - width) // 2
    slots = group * CAP
    me = lax.axis_index("dp")
    chunk = min(width, 1024)
    for k in range(group):
        start = pl.multiple_of((me ^ k) * q_dev, q_dev)
        inverse = inverse_length(blocks[k], width)
        for at in range(0, width, chunk):
            part = blocks[k][:, at : at + chunk].astype(F32)
            query_ref[pl.ds(start, q_dev), at : at + chunk] = (part * inverse).astype(BF16)
        coded = blocks[k][:, width:].astype(F32)
        coded_ref[pl.ds(start, q_dev), :] = coded
    dots = dot_nt(embed_ref[...], query_ref[...])
    dots_ref[...] = dots
    scores = dots / SOFTMAX_HEAT

    coded = coded_ref[...].T
    ids = coded[:negatives] * float(ID_BASE) + coded[negatives:]
    home = jnp.broadcast_to(side_ref[:, 1:2], (rows, queries))
    count = jnp.zeros((rows, queries), F32)
    for j in range(negatives):
        count = count + jnp.where(ids[j : j + 1, :] == home, 1.0, 0.0)
    members = iota((slots, queries), 0) // CAP == iota((slots, queries), 1) // q_dev
    marked = dot_nt(members.astype(BF16), count.astype(BF16)) > 0.0
    before = (iota((rows, rows), 0) <= iota((rows, rows), 1)).astype(BF16)
    rank_in = dot_nn(marked.astype(F32).astype(BF16), before)
    wanted = (iota((slots, rows), 0) % CAP + 1).astype(F32)
    onehot = jnp.where(marked & (rank_in == wanted), 1.0, 0.0)
    onehot_ref[...] = onehot

    own = iota((rows, queries), 1) // q_dev == me
    count = count + jnp.where(own & (positive_ref[...] == iota((rows, queries), 0)), 1.0, 0.0)
    named = count > 0.0
    top = jnp.max(jnp.where(named, scores, LOWEST), axis=0, keepdims=True)
    weight = count * jnp.exp(jnp.where(named, scores - top, LOWEST))
    weight_ref[...] = weight
    total = jnp.sum(weight, axis=0, keepdims=True)
    dot_total = jnp.sum(weight * dots, axis=0, keepdims=True)
    slot_weight = dot_pieces(dot_nn, onehot, weight)
    tail_row = iota((HEAD_ROWS - CAP, queries), 0)
    tail = jnp.where(tail_row == 0, top, jnp.where(tail_row == 1, total, dot_total))
    lane_group = iota((CAP, queries), 1) // q_dev
    compact = jnp.zeros((CAP, queries), F32)
    for peer in range(group):
        part = slot_weight[peer * CAP : (peer + 1) * CAP]
        compact = jnp.where(lane_group == peer, part, compact)
    head_ref[:CAP, :] = compact
    head_ref[CAP:, :] = tail


def request_kernel(group, *refs):
    (
        embed_ref,
        onehot_ref,
        query_ref,
        weights_ref,
        low_ref,
        base_ref,
        weight_ref,
        positive_ref,
        back_ref,
        local_ref,
        target_ref,
    ) = refs[:11]
    blocks = refs[11:]
    width = embed_ref.shape[1]
    rows, queries = weight_ref.shape
    me = lax.axis_index("dp")
    onehot = [
        onehot_ref[pl.ds(pl.multiple_of((me ^ k) * CAP, CAP), CAP), :] for k in range(group)
    ]
    onehot = jnp.concatenate(onehot, axis=0).astype(BF16)
    chunk = min(width, 1024)
    for at in range(0, width, chunk):
        part = dot_nn(onehot, embed_ref[:, at : at + chunk]).astype(BF16)
        for i, block in enumerate(blocks):
            block[:, at : at + chunk] = part[2 * i * CAP : 2 * (i + 1) * CAP]
    back_ref[...] = dot_nt(weights_ref[weights_ref.shape[0] // 2 :, :], query_ref[...])
    both = jnp.concatenate([low_ref[...], base_ref[...]], axis=0)
    local_ref[...] = dot_pieces(dot_nn, both, weight_ref[...])
    target = own_target(positive_ref, rows, queries, queries // group, me)
    target_ref[...] = dot_pieces(dot_nn, both, target)


def forward_kernel(*refs):
    halves = [ref[...].astype(F32)[CAP:] for ref in refs[:-1]]
    refs[-1][...] = jnp.concatenate(halves, axis=0).astype(BF16)


def message_parts(near_ref, far_ref, group):
    rows = near_ref.shape[0] // (group // 2)
    return [((near_ref, far_ref)[k % 2], k // 2 * rows) for k in range(group)]


def combine(parts):
    tops = [ref[at + TOP_ROW : at + TOP_ROW + 1, :] for ref, at in parts]
    sums = [ref[at + SUM_ROW : at + SUM_ROW + 1, :] for ref, at in parts]
    top = functools.reduce(jnp.maximum, tops)
    scales = [jnp.exp(t - top) for t in tops]
    inverse_total = 1.0 / sum(t * s for t, s in zip(scales, sums))
    return [scale * inverse_total for scale in scales]


def own_target(positive_ref, rows, queries, q_dev, me):
    own = iota((rows, queries), 1) // q_dev == me
    return jnp.where(own & (positive_ref[...] == iota((rows, queries), 0)), 1.0, 0.0)


def terms_kernel(group, shards, near_ref, far_ref, *refs):
    parts = message_parts(near_ref, far_ref, group)
    (
        weight_ref,
        dots_ref,
        positive_ref,
        query_ref,
        embed_ref,
        back_query_ref,
        back_passage_ref,
        passage_low_ref,
        row_ref,
        own_ref,
        passage_in_ref,
        query_in_ref,
        local_ref,
        target_ref,
    ) = refs[:14]
    final_ref = refs[14]
    blocks = refs[15 : 15 + shards]
    (sum_ref,) = refs[15 + shards :]
    rows, queries = weight_ref.shape
    q_dev = queries // group
    rank = passage_low_ref.shape[0]
    width = query_ref.shape[1]
    me = lax.axis_index("dp")

    scales = combine(parts)
    target = own_target(positive_ref, rows, queries, q_dev, me)
    weight = (weight_ref[...] * scales[0] - target) / SOFTMAX_HEAT
    final_ref[...] = weight
    dots = dots_ref[...]
    ones = jnp.ones((16, queries), F32)
    inner = dot_pieces(dot_nt, ones, weight * dots)[0:1, :]

    inner_query = -jnp.sum(target * dots, axis=0, keepdims=True)
    own_dots = near_ref[DOT_ROW : DOT_ROW + 1, :]
    share = (scales[0] * own_dots + inner_query) / SOFTMAX_HEAT
    slots = group * CAP
    bases, query_low = [], []
    for (ref, at), scale in zip(parts, scales):
        inner_query = inner_query + scale * ref[at + DOT_ROW : at + DOT_ROW + 1, :]
        bases.append(ref[at + HEAD_ROWS : at + HEAD_ROWS + rank, :])
        query_low.append(ref[at + HEAD_ROWS : at + HEAD_ROWS + rank, :])
    low_total = jnp.zeros((rank, queries), F32)
    lane_group = iota((rank, queries), 1) // q_dev
    for k, rows_at in enumerate(query_low):
        shift = lax.rem((me ^ k) * q_dev + queries - slots, queries)
        rolled = pltpu.roll(rows_at, shift, 1)
        low_total = low_total + jnp.where(lane_group == (me ^ k), rolled, 0.0)
    query_low = low_total
    shift = lax.rem(queries - me * CAP, queries)
    bases = pltpu.roll(jnp.concatenate(bases[1:], axis=0), shift, 1)[:, :CAP]
    far_base = [bases[k * rank : (k + 1) * rank] for k in range(group - 1)]
    far_weight = [
        ref[at : at + CAP, :] * (scale / SOFTMAX_HEAT)
        for (ref, at), scale in zip(parts[1:], scales[1:])
    ]
    inner_query = inner_query / SOFTMAX_HEAT

    passage_low = passage_low_ref[...]
    local = (local_ref[...] * scales[0] - target_ref[...]) / SOFTMAX_HEAT
    from_query = local[:rank] - query_low * share
    from_passage = dot_pieces(dot_nt, query_low, weight) - passage_low * inner
    query_parts = jnp.concatenate(split_two(from_query), axis=0)
    passage_parts = jnp.concatenate(split_two(from_passage), axis=0)

    back_passage = dot_pieces(dot_nt, back_query_ref[...], weight)
    back_passage = (back_passage - back_passage_ref[...] * inner) * row_ref[0:1, :]
    back_passage = back_passage.astype(BF16)
    back_query = local[rank:] + dot_pieces(
        dot_nn, jnp.concatenate(far_base, axis=1), jnp.concatenate(far_weight, axis=0)
    )
    back_query = (back_query - back_query_ref[...] * inner_query) * own_ref[0:1, :]
    pick = (iota((q_dev, queries), 1) == iota((q_dev, queries), 0) + me * q_dev).astype(BF16)
    back_query = dot_nt(back_query.astype(BF16), pick).astype(BF16)

    chunk = min(width, 512)
    for at in range(0, width, chunk):
        cols = slice(at, at + chunk)
        both = dot_nn(query_parts, query_ref[:, cols]) + dot_nn(passage_parts, embed_ref[:, cols])
        sum_ref[rank:, cols] = ADAPTER_SCALE * (both[:rank] + both[rank:])
        sum_ref[:rank, cols] = ADAPTER_SCALE * (
            dot_nn(back_passage, passage_in_ref[:, cols])
            + dot_nn(back_query, query_in_ref[:, cols])
        )
    part = width // shards
    home = lax.axis_index("fsdp")
    for k in range(shards):
        start = pl.multiple_of((home ^ k) * part, part)
        blocks[k][...] = sum_ref[:, pl.ds(start, part)].astype(blocks[k].dtype)


def backward(upstream_of, raw_ref, inverse, grad_ref, up_ref):
    rows, width = raw_ref.shape
    chunk = min(width, 512)
    inner = jnp.zeros((rows, 1), F32)
    for at in range(0, width, chunk):
        upstream = upstream_of(at, chunk)
        up_ref[:, at : at + chunk] = upstream
        unit = raw_ref[:, at : at + chunk].astype(F32) * inverse
        inner = inner + jnp.sum(unit * upstream, axis=-1, keepdims=True)
    for at in range(0, width, chunk):
        unit = raw_ref[:, at : at + chunk].astype(F32) * inverse
        grad = (up_ref[:, at : at + chunk] - unit * inner) * inverse
        grad_ref[:, at : at + chunk] = grad.astype(BF16)


def passage_kernel(final_ref, query_ref, raw_ref, side_ref, grad_ref, up_ref):
    high, low = split_two(final_ref[...])

    def upstream_of(at, chunk):
        embed = query_ref[:, at : at + chunk]
        return dot_nn(high, embed) + dot_nn(low, embed)

    backward(upstream_of, raw_ref, side_ref[:, 0:1], grad_ref, up_ref)


def query_kernel(group, near_ref, far_ref, *refs):
    parts = message_parts(near_ref, far_ref, group)
    near = refs[: group // 2 - 1]
    forwarded_ref, final_ref, embed_ref, raw_ref, grad_ref, up_ref = refs[group // 2 - 1 :]
    q_dev, width = raw_ref.shape
    queries = final_ref.shape[1]
    me = lax.axis_index("dp")
    scales = combine(parts)
    pick = (iota((q_dev, queries), 1) == iota((q_dev, queries), 0) + me * q_dev).astype(F32)
    far = [
        ref[at : at + CAP, :] * (scale / SOFTMAX_HEAT) for (ref, at), scale in zip(parts, scales)
    ]
    far = far[2::2] + far[1::2] + [jnp.zeros((CAP, queries), F32)]
    own_parts = split_two(dot_pieces(dot_nt, pick, final_ref[...]))
    far_parts = split_two(dot_pieces(dot_nt, pick, jnp.concatenate(far, axis=0)))
    own_parts = jnp.concatenate(own_parts, axis=0)
    far_parts = jnp.concatenate(far_parts, axis=0)

    def upstream_of(at, chunk):
        rows = [ref[:, at : at + chunk].astype(F32)[:CAP] for ref in near]
        rows.append(forwarded_ref[:, at : at + chunk].astype(F32))
        rows.append(jnp.zeros((CAP, chunk), F32))
        both = dot_nn(own_parts, embed_ref[:, at : at + chunk])
        both = both + dot_nn(far_parts, jnp.concatenate(rows, axis=0).astype(BF16))
        return both[:q_dev] + both[q_dev:]

    backward(upstream_of, raw_ref, inverse_length(raw_ref, width), grad_ref, up_ref)


def sum_kernel(*refs):
    total = refs[0][...].astype(F32)
    for ref in refs[1:-1]:
        total = total + ref[...].astype(F32)
    refs[-1][...] = total


def sum_two_kernel(left_ref, right_ref, sent_ref):
    sent_ref[...] = (left_ref[...] + right_ref[...]).astype(BF16)


def sum_split_kernel(*refs):
    terms = [ref[...].astype(F32) for ref in refs[:-2]]
    while len(terms) > 1:
        terms = [a + b for a, b in zip(terms[::2], terms[1::2])]
    rank = refs[-1].shape[0]
    refs[-2][...] = terms[0][:rank]
    refs[-1][...] = terms[0][rank:]


def exchange(values, axis, k):
    size = lax.axis_size(axis)
    return lax.ppermute(values, axis, [(i, i ^ k) for i in range(size)])


def core_step(values, even_step, odd_step):
    outer, inner = lax.axis_size("dp"), lax.axis_size("fsdp")
    pairs = []
    for d in range(outer):
        step = odd_step if d % 2 else even_step
        pairs += [(d * inner + f, d * inner + (f ^ step)) for f in range(inner)]
    return lax.ppermute(values, ("dp", "fsdp"), pairs)


def per_device(
    query_pooled_states,
    passage_pooled_states,
    query_attention_output,
    passage_attention_output,
    positive_passage_row,
    hard_negative_ids,
    passage_home_row,
    adapter_down_weight,
    adapter_up_weight,
):
    group = lax.axis_size("dp")
    shards = lax.axis_size("fsdp")
    query_raw = query_pooled_states[0]
    passage_raw = passage_pooled_states[0]
    query_in = query_attention_output[0]
    passage_in = passage_attention_output[0]
    ids = hard_negative_ids[0]
    q_dev, width = query_raw.shape
    p_dev = passage_raw.shape[0]
    rank, part = adapter_down_weight.shape
    queries = group * q_dev
    slots = group * CAP
    work = 2 * p_dev * width

    packed, adapter, half, positive_row = run(
        front_kernel,
        (
            shape_of((q_dev, width + 2 * ids.shape[1]), BF16),
            shape_of((2 * rank, part), BF16),
            shape_of((rank, part), BF16),
            shape_of((1, queries), jnp.int32),
        ),
        (query_raw, ids, adapter_down_weight, adapter_up_weight, positive_passage_row),
        1,
        [
            pltpu.VMEM(ids.shape, jnp.int32),
            pltpu.VMEM(positive_passage_row.shape, jnp.int32),
            pltpu.SemaphoreType.DMA((5,)),
        ],
        in_hbm=True,
    )
    embed, side, side_row = run(
        passage_norm_kernel,
        (
            shape_of((p_dev, width), BF16),
            shape_of((p_dev, 128), F32),
            shape_of((8, p_dev), F32),
        ),
        (passage_raw, passage_home_row),
        work,
        [
            pltpu.VMEM(passage_raw.shape, BF16),
            pltpu.VMEM(passage_home_row.shape, jnp.int32),
            pltpu.SemaphoreType.DMA((1 + PASSAGE_CHUNKS,)),
        ],
        in_hbm=True,
    )
    blocks = {0: packed}
    for k in range(2, group, 2):
        blocks[k] = exchange(packed, "dp", k)
    blocks[1] = exchange(packed, "dp", 1)
    for k in range(2, group, 2):
        blocks[k], embed = lax.optimization_barrier((blocks[k], embed))
        blocks[k ^ 1] = exchange(blocks[k], "dp", 1)
    if shards == 4:
        half_block = exchange(half, "fsdp", 3)
        whole_block = core_step(adapter, 1, 2)
        adapter_near = run(
            join_kernel,
            (shape_of((3 * rank, part), BF16),),
            (whole_block, half_block),
            1,
        )[0]
        adapter_blocks = [adapter, adapter_near, exchange(adapter_near, "dp", 1)]
    else:
        adapter_blocks = [adapter] + [exchange(adapter, "fsdp", k) for k in range(1, shards)]
    query_embed, weight, dots, onehot, head = run(
        functools.partial(score_kernel, group),
        (
            shape_of((queries, width), BF16),
            shape_of((p_dev, queries), F32),
            shape_of((p_dev, queries), F32),
            shape_of((slots, p_dev), F32),
            shape_of((HEAD_ROWS, queries), F32),
        ),
        (
            *[blocks[k] for k in range(group)],
            embed,
            side,
            positive_row,
        ),
        work * queries,
        [pltpu.VMEM((queries, 2 * ids.shape[1]), F32)],
    )
    adapter_full, passage_low, message, own_side, slot_base = run(
        functools.partial(rank_kernel, shards),
        (
            shape_of((2 * rank, width), BF16),
            shape_of((rank, p_dev), F32),
            shape_of((HEAD_ROWS + rank, queries), F32),
            shape_of((8, queries), F32),
            shape_of((rank, p_dev), F32),
        ),
        (
            *adapter_blocks,
            query_raw,
            query_in,
            passage_in,
            embed,
            side_row,
            onehot,
            head,
        ),
        work * rank,
    )
    stats = [message] + [exchange(message, "dp", k) for k in range(2, group, 2)]
    chips = group // 2
    back_query, local, targets, *row_blocks = run(
        functools.partial(request_kernel, group),
        (
            shape_of((rank, queries), F32),
            shape_of((2 * rank, queries), F32),
            shape_of((2 * rank, queries), F32),
            *[shape_of((2 * CAP, width), BF16)] * chips,
        ),
        (
            embed,
            onehot,
            query_embed,
            adapter_full,
            passage_low,
            slot_base,
            weight,
            positive_row,
        ),
        work * slots,
    )
    stats, row_blocks = lax.optimization_barrier((stats, row_blocks))
    near = [exchange(row_blocks[i], "dp", 2 * i) for i in range(1, chips)]
    near_stats = stack(*stats)
    far_stats = exchange(near_stats, "dp", 1)
    final, *terms = run(
        functools.partial(terms_kernel, group, shards),
        (
            shape_of((p_dev, queries), F32),
            shape_of((2 * rank, part), F32),
            *[shape_of((2 * rank, part), BF16)] * (shards - 1),
        ),
        (
            near_stats,
            far_stats,
            weight,
            dots,
            positive_row,
            query_embed,
            embed,
            back_query,
            slot_base,
            passage_low,
            side_row,
            own_side,
            passage_in,
            query_in,
            local,
            targets,
        ),
        work * rank * 4,
        [pltpu.VMEM((2 * rank, width), F32)],
    )
    arrived = [exchange(terms[k], "fsdp", k) for k in range(1, shards)]
    final, near[0] = lax.optimization_barrier((final, near[0]))
    grad_passage = run(
        passage_kernel,
        (shape_of((p_dev, width), BF16),),
        (final, query_embed, passage_raw, side),
        2 * work * queries,
        [pltpu.VMEM((p_dev, width), F32)],
    )[0]
    terms[0], grad_passage = lax.optimization_barrier((terms[0], grad_passage))
    total = run(sum_kernel, (shape_of((2 * rank, part), F32),), (terms[0], *arrived), 1)[0]
    total, near = lax.optimization_barrier((total, near))
    to_sibling = run(
        forward_kernel,
        (shape_of((group // 2 * CAP, width), BF16),),
        (row_blocks[0], *near),
        1,
    )[0]
    forwarded = exchange(to_sibling, "dp", 1)
    sent = run(
        sum_two_kernel,
        (shape_of((2 * rank, part), BF16),),
        (total, exchange(total, "dp", 1)),
        1,
    )[0]
    arrived = [exchange(sent, "dp", k) for k in range(2, group, 2)]
    grad_query = run(
        functools.partial(query_kernel, group),
        (shape_of((q_dev, width), BF16),),
        (near_stats, far_stats, *near, forwarded, final, embed, query_raw),
        4 * q_dev * width * (p_dev + slots),
        [pltpu.VMEM((q_dev, width), F32)],
    )[0]
    sent, grad_query = lax.optimization_barrier((sent, grad_query))
    down_total, up_total = run(
        sum_split_kernel, (shape_of((rank, part), F32),) * 2, (sent, *arrived), 1
    )
    return (grad_query[None], grad_passage[None], down_total, up_total)


def solution(mesh):
    in_specs = (
        P("fsdp", "dp", None),
        P("fsdp", "dp", None),
        P("fsdp", "dp", None),
        P("fsdp", "dp", None),
        P("fsdp", "dp"),
        P("fsdp", "dp", None),
        P("fsdp", None),
        P(None, "fsdp"),
        P(None, "fsdp"),
    )
    out_specs = (P("fsdp", "dp", None), P("fsdp", "dp", None), P(None, "fsdp"), P(None, "fsdp"))
    return jax.shard_map(
        per_device, mesh=mesh, in_specs=in_specs, out_specs=out_specs, check_vma=False
    )
```

```python
import functools

import jax
import jax.numpy as jnp
from jax import lax
from jax.experimental import pallas as pl
from jax.experimental.pallas import tpu as pltpu
from jax.sharding import PartitionSpec as P

CAP = 8
SOFTMAX_HEAT = 0.01
ADAPTER_SCALE = 2.0
EPSILON = 1e-06
LOWEST = -1e30
ID_BASE = 256
TOP_ROW, SUM_ROW, DOT_ROW, HEAD_ROWS = 8, 9, 10, 16
VMEM_BYTES = 16 * 1024 * 1024
PASSAGE_CHUNKS = 4
F32 = jnp.float32
BF16 = jnp.bfloat16


def dot_nn(a, b, precision=None):
    return lax.dot_general(
        a, b, (((1,), (0,)), ((), ())), precision=precision, preferred_element_type=F32
    )


def dot_nt(a, b, precision=None):
    return lax.dot_general(
        a, b, (((1,), (1,)), ((), ())), precision=precision, preferred_element_type=F32
    )


def split_two(values):
    high = values.astype(BF16)
    low = (values - high.astype(F32)).astype(BF16)
    return high, low


def dot_pieces(dot, a, b):
    rows = a.shape[0]
    a_high, a_low = split_two(a)
    b_high, b_low = split_two(b)
    both = dot(jnp.concatenate([a_high, a_low], axis=0), b_high)
    return both[:rows] + both[rows:] + dot(a_high, b_low)


def iota(shape, dim):
    return lax.broadcasted_iota(jnp.int32, shape, dim)


def shape_of(dims, kind):
    return jax.ShapeDtypeStruct(dims, kind)


def run(body, out_shape, args, flops, scratch=(), in_hbm=False):
    grant = VMEM_BYTES * max(1, size_ratio(args))
    if in_hbm:
        args = [pltpu.with_memory_space_constraint(a, pltpu.HBM) for a in args]
    vmem = pl.BlockSpec(memory_space=pltpu.VMEM)
    hbm = pl.BlockSpec(memory_space=pltpu.HBM)
    moved = sum(a.size * a.dtype.itemsize for a in (*args, *out_shape))
    return pl.pallas_call(
        body,
        out_shape=out_shape,
        in_specs=[hbm if in_hbm else vmem] * len(args),
        out_specs=tuple(vmem for _ in out_shape),
        scratch_shapes=list(scratch),
        compiler_params=pltpu.CompilerParams(vmem_limit_bytes=grant),
        cost_estimate=pl.CostEstimate(flops=flops, bytes_accessed=moved, transcendentals=0),
    )(*args)


def size_ratio(args):
    moved = sum(a.size * a.dtype.itemsize for a in args)
    return -(-moved * 3 // VMEM_BYTES)


def inverse_length(raw_ref, width):
    chunk = min(width, 512)
    total = jnp.zeros((raw_ref.shape[0], 1), F32)
    for at in range(0, width, chunk):
        part = raw_ref[:, at : at + chunk].astype(F32)
        total = total + jnp.sum(part * part, axis=-1, keepdims=True)
    return 1.0 / jnp.sqrt(total + EPSILON)


def front_kernel(
    query_ref,
    ids_ref,
    down_ref,
    up_ref,
    positive_ref,
    out_ref,
    adapter_ref,
    half_ref,
    tiled_ref,
    ids_here,
    positive_here,
    sems,
):
    width = query_ref.shape[1]
    rank = down_ref.shape[0]
    me = lax.axis_index("dp")
    pairs = (
        (ids_ref, ids_here),
        (query_ref, out_ref.at[:, pl.ds(0, width)]),
        (positive_ref, positive_here),
        (down_ref, adapter_ref.at[pl.ds(0, rank), :]),
        (up_ref, adapter_ref.at[pl.ds(rank, rank), :]),
    )
    copies = [pltpu.make_async_copy(a, b, sems.at[i]) for i, (a, b) in enumerate(pairs)]
    for copy in copies:
        copy.start()
    copies[0].wait()
    ids = ids_here[...]
    coded = jnp.concatenate([ids // ID_BASE, ids % ID_BASE], axis=1)
    out_ref[:, width:] = coded.astype(F32).astype(BF16)
    copies[2].wait()
    q_dev = positive_here.shape[1]
    for at in range(0, tiled_ref.shape[1], q_dev):
        tiled_ref[:, at : at + q_dev] = positive_here[...]
    copies[3].wait()
    copies[4].wait()

    @pl.when(me % 2 == 0)
    def _():
        half_ref[...] = adapter_ref[:rank, :]

    @pl.when(me % 2 == 1)
    def _():
        half_ref[...] = adapter_ref[rank:, :]

    copies[1].wait()


def passage_norm_kernel(
    passage_ref, home_ref, embed_ref, side_ref, row_ref, passage_here, home_here, sems
):
    rows, width = passage_ref.shape
    total = home_ref.shape[1]
    me = lax.axis_index("dp")
    part = rows // PASSAGE_CHUNKS
    home_copy = pltpu.make_async_copy(home_ref, home_here, sems.at[0])
    home_copy.start()
    passage_copies = []
    for c in range(PASSAGE_CHUNKS):
        here = pl.ds(c * part, part)
        passage_copies.append(
            pltpu.make_async_copy(
                passage_ref.at[here, :], passage_here.at[here, :], sems.at[1 + c]
            )
        )
        passage_copies[c].start()

    home_copy.wait()
    row_id = iota((rows, total), 0) + me * rows
    number = iota((rows, total), 1)
    home = jnp.where(home_here[...] == row_id, number, 0).astype(F32)
    home = jnp.sum(home, axis=1, keepdims=True)

    chunk = min(width, 512)
    inverses = []
    for c in range(PASSAGE_CHUNKS):
        passage_copies[c].wait()
        here = slice(c * part, (c + 1) * part)
        inverse = inverse_length(passage_here.at[here, :], width)
        for at in range(0, width, chunk):
            values = passage_here[here, at : at + chunk].astype(F32)
            embed_ref[here, at : at + chunk] = (values * inverse).astype(BF16)
        inverses.append(inverse)
    inverse = jnp.concatenate(inverses, axis=0)
    side_ref[...] = jnp.where(iota(side_ref.shape, 1) == 0, inverse, home)
    row_ref[...] = jnp.broadcast_to(inverse, (rows, rows)).T[: row_ref.shape[0]]


def stack_kernel(*refs):
    out_ref = refs[-1]
    rows = refs[0].shape[0]
    for i, ref in enumerate(refs[:-1]):
        out_ref[i * rows : (i + 1) * rows, :] = ref[...]


def stack(*parts):
    rows, cols = parts[0].shape
    return run(stack_kernel, (shape_of((len(parts) * rows, cols), parts[0].dtype),), parts, 1)[0]


def join_kernel(first_ref, second_ref, out_ref):
    rows = first_ref.shape[0]
    out_ref[:rows, :] = first_ref[...]
    out_ref[rows:, :] = second_ref[...]


def place_paired(own_ref, near_ref, far_ref, weights_ref):
    rank, part = own_ref.shape[0] // 2, own_ref.shape[1]
    me = lax.axis_index("fsdp")
    core = lax.axis_index("dp") % 2

    def columns(k):
        return pl.ds(pl.multiple_of((me ^ k) * part, part), part)

    def place(even_ref, odd_ref):
        weights_ref[:, columns(1)] = even_ref[: 2 * rank, :]
        weights_ref[:, columns(2)] = odd_ref[: 2 * rank, :]
        weights_ref[:rank, columns(3)] = even_ref[2 * rank :, :]
        weights_ref[rank:, columns(3)] = odd_ref[2 * rank :, :]

    weights_ref[:, columns(0)] = own_ref[...]
    pl.when(core == 0)(functools.partial(place, near_ref, far_ref))
    pl.when(core == 1)(functools.partial(place, far_ref, near_ref))


def place_blocks(*refs):
    part = refs[0].shape[1]
    me = lax.axis_index("fsdp")
    for k, ref in enumerate(refs[:-1]):
        refs[-1][:, pl.ds(pl.multiple_of((me ^ k) * part, part), part)] = ref[...]


def rank_kernel(shards, *refs):
    blocks = refs[:-12]
    query_ref, query_in_ref, passage_in_ref, embed_ref, row_ref = refs[-12:-7]
    onehot_ref, head_ref = refs[-7:-5]
    weights_ref, passage_low_ref, message_ref, own_ref, base_ref = refs[-5:]
    slots = onehot_ref.shape[0]
    rank = blocks[0].shape[0] // 2
    q_dev, width = query_ref.shape
    queries = own_ref.shape[1]
    place = place_paired if shards == 4 else place_blocks
    place(*blocks, weights_ref)
    down, up = weights_ref[:rank, :], weights_ref[rank:, :]
    start = lax.axis_index("dp") * q_dev
    place = iota((q_dev, queries), 1) == iota((q_dev, queries), 0) + start
    inverse = inverse_length(query_ref, width)
    own = jnp.sum(jnp.where(place, inverse, 0.0), axis=0, keepdims=True)
    own_ref[...] = jnp.broadcast_to(own, own_ref.shape)
    same = iota((q_dev, q_dev), 0) == iota((q_dev, q_dev), 1)
    inverse_row = jnp.sum(jnp.where(same, inverse, 0.0), axis=0, keepdims=True)
    query_low = dot_nt(down, query_in_ref[...]).astype(BF16)
    message_ref[HEAD_ROWS:, slots : slots + q_dev] = query_low.astype(F32) * inverse_row
    passage_low = dot_nt(down, passage_in_ref[...]).astype(BF16)
    passage_low_ref[...] = passage_low.astype(F32) * row_ref[0:1, :]
    base = dot_nt(up, embed_ref[...])
    base_ref[...] = base
    message_ref[:HEAD_ROWS, :] = head_ref[...]
    message_ref[HEAD_ROWS:, :slots] = dot_pieces(dot_nt, base, onehot_ref[...])
    unused = jnp.zeros((rank, queries - slots - q_dev), F32)
    message_ref[HEAD_ROWS:, slots + q_dev :] = unused


def near_norm_kernel(width, *refs):
    out_ref = refs[-1]
    rows = refs[0].shape[0]
    chunk = min(width, 1024)
    for i, ref in enumerate(refs[:-1]):
        here = slice(i * rows, (i + 1) * rows)
        inverse = inverse_length(ref, width)
        for at in range(0, width, chunk):
            part = ref[:, at : at + chunk].astype(F32)
            out_ref[here, at : at + chunk] = (part * inverse).astype(BF16)
        out_ref[here, width:] = ref[:, width:]


def score_kernel(group, *refs):
    near_ref, *blocks = refs[: group // 2 + 1]
    embed_ref, side_ref, positive_ref = refs[-9:-6]
    query_ref, weight_ref, dots_ref, onehot_ref, head_ref, coded_ref = refs[-6:]
    rows, width = embed_ref.shape
    queries = query_ref.shape[0]
    q_dev = queries // group
    negatives = (near_ref.shape[1] - width) // 2
    slots = group * CAP
    me = lax.axis_index("dp")
    chunk = min(width, 1024)
    for k in range(group):
        start = pl.multiple_of((me ^ k) * q_dev, q_dev)
        block = blocks[k // 2]
        coded_ref[pl.ds(start, q_dev), :] = (
            near_ref[k // 2 * q_dev : (k // 2 + 1) * q_dev, width:] if k % 2 == 0
            else block[:, width:]
        ).astype(F32)
        if k % 2 == 0:
            near = near_ref[k // 2 * q_dev : (k // 2 + 1) * q_dev, :width]
            query_ref[pl.ds(start, q_dev), :] = near
            continue
        inverse = inverse_length(block, width)
        for at in range(0, width, chunk):
            part = block[:, at : at + chunk].astype(F32)
            query_ref[pl.ds(start, q_dev), at : at + chunk] = (part * inverse).astype(BF16)
    dots = dot_nt(embed_ref[...], query_ref[...])
    dots_ref[...] = dots
    scores = dots / SOFTMAX_HEAT

    coded = coded_ref[...].T
    ids = coded[:negatives] * float(ID_BASE) + coded[negatives:]
    home = jnp.broadcast_to(side_ref[:, 1:2], (rows, queries))
    count = jnp.zeros((rows, queries), F32)
    for j in range(negatives):
        count = count + jnp.where(ids[j : j + 1, :] == home, 1.0, 0.0)
    members = iota((slots, queries), 0) // CAP == iota((slots, queries), 1) // q_dev
    marked = dot_nt(members.astype(BF16), count.astype(BF16)) > 0.0
    before = (iota((rows, rows), 0) <= iota((rows, rows), 1)).astype(BF16)
    rank_in = dot_nn(marked.astype(F32).astype(BF16), before)
    wanted = (iota((slots, rows), 0) % CAP + 1).astype(F32)
    onehot = jnp.where(marked & (rank_in == wanted), 1.0, 0.0)
    onehot_ref[...] = onehot

    own = iota((rows, queries), 1) // q_dev == me
    count = count + jnp.where(own & (positive_ref[...] == iota((rows, queries), 0)), 1.0, 0.0)
    named = count > 0.0
    top = jnp.max(jnp.where(named, scores, LOWEST), axis=0, keepdims=True)
    weight = count * jnp.exp(jnp.where(named, scores - top, LOWEST))
    weight_ref[...] = weight
    total = jnp.sum(weight, axis=0, keepdims=True)
    dot_total = jnp.sum(weight * dots, axis=0, keepdims=True)
    slot_weight = dot_pieces(dot_nn, onehot, weight)
    tail_row = iota((HEAD_ROWS - CAP, queries), 0)
    tail = jnp.where(tail_row == 0, top, jnp.where(tail_row == 1, total, dot_total))
    lane_group = iota((CAP, queries), 1) // q_dev
    compact = jnp.zeros((CAP, queries), F32)
    for peer in range(group):
        part = slot_weight[peer * CAP : (peer + 1) * CAP]
        compact = jnp.where(lane_group == peer, part, compact)
    head_ref[:CAP, :] = compact
    head_ref[CAP:, :] = tail


def request_kernel(group, *refs):
    (
        embed_ref,
        onehot_ref,
        query_ref,
        weights_ref,
        low_ref,
        base_ref,
        weight_ref,
        positive_ref,
        back_ref,
        local_ref,
        target_ref,
    ) = refs[:11]
    blocks = refs[11:]
    width = embed_ref.shape[1]
    rows, queries = weight_ref.shape
    me = lax.axis_index("dp")
    onehot = [
        onehot_ref[pl.ds(pl.multiple_of((me ^ k) * CAP, CAP), CAP), :] for k in range(group)
    ]
    onehot = jnp.concatenate(onehot, axis=0).astype(BF16)
    chunk = min(width, 1024)
    for at in range(0, width, chunk):
        part = dot_nn(onehot, embed_ref[:, at : at + chunk]).astype(BF16)
        for i, block in enumerate(blocks):
            block[:, at : at + chunk] = part[2 * i * CAP : 2 * (i + 1) * CAP]
    back_ref[...] = dot_nt(weights_ref[weights_ref.shape[0] // 2 :, :], query_ref[...])
    both = jnp.concatenate([low_ref[...], base_ref[...]], axis=0)
    local_ref[...] = dot_pieces(dot_nn, both, weight_ref[...])
    target = own_target(positive_ref, rows, queries, queries // group, me)
    target_ref[...] = dot_pieces(dot_nn, both, target)


def forward_kernel(*refs):
    halves = [ref[...].astype(F32)[CAP:] for ref in refs[:-1]]
    refs[-1][...] = jnp.concatenate(halves, axis=0).astype(BF16)


def message_parts(near_ref, far_ref, group):
    rows = near_ref.shape[0] // (group // 2)
    return [((near_ref, far_ref)[k % 2], k // 2 * rows) for k in range(group)]


def combine(parts):
    tops = [ref[at + TOP_ROW : at + TOP_ROW + 1, :] for ref, at in parts]
    sums = [ref[at + SUM_ROW : at + SUM_ROW + 1, :] for ref, at in parts]
    top = functools.reduce(jnp.maximum, tops)
    scales = [jnp.exp(t - top) for t in tops]
    inverse_total = 1.0 / sum(t * s for t, s in zip(scales, sums))
    return [scale * inverse_total for scale in scales]


def own_target(positive_ref, rows, queries, q_dev, me):
    own = iota((rows, queries), 1) // q_dev == me
    return jnp.where(own & (positive_ref[...] == iota((rows, queries), 0)), 1.0, 0.0)


def terms_kernel(group, shards, near_ref, far_ref, *refs):
    parts = message_parts(near_ref, far_ref, group)
    (
        weight_ref,
        dots_ref,
        positive_ref,
        query_ref,
        embed_ref,
        back_query_ref,
        back_passage_ref,
        passage_low_ref,
        row_ref,
        own_ref,
        passage_in_ref,
        query_in_ref,
        local_ref,
        target_ref,
    ) = refs[:14]
    final_ref = refs[14]
    blocks = refs[15 : 15 + shards]
    (sum_ref,) = refs[15 + shards :]
    rows, queries = weight_ref.shape
    q_dev = queries // group
    rank = passage_low_ref.shape[0]
    width = query_ref.shape[1]
    me = lax.axis_index("dp")

    scales = combine(parts)
    target = own_target(positive_ref, rows, queries, q_dev, me)
    weight = (weight_ref[...] * scales[0] - target) / SOFTMAX_HEAT
    final_ref[...] = weight
    dots = dots_ref[...]
    ones = jnp.ones((16, queries), F32)
    inner = dot_pieces(dot_nt, ones, weight * dots)[0:1, :]

    inner_query = -jnp.sum(target * dots, axis=0, keepdims=True)
    own_dots = near_ref[DOT_ROW : DOT_ROW + 1, :]
    share = (scales[0] * own_dots + inner_query) / SOFTMAX_HEAT
    slots = group * CAP
    bases, query_low = [], []
    for (ref, at), scale in zip(parts, scales):
        inner_query = inner_query + scale * ref[at + DOT_ROW : at + DOT_ROW + 1, :]
        bases.append(ref[at + HEAD_ROWS : at + HEAD_ROWS + rank, :])
        query_low.append(ref[at + HEAD_ROWS : at + HEAD_ROWS + rank, :])
    low_total = jnp.zeros((rank, queries), F32)
    lane_group = iota((rank, queries), 1) // q_dev
    for k, rows_at in enumerate(query_low):
        shift = lax.rem((me ^ k) * q_dev + queries - slots, queries)
        rolled = pltpu.roll(rows_at, shift, 1)
        low_total = low_total + jnp.where(lane_group == (me ^ k), rolled, 0.0)
    query_low = low_total
    shift = lax.rem(queries - me * CAP, queries)
    bases = pltpu.roll(jnp.concatenate(bases[1:], axis=0), shift, 1)[:, :CAP]
    far_base = [bases[k * rank : (k + 1) * rank] for k in range(group - 1)]
    far_weight = [
        ref[at : at + CAP, :] * (scale / SOFTMAX_HEAT)
        for (ref, at), scale in zip(parts[1:], scales[1:])
    ]
    inner_query = inner_query / SOFTMAX_HEAT

    passage_low = passage_low_ref[...]
    local = (local_ref[...] * scales[0] - target_ref[...]) / SOFTMAX_HEAT
    from_query = local[:rank] - query_low * share
    from_passage = dot_pieces(dot_nt, query_low, weight) - passage_low * inner
    query_parts = jnp.concatenate(split_two(from_query), axis=0)
    passage_parts = jnp.concatenate(split_two(from_passage), axis=0)

    back_passage = dot_pieces(dot_nt, back_query_ref[...], weight)
    back_passage = (back_passage - back_passage_ref[...] * inner) * row_ref[0:1, :]
    back_passage = back_passage.astype(BF16)
    back_query = local[rank:] + dot_pieces(
        dot_nn, jnp.concatenate(far_base, axis=1), jnp.concatenate(far_weight, axis=0)
    )
    back_query = (back_query - back_query_ref[...] * inner_query) * own_ref[0:1, :]
    pick = (iota((q_dev, queries), 1) == iota((q_dev, queries), 0) + me * q_dev).astype(BF16)
    back_query = dot_nt(back_query.astype(BF16), pick).astype(BF16)

    chunk = min(width, 512)
    for at in range(0, width, chunk):
        cols = slice(at, at + chunk)
        both = dot_nn(query_parts, query_ref[:, cols]) + dot_nn(passage_parts, embed_ref[:, cols])
        sum_ref[rank:, cols] = ADAPTER_SCALE * (both[:rank] + both[rank:])
        sum_ref[:rank, cols] = ADAPTER_SCALE * (
            dot_nn(back_passage, passage_in_ref[:, cols])
            + dot_nn(back_query, query_in_ref[:, cols])
        )
    part = width // shards
    home = lax.axis_index("fsdp")
    for k in range(shards):
        start = pl.multiple_of((home ^ k) * part, part)
        blocks[k][...] = sum_ref[:, pl.ds(start, part)].astype(blocks[k].dtype)


def backward(upstream_of, raw_ref, inverse, grad_ref, up_ref):
    rows, width = raw_ref.shape
    chunk = min(width, 512)
    inner = jnp.zeros((rows, 1), F32)
    for at in range(0, width, chunk):
        upstream = upstream_of(at, chunk)
        up_ref[:, at : at + chunk] = upstream
        unit = raw_ref[:, at : at + chunk].astype(F32) * inverse
        inner = inner + jnp.sum(unit * upstream, axis=-1, keepdims=True)
    for at in range(0, width, chunk):
        unit = raw_ref[:, at : at + chunk].astype(F32) * inverse
        grad = (up_ref[:, at : at + chunk] - unit * inner) * inverse
        grad_ref[:, at : at + chunk] = grad.astype(BF16)


def passage_kernel(final_ref, query_ref, raw_ref, side_ref, grad_ref, up_ref):
    high, low = split_two(final_ref[...])

    def upstream_of(at, chunk):
        embed = query_ref[:, at : at + chunk]
        return dot_nn(high, embed) + dot_nn(low, embed)

    backward(upstream_of, raw_ref, side_ref[:, 0:1], grad_ref, up_ref)


def query_kernel(group, near_ref, far_ref, *refs):
    parts = message_parts(near_ref, far_ref, group)
    near = refs[: group // 2 - 1]
    forwarded_ref, final_ref, embed_ref, raw_ref, grad_ref, up_ref = refs[group // 2 - 1 :]
    q_dev, width = raw_ref.shape
    queries = final_ref.shape[1]
    me = lax.axis_index("dp")
    scales = combine(parts)
    pick = (iota((q_dev, queries), 1) == iota((q_dev, queries), 0) + me * q_dev).astype(F32)
    far = [
        ref[at : at + CAP, :] * (scale / SOFTMAX_HEAT) for (ref, at), scale in zip(parts, scales)
    ]
    far = far[2::2] + far[1::2] + [jnp.zeros((CAP, queries), F32)]
    own_parts = split_two(dot_pieces(dot_nt, pick, final_ref[...]))
    far_parts = split_two(dot_pieces(dot_nt, pick, jnp.concatenate(far, axis=0)))
    own_parts = jnp.concatenate(own_parts, axis=0)
    far_parts = jnp.concatenate(far_parts, axis=0)

    def upstream_of(at, chunk):
        rows = [ref[:, at : at + chunk].astype(F32)[:CAP] for ref in near]
        rows.append(forwarded_ref[:, at : at + chunk].astype(F32))
        rows.append(jnp.zeros((CAP, chunk), F32))
        both = dot_nn(own_parts, embed_ref[:, at : at + chunk])
        both = both + dot_nn(far_parts, jnp.concatenate(rows, axis=0).astype(BF16))
        return both[:q_dev] + both[q_dev:]

    backward(upstream_of, raw_ref, inverse_length(raw_ref, width), grad_ref, up_ref)


def sum_kernel(*refs):
    total = refs[0][...].astype(F32)
    for ref in refs[1:-1]:
        total = total + ref[...].astype(F32)
    refs[-1][...] = total


def sum_two_kernel(left_ref, right_ref, sent_ref):
    sent_ref[...] = (left_ref[...] + right_ref[...]).astype(BF16)


def sum_split_kernel(*refs):
    terms = [ref[...].astype(F32) for ref in refs[:-2]]
    while len(terms) > 1:
        terms = [a + b for a, b in zip(terms[::2], terms[1::2])]
    rank = refs[-1].shape[0]
    refs[-2][...] = terms[0][:rank]
    refs[-1][...] = terms[0][rank:]


def exchange(values, axis, k):
    size = lax.axis_size(axis)
    return lax.ppermute(values, axis, [(i, i ^ k) for i in range(size)])


def core_step(values, even_step, odd_step):
    outer, inner = lax.axis_size("dp"), lax.axis_size("fsdp")
    pairs = []
    for d in range(outer):
        step = odd_step if d % 2 else even_step
        pairs += [(d * inner + f, d * inner + (f ^ step)) for f in range(inner)]
    return lax.ppermute(values, ("dp", "fsdp"), pairs)


def per_device(
    query_pooled_states,
    passage_pooled_states,
    query_attention_output,
    passage_attention_output,
    positive_passage_row,
    hard_negative_ids,
    passage_home_row,
    adapter_down_weight,
    adapter_up_weight,
):
    group = lax.axis_size("dp")
    shards = lax.axis_size("fsdp")
    query_raw = query_pooled_states[0]
    passage_raw = passage_pooled_states[0]
    query_in = query_attention_output[0]
    passage_in = passage_attention_output[0]
    ids = hard_negative_ids[0]
    q_dev, width = query_raw.shape
    p_dev = passage_raw.shape[0]
    rank, part = adapter_down_weight.shape
    queries = group * q_dev
    slots = group * CAP
    work = 2 * p_dev * width

    packed, adapter, half, positive_row = run(
        front_kernel,
        (
            shape_of((q_dev, width + 2 * ids.shape[1]), BF16),
            shape_of((2 * rank, part), BF16),
            shape_of((rank, part), BF16),
            shape_of((1, queries), jnp.int32),
        ),
        (query_raw, ids, adapter_down_weight, adapter_up_weight, positive_passage_row),
        1,
        [
            pltpu.VMEM(ids.shape, jnp.int32),
            pltpu.VMEM(positive_passage_row.shape, jnp.int32),
            pltpu.SemaphoreType.DMA((5,)),
        ],
        in_hbm=True,
    )
    embed, side, side_row = run(
        passage_norm_kernel,
        (
            shape_of((p_dev, width), BF16),
            shape_of((p_dev, 128), F32),
            shape_of((8, p_dev), F32),
        ),
        (passage_raw, passage_home_row),
        work,
        [
            pltpu.VMEM(passage_raw.shape, BF16),
            pltpu.VMEM(passage_home_row.shape, jnp.int32),
            pltpu.SemaphoreType.DMA((1 + PASSAGE_CHUNKS,)),
        ],
        in_hbm=True,
    )
    blocks = {0: packed}
    for k in range(2, group, 2):
        blocks[k] = exchange(packed, "dp", k)
    blocks[1] = exchange(packed, "dp", 1)
    for k in range(2, group, 2):
        blocks[k], embed = lax.optimization_barrier((blocks[k], embed))
        blocks[k ^ 1] = exchange(blocks[k], "dp", 1)
    near_queries = run(
        functools.partial(near_norm_kernel, width),
        (shape_of((group // 2 * q_dev, packed.shape[1]), BF16),),
        tuple(blocks[k] for k in range(0, group, 2)),
        queries * width,
    )[0]
    if shards == 4:
        half_block = exchange(half, "fsdp", 3)
        whole_block = core_step(adapter, 1, 2)
        half_block, near_queries = lax.optimization_barrier((half_block, near_queries))
        adapter_near = run(
            join_kernel,
            (shape_of((3 * rank, part), BF16),),
            (whole_block, half_block),
            1,
        )[0]
        adapter_blocks = [adapter, adapter_near, exchange(adapter_near, "dp", 1)]
    else:
        adapter_blocks = [adapter] + [exchange(adapter, "fsdp", k) for k in range(1, shards)]
    query_embed, weight, dots, onehot, head = run(
        functools.partial(score_kernel, group),
        (
            shape_of((queries, width), BF16),
            shape_of((p_dev, queries), F32),
            shape_of((p_dev, queries), F32),
            shape_of((slots, p_dev), F32),
            shape_of((HEAD_ROWS, queries), F32),
        ),
        (
            near_queries,
            *[blocks[k] for k in range(1, group, 2)],
            embed,
            side,
            positive_row,
        ),
        work * queries,
        [pltpu.VMEM((queries, 2 * ids.shape[1]), F32)],
    )
    adapter_full, passage_low, message, own_side, slot_base = run(
        functools.partial(rank_kernel, shards),
        (
            shape_of((2 * rank, width), BF16),
            shape_of((rank, p_dev), F32),
            shape_of((HEAD_ROWS + rank, queries), F32),
            shape_of((8, queries), F32),
            shape_of((rank, p_dev), F32),
        ),
        (
            *adapter_blocks,
            query_raw,
            query_in,
            passage_in,
            embed,
            side_row,
            onehot,
            head,
        ),
        work * rank,
    )
    stats = [message] + [exchange(message, "dp", k) for k in range(2, group, 2)]
    chips = group // 2
    back_query, local, targets, *row_blocks = run(
        functools.partial(request_kernel, group),
        (
            shape_of((rank, queries), F32),
            shape_of((2 * rank, queries), F32),
            shape_of((2 * rank, queries), F32),
            *[shape_of((2 * CAP, width), BF16)] * chips,
        ),
        (
            embed,
            onehot,
            query_embed,
            adapter_full,
            passage_low,
            slot_base,
            weight,
            positive_row,
        ),
        work * slots,
    )
    stats, row_blocks = lax.optimization_barrier((stats, row_blocks))
    near = [exchange(row_blocks[i], "dp", 2 * i) for i in range(1, chips)]
    near_stats = stack(*stats)
    far_stats = exchange(near_stats, "dp", 1)
    final, *terms = run(
        functools.partial(terms_kernel, group, shards),
        (
            shape_of((p_dev, queries), F32),
            shape_of((2 * rank, part), F32),
            *[shape_of((2 * rank, part), BF16)] * (shards - 1),
        ),
        (
            near_stats,
            far_stats,
            weight,
            dots,
            positive_row,
            query_embed,
            embed,
            back_query,
            slot_base,
            passage_low,
            side_row,
            own_side,
            passage_in,
            query_in,
            local,
            targets,
        ),
        work * rank * 4,
        [pltpu.VMEM((2 * rank, width), F32)],
    )
    arrived = [exchange(terms[k], "fsdp", k) for k in range(1, shards)]
    final, near[0] = lax.optimization_barrier((final, near[0]))
    grad_passage = run(
        passage_kernel,
        (shape_of((p_dev, width), BF16),),
        (final, query_embed, passage_raw, side),
        2 * work * queries,
        [pltpu.VMEM((p_dev, width), F32)],
    )[0]
    terms[0], grad_passage = lax.optimization_barrier((terms[0], grad_passage))
    total = run(sum_kernel, (shape_of((2 * rank, part), F32),), (terms[0], *arrived), 1)[0]
    total, near = lax.optimization_barrier((total, near))
    to_sibling = run(
        forward_kernel,
        (shape_of((group // 2 * CAP, width), BF16),),
        (row_blocks[0], *near),
        1,
    )[0]
    forwarded = exchange(to_sibling, "dp", 1)
    sent = run(
        sum_two_kernel,
        (shape_of((2 * rank, part), BF16),),
        (total, exchange(total, "dp", 1)),
        1,
    )[0]
    arrived = [exchange(sent, "dp", k) for k in range(2, group, 2)]
    grad_query = run(
        functools.partial(query_kernel, group),
        (shape_of((q_dev, width), BF16),),
        (near_stats, far_stats, *near, forwarded, final, embed, query_raw),
        4 * q_dev * width * (p_dev + slots),
        [pltpu.VMEM((q_dev, width), F32)],
    )[0]
    sent, grad_query = lax.optimization_barrier((sent, grad_query))
    down_total, up_total = run(
        sum_split_kernel, (shape_of((rank, part), F32),) * 2, (sent, *arrived), 1
    )
    return (grad_query[None], grad_passage[None], down_total, up_total)


def solution(mesh):
    in_specs = (
        P("fsdp", "dp", None),
        P("fsdp", "dp", None),
        P("fsdp", "dp", None),
        P("fsdp", "dp", None),
        P("fsdp", "dp"),
        P("fsdp", "dp", None),
        P("fsdp", None),
        P(None, "fsdp"),
        P(None, "fsdp"),
    )
    out_specs = (P("fsdp", "dp", None), P("fsdp", "dp", None), P(None, "fsdp"), P(None, "fsdp"))
    return jax.shard_map(
        per_device, mesh=mesh, in_specs=in_specs, out_specs=out_specs, check_vma=False
    )
```

```python
import functools

import jax
import jax.numpy as jnp
from jax import lax
from jax.experimental import pallas as pl
from jax.experimental.pallas import tpu as pltpu
from jax.sharding import PartitionSpec as P

CAP = 8
SOFTMAX_HEAT = 0.01
ADAPTER_SCALE = 2.0
EPSILON = 1e-06
LOWEST = -1e30
ID_BASE = 256
TOP_ROW, SUM_ROW, DOT_ROW, HEAD_ROWS = 8, 9, 10, 16
VMEM_BYTES = 16 * 1024 * 1024
PASSAGE_CHUNKS = 4
F32 = jnp.float32
BF16 = jnp.bfloat16


def dot_nn(a, b, precision=None):
    return lax.dot_general(
        a, b, (((1,), (0,)), ((), ())), precision=precision, preferred_element_type=F32
    )


def dot_nt(a, b, precision=None):
    return lax.dot_general(
        a, b, (((1,), (1,)), ((), ())), precision=precision, preferred_element_type=F32
    )


def split_two(values):
    high = values.astype(BF16)
    low = (values - high.astype(F32)).astype(BF16)
    return high, low


def dot_pieces(dot, a, b):
    rows = a.shape[0]
    a_high, a_low = split_two(a)
    b_high, b_low = split_two(b)
    both = dot(jnp.concatenate([a_high, a_low], axis=0), b_high)
    return both[:rows] + both[rows:] + dot(a_high, b_low)


def iota(shape, dim):
    return lax.broadcasted_iota(jnp.int32, shape, dim)


def shape_of(dims, kind):
    return jax.ShapeDtypeStruct(dims, kind)


def run(body, out_shape, args, flops, scratch=(), in_hbm=False):
    grant = VMEM_BYTES * max(1, size_ratio(args))
    if in_hbm:
        args = [pltpu.with_memory_space_constraint(a, pltpu.HBM) for a in args]
    vmem = pl.BlockSpec(memory_space=pltpu.VMEM)
    hbm = pl.BlockSpec(memory_space=pltpu.HBM)
    moved = sum(a.size * a.dtype.itemsize for a in (*args, *out_shape))
    return pl.pallas_call(
        body,
        out_shape=out_shape,
        in_specs=[hbm if in_hbm else vmem] * len(args),
        out_specs=tuple(vmem for _ in out_shape),
        scratch_shapes=list(scratch),
        compiler_params=pltpu.CompilerParams(vmem_limit_bytes=grant),
        cost_estimate=pl.CostEstimate(flops=flops, bytes_accessed=moved, transcendentals=0),
    )(*args)


def size_ratio(args):
    moved = sum(a.size * a.dtype.itemsize for a in args)
    return -(-moved * 3 // VMEM_BYTES)


def inverse_length(raw_ref, width):
    chunk = min(width, 512)
    total = jnp.zeros((raw_ref.shape[0], 1), F32)
    for at in range(0, width, chunk):
        part = raw_ref[:, at : at + chunk].astype(F32)
        total = total + jnp.sum(part * part, axis=-1, keepdims=True)
    return 1.0 / jnp.sqrt(total + EPSILON)


def front_kernel(
    query_ref,
    ids_ref,
    down_ref,
    up_ref,
    positive_ref,
    out_ref,
    adapter_ref,
    half_ref,
    tiled_ref,
    ids_here,
    positive_here,
    sems,
):
    width = query_ref.shape[1]
    rank = down_ref.shape[0]
    me = lax.axis_index("dp")
    pairs = (
        (ids_ref, ids_here),
        (query_ref, out_ref.at[:, pl.ds(0, width)]),
        (positive_ref, positive_here),
        (down_ref, adapter_ref.at[pl.ds(0, rank), :]),
        (up_ref, adapter_ref.at[pl.ds(rank, rank), :]),
    )
    copies = [pltpu.make_async_copy(a, b, sems.at[i]) for i, (a, b) in enumerate(pairs)]
    for copy in copies:
        copy.start()
    copies[0].wait()
    ids = ids_here[...]
    coded = jnp.concatenate([ids // ID_BASE, ids % ID_BASE], axis=1)
    out_ref[:, width:] = coded.astype(F32).astype(BF16)
    copies[2].wait()
    q_dev = positive_here.shape[1]
    for at in range(0, tiled_ref.shape[1], q_dev):
        tiled_ref[:, at : at + q_dev] = positive_here[...]
    copies[3].wait()
    copies[4].wait()

    @pl.when(me % 2 == 0)
    def _():
        half_ref[...] = adapter_ref[:rank, :]

    @pl.when(me % 2 == 1)
    def _():
        half_ref[...] = adapter_ref[rank:, :]

    copies[1].wait()


def passage_norm_kernel(
    passage_ref, home_ref, embed_ref, side_ref, row_ref, passage_here, home_here, sems
):
    rows, width = passage_ref.shape
    total = home_ref.shape[1]
    me = lax.axis_index("dp")
    part = rows // PASSAGE_CHUNKS
    home_copy = pltpu.make_async_copy(home_ref, home_here, sems.at[0])
    home_copy.start()
    passage_copies = []
    for c in range(PASSAGE_CHUNKS):
        here = pl.ds(c * part, part)
        passage_copies.append(
            pltpu.make_async_copy(
                passage_ref.at[here, :], passage_here.at[here, :], sems.at[1 + c]
            )
        )
        passage_copies[c].start()

    home_copy.wait()
    row_id = iota((rows, total), 0) + me * rows
    number = iota((rows, total), 1)
    home = jnp.where(home_here[...] == row_id, number, 0).astype(F32)
    home = jnp.sum(home, axis=1, keepdims=True)

    chunk = min(width, 512)
    inverses = []
    for c in range(PASSAGE_CHUNKS):
        passage_copies[c].wait()
        here = slice(c * part, (c + 1) * part)
        inverse = inverse_length(passage_here.at[here, :], width)
        for at in range(0, width, chunk):
            values = passage_here[here, at : at + chunk].astype(F32)
            embed_ref[here, at : at + chunk] = (values * inverse).astype(BF16)
        inverses.append(inverse)
    inverse = jnp.concatenate(inverses, axis=0)
    side_ref[...] = jnp.where(iota(side_ref.shape, 1) == 0, inverse, home)
    row_ref[...] = jnp.broadcast_to(inverse, (rows, rows)).T[: row_ref.shape[0]]


def stack_kernel(*refs):
    out_ref = refs[-1]
    rows = refs[0].shape[0]
    for i, ref in enumerate(refs[:-1]):
        out_ref[i * rows : (i + 1) * rows, :] = ref[...]


def stack(*parts):
    rows, cols = parts[0].shape
    return run(stack_kernel, (shape_of((len(parts) * rows, cols), parts[0].dtype),), parts, 1)[0]


def join_kernel(first_ref, second_ref, out_ref):
    rows = first_ref.shape[0]
    out_ref[:rows, :] = first_ref[...]
    out_ref[rows:, :] = second_ref[...]


def place_paired(own_ref, near_ref, far_ref, weights_ref):
    rank, part = own_ref.shape[0] // 2, own_ref.shape[1]
    me = lax.axis_index("fsdp")
    core = lax.axis_index("dp") % 2

    def columns(k):
        return pl.ds(pl.multiple_of((me ^ k) * part, part), part)

    def place(even_ref, odd_ref):
        weights_ref[:, columns(1)] = even_ref[: 2 * rank, :]
        weights_ref[:, columns(2)] = odd_ref[: 2 * rank, :]
        weights_ref[:rank, columns(3)] = even_ref[2 * rank :, :]
        weights_ref[rank:, columns(3)] = odd_ref[2 * rank :, :]

    weights_ref[:, columns(0)] = own_ref[...]
    pl.when(core == 0)(functools.partial(place, near_ref, far_ref))
    pl.when(core == 1)(functools.partial(place, far_ref, near_ref))


def place_blocks(*refs):
    part = refs[0].shape[1]
    me = lax.axis_index("fsdp")
    for k, ref in enumerate(refs[:-1]):
        refs[-1][:, pl.ds(pl.multiple_of((me ^ k) * part, part), part)] = ref[...]


def rank_kernel(shards, *refs):
    blocks = refs[:-12]
    query_ref, query_in_ref, passage_in_ref, embed_ref, row_ref = refs[-12:-7]
    onehot_ref, head_ref = refs[-7:-5]
    weights_ref, passage_low_ref, message_ref, own_ref, base_ref = refs[-5:]
    slots = onehot_ref.shape[0]
    rank = blocks[0].shape[0] // 2
    q_dev, width = query_ref.shape
    queries = own_ref.shape[1]
    place = place_paired if shards == 4 else place_blocks
    place(*blocks, weights_ref)
    down, up = weights_ref[:rank, :], weights_ref[rank:, :]
    start = lax.axis_index("dp") * q_dev
    place = iota((q_dev, queries), 1) == iota((q_dev, queries), 0) + start
    inverse = inverse_length(query_ref, width)
    own = jnp.sum(jnp.where(place, inverse, 0.0), axis=0, keepdims=True)
    own_ref[...] = jnp.broadcast_to(own, own_ref.shape)
    same = iota((q_dev, q_dev), 0) == iota((q_dev, q_dev), 1)
    inverse_row = jnp.sum(jnp.where(same, inverse, 0.0), axis=0, keepdims=True)
    query_low = dot_nt(down, query_in_ref[...]).astype(BF16)
    message_ref[HEAD_ROWS:, slots : slots + q_dev] = query_low.astype(F32) * inverse_row
    passage_low = dot_nt(down, passage_in_ref[...]).astype(BF16)
    passage_low_ref[...] = passage_low.astype(F32) * row_ref[0:1, :]
    base = dot_nt(up, embed_ref[...])
    base_ref[...] = base
    message_ref[:HEAD_ROWS, :] = head_ref[...]
    message_ref[HEAD_ROWS:, :slots] = dot_pieces(dot_nt, base, onehot_ref[...])
    unused = jnp.zeros((rank, queries - slots - q_dev), F32)
    message_ref[HEAD_ROWS:, slots + q_dev :] = unused


def near_norm_kernel(width, *refs):
    out_ref = refs[-1]
    rows = refs[0].shape[0]
    chunk = min(width, 1024)
    for i, ref in enumerate(refs[:-1]):
        here = slice(i * rows, (i + 1) * rows)
        inverse = inverse_length(ref, width)
        for at in range(0, width, chunk):
            part = ref[:, at : at + chunk].astype(F32)
            out_ref[here, at : at + chunk] = (part * inverse).astype(BF16)
        out_ref[here, width:] = ref[:, width:]


def score_kernel(group, *refs):
    near_ref, *blocks = refs[: group // 2 + 1]
    embed_ref, side_ref, positive_ref = refs[-9:-6]
    query_ref, weight_ref, dots_ref, onehot_ref, head_ref, coded_ref = refs[-6:]
    rows, width = embed_ref.shape
    queries = query_ref.shape[0]
    q_dev = queries // group
    negatives = (near_ref.shape[1] - width) // 2
    slots = group * CAP
    me = lax.axis_index("dp")
    chunk = min(width, 1024)
    for k in range(group):
        start = pl.multiple_of((me ^ k) * q_dev, q_dev)
        block = blocks[k // 2]
        coded_ref[pl.ds(start, q_dev), :] = (
            near_ref[k // 2 * q_dev : (k // 2 + 1) * q_dev, width:] if k % 2 == 0
            else block[:, width:]
        ).astype(F32)
        if k % 2 == 0:
            near = near_ref[k // 2 * q_dev : (k // 2 + 1) * q_dev, :width]
            query_ref[pl.ds(start, q_dev), :] = near
            continue
        inverse = inverse_length(block, width)
        for at in range(0, width, chunk):
            part = block[:, at : at + chunk].astype(F32)
            query_ref[pl.ds(start, q_dev), at : at + chunk] = (part * inverse).astype(BF16)
    dots = dot_nt(embed_ref[...], query_ref[...])
    dots_ref[...] = dots
    scores = dots / SOFTMAX_HEAT

    coded = coded_ref[...].T
    ids = coded[:negatives] * float(ID_BASE) + coded[negatives:]
    home = jnp.broadcast_to(side_ref[:, 1:2], (rows, queries))
    count = jnp.zeros((rows, queries), F32)
    for j in range(negatives):
        count = count + jnp.where(ids[j : j + 1, :] == home, 1.0, 0.0)
    members = iota((slots, queries), 0) // CAP == iota((slots, queries), 1) // q_dev
    marked = dot_nt(members.astype(BF16), count.astype(BF16)) > 0.0
    before = (iota((rows, rows), 0) <= iota((rows, rows), 1)).astype(BF16)
    rank_in = dot_nn(marked.astype(F32).astype(BF16), before)
    wanted = (iota((slots, rows), 0) % CAP + 1).astype(F32)
    onehot = jnp.where(marked & (rank_in == wanted), 1.0, 0.0)
    onehot_ref[...] = onehot

    own = iota((rows, queries), 1) // q_dev == me
    count = count + jnp.where(own & (positive_ref[...] == iota((rows, queries), 0)), 1.0, 0.0)
    named = count > 0.0
    top = jnp.max(jnp.where(named, scores, LOWEST), axis=0, keepdims=True)
    weight = count * jnp.exp(jnp.where(named, scores - top, LOWEST))
    weight_ref[...] = weight
    total = jnp.sum(weight, axis=0, keepdims=True)
    dot_total = jnp.sum(weight * dots, axis=0, keepdims=True)
    slot_weight = dot_pieces(dot_nn, onehot, weight)
    tail_row = iota((HEAD_ROWS - CAP, queries), 0)
    tail = jnp.where(tail_row == 0, top, jnp.where(tail_row == 1, total, dot_total))
    lane_group = iota((CAP, queries), 1) // q_dev
    compact = jnp.zeros((CAP, queries), F32)
    for peer in range(group):
        part = slot_weight[peer * CAP : (peer + 1) * CAP]
        compact = jnp.where(lane_group == peer, part, compact)
    head_ref[:CAP, :] = compact
    head_ref[CAP:, :] = tail


def request_kernel(group, *refs):
    (
        embed_ref,
        onehot_ref,
        query_ref,
        weights_ref,
        low_ref,
        base_ref,
        weight_ref,
        positive_ref,
        back_ref,
        local_ref,
        target_ref,
    ) = refs[:11]
    blocks = refs[11:]
    width = embed_ref.shape[1]
    rows, queries = weight_ref.shape
    me = lax.axis_index("dp")
    onehot = [
        onehot_ref[pl.ds(pl.multiple_of((me ^ k) * CAP, CAP), CAP), :] for k in range(group)
    ]
    onehot = jnp.concatenate(onehot, axis=0).astype(BF16)
    chunk = min(width, 1024)
    for at in range(0, width, chunk):
        part = dot_nn(onehot, embed_ref[:, at : at + chunk]).astype(BF16)
        for i, block in enumerate(blocks):
            block[:, at : at + chunk] = part[2 * i * CAP : 2 * (i + 1) * CAP]
    back_ref[...] = dot_nt(weights_ref[weights_ref.shape[0] // 2 :, :], query_ref[...])
    both = jnp.concatenate([low_ref[...], base_ref[...]], axis=0)
    local_ref[...] = dot_pieces(dot_nn, both, weight_ref[...])
    target = own_target(positive_ref, rows, queries, queries // group, me)
    target_ref[...] = dot_pieces(dot_nn, both, target)


def forward_kernel(*refs):
    halves = [ref[...].astype(F32)[CAP:] for ref in refs[:-1]]
    refs[-1][...] = jnp.concatenate(halves, axis=0).astype(BF16)


def message_parts(near_ref, far_ref, group):
    rows = near_ref.shape[0] // (group // 2)
    return [((near_ref, far_ref)[k % 2], k // 2 * rows) for k in range(group)]


def combine(parts):
    tops = [ref[at + TOP_ROW : at + TOP_ROW + 1, :] for ref, at in parts]
    sums = [ref[at + SUM_ROW : at + SUM_ROW + 1, :] for ref, at in parts]
    top = functools.reduce(jnp.maximum, tops)
    scales = [jnp.exp(t - top) for t in tops]
    inverse_total = 1.0 / sum(t * s for t, s in zip(scales, sums))
    return [scale * inverse_total for scale in scales]


def own_target(positive_ref, rows, queries, q_dev, me):
    own = iota((rows, queries), 1) // q_dev == me
    return jnp.where(own & (positive_ref[...] == iota((rows, queries), 0)), 1.0, 0.0)


def terms_kernel(group, shards, near_ref, far_ref, *refs):
    parts = message_parts(near_ref, far_ref, group)
    (
        weight_ref,
        dots_ref,
        positive_ref,
        query_ref,
        embed_ref,
        back_query_ref,
        back_passage_ref,
        passage_low_ref,
        row_ref,
        own_ref,
        passage_in_ref,
        query_in_ref,
        local_ref,
        target_ref,
    ) = refs[:14]
    final_ref = refs[14]
    blocks = refs[15 : 15 + shards]
    (sum_ref,) = refs[15 + shards :]
    rows, queries = weight_ref.shape
    q_dev = queries // group
    rank = passage_low_ref.shape[0]
    width = query_ref.shape[1]
    me = lax.axis_index("dp")

    scales = combine(parts)
    target = own_target(positive_ref, rows, queries, q_dev, me)
    weight = (weight_ref[...] * scales[0] - target) / SOFTMAX_HEAT
    final_ref[...] = weight
    dots = dots_ref[...]
    ones = jnp.ones((16, queries), F32)
    inner = dot_pieces(dot_nt, ones, weight * dots)[0:1, :]

    inner_query = -jnp.sum(target * dots, axis=0, keepdims=True)
    own_dots = near_ref[DOT_ROW : DOT_ROW + 1, :]
    share = (scales[0] * own_dots + inner_query) / SOFTMAX_HEAT
    slots = group * CAP
    bases, query_low = [], []
    for (ref, at), scale in zip(parts, scales):
        inner_query = inner_query + scale * ref[at + DOT_ROW : at + DOT_ROW + 1, :]
        bases.append(ref[at + HEAD_ROWS : at + HEAD_ROWS + rank, :])
        query_low.append(ref[at + HEAD_ROWS : at + HEAD_ROWS + rank, :])
    low_total = jnp.zeros((rank, queries), F32)
    lane_group = iota((rank, queries), 1) // q_dev
    for k, rows_at in enumerate(query_low):
        shift = lax.rem((me ^ k) * q_dev + queries - slots, queries)
        rolled = pltpu.roll(rows_at, shift, 1)
        low_total = low_total + jnp.where(lane_group == (me ^ k), rolled, 0.0)
    query_low = low_total
    shift = lax.rem(queries - me * CAP, queries)
    bases = pltpu.roll(jnp.concatenate(bases[1:], axis=0), shift, 1)[:, :CAP]
    far_base = [bases[k * rank : (k + 1) * rank] for k in range(group - 1)]
    far_weight = [
        ref[at : at + CAP, :] * (scale / SOFTMAX_HEAT)
        for (ref, at), scale in zip(parts[1:], scales[1:])
    ]
    inner_query = inner_query / SOFTMAX_HEAT

    passage_low = passage_low_ref[...]
    local = (local_ref[...] * scales[0] - target_ref[...]) / SOFTMAX_HEAT
    from_query = local[:rank] - query_low * share
    from_passage = dot_pieces(dot_nt, query_low, weight) - passage_low * inner
    query_parts = jnp.concatenate(split_two(from_query), axis=0)
    passage_parts = jnp.concatenate(split_two(from_passage), axis=0)

    back_passage = dot_pieces(dot_nt, back_query_ref[...], weight)
    back_passage = (back_passage - back_passage_ref[...] * inner) * row_ref[0:1, :]
    back_passage = back_passage.astype(BF16)
    back_query = local[rank:] + dot_pieces(
        dot_nn, jnp.concatenate(far_base, axis=1), jnp.concatenate(far_weight, axis=0)
    )
    back_query = (back_query - back_query_ref[...] * inner_query) * own_ref[0:1, :]
    pick = (iota((q_dev, queries), 1) == iota((q_dev, queries), 0) + me * q_dev).astype(BF16)
    back_query = dot_nt(back_query.astype(BF16), pick).astype(BF16)

    chunk = min(width, 2048)
    for at in range(0, width, chunk):
        cols = slice(at, at + chunk)
        both = dot_nn(query_parts, query_ref[:, cols]) + dot_nn(passage_parts, embed_ref[:, cols])
        sum_ref[rank:, cols] = ADAPTER_SCALE * (both[:rank] + both[rank:])
        sum_ref[:rank, cols] = ADAPTER_SCALE * (
            dot_nn(back_passage, passage_in_ref[:, cols])
            + dot_nn(back_query, query_in_ref[:, cols])
        )
    part = width // shards
    home = lax.axis_index("fsdp")
    for k in range(shards):
        start = pl.multiple_of((home ^ k) * part, part)
        blocks[k][...] = sum_ref[:, pl.ds(start, part)].astype(blocks[k].dtype)


def backward(upstream_of, raw_ref, inverse, grad_ref, up_ref):
    rows, width = raw_ref.shape
    chunk = min(width, 512)
    inner = jnp.zeros((rows, 1), F32)
    for at in range(0, width, chunk):
        upstream = upstream_of(at, chunk)
        up_ref[:, at : at + chunk] = upstream
        unit = raw_ref[:, at : at + chunk].astype(F32) * inverse
        inner = inner + jnp.sum(unit * upstream, axis=-1, keepdims=True)
    for at in range(0, width, chunk):
        unit = raw_ref[:, at : at + chunk].astype(F32) * inverse
        grad = (up_ref[:, at : at + chunk] - unit * inner) * inverse
        grad_ref[:, at : at + chunk] = grad.astype(BF16)


def passage_kernel(final_ref, query_ref, raw_ref, side_ref, grad_ref, up_ref):
    high, low = split_two(final_ref[...])

    def upstream_of(at, chunk):
        embed = query_ref[:, at : at + chunk]
        return dot_nn(high, embed) + dot_nn(low, embed)

    backward(upstream_of, raw_ref, side_ref[:, 0:1], grad_ref, up_ref)


def query_kernel(group, near_ref, far_ref, *refs):
    parts = message_parts(near_ref, far_ref, group)
    near = refs[: group // 2 - 1]
    forwarded_ref, final_ref, embed_ref, raw_ref, grad_ref, up_ref = refs[group // 2 - 1 :]
    q_dev, width = raw_ref.shape
    queries = final_ref.shape[1]
    me = lax.axis_index("dp")
    scales = combine(parts)
    pick = (iota((q_dev, queries), 1) == iota((q_dev, queries), 0) + me * q_dev).astype(F32)
    far = [
        ref[at : at + CAP, :] * (scale / SOFTMAX_HEAT) for (ref, at), scale in zip(parts, scales)
    ]
    far = far[2::2] + far[1::2] + [jnp.zeros((CAP, queries), F32)]
    own_parts = split_two(dot_pieces(dot_nt, pick, final_ref[...]))
    far_parts = split_two(dot_pieces(dot_nt, pick, jnp.concatenate(far, axis=0)))
    own_parts = jnp.concatenate(own_parts, axis=0)
    far_parts = jnp.concatenate(far_parts, axis=0)

    def upstream_of(at, chunk):
        rows = [ref[:, at : at + chunk].astype(F32)[:CAP] for ref in near]
        rows.append(forwarded_ref[:, at : at + chunk].astype(F32))
        rows.append(jnp.zeros((CAP, chunk), F32))
        both = dot_nn(own_parts, embed_ref[:, at : at + chunk])
        both = both + dot_nn(far_parts, jnp.concatenate(rows, axis=0).astype(BF16))
        return both[:q_dev] + both[q_dev:]

    backward(upstream_of, raw_ref, inverse_length(raw_ref, width), grad_ref, up_ref)


def sum_kernel(*refs):
    total = refs[0][...].astype(F32)
    for ref in refs[1:-1]:
        total = total + ref[...].astype(F32)
    refs[-1][...] = total


def sum_two_kernel(left_ref, right_ref, sent_ref):
    sent_ref[...] = (left_ref[...] + right_ref[...]).astype(BF16)


def sum_split_kernel(*refs):
    terms = [ref[...].astype(F32) for ref in refs[:-2]]
    while len(terms) > 1:
        terms = [a + b for a, b in zip(terms[::2], terms[1::2])]
    rank = refs[-1].shape[0]
    refs[-2][...] = terms[0][:rank]
    refs[-1][...] = terms[0][rank:]


def exchange(values, axis, k):
    size = lax.axis_size(axis)
    return lax.ppermute(values, axis, [(i, i ^ k) for i in range(size)])


def core_step(values, even_step, odd_step):
    outer, inner = lax.axis_size("dp"), lax.axis_size("fsdp")
    pairs = []
    for d in range(outer):
        step = odd_step if d % 2 else even_step
        pairs += [(d * inner + f, d * inner + (f ^ step)) for f in range(inner)]
    return lax.ppermute(values, ("dp", "fsdp"), pairs)


def per_device(
    query_pooled_states,
    passage_pooled_states,
    query_attention_output,
    passage_attention_output,
    positive_passage_row,
    hard_negative_ids,
    passage_home_row,
    adapter_down_weight,
    adapter_up_weight,
):
    group = lax.axis_size("dp")
    shards = lax.axis_size("fsdp")
    query_raw = query_pooled_states[0]
    passage_raw = passage_pooled_states[0]
    query_in = query_attention_output[0]
    passage_in = passage_attention_output[0]
    ids = hard_negative_ids[0]
    q_dev, width = query_raw.shape
    p_dev = passage_raw.shape[0]
    rank, part = adapter_down_weight.shape
    queries = group * q_dev
    slots = group * CAP
    work = 2 * p_dev * width

    packed, adapter, half, positive_row = run(
        front_kernel,
        (
            shape_of((q_dev, width + 2 * ids.shape[1]), BF16),
            shape_of((2 * rank, part), BF16),
            shape_of((rank, part), BF16),
            shape_of((1, queries), jnp.int32),
        ),
        (query_raw, ids, adapter_down_weight, adapter_up_weight, positive_passage_row),
        1,
        [
            pltpu.VMEM(ids.shape, jnp.int32),
            pltpu.VMEM(positive_passage_row.shape, jnp.int32),
            pltpu.SemaphoreType.DMA((5,)),
        ],
        in_hbm=True,
    )
    embed, side, side_row = run(
        passage_norm_kernel,
        (
            shape_of((p_dev, width), BF16),
            shape_of((p_dev, 128), F32),
            shape_of((8, p_dev), F32),
        ),
        (passage_raw, passage_home_row),
        work,
        [
            pltpu.VMEM(passage_raw.shape, BF16),
            pltpu.VMEM(passage_home_row.shape, jnp.int32),
            pltpu.SemaphoreType.DMA((1 + PASSAGE_CHUNKS,)),
        ],
        in_hbm=True,
    )
    blocks = {0: packed}
    for k in range(2, group, 2):
        blocks[k] = exchange(packed, "dp", k)
    blocks[1] = exchange(packed, "dp", 1)
    for k in range(2, group, 2):
        blocks[k], embed = lax.optimization_barrier((blocks[k], embed))
        blocks[k ^ 1] = exchange(blocks[k], "dp", 1)
    near_queries = run(
        functools.partial(near_norm_kernel, width),
        (shape_of((group // 2 * q_dev, packed.shape[1]), BF16),),
        tuple(blocks[k] for k in range(0, group, 2)),
        queries * width,
    )[0]
    if shards == 4:
        half_block = exchange(half, "fsdp", 3)
        whole_block = core_step(adapter, 1, 2)
        half_block, near_queries = lax.optimization_barrier((half_block, near_queries))
        adapter_near = run(
            join_kernel,
            (shape_of((3 * rank, part), BF16),),
            (whole_block, half_block),
            1,
        )[0]
        adapter_blocks = [adapter, adapter_near, exchange(adapter_near, "dp", 1)]
    else:
        adapter_blocks = [adapter] + [exchange(adapter, "fsdp", k) for k in range(1, shards)]
    query_embed, weight, dots, onehot, head = run(
        functools.partial(score_kernel, group),
        (
            shape_of((queries, width), BF16),
            shape_of((p_dev, queries), F32),
            shape_of((p_dev, queries), F32),
            shape_of((slots, p_dev), F32),
            shape_of((HEAD_ROWS, queries), F32),
        ),
        (
            near_queries,
            *[blocks[k] for k in range(1, group, 2)],
            embed,
            side,
            positive_row,
        ),
        work * queries,
        [pltpu.VMEM((queries, 2 * ids.shape[1]), F32)],
    )
    adapter_full, passage_low, message, own_side, slot_base = run(
        functools.partial(rank_kernel, shards),
        (
            shape_of((2 * rank, width), BF16),
            shape_of((rank, p_dev), F32),
            shape_of((HEAD_ROWS + rank, queries), F32),
            shape_of((8, queries), F32),
            shape_of((rank, p_dev), F32),
        ),
        (
            *adapter_blocks,
            query_raw,
            query_in,
            passage_in,
            embed,
            side_row,
            onehot,
            head,
        ),
        work * rank,
    )
    stats = [message] + [exchange(message, "dp", k) for k in range(2, group, 2)]
    chips = group // 2
    back_query, local, targets, *row_blocks = run(
        functools.partial(request_kernel, group),
        (
            shape_of((rank, queries), F32),
            shape_of((2 * rank, queries), F32),
            shape_of((2 * rank, queries), F32),
            *[shape_of((2 * CAP, width), BF16)] * chips,
        ),
        (
            embed,
            onehot,
            query_embed,
            adapter_full,
            passage_low,
            slot_base,
            weight,
            positive_row,
        ),
        work * slots,
    )
    stats, row_blocks = lax.optimization_barrier((stats, row_blocks))
    near = [exchange(row_blocks[i], "dp", 2 * i) for i in range(1, chips)]
    near_stats = stack(*stats)
    far_stats = exchange(near_stats, "dp", 1)
    final, *terms = run(
        functools.partial(terms_kernel, group, shards),
        (
            shape_of((p_dev, queries), F32),
            shape_of((2 * rank, part), F32),
            *[shape_of((2 * rank, part), BF16)] * (shards - 1),
        ),
        (
            near_stats,
            far_stats,
            weight,
            dots,
            positive_row,
            query_embed,
            embed,
            back_query,
            slot_base,
            passage_low,
            side_row,
            own_side,
            passage_in,
            query_in,
            local,
            targets,
        ),
        work * rank * 4,
        [pltpu.VMEM((2 * rank, width), F32)],
    )
    arrived = [exchange(terms[k], "fsdp", k) for k in range(1, shards)]
    final, near[0] = lax.optimization_barrier((final, near[0]))
    grad_passage = run(
        passage_kernel,
        (shape_of((p_dev, width), BF16),),
        (final, query_embed, passage_raw, side),
        2 * work * queries,
        [pltpu.VMEM((p_dev, width), F32)],
    )[0]
    terms[0], grad_passage = lax.optimization_barrier((terms[0], grad_passage))
    total = run(sum_kernel, (shape_of((2 * rank, part), F32),), (terms[0], *arrived), 1)[0]
    total, near = lax.optimization_barrier((total, near))
    to_sibling = run(
        forward_kernel,
        (shape_of((group // 2 * CAP, width), BF16),),
        (row_blocks[0], *near),
        1,
    )[0]
    forwarded = exchange(to_sibling, "dp", 1)
    sent = run(
        sum_two_kernel,
        (shape_of((2 * rank, part), BF16),),
        (total, exchange(total, "dp", 1)),
        1,
    )[0]
    arrived = [exchange(sent, "dp", k) for k in range(2, group, 2)]
    grad_query = run(
        functools.partial(query_kernel, group),
        (shape_of((q_dev, width), BF16),),
        (near_stats, far_stats, *near, forwarded, final, embed, query_raw),
        4 * q_dev * width * (p_dev + slots),
        [pltpu.VMEM((q_dev, width), F32)],
    )[0]
    sent, grad_query = lax.optimization_barrier((sent, grad_query))
    down_total, up_total = run(
        sum_split_kernel, (shape_of((rank, part), F32),) * 2, (sent, *arrived), 1
    )
    return (grad_query[None], grad_passage[None], down_total, up_total)


def solution(mesh):
    in_specs = (
        P("fsdp", "dp", None),
        P("fsdp", "dp", None),
        P("fsdp", "dp", None),
        P("fsdp", "dp", None),
        P("fsdp", "dp"),
        P("fsdp", "dp", None),
        P("fsdp", None),
        P(None, "fsdp"),
        P(None, "fsdp"),
    )
    out_specs = (P("fsdp", "dp", None), P("fsdp", "dp", None), P(None, "fsdp"), P(None, "fsdp"))
    return jax.shard_map(
        per_device, mesh=mesh, in_specs=in_specs, out_specs=out_specs, check_vma=False
    )
```
